32 devices in a mesh: groups: 2 (over x), pool: 8 (over z, y), tp: 2 (over core).
Axes of the slice: x: 2, y: 2, z: 4, core: 2. Of those that a mesh axis runs over, the one named last changes fastest.
Arguments:
- x_prompt: bfloat16 [4096, 8192], P(('groups', 'pool')), parts along dimension 0, may hold values from -6 to 6
- kv_weight: bfloat16 [8192, 8, 256], P('pool', 'tp'), may hold values from -0.0625 to 0.0625
- block_dest: int32 [512, 1], P('groups'), parts along dimension 0, may hold values from 0 to 7; in each aligned block of 32 rows (0 to 31, 32 to 63, ...) at most 8 rows name the same one
- block_row: int32 [512], P('groups'), parts along dimension 0, may hold values from 0 to 7
- block_fill: int32 [512], P('groups'), parts along dimension 0, may hold values from 1 to 8
- queries: bfloat16 [128, 64, 128], P(('groups', 'pool'), 'tp'), parts along dimension 0
- kv_cache: bfloat16 [128, 256, 8, 256], P(('groups', 'pool'), None, 'tp'), parts along dimension 0
- cache_len: int32 [128], P(('groups', 'pool')), parts along dimension 0, may hold values from 2 to 256, as said below
- out_weight: bfloat16 [8192, 8192], P('tp', 'pool'), may hold values from -0.0625 to 0.0625
Outputs:
- decode_out: bfloat16 [128, 8192], P('groups', ('pool', 'tp')), parts along dimension 0
The draws below stay inside these ranges and needn't reach their ends.
There are 2 independent parts, one for each index of `groups`. The reference program is written for one: setup_inputs(seed, part) draws one part's arguments, and reference() takes and returns one part's arrays. A program takes and returns all parts, laid end to end along the dimension named above; an argument that names none is the same for every part. Nothing has to cross between parts.
Inputs may be any that keep to these rules, and one draw needn't show every extreme that they name: `block_dest`: in the blocks of one index of pool, at most 8 name the same owner index; some index receives exactly 8 from one sender. `cache_len`: every index of pool holds a request whose cache is full.
All inputs are finite; a program needn't handle non-finite values.
Results may differ from the reference program's by a relative error of at most 0.006.
Values may be sent and summed in bfloat16 or wider, within the bound.
No kernel may reach another device: no remote copies, remote signals or barrier semaphores. Data moves between devices by JAX's collectives and lax.ppermute only.
A program may use at most 128 MiB of HBM per device.

```python
import math
import jax
import jax.numpy as jnp
import numpy as np
from jax import lax

D = 8192
HQ = 64
KVH = 8
HD = 128
BLK = 8
ROWS_DEV = 8
CACHE = 256
NB_DEV = 32
NB_TOTAL = 256
TOKENS = 2048
ROWS_ALL = 64
CAP = 8
N_POOL = 8


def first_keys(key):
    return jax.random.normal(key, (ROWS_ALL, KVH, HD), jnp.float32)


def draw_kv_cache(key, part):
    leading = first_keys(key)
    key = jax.random.fold_in(key, 11)
    values = jax.random.normal(key, (ROWS_ALL, CACHE, KVH, 2 * HD), jnp.float32)
    values = values.at[:, 0, :, :HD].set(leading)
    return values.astype(jnp.bfloat16)


def draw_queries(key, part):
    key = jax.random.fold_in(key, 12)
    noise_key = jax.random.fold_in(key, 0)
    noise = jax.random.normal(noise_key, (ROWS_ALL, HQ, HD), jnp.float32)
    return noise.astype(jnp.bfloat16)


def draw_cache_len(key, part):
    key = jax.random.fold_in(key, 13)
    first, second = jax.random.split(key)
    lengths = jax.random.randint(first, (ROWS_ALL,), 2, CACHE + 1)
    full_row = jax.random.randint(second, (ROWS_ALL // ROWS_DEV,), 0, ROWS_DEV)
    full = (jnp.arange(ROWS_DEV)[None, :] == full_row[:, None]).reshape(-1)
    return jnp.where(full, CACHE, lengths).astype(jnp.int32)


def plant(entries, stream_key, smallest, high):
    longest = entries.shape.index(max(entries.shape))
    spots = []
    for shift in (0, 1):
        where = [jax.random.randint(jax.random.fold_in(stream_key, axis), (), 0, length) for axis, length in enumerate(entries.shape)]
        where[longest] = (where[longest] + shift) % entries.shape[longest]
        spots.append(tuple(where))
    return entries.at[spots[0]].set(smallest).at[spots[1]].set(high)


def levels(rng, extent, shards, smallest, top_value):
    def one(dim, blocks):
        heights = jax.random.uniform(jax.random.fold_in(jax.random.fold_in(rng, 6), dim), (blocks,), jnp.float32, smallest / len(shards), top_value / len(shards))
        return jnp.repeat(jnp.exp(heights), extent[dim] // blocks).reshape((-1,) + (1,) * (len(extent) - dim - 1))

    loudness = one(*shards[0])
    for cut in shards[1:]:
        loudness = loudness * one(*cut)
    return loudness


def assign_block(own_key, own, number, rows, amount, top, reach, slope):
    order = jax.random.permutation(own_key, amount)
    packed, usual = shares(amount, rows * top, reach, slope, True), shares(amount, rows * top, reach, slope, False)
    places = jnp.arange(amount)

    def named(tallies, rotation):
        used = int((tallies > 0).sum())
        fixed = max(1, used // 4)
        shifted = fixed + (places - fixed + rotation * (used - fixed)) % max(1, amount - fixed)
        return jnp.zeros((amount,), jnp.int32).at[order[jnp.where(places < fixed, places, shifted)]].set(jnp.asarray(tallies, jnp.int32))

    tallies = jnp.where(number % 4 == 0, named(packed, number // 4), named(usual, number - number // 4 - 1))
    mixed = jax.random.permutation(jax.random.fold_in(own, 3), amount)
    donor, receiver = mixed[0:amount // 2 * 2:2], mixed[1:amount // 2 * 2:2]
    slack = jnp.minimum(tallies[donor] - 1, reach - tallies[receiver]) // 2
    slack = jnp.where((donor == order[0]) | (receiver == order[0]) | (tallies[receiver] == 0), 0, jnp.maximum(slack, 0))
    shifted = jax.random.randint(jax.random.fold_in(own, 4), (amount // 2,), 0, 1 << 20) % (slack + 1)
    tallies = tallies.at[donor].add(-shifted).at[receiver].add(shifted)
    members = jnp.searchsorted(jnp.cumsum(tallies), jnp.arange(rows * top), side="right").astype(jnp.int32)
    grid = members.reshape(top, rows).T
    grid = grid[jax.random.permutation(jax.random.fold_in(own, 1), rows)]
    rotation = jax.random.randint(jax.random.fold_in(own, 2), (rows, 1), 0, top)
    return jnp.take_along_axis(grid, (jnp.arange(top)[None, :] + rotation) % top, axis=1)


def shares(number_of, total, bound, slope, full):
    loads = [(1 << 20) // math.isqrt(standing ** slope) + 1 for standing in range(1, number_of + 1)]
    largest = bound if full else min(bound, max(-(-total // number_of), total * loads[0] // sum(loads)))
    least = 1 if total - largest >= number_of - 1 else 0
    counts, surplus = [largest] + [least] * (number_of - 1), total - largest - least * (number_of - 1)
    while surplus > 0:
        free = [i for i in range(1, number_of) if counts[i] < largest] or [i for i in range(1, number_of) if counts[i] < bound]
        mass, remaining = sum([loads[i] for i in free]), surplus
        for i in free:
            extra = min(bound - counts[i], max(1, remaining * loads[i] // mass), surplus)
            counts[i] = counts[i] + extra
            surplus = surplus - extra
    return np.array(counts)


def scatter_about(own_key, dims, spread, reach, pieces=(), kind=jnp.bfloat16):
    entries = spread * jax.random.normal(own_key, dims, jnp.float32)
    if pieces:
        entries = entries * levels(own_key, dims, pieces, -0.22, 0.18)
    return jnp.clip(entries, -reach, reach).astype(kind)


def setup_inputs(seed: int = 0, part: int = 0) -> dict:
    seeds = jax.random.split(jax.random.key(seed), 10)
    own_keys = jax.random.split(jax.random.fold_in(seeds[9], part), 10)
    x_prompt = scatter_about(own_keys[0], (TOKENS, D), 1.0, 6.0, ((0, 8),))
    kv_weight = scatter_about(seeds[1], (D, KVH, 2 * HD), D ** -0.5, 0.0625, ((0, 8), (1, 2)))
    block_dest_keys = jax.random.split(jax.random.fold_in(own_keys[2], 1), NB_TOTAL // NB_DEV)
    block_dest_turns = jax.random.permutation(jax.random.fold_in(own_keys[2], 3), NB_TOTAL // NB_DEV)
    block_dest = jax.vmap(lambda own, number: assign_block(jax.random.fold_in(own_keys[2], 2), own, number, NB_DEV, N_POOL, 1, CAP, 2))(block_dest_keys, block_dest_turns).reshape((NB_TOTAL, 1))
    block_row = plant(jax.random.randint(own_keys[3], (NB_TOTAL,), 0, ROWS_DEV), jax.random.fold_in(own_keys[3], 1), 0, ROWS_DEV - 1).astype(jnp.int32)
    block_fill = plant(jax.random.randint(own_keys[4], (NB_TOTAL,), 1, BLK + 1), jax.random.fold_in(own_keys[4], 1), 1, BLK).astype(jnp.int32)
    queries = draw_queries(jax.random.fold_in(jax.random.fold_in(seeds[9], part), 71), part)
    kv_cache = draw_kv_cache(jax.random.fold_in(jax.random.fold_in(seeds[9], part), 71), part)
    cache_len = draw_cache_len(jax.random.fold_in(jax.random.fold_in(seeds[9], part), 71), part)
    out_weight = scatter_about(seeds[8], (HQ * HD, D), (HQ * HD) ** -0.5, 0.0625, ((0, 2), (1, 8)))
    return {"x_prompt": x_prompt, "kv_weight": kv_weight, "block_dest": block_dest, "block_row": block_row, "block_fill": block_fill, "queries": queries, "kv_cache": kv_cache, "cache_len": cache_len, "out_weight": out_weight}


def reference(x_prompt, kv_weight, block_dest, block_row, block_fill, queries, kv_cache, cache_len, out_weight):
    flat_weight = kv_weight.reshape(D, KVH * 2 * HD)
    prompt_kv = jnp.dot(x_prompt, flat_weight, preferred_element_type=jnp.float32).astype(jnp.bfloat16)
    prompt = prompt_kv.reshape(NB_TOTAL * BLK, KVH, 2 * HD).astype(jnp.float32)
    owner = (block_dest[:, 0] * ROWS_DEV + block_row).astype(jnp.int32)
    owner_tok = jnp.repeat(owner, BLK)
    position = jnp.tile(jnp.arange(BLK, dtype=jnp.int32), NB_TOTAL)
    live_tok = position < jnp.repeat(block_fill, BLK)
    prompt_keys = prompt[:, :, :HD]
    prompt_vals = prompt[:, :, HD:]
    scale = 1.0 / (HD ** 0.5)
    group = HQ // KVH

    def one_row(args):
        query, cache, length, index = args
        query = query.astype(jnp.float32).reshape(KVH, group, HD)
        cache = cache.astype(jnp.float32)
        cache_scores = jnp.einsum("kgd,tkd->kgt", query, cache[:, :, :HD]) * scale
        cache_live = jnp.arange(CACHE, dtype=jnp.int32) < length
        cache_scores = jnp.where(cache_live[None, None, :], cache_scores, -jnp.inf)
        prompt_scores = jnp.einsum("kgd,pkd->kgp", query, prompt_keys) * scale
        prompt_live = live_tok & (owner_tok == index)
        prompt_scores = jnp.where(prompt_live[None, None, :], prompt_scores, -jnp.inf)
        top = jnp.maximum(jnp.max(cache_scores, -1), jnp.max(prompt_scores, -1))
        cache_exp = jnp.exp(cache_scores - top[:, :, None])
        prompt_exp = jnp.exp(prompt_scores - top[:, :, None])
        total = jnp.sum(cache_exp, -1) + jnp.sum(prompt_exp, -1)
        cache_w = lax.optimization_barrier((cache_exp / total[:, :, None]).astype(jnp.bfloat16)).astype(jnp.float32)
        prompt_w = lax.optimization_barrier((prompt_exp / total[:, :, None]).astype(jnp.bfloat16)).astype(jnp.float32)
        mixed = jnp.einsum("kgt,tkd->kgd", cache_w, cache[:, :, HD:]) + jnp.einsum("kgp,pkd->kgd", prompt_w, prompt_vals)
        return mixed.reshape(HQ * HD).astype(jnp.bfloat16)

    attended = lax.map(one_row, (queries, kv_cache, cache_len, jnp.arange(ROWS_ALL, dtype=jnp.int32)))
    return jnp.dot(attended, out_weight, preferred_element_type=jnp.float32).astype(jnp.bfloat16)
```

```python
import jax
import jax.numpy as jnp
from jax import lax
from jax.sharding import PartitionSpec as P

BLK = 8


def local(
    x_prompt, kv_weight, block_dest, block_row, block_fill, queries, kv_cache, cache_len, out_weight
):
    n = lax.axis_size("pool")
    ntp = lax.axis_size("tp")
    me = lax.axis_index("pool")
    core = lax.axis_index("tp")
    tokens, width = x_prompt.shape
    part = width // n
    kvh = kv_weight.shape[1]
    hd = kv_weight.shape[2] // 2
    rows, heads = queries.shape[0], queries.shape[1]
    group = heads // kvh
    cache_slots = kv_cache.shape[1]
    blocks = tokens // BLK
    cap = max(2, 2 * blocks // n)
    slots = cap * BLK
    scale = 1.0 / hd**0.5

    half = tokens // ntp
    first, second = [], []
    for k in range(1, n):
        sent = lax.dynamic_slice(x_prompt, (core * half, (me ^ k) * part), (half, part))
        first.append(lax.ppermute(sent, "pool", [(i, i ^ k) for i in range(n)]))
    for got in first:
        second.append(lax.ppermute(got, "tp", [(i, (i + 1) % ntp) for i in range(ntp)]))
    own = lax.dynamic_slice(x_prompt, (0, me * part), (tokens, part))
    chunks = [own]
    for a, b in zip(first, second):
        chunks.append(jnp.where(core == 0, jnp.concatenate([a, b]), jnp.concatenate([b, a])))
    arrived = jnp.stack(chunks)

    dests = block_dest[:, 0].reshape(n, blocks)
    owners = jnp.arange(n, dtype=jnp.int32)
    hits = (dests[:, :, None] == owners[None, None, :]).astype(jnp.int32)
    ranks = jnp.sum((jnp.cumsum(hits, 1) - hits) * hits, -1)
    match = (
        (dests[None, :, None, :] == owners[:, None, None, None])
        & (ranks[None, :, None, :] == jnp.arange(cap, dtype=jnp.int32)[None, None, :, None])
    ).astype(jnp.int32)
    slot_row = jnp.sum(match * block_row.reshape(1, n, 1, blocks), -1)
    slot_fill = jnp.sum(match * block_fill.reshape(1, n, 1, blocks), -1)
    live = jnp.arange(BLK, dtype=jnp.int32) < slot_fill[..., None]
    rowof = jnp.where(live, slot_row[..., None], -1).reshape(n, n * slots)
    rowmask = rowof[:, None, :] == jnp.arange(rows, dtype=jnp.int32)[None, :, None]

    place = (
        match.astype(jnp.bfloat16)[:, :, :, None, :, None]
        * jnp.eye(BLK, dtype=jnp.bfloat16)[None, None, None, :, None, :]
    ).reshape(n, n, slots, tokens)
    place = jnp.take(place, me ^ owners, axis=1)
    padded = jnp.einsum("qkst,ktp->qksp", place, arrived, preferred_element_type=jnp.bfloat16)
    padded = jnp.take(padded, me ^ owners, axis=1).reshape(n, n * slots, part)

    allq = lax.all_gather(queries, "pool", axis=0, tiled=True).reshape(n, rows, kvh, group, hd)
    keyed = jnp.einsum(
        "qrhgd,phd->qhrgp", allq, kv_weight[:, :, :hd], preferred_element_type=jnp.float32
    ).astype(jnp.bfloat16)
    raw = jnp.einsum("qhrgp,qtp->qhrgt", keyed, padded, preferred_element_type=jnp.float32)
    raw = jnp.sum(jnp.where(rowmask[:, None, :, None, :], raw, 0.0), 2)
    parts = lax.all_to_all(raw, "pool", split_axis=0, concat_axis=0, tiled=True)
    scores = jnp.sum(parts, 0) * scale

    mymask = lax.dynamic_index_in_dim(rowmask, me, 0, keepdims=False)
    prompt_scores = jnp.where(mymask[:, None, None, :], scores[None], -jnp.inf)
    query = queries.reshape(rows, kvh, group, hd)
    cache_scores = (
        jnp.einsum(
            "rhgd,rthd->rhgt", query, kv_cache[:, :, :, :hd], preferred_element_type=jnp.float32
        )
        * scale
    )
    cache_live = jnp.arange(cache_slots, dtype=jnp.int32)[None, :] < cache_len[:, None]
    cache_scores = jnp.where(cache_live[:, None, None, :], cache_scores, -jnp.inf)
    top = jnp.maximum(jnp.max(cache_scores, -1), jnp.max(prompt_scores, -1))
    cache_exp = jnp.exp(cache_scores - top[..., None])
    prompt_exp = jnp.exp(prompt_scores - top[..., None])
    total = jnp.sum(cache_exp, -1) + jnp.sum(prompt_exp, -1)
    cache_w = (cache_exp / total[..., None]).astype(jnp.bfloat16)
    prompt_w = jnp.sum(prompt_exp / total[..., None], 0).astype(jnp.bfloat16)
    cached = jnp.einsum(
        "rhgt,rthd->rhgd", cache_w, kv_cache[:, :, :, hd:], preferred_element_type=jnp.float32
    )

    allw = lax.all_gather(prompt_w, "pool", axis=0)
    spread = jnp.where(rowmask[:, None, :, None, :], allw[:, :, None], 0).astype(jnp.bfloat16)
    mixed = jnp.einsum(
        "qhrgt,qtp->qhrgp", spread, padded, preferred_element_type=jnp.float32
    ).astype(jnp.bfloat16)
    terms = jnp.einsum(
        "qhrgp,phd->qrhgd", mixed, kv_weight[:, :, hd:], preferred_element_type=jnp.float32
    ).astype(jnp.bfloat16)
    total_terms = cached
    for k in range(n):
        sent = lax.dynamic_index_in_dim(terms, me ^ k, 0, keepdims=False)
        if k:
            sent = lax.ppermute(sent, "pool", [(i, i ^ k) for i in range(n)])
        total_terms = total_terms + sent.astype(jnp.float32)
    attended = total_terms.reshape(rows, heads * hd).astype(jnp.bfloat16)

    cols = out_weight.shape[1] // ntp
    weights = []
    for j in range(ntp):
        piece = lax.dynamic_slice(
            out_weight, (0, ((core + j) % ntp) * cols), (out_weight.shape[0], cols)
        )
        if j:
            piece = lax.ppermute(piece, "tp", [(i, (i + j) % ntp) for i in range(ntp)])
        weights.append(piece)
    full = lax.all_gather(attended, ("tp", "pool"), axis=0).reshape(ntp, n * rows, heads * hd)
    out = jnp.zeros((n * rows, cols), jnp.float32)
    for j in range(ntp):
        out = out + jnp.dot(
            lax.dynamic_index_in_dim(full, (core - j) % ntp, 0, keepdims=False),
            weights[j],
            preferred_element_type=jnp.float32,
        )
    return out.astype(jnp.bfloat16)


def solution(mesh):
    in_specs = (
        P(("groups", "pool"), None),
        P("pool", "tp", None),
        P("groups", None),
        P("groups"),
        P("groups"),
        P(("groups", "pool"), "tp", None),
        P(("groups", "pool"), None, "tp", None),
        P(("groups", "pool")),
        P("tp", "pool"),
    )
    out_specs = P("groups", ("pool", "tp"))
    return jax.shard_map(local, mesh=mesh, in_specs=in_specs, out_specs=out_specs, check_vma=False)
```

```python
import functools

import jax
import jax.numpy as jnp
from jax import lax
from jax.experimental import pallas as pl
from jax.experimental.pallas import tpu as pltpu
from jax.sharding import PartitionSpec as P

BLK = 8
MIB = 1 << 20


def score_kernel(rows, src_ref, core_ref, mine_ref, other_ref, keyed_ref, row_ref, out_ref, slot_ref, wide):
    q = pl.program_id(0)
    held = mine_ref.shape[0]
    step = 256

    @pl.when(q == 0)
    def _():
        core = core_ref[0]
        for side, ref in ((core, mine_ref), (1 - core, other_ref)):
            for i in range(0, held, step):
                wide[pl.ds(pl.multiple_of(side * held + i, step), step), :] = ref[
                    i : i + step, :
                ].astype(jnp.float32)

    slots = slot_ref.shape[1]
    count = slots // BLK
    for i in range(0, count, 2):
        pair = [
            wide[pl.ds(pl.multiple_of(src_ref[q * count + i + j] * BLK, BLK), BLK), :]
            for j in range(2)
        ]
        slot_ref[0, i * BLK : (i + 2) * BLK, :] = jnp.concatenate(pair).astype(jnp.bfloat16)
    kvh, per, part = keyed_ref.shape
    raw = lax.dot_general(
        keyed_ref[...].reshape(kvh * per, part),
        slot_ref[0],
        (((1,), (1,)), ((), ())),
        preferred_element_type=jnp.float32,
    ).reshape(kvh, rows, per // rows, slots)
    owner_row = row_ref[0]
    picked = jnp.zeros((kvh, per // rows, slots), jnp.float32)
    for r in range(rows):
        picked = picked + jnp.where((owner_row == r)[None], raw[:, r], 0.0)
    out_ref[0] = picked.reshape(kvh * (per // rows), slots).astype(out_ref.dtype)


def weight_kernel(scale, parts_ref, row_ref, top_ref, sum_ref, cached_ref, w_ref, kept_ref):
    n = parts_ref.shape[0]
    scores = parts_ref[0].astype(jnp.float32)
    for i in range(1, n):
        scores = scores + parts_ref[i].astype(jnp.float32)
    scores = scores * scale
    owner_row = row_ref[...]
    weights = jnp.zeros(scores.shape, jnp.float32)
    for r in range(top_ref.shape[0]):
        own = jnp.where(owner_row == r, scores, -jnp.inf)
        cache_top = top_ref[r]
        top = jnp.maximum(jnp.max(own, 1, keepdims=True), cache_top)
        held = jnp.exp(own - top)
        fade = jnp.exp(cache_top - top)
        total = jnp.sum(held, 1, keepdims=True) + sum_ref[r] * fade
        weights = weights + held / total
        kept_ref[r] = cached_ref[r] * (fade / total)
    weights = weights.astype(w_ref.dtype)
    for i in range(n):
        w_ref[i] = weights


def value_kernel(rows, w_ref, row_ref, slot_ref, value_ref, out_ref, mixed):
    q = pl.program_id(0)
    kvh = value_ref.shape[0]
    heads, slots = w_ref.shape[1:]
    per = rows * heads // kvh
    weights = w_ref[0].astype(jnp.float32).reshape(kvh, 1, heads // kvh, slots)
    owner_row = row_ref[0]
    spread = jnp.concatenate(
        [jnp.where((owner_row == r)[None, None], weights, 0.0) for r in range(rows)], 1
    ).reshape(kvh * per, slots)
    got = jnp.dot(
        spread.astype(jnp.bfloat16), slot_ref[0], preferred_element_type=jnp.float32
    ).astype(jnp.bfloat16)
    for h in range(kvh):
        mixed[h, pl.ds(pl.multiple_of(q * per, per), per), :] = got[h * per : (h + 1) * per]

    @pl.when(q == pl.num_programs(0) - 1)
    def _():
        n = out_ref.shape[0]
        for h in range(kvh):
            done = jnp.dot(mixed[h], value_ref[h], preferred_element_type=jnp.float32)
            out_ref[:, h] = done.reshape(n, per, done.shape[1]).astype(out_ref.dtype)


def sum_kernel(parts_ref, kept_ref, out_ref, total):
    n, kvh, per, hd = parts_ref.shape
    rows, heads = kept_ref.shape[:2]
    group = heads // kvh
    for h in range(kvh):
        terms = parts_ref[0, h].astype(jnp.float32)
        for i in range(1, n):
            terms = terms + parts_ref[i, h].astype(jnp.float32)
        for r in range(rows):
            here = slice((h * rows + r) * group, (h * rows + r + 1) * group)
            total[here, :] = (
                terms[r * group : (r + 1) * group] + kept_ref[r, h * group : (h + 1) * group, :]
            )
    pieces = [
        total[pl.ds(h * per + g, rows, stride=group), :]
        for h in range(kvh)
        for g in range(group)
    ]
    attended = jnp.concatenate(pieces, 1).astype(out_ref.dtype)
    for i in range(n):
        out_ref[i] = attended


def everywhere(x, n):
    at = 0
    k = n // 2
    while k >= 1:
        got = lax.ppermute(x, "pool", [(i, i ^ k) for i in range(n)])
        low = (lax.axis_index("pool") & k) == 0
        x = jnp.where(low, jnp.stack([x, got], at), jnp.stack([got, x], at))
        at += 1
        k //= 2
    return x.reshape((n,) + x.shape[at:])


def local(
    x_prompt, kv_weight, block_dest, block_row, block_fill, queries, kv_cache, cache_len, out_weight
):
    n = lax.axis_size("pool")
    ntp = lax.axis_size("tp")
    me = lax.axis_index("pool")
    core = lax.axis_index("tp")
    tokens, width = x_prompt.shape
    part = width // n
    kvh = kv_weight.shape[1]
    hd = kv_weight.shape[2] // 2
    rows, heads = queries.shape[0], queries.shape[1]
    group = heads // kvh
    per = rows * group
    cache_slots = kv_cache.shape[1]
    blocks = tokens // BLK
    cap = max(2, 2 * blocks // n)
    count = n * cap
    slots = count * BLK
    half = tokens // ntp
    scale = 1.0 / hd**0.5
    swap = [(i, (i + 1) % ntp) for i in range(ntp)]

    sent = lax.dynamic_slice_in_dim(x_prompt, core * half, half, 0)
    sent = sent.reshape(half, n, part).transpose(1, 0, 2)
    mine = lax.all_to_all(sent, "pool", 0, 0, tiled=True).reshape(n * half, part)
    other = lax.ppermute(mine, "tp", swap)

    dest = block_dest[:, 0]
    index = jnp.arange(n * blocks, dtype=jnp.int32)
    sender = index // blocks
    key = dest * n + sender
    earlier = (key[:, None] == key[None, :]) & (index[None, :] < index[:, None])
    rank = jnp.sum(earlier.astype(jnp.int32), 1)
    hit = (
        jnp.arange(n * count, dtype=jnp.int32)[:, None] == (key * cap + rank)[None, :]
    ).astype(jnp.int32)
    inner = index % blocks
    held = half // BLK
    source = (inner // held) * (n * held) + sender * held + inner % held
    slot_src = jnp.sum(hit * source[None, :], 1)
    slot_row = jnp.sum(hit * (block_row + 1)[None, :], 1) - 1
    slot_fill = jnp.sum(hit * block_fill[None, :], 1)
    live = jnp.arange(BLK, dtype=jnp.int32)[None, :] < slot_fill[:, None]
    rowof = jnp.where(live, slot_row[:, None], -1).reshape(n, 1, slots)

    allq = everywhere(queries, n).reshape(n, rows, kvh, group, hd)
    keyed = jnp.einsum(
        "qrhgd,phd->hqrgp", allq, kv_weight[:, :, :hd], preferred_element_type=jnp.float32
    ).astype(jnp.bfloat16)
    keyed = keyed.reshape(kvh, n * per, part)
    values = kv_weight[:, :, hd:].transpose(1, 0, 2)

    query = queries.reshape(rows, kvh, group, hd)
    cache_scores = (
        jnp.einsum(
            "rhgd,rthd->rhgt", query, kv_cache[:, :, :, :hd], preferred_element_type=jnp.float32
        )
        * scale
    )
    cache_live = jnp.arange(cache_slots, dtype=jnp.int32)[None, :] < cache_len[:, None]
    cache_scores = jnp.where(cache_live[:, None, None, :], cache_scores, -jnp.inf)
    cache_top = jnp.max(cache_scores, -1, keepdims=True)
    cache_exp = jnp.exp(cache_scores - cache_top)
    cache_sum = jnp.sum(cache_exp, -1, keepdims=True)
    cached = jnp.einsum(
        "rhgt,rthd->rhgd",
        cache_exp.astype(jnp.bfloat16),
        kv_cache[:, :, :, hd:],
        preferred_element_type=jnp.float32,
    )

    partial_scores, slot_x = pl.pallas_call(
        functools.partial(score_kernel, rows),
        grid_spec=pltpu.PrefetchScalarGridSpec(
            num_scalar_prefetch=2,
            grid=(n,),
            in_specs=[
                pl.BlockSpec((n * half, part), lambda q, *_: (0, 0)),
                pl.BlockSpec((n * half, part), lambda q, *_: (0, 0)),
                pl.BlockSpec((kvh, per, part), lambda q, *_: (0, q, 0)),
                pl.BlockSpec((1, 1, slots), lambda q, *_: (q, 0, 0)),
            ],
            out_specs=[
                pl.BlockSpec((1, heads, slots), lambda q, *_: (q, 0, 0)),
                pl.BlockSpec((1, slots, part), lambda q, *_: (q, 0, 0)),
            ],
            scratch_shapes=[pltpu.VMEM((ntp * n * half, part), jnp.float32)],
        ),
        out_shape=[
            jax.ShapeDtypeStruct((n, heads, slots), jnp.bfloat16),
            jax.ShapeDtypeStruct((n, slots, part), jnp.bfloat16),
        ],
        compiler_params=pltpu.CompilerParams(vmem_limit_bytes=32 * MIB),
        name="prompt_scores",
    )(slot_src, core.astype(jnp.int32).reshape(1), mine, other, keyed, rowof)

    parts = lax.all_to_all(partial_scores, "pool", 0, 0, tiled=True)
    my_rows = lax.dynamic_index_in_dim(rowof, me, 0, keepdims=False)
    weights, kept = pl.pallas_call(
        functools.partial(weight_kernel, scale),
        out_shape=[
            jax.ShapeDtypeStruct((n, heads, slots), jnp.bfloat16),
            jax.ShapeDtypeStruct((rows, heads, hd), jnp.float32),
        ],
        compiler_params=pltpu.CompilerParams(vmem_limit_bytes=16 * MIB),
        name="softmax_weights",
    )(
        parts,
        my_rows,
        cache_top.reshape(rows, heads, 1),
        cache_sum.reshape(rows, heads, 1),
        cached.reshape(rows, heads, hd),
    )

    all_weights = lax.all_to_all(weights, "pool", 0, 0, tiled=True)
    terms = pl.pallas_call(
        functools.partial(value_kernel, rows),
        grid=(n,),
        in_specs=[
            pl.BlockSpec((1, heads, slots), lambda q: (q, 0, 0)),
            pl.BlockSpec((1, 1, slots), lambda q: (q, 0, 0)),
            pl.BlockSpec((1, slots, part), lambda q: (q, 0, 0)),
            pl.BlockSpec((kvh, part, hd), lambda q: (0, 0, 0)),
        ],
        out_specs=pl.BlockSpec((n, kvh, per, hd), lambda q: (0, 0, 0, 0)),
        out_shape=jax.ShapeDtypeStruct((n, kvh, per, hd), jnp.bfloat16),
        scratch_shapes=[pltpu.VMEM((kvh, n * per, part), jnp.bfloat16)],
        compiler_params=pltpu.CompilerParams(vmem_limit_bytes=24 * MIB),
        name="weighted_values",
    )(all_weights, rowof, slot_x, values)

    term_parts = lax.all_to_all(terms, "pool", 0, 0, tiled=True)
    attended = pl.pallas_call(
        sum_kernel,
        out_shape=jax.ShapeDtypeStruct((n, rows, heads * hd), jnp.bfloat16),
        scratch_shapes=[pltpu.VMEM((kvh * per, hd), jnp.float32)],
        compiler_params=pltpu.CompilerParams(vmem_limit_bytes=16 * MIB),
        name="attended_sum",
    )(term_parts, kept)

    everyone = lax.all_to_all(attended, "pool", 0, 0, tiled=True).reshape(n * rows, heads * hd)
    product = jnp.dot(everyone, out_weight, preferred_element_type=jnp.float32)
    cols = out_weight.shape[1] // ntp
    out = lax.dynamic_slice_in_dim(product, core * cols, cols, 1)
    for j in range(1, ntp):
        away = lax.dynamic_slice_in_dim(product, ((core + j) % ntp) * cols, cols, 1)
        out = out + lax.ppermute(away, "tp", [(i, (i + j) % ntp) for i in range(ntp)])
    return out.astype(jnp.bfloat16)


def solution(mesh):
    in_specs = (
        P(("groups", "pool"), None),
        P("pool", "tp", None),
        P("groups", None),
        P("groups"),
        P("groups"),
        P(("groups", "pool"), "tp", None),
        P(("groups", "pool"), None, "tp", None),
        P(("groups", "pool")),
        P("tp", "pool"),
    )
    out_specs = P("groups", ("pool", "tp"))
    return jax.shard_map(local, mesh=mesh, in_specs=in_specs, out_specs=out_specs, check_vma=False)
```

```python
import functools

import jax
import jax.numpy as jnp
from jax import lax
from jax.experimental import pallas as pl
from jax.experimental.pallas import tpu as pltpu
from jax.sharding import PartitionSpec as P

BLK = 8
MIB = 1 << 20


def score_kernel(rows, pieces, src_ref, core_ref, *refs):
    keyed_ref, row_ref, out_ref, slot_ref, wide = refs[2 * pieces :]
    q = pl.program_id(0)
    held = refs[0].shape[0]
    step = 256

    @pl.when(q == 0)
    def _():
        core = core_ref[0]
        for j in range(2 * pieces):
            side = core if j < pieces else 1 - core
            base = (side * pieces + j % pieces) * held
            for i in range(0, held, step):
                wide[pl.ds(pl.multiple_of(base + i, step), step), :] = refs[j][
                    i : i + step, :
                ].astype(jnp.float32)

    slots = slot_ref.shape[1]
    count = slots // BLK
    for i in range(0, count, 2):
        pair = [
            wide[pl.ds(pl.multiple_of(src_ref[q * count + i + j] * BLK, BLK), BLK), :]
            for j in range(2)
        ]
        slot_ref[0, i * BLK : (i + 2) * BLK, :] = jnp.concatenate(pair).astype(jnp.bfloat16)
    kvh, per, part = keyed_ref.shape
    raw = lax.dot_general(
        keyed_ref[...].reshape(kvh * per, part),
        slot_ref[0],
        (((1,), (1,)), ((), ())),
        preferred_element_type=jnp.float32,
    ).reshape(kvh, rows, per // rows, slots)
    owner_row = row_ref[0]
    picked = jnp.zeros((kvh, per // rows, slots), jnp.float32)
    for r in range(rows):
        picked = picked + jnp.where((owner_row == r)[None], raw[:, r], 0.0)
    out_ref[0] = picked.reshape(kvh * (per // rows), slots).astype(out_ref.dtype)


def weight_kernel(scale, parts_ref, row_ref, top_ref, sum_ref, cached_ref, w_ref, kept_ref):
    n = parts_ref.shape[0]
    scores = parts_ref[0].astype(jnp.float32)
    for i in range(1, n):
        scores = scores + parts_ref[i].astype(jnp.float32)
    scores = scores * scale
    owner_row = row_ref[...]
    weights = jnp.zeros(scores.shape, jnp.float32)
    for r in range(top_ref.shape[0]):
        own = jnp.where(owner_row == r, scores, -jnp.inf)
        cache_top = top_ref[r]
        top = jnp.maximum(jnp.max(own, 1, keepdims=True), cache_top)
        held = jnp.exp(own - top)
        fade = jnp.exp(cache_top - top)
        total = jnp.sum(held, 1, keepdims=True) + sum_ref[r] * fade
        weights = weights + held / total
        kept_ref[r] = cached_ref[r] * (fade / total)
    weights = weights.astype(w_ref.dtype)
    for i in range(n):
        w_ref[i] = weights


def value_kernel(rows, w_ref, row_ref, slot_ref, value_ref, out_ref, mixed):
    q = pl.program_id(0)
    kvh = value_ref.shape[0]
    heads, slots = w_ref.shape[1:]
    per = rows * heads // kvh
    weights = w_ref[0].astype(jnp.float32).reshape(kvh, 1, heads // kvh, slots)
    owner_row = row_ref[0]
    spread = jnp.concatenate(
        [jnp.where((owner_row == r)[None, None], weights, 0.0) for r in range(rows)], 1
    ).reshape(kvh * per, slots)
    got = jnp.dot(
        spread.astype(jnp.bfloat16), slot_ref[0], preferred_element_type=jnp.float32
    ).astype(jnp.bfloat16)
    for h in range(kvh):
        mixed[h, pl.ds(pl.multiple_of(q * per, per), per), :] = got[h * per : (h + 1) * per]

    @pl.when(q == pl.num_programs(0) - 1)
    def _():
        n = out_ref.shape[0]
        for h in range(kvh):
            done = jnp.dot(mixed[h], value_ref[h], preferred_element_type=jnp.float32)
            out_ref[:, h] = done.reshape(n, per, done.shape[1]).astype(out_ref.dtype)


def sum_kernel(parts_ref, kept_ref, out_ref, total):
    n, kvh, per, hd = parts_ref.shape
    rows, heads = kept_ref.shape[:2]
    group = heads // kvh
    for h in range(kvh):
        terms = parts_ref[0, h].astype(jnp.float32)
        for i in range(1, n):
            terms = terms + parts_ref[i, h].astype(jnp.float32)
        for r in range(rows):
            here = slice((h * rows + r) * group, (h * rows + r + 1) * group)
            total[here, :] = (
                terms[r * group : (r + 1) * group] + kept_ref[r, h * group : (h + 1) * group, :]
            )
    pieces = [
        total[pl.ds(h * per + g, rows, stride=group), :]
        for h in range(kvh)
        for g in range(group)
    ]
    attended = jnp.concatenate(pieces, 1).astype(out_ref.dtype)
    for i in range(n):
        out_ref[i] = attended


def pack_kernel(core_ref, x_ref, *out_refs):
    size = out_refs[0].shape[1]
    for i, out_ref in enumerate(out_refs):
        out_ref[0] = x_ref[i * size : (i + 1) * size, :]


def everywhere(x, n):
    at = 0
    k = n // 2
    while k >= 1:
        got = lax.ppermute(x, "pool", [(i, i ^ k) for i in range(n)])
        low = (lax.axis_index("pool") & k) == 0
        x = jnp.where(low, jnp.stack([x, got], at), jnp.stack([got, x], at))
        at += 1
        k //= 2
    return x.reshape((n,) + x.shape[at:])


def local(
    x_prompt, kv_weight, block_dest, block_row, block_fill, queries, kv_cache, cache_len, out_weight
):
    n = lax.axis_size("pool")
    ntp = lax.axis_size("tp")
    me = lax.axis_index("pool")
    core = lax.axis_index("tp")
    tokens, width = x_prompt.shape
    part = width // n
    kvh = kv_weight.shape[1]
    hd = kv_weight.shape[2] // 2
    rows, heads = queries.shape[0], queries.shape[1]
    group = heads // kvh
    per = rows * group
    cache_slots = kv_cache.shape[1]
    blocks = tokens // BLK
    cap = max(2, 2 * blocks // n)
    count = n * cap
    slots = count * BLK
    half = tokens // ntp
    scale = 1.0 / hd**0.5
    swap = [(i, (i + 1) % ntp) for i in range(ntp)]

    pieces = 2
    size = half // pieces
    which = core.astype(jnp.int32).reshape(1)
    packed = pl.pallas_call(
        pack_kernel,
        grid_spec=pltpu.PrefetchScalarGridSpec(
            num_scalar_prefetch=1,
            grid=(n,),
            in_specs=[pl.BlockSpec((half, part), lambda q, c: (c[0], q))],
            out_specs=[pl.BlockSpec((1, size, part), lambda q, c: (q, 0, 0))] * pieces,
        ),
        out_shape=[jax.ShapeDtypeStruct((n, size, part), jnp.bfloat16)] * pieces,
        compiler_params=pltpu.CompilerParams(vmem_limit_bytes=16 * MIB),
        name="pack_columns",
    )(which, x_prompt)
    mine = [lax.all_to_all(p, "pool", 0, 0, tiled=True).reshape(n * size, part) for p in packed]

    dest = block_dest[:, 0]
    index = jnp.arange(n * blocks, dtype=jnp.int32)
    sender = index // blocks
    key = dest * n + sender
    earlier = (key[:, None] == key[None, :]) & (index[None, :] < index[:, None])
    rank = jnp.sum(earlier.astype(jnp.int32), 1)
    hit = (
        jnp.arange(n * count, dtype=jnp.int32)[:, None] == (key * cap + rank)[None, :]
    ).astype(jnp.int32)
    inner = index % blocks
    held = size // BLK
    source = (inner // held) * (n * held) + sender * held + inner % held
    slot_src = jnp.sum(hit * source[None, :], 1)
    slot_row = jnp.sum(hit * (block_row + 1)[None, :], 1) - 1
    slot_fill = jnp.sum(hit * block_fill[None, :], 1)
    live = jnp.arange(BLK, dtype=jnp.int32)[None, :] < slot_fill[:, None]
    rowof = jnp.where(live, slot_row[:, None], -1).reshape(n, 1, slots)

    allq = everywhere(queries, n).reshape(n, rows, kvh, group, hd)
    keyed = jnp.einsum(
        "qrhgd,phd->hqrgp", allq, kv_weight[:, :, :hd], preferred_element_type=jnp.float32
    ).astype(jnp.bfloat16)
    keyed = keyed.reshape(kvh, n * per, part)
    values = kv_weight[:, :, hd:].transpose(1, 0, 2)

    query = queries.reshape(rows, kvh, group, hd)
    cache_scores = (
        jnp.einsum(
            "rhgd,rthd->rhgt", query, kv_cache[:, :, :, :hd], preferred_element_type=jnp.float32
        )
        * scale
    )
    cache_live = jnp.arange(cache_slots, dtype=jnp.int32)[None, :] < cache_len[:, None]
    cache_scores = jnp.where(cache_live[:, None, None, :], cache_scores, -jnp.inf)
    cache_top = jnp.max(cache_scores, -1, keepdims=True)
    cache_exp = jnp.exp(cache_scores - cache_top)
    cache_sum = jnp.sum(cache_exp, -1, keepdims=True)
    cached = jnp.einsum(
        "rhgt,rthd->rhgd",
        cache_exp.astype(jnp.bfloat16),
        kv_cache[:, :, :, hd:],
        preferred_element_type=jnp.float32,
    )

    mine[-1], slot_src, rowof, keyed, values, cache_top, cache_sum, cached = (
        lax.optimization_barrier(
            (mine[-1], slot_src, rowof, keyed, values, cache_top, cache_sum, cached)
        )
    )
    other = [lax.ppermute(m, "tp", swap) for m in mine]

    partial_scores, slot_x = pl.pallas_call(
        functools.partial(score_kernel, rows, pieces),
        grid_spec=pltpu.PrefetchScalarGridSpec(
            num_scalar_prefetch=2,
            grid=(n,),
            in_specs=[
                *[pl.BlockSpec((n * size, part), lambda q, *_: (0, 0))] * (2 * pieces),
                pl.BlockSpec((kvh, per, part), lambda q, *_: (0, q, 0)),
                pl.BlockSpec((1, 1, slots), lambda q, *_: (q, 0, 0)),
            ],
            out_specs=[
                pl.BlockSpec((1, heads, slots), lambda q, *_: (q, 0, 0)),
                pl.BlockSpec((1, slots, part), lambda q, *_: (q, 0, 0)),
            ],
            scratch_shapes=[pltpu.VMEM((ntp * n * half, part), jnp.float32)],
        ),
        out_shape=[
            jax.ShapeDtypeStruct((n, heads, slots), jnp.bfloat16),
            jax.ShapeDtypeStruct((n, slots, part), jnp.bfloat16),
        ],
        compiler_params=pltpu.CompilerParams(vmem_limit_bytes=56 * MIB),
        name="prompt_scores",
    )(slot_src, which, *mine, *other, keyed, rowof)

    parts = lax.all_to_all(partial_scores, "pool", 0, 0, tiled=True)
    my_rows = lax.dynamic_index_in_dim(rowof, me, 0, keepdims=False)
    weights, kept = pl.pallas_call(
        functools.partial(weight_kernel, scale),
        out_shape=[
            jax.ShapeDtypeStruct((n, heads, slots), jnp.bfloat16),
            jax.ShapeDtypeStruct((rows, heads, hd), jnp.float32),
        ],
        compiler_params=pltpu.CompilerParams(vmem_limit_bytes=16 * MIB),
        name="softmax_weights",
    )(
        parts,
        my_rows,
        cache_top.reshape(rows, heads, 1),
        cache_sum.reshape(rows, heads, 1),
        cached.reshape(rows, heads, hd),
    )

    all_weights = lax.all_to_all(weights, "pool", 0, 0, tiled=True)
    terms = pl.pallas_call(
        functools.partial(value_kernel, rows),
        grid=(n,),
        in_specs=[
            pl.BlockSpec((1, heads, slots), lambda q: (q, 0, 0)),
            pl.BlockSpec((1, 1, slots), lambda q: (q, 0, 0)),
            pl.BlockSpec((1, slots, part), lambda q: (q, 0, 0)),
            pl.BlockSpec((kvh, part, hd), lambda q: (0, 0, 0)),
        ],
        out_specs=pl.BlockSpec((n, kvh, per, hd), lambda q: (0, 0, 0, 0)),
        out_shape=jax.ShapeDtypeStruct((n, kvh, per, hd), jnp.bfloat16),
        scratch_shapes=[pltpu.VMEM((kvh, n * per, part), jnp.bfloat16)],
        compiler_params=pltpu.CompilerParams(vmem_limit_bytes=56 * MIB),
        name="weighted_values",
    )(all_weights, rowof, slot_x, values)

    term_parts = lax.all_to_all(terms, "pool", 0, 0, tiled=True)
    attended = pl.pallas_call(
        sum_kernel,
        out_shape=jax.ShapeDtypeStruct((n, rows, heads * hd), jnp.bfloat16),
        scratch_shapes=[pltpu.VMEM((kvh * per, hd), jnp.float32)],
        compiler_params=pltpu.CompilerParams(vmem_limit_bytes=16 * MIB),
        name="attended_sum",
    )(term_parts, kept)

    everyone = lax.all_to_all(attended, "pool", 0, 0, tiled=True).reshape(n * rows, heads * hd)
    product = jnp.dot(everyone, out_weight, preferred_element_type=jnp.float32)
    cols = out_weight.shape[1] // ntp
    out = lax.dynamic_slice_in_dim(product, core * cols, cols, 1)
    for j in range(1, ntp):
        away = lax.dynamic_slice_in_dim(product, ((core + j) % ntp) * cols, cols, 1)
        out = out + lax.ppermute(away, "tp", [(i, (i + j) % ntp) for i in range(ntp)])
    return out.astype(jnp.bfloat16)


def solution(mesh):
    in_specs = (
        P(("groups", "pool"), None),
        P("pool", "tp", None),
        P("groups", None),
        P("groups"),
        P("groups"),
        P(("groups", "pool"), "tp", None),
        P(("groups", "pool"), None, "tp", None),
        P(("groups", "pool")),
        P("tp", "pool"),
    )
    out_specs = P("groups", ("pool", "tp"))
    return jax.shard_map(local, mesh=mesh, in_specs=in_specs, out_specs=out_specs, check_vma=False)
```

```python
import functools

import jax
import jax.numpy as jnp
from jax import lax
from jax.experimental import pallas as pl
from jax.experimental.pallas import tpu as pltpu
from jax.sharding import PartitionSpec as P

BLK = 8
MIB = 1 << 20


def pack_kernel(base, at_ref, fill_ref, *refs):
    *x_refs, out_ref, ranks, pick = refs
    q = pl.program_id(0)
    rows = out_ref.shape[1]
    tokens = ranks.shape[1]

    @pl.when(q == 0)
    def _():
        fills = fill_ref[...].astype(jnp.float32)
        blocks = fills.shape[1]
        block = lax.broadcasted_iota(jnp.int32, (blocks, tokens), 0)
        token = lax.broadcasted_iota(jnp.int32, (blocks, tokens), 1) // BLK
        fill = jnp.dot(
            fills, (block == token).astype(jnp.float32), preferred_element_type=jnp.float32
        )
        ahead = jnp.dot(
            fills, (block < token).astype(jnp.float32), preferred_element_type=jnp.float32
        )
        place = lax.broadcasted_iota(jnp.int32, fill.shape, 1) % BLK
        rank = ahead.astype(jnp.int32) + place
        ranks[...] = jnp.where(place < fill.astype(jnp.int32), rank, -1)
        wanted = (
            base + at_ref[1] * rows + lax.broadcasted_iota(jnp.int32, (rows, tokens), 0)
        )
        pick[...] = (wanted == ranks[pl.ds(at_ref[0], 1), :]).astype(pick.dtype)

    x = jnp.concatenate([ref[...] for ref in x_refs])
    out_ref[0] = jnp.dot(pick[...], x, preferred_element_type=jnp.float32).astype(out_ref.dtype)


def pack(x_prompt, fills, at, base, size):
    tokens, width = x_prompt.shape
    n = fills.shape[0]
    part = width // n
    cuts = 4
    return pl.pallas_call(
        functools.partial(pack_kernel, base),
        grid_spec=pltpu.PrefetchScalarGridSpec(
            num_scalar_prefetch=1,
            grid=(n,),
            in_specs=[pl.BlockSpec(fills.shape, lambda q, a: (0, 0))]
            + [
                pl.BlockSpec((tokens // cuts, part), functools.partial(lambda i, q, a: (i, q), i))
                for i in range(cuts)
            ],
            out_specs=pl.BlockSpec((1, size, part), lambda q, a: (q, 0, 0)),
            scratch_shapes=[
                pltpu.VMEM((n, tokens), jnp.int32),
                pltpu.VMEM((size, tokens), jnp.bfloat16),
            ],
        ),
        out_shape=jax.ShapeDtypeStruct((n, size, part), jnp.bfloat16),
        compiler_params=pltpu.CompilerParams(vmem_limit_bytes=56 * MIB),
        name="pack_live_tokens",
    )(at, fills, *([x_prompt] * cuts))


def score_kernel(
    rows, meta_ref, mine_ref, other_ref, more_mine_ref, more_other_ref, keyed_ref, row_ref,
    out_ref, tile_ref, first, last, wide, line, tiles, in_sem, out_sem,
):
    q = pl.program_id(0)
    n, count = tiles.shape[0], (meta_ref.shape[0] - 2) // (2 * tiles.shape[0]) - 1
    size, extra = first.shape[1] // n, last.shape[1] // n
    tokens = 2 * (size + extra)
    tile, part = tile_ref.shape[2:]
    lanes = wide.shape[1]
    blocks_here = meta_ref[2 * n * count + q]
    rows_here = meta_ref[2 * n * count + n + q]
    core = meta_ref[2 * n * (count + 1)]
    over = meta_ref[2 * n * (count + 1) + 1]
    cuts = in_sem.shape[1]
    span = n * size // cuts

    @pl.when(q == 0)
    def _():
        copies = [
            pltpu.make_async_copy(
                ref.at[pl.ds(i * span, span)], first.at[j, pl.ds(i * span, span)], in_sem.at[j, i]
            )
            for i in range(cuts)
            for j, ref in enumerate((mine_ref, other_ref))
        ]
        for copy in copies:
            copy.start()

        @pl.loop(0, line.shape[0] // (BLK * BLK))
        def _(i):
            line[pl.ds(pl.multiple_of(i * BLK * BLK, BLK), BLK * BLK), :] = jnp.zeros(
                (BLK * BLK, lanes), line.dtype
            )

        wide[n * tokens * BLK :, :] = jnp.zeros((BLK * BLK, lanes), wide.dtype)
        for copy in copies:
            copy.wait()

        def widen(held, j, s, at, length):
            for k in range(part // lanes):
                wide[pl.ds(at * BLK + k, length, stride=BLK), :] = held[
                    j,
                    pl.ds(pl.multiple_of(s * length, length), length),
                    k * lanes : (k + 1) * lanes,
                ].astype(wide.dtype)

        @pl.loop(0, n)
        def _(s):
            for j in range(2):
                side = core if j == 0 else 1 - core
                widen(first, j, s, s * tokens + side * size, size)

        @pl.when(over == 0)
        def _():
            @pl.loop(0, n)
            def _(s):
                at = pl.multiple_of((s * tokens + 2 * size) * BLK, BLK)
                wide[pl.ds(at, 2 * extra * BLK), :] = jnp.zeros(
                    (2 * extra * BLK, lanes), wide.dtype
                )

        @pl.when(over != 0)
        def _():
            rest = [
                pltpu.make_async_copy(ref, last.at[j], in_sem.at[j, 0])
                for j, ref in enumerate((more_mine_ref, more_other_ref))
            ]
            for copy in rest:
                copy.start()
            for copy in rest:
                copy.wait()

            @pl.loop(0, n)
            def _(s):
                for j in range(2):
                    side = core if j == 0 else 1 - core
                    widen(last, j, s, s * tokens + 2 * size + side * extra, extra)

    @pl.loop(0, blocks_here)
    def _(i):
        source = pl.multiple_of(meta_ref[q * count + i] * BLK, BLK)
        target = pl.multiple_of(meta_ref[n * count + q * count + i] * BLK, BLK)
        line[pl.ds(target, BLK * BLK), :] = wide[pl.ds(source, BLK * BLK), :]

    kvh, per, _ = keyed_ref.shape
    group = per // rows

    def one(t):
        here = slice(t * tile, (t + 1) * tile)
        for k in range(part // lanes):
            tiles[q, t, :, k * lanes : (k + 1) * lanes] = line[
                pl.ds(t * tile * BLK + k, tile, stride=BLK), :
            ].astype(tiles.dtype)
        pltpu.make_async_copy(tiles.at[q, t], tile_ref.at[q, t], out_sem.at[q, t]).start()
        raw = lax.dot_general(
            keyed_ref[...].reshape(kvh * per, part),
            tiles[q, t],
            (((1,), (1,)), ((), ())),
            preferred_element_type=jnp.float32,
        ).reshape(kvh, rows, group, tile)
        owner_row = row_ref[0, :, here]
        picked = jnp.zeros((kvh, group, tile), jnp.float32)
        for r in range(rows):
            picked = picked + jnp.where((owner_row == r)[None], raw[:, r], 0.0)
        out_ref[0, :, here] = picked.reshape(kvh * group, tile).astype(out_ref.dtype)

    one(0)
    for t in range(1, tiles.shape[1]):
        pl.when(rows_here > t * tile)(functools.partial(one, t))

    @pl.when(q == n - 1)
    def _():
        for o in range(n):
            for t in range(tiles.shape[1]):

                def done(o=o, t=t):
                    pltpu.make_async_copy(
                        tiles.at[o, t], tile_ref.at[o, t], out_sem.at[o, t]
                    ).wait()

                if t:
                    pl.when(meta_ref[2 * n * count + n + o] > t * tile)(done)
                else:
                    done()


def weight_kernel(scale, parts_ref, row_ref, top_ref, sum_ref, cached_ref, w_ref, kept_ref):
    n = parts_ref.shape[0]
    scores = parts_ref[0].astype(jnp.float32)
    for i in range(1, n):
        scores = scores + parts_ref[i].astype(jnp.float32)
    scores = scores * scale
    owner_row = row_ref[...]
    weights = jnp.zeros(scores.shape, jnp.float32)
    for r in range(top_ref.shape[0]):
        own = jnp.where(owner_row == r, scores, -jnp.inf)
        cache_top = top_ref[r]
        top = jnp.maximum(jnp.max(own, 1, keepdims=True), cache_top)
        held = jnp.exp(own - top)
        fade = jnp.exp(cache_top - top)
        total = jnp.sum(held, 1, keepdims=True) + sum_ref[r] * fade
        weights = weights + held / total
        kept_ref[r] = cached_ref[r] * (fade / total)
    weights = weights.astype(w_ref.dtype)
    for i in range(n):
        w_ref[i] = weights


def value_kernel(rows, size_ref, w_ref, row_ref, tile_ref, value_ref, out_ref, tiles, acc, mixed, sem):
    q = pl.program_id(0)
    n, cuts, tile, _ = tiles.shape
    kvh = value_ref.shape[0]
    heads = w_ref.shape[1]
    per = rows * heads // kvh

    def copy(o, t):
        return pltpu.make_async_copy(tile_ref.at[o, t], tiles.at[o, t], sem.at[o, t])

    @pl.when(q == 0)
    def _():
        for o in range(n):
            copy(o, 0).start()
            for t in range(1, cuts):
                pl.when(size_ref[o] > t * tile)(lambda o=o, t=t: copy(o, t).start())

    def one(t):
        copy(q, t).wait()
        here = slice(t * tile, (t + 1) * tile)
        weights = w_ref[0, :, here].astype(jnp.float32).reshape(kvh, 1, heads // kvh, tile)
        owner_row = row_ref[0, :, here]
        spread = jnp.concatenate(
            [jnp.where((owner_row == r)[None, None], weights, 0.0) for r in range(rows)], 1
        ).reshape(kvh * per, tile)
        got = jnp.dot(
            spread.astype(jnp.bfloat16), tiles[q, t], preferred_element_type=jnp.float32
        )
        if t:
            acc[...] += got
        else:
            acc[...] = got

    one(0)
    for t in range(1, cuts):
        pl.when(size_ref[q] > t * tile)(functools.partial(one, t))
    for h in range(kvh):
        mixed[h, pl.ds(pl.multiple_of(q * per, per), per), :] = acc[
            h * per : (h + 1) * per, :
        ].astype(mixed.dtype)

    @pl.when(q == n - 1)
    def _():
        for h in range(kvh):
            done = jnp.dot(mixed[h], value_ref[h], preferred_element_type=jnp.float32)
            out_ref[:, h] = done.reshape(n, per, done.shape[1]).astype(out_ref.dtype)


def sum_kernel(parts_ref, kept_ref, out_ref, total):
    n, kvh, per, hd = parts_ref.shape
    rows, heads = kept_ref.shape[:2]
    group = heads // kvh
    for h in range(kvh):
        terms = parts_ref[0, h].astype(jnp.float32)
        for i in range(1, n):
            terms = terms + parts_ref[i, h].astype(jnp.float32)
        for r in range(rows):
            here = slice((h * rows + r) * group, (h * rows + r + 1) * group)
            total[here, :] = (
                terms[r * group : (r + 1) * group] + kept_ref[r, h * group : (h + 1) * group, :]
            )
    pieces = [
        total[pl.ds(h * per + g, rows, stride=group), :]
        for h in range(kvh)
        for g in range(group)
    ]
    attended = jnp.concatenate(pieces, 1).astype(out_ref.dtype)
    for i in range(n):
        out_ref[i] = attended


def everywhere(x, n):
    at = 0
    k = n // 2
    while k >= 1:
        got = lax.ppermute(x, "pool", [(i, i ^ k) for i in range(n)])
        low = (lax.axis_index("pool") & k) == 0
        x = jnp.where(low, jnp.stack([x, got], at), jnp.stack([got, x], at))
        at += 1
        k //= 2
    return x.reshape((n,) + x.shape[at:])


def local(
    x_prompt, kv_weight, block_dest, block_row, block_fill, queries, kv_cache, cache_len, out_weight
):
    n = lax.axis_size("pool")
    ntp = lax.axis_size("tp")
    me = lax.axis_index("pool")
    core = lax.axis_index("tp")
    tokens, width = x_prompt.shape
    part = width // n
    kvh = kv_weight.shape[1]
    hd = kv_weight.shape[2] // 2
    rows, heads = queries.shape[0], queries.shape[1]
    group = heads // kvh
    per = rows * group
    cache_slots = kv_cache.shape[1]
    blocks = tokens // BLK
    cap = max(2, 2 * blocks // n)
    count = n * cap
    slots = count * BLK
    half = tokens // ntp
    scale = 1.0 / hd**0.5
    swap = [(i, (i + 1) % ntp) for i in range(ntp)]

    size = half * 3 // 4
    extra = half - size
    at = jnp.stack([me, core]).astype(jnp.int32)
    fills = block_fill.reshape(n, blocks)
    mine = lax.all_to_all(pack(x_prompt, fills, at, 0, size), "pool", 0, 0, tiled=True)
    mine = mine.reshape(n * size, part)

    dest = block_dest[:, 0]
    index = jnp.arange(n * blocks, dtype=jnp.int32)
    sender = index // blocks
    ahead = index[None, :] < index[:, None]
    kin = ahead & (sender[None, :] == sender[:, None])
    rival = ahead & (dest[None, :] == dest[:, None])
    sent_at = jnp.sum(jnp.where(kin, block_fill[None, :], 0), 1)
    list_at = jnp.sum(jnp.where(rival, block_fill[None, :], 0), 1)
    rank = jnp.sum(rival.astype(jnp.int32), 1)
    hit = jnp.arange(n * count, dtype=jnp.int32)[:, None] == (dest * count + rank)[None, :]
    slot_src = jnp.sum(jnp.where(hit, (sender * tokens + sent_at)[None, :], 0), 1)
    slot_dst = jnp.sum(jnp.where(hit, list_at[None, :], 0), 1)
    owned = jnp.arange(n, dtype=jnp.int32)[:, None] == dest[None, :]
    list_blocks = jnp.sum(owned.astype(jnp.int32), 1)
    list_rows = jnp.sum(jnp.where(owned, block_fill[None, :], 0), 1)
    spot = jnp.arange(n * slots, dtype=jnp.int32)[:, None]
    start = (dest * slots + list_at)[None, :]
    inside = (spot >= start) & (spot < start + block_fill[None, :])
    rowof = jnp.sum(jnp.where(inside, (block_row + 1)[None, :], 0), 1) - 1
    rowof = rowof.reshape(n, 1, slots)

    most = jnp.max(jnp.sum(fills, 1))
    groups = lax.axis_size("groups")
    k = 1
    while k < groups:
        most = jnp.maximum(
            most, lax.ppermute(most, "groups", [(i, i ^ k) for i in range(groups)])
        )
        k *= 2
    over = most > ntp * size

    def exchange_rest():
        rest = pack(x_prompt, fills, at, ntp * size, extra)
        rest = lax.all_to_all(rest, "pool", 0, 0, tiled=True).reshape(n * extra, part)
        return rest, lax.ppermute(rest, "tp", swap)

    def no_rest():
        return (jnp.zeros((n * extra, part), jnp.bfloat16),) * 2

    more_mine, more_other = lax.cond(over, exchange_rest, no_rest)
    meta = jnp.concatenate(
        [
            slot_src,
            slot_dst,
            list_blocks,
            list_rows,
            jnp.stack([core.astype(jnp.int32), over.astype(jnp.int32)]),
        ]
    )

    allq = everywhere(queries, n).reshape(n, rows, kvh, group, hd)
    keyed = jnp.einsum(
        "qrhgd,phd->hqrgp", allq, kv_weight[:, :, :hd], preferred_element_type=jnp.float32
    ).astype(jnp.bfloat16)
    keyed = keyed.reshape(kvh, n * per, part)
    values = kv_weight[:, :, hd:].transpose(1, 0, 2)

    query = queries.reshape(rows, kvh, group, hd)
    cache_scores = (
        jnp.einsum(
            "rhgd,rthd->rhgt", query, kv_cache[:, :, :, :hd], preferred_element_type=jnp.float32
        )
        * scale
    )
    cache_live = jnp.arange(cache_slots, dtype=jnp.int32)[None, :] < cache_len[:, None]
    cache_scores = jnp.where(cache_live[:, None, None, :], cache_scores, -jnp.inf)
    cache_top = jnp.max(cache_scores, -1, keepdims=True)
    cache_exp = jnp.exp(cache_scores - cache_top)
    cache_sum = jnp.sum(cache_exp, -1, keepdims=True)
    cached = jnp.einsum(
        "rhgt,rthd->rhgd",
        cache_exp.astype(jnp.bfloat16),
        kv_cache[:, :, :, hd:],
        preferred_element_type=jnp.float32,
    )

    mine, meta, list_rows, rowof, keyed, values, cache_top, cache_sum, cached = (
        lax.optimization_barrier(
            (mine, meta, list_rows, rowof, keyed, values, cache_top, cache_sum, cached)
        )
    )
    other = lax.ppermute(mine, "tp", swap)

    tile = min(256, slots)
    tiles = slots // tile
    cuts = 4
    anywhere = pl.BlockSpec(memory_space=pl.ANY)
    partial_scores, listed = pl.pallas_call(
        functools.partial(score_kernel, rows),
        grid_spec=pltpu.PrefetchScalarGridSpec(
            num_scalar_prefetch=1,
            grid=(n,),
            in_specs=[
                *[anywhere] * 4,
                pl.BlockSpec((kvh, per, part), lambda q, *_: (0, q, 0)),
                pl.BlockSpec((1, 1, slots), lambda q, *_: (q, 0, 0)),
            ],
            out_specs=[pl.BlockSpec((1, heads, slots), lambda q, *_: (q, 0, 0)), anywhere],
            scratch_shapes=[
                pltpu.VMEM((ntp, n * size, part), jnp.bfloat16),
                pltpu.VMEM((ntp, n * extra, part), jnp.bfloat16),
                pltpu.VMEM(((n * tokens + BLK) * BLK, 128), jnp.float32),
                pltpu.VMEM(((slots + BLK) * BLK, 128), jnp.float32),
                pltpu.VMEM((n, tiles, tile, part), jnp.bfloat16),
                pltpu.SemaphoreType.DMA((ntp, cuts)),
                pltpu.SemaphoreType.DMA((n, tiles)),
            ],
        ),
        out_shape=[
            jax.ShapeDtypeStruct((n, heads, slots), jnp.bfloat16),
            jax.ShapeDtypeStruct((n, tiles, tile, part), jnp.bfloat16),
        ],
        compiler_params=pltpu.CompilerParams(vmem_limit_bytes=56 * MIB),
        name="prompt_scores",
    )(meta, mine, other, more_mine, more_other, keyed, rowof)

    parts = lax.all_to_all(partial_scores, "pool", 0, 0, tiled=True)
    my_rows = lax.dynamic_index_in_dim(rowof, me, 0, keepdims=False)
    weights, kept = pl.pallas_call(
        functools.partial(weight_kernel, scale),
        out_shape=[
            jax.ShapeDtypeStruct((n, heads, slots), jnp.bfloat16),
            jax.ShapeDtypeStruct((rows, heads, hd), jnp.float32),
        ],
        compiler_params=pltpu.CompilerParams(vmem_limit_bytes=16 * MIB),
        name="softmax_weights",
    )(
        parts,
        my_rows,
        cache_top.reshape(rows, heads, 1),
        cache_sum.reshape(rows, heads, 1),
        cached.reshape(rows, heads, hd),
    )

    all_weights = lax.all_to_all(weights, "pool", 0, 0, tiled=True)
    terms = pl.pallas_call(
        functools.partial(value_kernel, rows),
        grid_spec=pltpu.PrefetchScalarGridSpec(
            num_scalar_prefetch=1,
            grid=(n,),
            in_specs=[
                pl.BlockSpec((1, heads, slots), lambda q, *_: (q, 0, 0)),
                pl.BlockSpec((1, 1, slots), lambda q, *_: (q, 0, 0)),
                anywhere,
                pl.BlockSpec((kvh, part, hd), lambda q, *_: (0, 0, 0)),
            ],
            out_specs=pl.BlockSpec((n, kvh, per, hd), lambda q, *_: (0, 0, 0, 0)),
            scratch_shapes=[
                pltpu.VMEM((n, tiles, tile, part), jnp.bfloat16),
                pltpu.VMEM((kvh * per, part), jnp.float32),
                pltpu.VMEM((kvh, n * per, part), jnp.bfloat16),
                pltpu.SemaphoreType.DMA((n, tiles)),
            ],
        ),
        out_shape=jax.ShapeDtypeStruct((n, kvh, per, hd), jnp.bfloat16),
        compiler_params=pltpu.CompilerParams(vmem_limit_bytes=56 * MIB),
        name="weighted_values",
    )(list_rows, all_weights, rowof, listed, values)

    term_parts = lax.all_to_all(terms, "pool", 0, 0, tiled=True)
    attended = pl.pallas_call(
        sum_kernel,
        out_shape=jax.ShapeDtypeStruct((n, rows, heads * hd), jnp.bfloat16),
        scratch_shapes=[pltpu.VMEM((kvh * per, hd), jnp.float32)],
        compiler_params=pltpu.CompilerParams(vmem_limit_bytes=16 * MIB),
        name="attended_sum",
    )(term_parts, kept)

    everyone = lax.all_to_all(attended, "pool", 0, 0, tiled=True).reshape(n * rows, heads * hd)
    product = jnp.dot(everyone, out_weight, preferred_element_type=jnp.float32)
    cols = out_weight.shape[1] // ntp
    out = lax.dynamic_slice_in_dim(product, core * cols, cols, 1)
    for j in range(1, ntp):
        away = lax.dynamic_slice_in_dim(product, ((core + j) % ntp) * cols, cols, 1)
        out = out + lax.ppermute(away, "tp", [(i, (i + j) % ntp) for i in range(ntp)])
    return out.astype(jnp.bfloat16)


def solution(mesh):
    in_specs = (
        P(("groups", "pool"), None),
        P("pool", "tp", None),
        P("groups", None),
        P("groups"),
        P("groups"),
        P(("groups", "pool"), "tp", None),
        P(("groups", "pool"), None, "tp", None),
        P(("groups", "pool")),
        P("tp", "pool"),
    )
    out_specs = P("groups", ("pool", "tp"))
    return jax.shard_map(local, mesh=mesh, in_specs=in_specs, out_specs=out_specs, check_vma=False)
```

```python
import functools

import jax
import jax.numpy as jnp
from jax import lax
from jax.experimental import pallas as pl
from jax.experimental.pallas import tpu as pltpu
from jax.sharding import PartitionSpec as P

BLK = 8
ROW = 16
MIB = 1 << 20


def pack_kernel(base, at_ref, fill_ref, dest_ref, x_ref, out_ref, held, packed, count, in_sem, out_sem):
    n, tokens, part = held.shape
    size = packed.shape[1]
    blocks = tokens // BLK

    def load(q):
        return pltpu.make_async_copy(
            x_ref.at[:, pl.ds(q * part, part)], held.at[q], in_sem.at[q]
        )

    def store(q):
        return pltpu.make_async_copy(packed.at[q], out_ref.at[q], out_sem.at[q])

    for q in range(n):
        load(q).start()
    first = at_ref[0] * blocks
    for q in range(n):
        count[q] = 0

    @pl.loop(0, blocks)
    def _(b):
        owner = dest_ref[first + b]
        count[owner] = count[owner] + fill_ref[first + b]

    def starts(q, total):
        here = count[q]
        count[q] = total
        return total + here

    lax.fori_loop(0, n, starts, jnp.int32(0))
    token = lax.broadcasted_iota(jnp.int32, (1, tokens), 1)

    def place(b, ranks):
        owner = dest_ref[first + b]
        fill = fill_ref[first + b]
        start = count[owner]
        count[owner] = start + fill
        inner = token - b * BLK
        return jnp.where((inner >= 0) & (inner < fill), start + inner, ranks)

    ranks = lax.fori_loop(0, blocks, place, jnp.full((1, tokens), -1, jnp.int32))
    wanted = base + at_ref[1] * size + lax.broadcasted_iota(jnp.int32, (size, tokens), 0)
    pick = (wanted == ranks).astype(jnp.bfloat16)
    for q in range(n):
        load(q).wait()
        packed[q] = jnp.dot(pick, held[q], preferred_element_type=jnp.float32).astype(
            packed.dtype
        )
        store(q).start()
    for q in range(n):
        store(q).wait()


def pack(x_prompt, fill, dest, at, n, base, size):
    tokens, width = x_prompt.shape
    part = width // n
    return pl.pallas_call(
        functools.partial(pack_kernel, base),
        grid_spec=pltpu.PrefetchScalarGridSpec(
            num_scalar_prefetch=3,
            grid=(1,),
            in_specs=[pl.BlockSpec(memory_space=pl.ANY)],
            out_specs=pl.BlockSpec(memory_space=pl.ANY),
            scratch_shapes=[
                pltpu.VMEM((n, tokens, part), jnp.bfloat16),
                pltpu.VMEM((n, size, part), jnp.bfloat16),
                pltpu.SMEM((n,), jnp.int32),
                pltpu.SemaphoreType.DMA((n,)),
                pltpu.SemaphoreType.DMA((n,)),
            ],
        ),
        out_shape=jax.ShapeDtypeStruct((n, size, part), jnp.bfloat16),
        compiler_params=pltpu.CompilerParams(vmem_limit_bytes=56 * MIB),
        name="pack_live_tokens",
    )(at, fill, dest, x_prompt)


def load_tokens(n, meta_ref, x_refs, x_all, sem):
    core, over = meta_ref[n * n + 1], meta_ref[n * n + 2]
    size, extra = x_refs[0].shape[0] // n, x_refs[2].shape[0] // n
    tokens = 2 * (size + extra)
    part = x_all.shape[1]

    def copies(refs, base, length):
        return [
            pltpu.make_async_copy(
                ref.at[pl.ds(s * length, length)],
                x_all.at[
                    pl.ds(
                        pl.multiple_of(
                            s * tokens + base + (core if j == 0 else 1 - core) * length, ROW
                        ),
                        length,
                    )
                ],
                sem.at[j, s],
            )
            for j, ref in enumerate(refs)
            for s in range(n)
        ]

    main = copies(x_refs[:2], 0, size)
    for copy in main:
        copy.start()
    x_all[n * tokens :, :] = jnp.zeros((x_all.shape[0] - n * tokens, part), x_all.dtype)

    @pl.when(over == 0)
    def _():
        for s in range(n):
            x_all[s * tokens + 2 * size : (s + 1) * tokens, :] = jnp.zeros(
                (2 * extra, part), x_all.dtype
            )

    for copy in main:
        copy.wait()

    @pl.when(over != 0)
    def _():
        rest = copies(x_refs[2:], 2 * size, extra)
        for copy in rest:
            copy.start()
        for copy in rest:
            copy.wait()


def cut_windows(n, q, window, meta_ref, x_all, stage):
    for s in range(n):
        start = pl.multiple_of(meta_ref[q * n + s], ROW)
        stage[s * window : (s + 1) * window, :] = x_all[pl.ds(start, window), :]


def score_kernel(n, rows, window, meta_ref, *refs):
    x_refs, (keyed_ref, row_ref), out_refs = refs[:4], refs[4:6], refs[6 : 6 + n]
    x_all, stage, sem = refs[6 + n :]
    k = pl.program_id(0)
    pl.when(k == 0)(lambda: load_tokens(n, meta_ref, x_refs, x_all, sem))
    cut_windows(n, meta_ref[n * n] ^ k, window, meta_ref, x_all, stage)
    kvh, per, part = keyed_ref.shape
    lanes = n * window
    raw = lax.dot_general(
        keyed_ref[...].reshape(kvh * per, part),
        stage[...],
        (((1,), (1,)), ((), ())),
        preferred_element_type=jnp.float32,
    ).reshape(kvh, rows, per // rows, lanes)
    owner_row = row_ref[0]
    picked = jnp.zeros((kvh, per // rows, lanes), jnp.float32)
    for r in range(rows):
        picked = picked + jnp.where((owner_row == r)[None], raw[:, r], 0.0)
    picked = picked.reshape(kvh * per // rows, lanes).astype(jnp.bfloat16)
    for j in range(n):

        @pl.when(k == j)
        def _(j=j):
            out_refs[j][...] = picked


def weight_kernel(n, scale, *refs):
    part_refs = refs[:n]
    row_ref, top_ref, sum_ref, cached_ref, w_ref, kept_ref = refs[n:]
    scores = part_refs[0][...].astype(jnp.float32)
    for ref in part_refs[1:]:
        scores = scores + ref[...].astype(jnp.float32)
    scores = scores * scale
    owner_row = row_ref[...]
    weights = jnp.zeros(scores.shape, jnp.float32)
    for r in range(top_ref.shape[0]):
        own = jnp.where(owner_row == r, scores, -jnp.inf)
        cache_top = top_ref[r]
        top = jnp.maximum(jnp.max(own, 1, keepdims=True), cache_top)
        held = jnp.exp(own - top)
        fade = jnp.exp(cache_top - top)
        total = jnp.sum(held, 1, keepdims=True) + sum_ref[r] * fade
        weights = weights + held / total
        kept_ref[r] = cached_ref[r] * (fade / total)
    w_ref[...] = weights.astype(w_ref.dtype)


def value_kernel(n, rows, window, meta_ref, *refs):
    x_refs, (row_ref, value_ref), w_refs = refs[:4], refs[4:6], refs[6 : 6 + n]
    out_refs = refs[6 + n : 6 + 2 * n]
    x_all, stage, chosen, mixed, sem = refs[6 + 2 * n :]
    k = pl.program_id(0)
    pl.when(k == 0)(lambda: load_tokens(n, meta_ref, x_refs, x_all, sem))
    for j in range(n):

        @pl.when(k == j)
        def _(j=j):
            chosen[...] = w_refs[j][...]

    cut_windows(n, meta_ref[n * n] ^ k, window, meta_ref, x_all, stage)
    kvh = value_ref.shape[0]
    heads, lanes = chosen.shape
    per = rows * heads // kvh
    weights = chosen[...].astype(jnp.float32).reshape(kvh, 1, heads // kvh, lanes)
    owner_row = row_ref[0]
    spread = jnp.concatenate(
        [jnp.where((owner_row == r)[None, None], weights, 0.0) for r in range(rows)], 1
    ).reshape(kvh * per, lanes)
    got = jnp.dot(
        spread.astype(jnp.bfloat16), stage[...], preferred_element_type=jnp.float32
    ).astype(jnp.bfloat16)
    for h in range(kvh):
        mixed[h, pl.ds(pl.multiple_of(k * per, per), per), :] = got[h * per : (h + 1) * per]

    @pl.when(k == n - 1)
    def _():
        for h in range(kvh):
            done = jnp.dot(mixed[h], value_ref[h], preferred_element_type=jnp.float32)
            done = done.astype(jnp.bfloat16)
            for j in range(n):
                out_refs[j][h] = done[j * per : (j + 1) * per]


def sum_kernel(n, *refs):
    part_refs = refs[:n]
    kept_ref, out_ref, total = refs[n:]
    kvh, per, hd = part_refs[0].shape
    rows, heads = kept_ref.shape[:2]
    group = heads // kvh
    for h in range(kvh):
        terms = part_refs[0][h].astype(jnp.float32)
        for ref in part_refs[1:]:
            terms = terms + ref[h].astype(jnp.float32)
        for r in range(rows):
            here = slice((h * rows + r) * group, (h * rows + r + 1) * group)
            total[here, :] = (
                terms[r * group : (r + 1) * group] + kept_ref[r, h * group : (h + 1) * group, :]
            )
    pieces = [
        total[pl.ds(h * per + g, rows, stride=group), :]
        for h in range(kvh)
        for g in range(group)
    ]
    out_ref[...] = jnp.concatenate(pieces, 1).astype(out_ref.dtype)


def order_kernel(n, me_ref, own_ref, got_ref, out_ref):
    rows = own_ref.shape[0] // n
    for q in range(0, n, 2):
        pair = []
        for j in range(2):
            here = pl.ds(pl.multiple_of((me_ref[0] ^ (q + j)) * rows, rows), rows)
            pair.append(own_ref[here, :] + got_ref[here, :])
        out_ref[q * rows : (q + 2) * rows, :] = jnp.concatenate(pair).astype(out_ref.dtype)


def with_partner(x, k, n):
    return lax.ppermute(x, "pool", [(i, i ^ k) for i in range(n)])


def from_all(x, n):
    order, held = [0], x[None]
    k = n // 2
    while k >= 1:
        held = jnp.concatenate([held, with_partner(held, k, n)])
        order = order + [i ^ k for i in order]
        k //= 2
    return [held[order.index(k)] for k in range(n)]


def far_first(n):
    return sorted(range(1, n), reverse=True)


def swap_parts(parts, n):
    got = [parts[0]] + [None] * (n - 1)
    for k in far_first(n):
        got[k] = with_partner(parts[k], k, n)
    return got


def local(
    x_prompt, kv_weight, block_dest, block_row, block_fill, queries, kv_cache, cache_len, out_weight
):
    n = lax.axis_size("pool")
    ntp = lax.axis_size("tp")
    me = lax.axis_index("pool").astype(jnp.int32)
    core = lax.axis_index("tp").astype(jnp.int32)
    tokens, width = x_prompt.shape
    part = width // n
    kvh = kv_weight.shape[1]
    hd = kv_weight.shape[2] // 2
    rows, heads = queries.shape[0], queries.shape[1]
    group = heads // kvh
    per = rows * group
    cache_slots = kv_cache.shape[1]
    blocks = tokens // BLK
    cap = max(2, 2 * blocks // n)
    window = cap * BLK + ROW
    lanes = n * window
    half = tokens // ntp
    scale = 1.0 / hd**0.5
    swap = [(i, (i + 1) % ntp) for i in range(ntp)]

    size = half * 3 // 4
    extra = half - size
    at = jnp.stack([me, core])
    dest = block_dest[:, 0]
    packed = pack(x_prompt, block_fill, dest, at, n, 0, size)
    mine = lax.all_to_all(packed, "pool", 0, 0, tiled=True).reshape(n * size, part)

    index = jnp.arange(n * blocks, dtype=jnp.int32)
    sender = index // blocks
    kin = sender[None, :] == sender[:, None]
    lower = kin & (dest[None, :] < dest[:, None])
    level = kin & (dest[None, :] == dest[:, None]) & (index[None, :] < index[:, None])
    before = jnp.sum(jnp.where(lower, block_fill[None, :], 0), 1)
    within = jnp.sum(jnp.where(level, block_fill[None, :], 0), 1)
    start = dest * lanes + sender * window + before % ROW + within
    spot = jnp.arange(n * lanes, dtype=jnp.int32)[:, None]
    inside = (spot >= start[None, :]) & (spot < (start + block_fill)[None, :])
    rowof = jnp.sum(jnp.where(inside, (block_row + 1)[None, :], 0), 1) - 1
    rowof = rowof.reshape(n, 1, lanes)
    pair = jnp.arange(n * n, dtype=jnp.int32)
    sooner = (sender[None, :] == (pair % n)[:, None]) & (dest[None, :] < (pair // n)[:, None])
    offset = jnp.sum(jnp.where(sooner, block_fill[None, :], 0), 1)
    starts = (pair % n) * tokens + offset // ROW * ROW

    most = jnp.max(jnp.sum(block_fill.reshape(n, blocks), 1))
    groups = lax.axis_size("groups")
    k = 1
    while k < groups:
        most = jnp.maximum(
            most, lax.ppermute(most, "groups", [(i, i ^ k) for i in range(groups)])
        )
        k *= 2
    over = most > ntp * size

    def exchange_rest():
        rest = pack(x_prompt, block_fill, dest, at, n, ntp * size, extra)
        rest = lax.all_to_all(rest, "pool", 0, 0, tiled=True).reshape(n * extra, part)
        return rest, lax.ppermute(rest, "tp", swap)

    def no_rest():
        return (jnp.zeros((n * extra, part), jnp.bfloat16),) * 2

    more_mine, more_other = lax.cond(over, exchange_rest, no_rest)
    meta = jnp.concatenate([starts, jnp.stack([me, core, over.astype(jnp.int32)])])

    allq = jnp.stack(from_all(queries, n)).reshape(n, rows, kvh, group, hd)
    keyed = jnp.einsum(
        "qrhgd,phd->hqrgp", allq, kv_weight[:, :, :hd], preferred_element_type=jnp.float32
    ).astype(jnp.bfloat16)
    keyed = keyed.reshape(kvh, n * per, part)
    values = kv_weight[:, :, hd:].transpose(1, 0, 2)

    query = queries.reshape(rows, kvh, group, hd)
    cache_scores = (
        jnp.einsum(
            "rhgd,rthd->rhgt", query, kv_cache[:, :, :, :hd], preferred_element_type=jnp.float32
        )
        * scale
    )
    cache_live = jnp.arange(cache_slots, dtype=jnp.int32)[None, :] < cache_len[:, None]
    cache_scores = jnp.where(cache_live[:, None, None, :], cache_scores, -jnp.inf)
    cache_top = jnp.max(cache_scores, -1, keepdims=True)
    cache_exp = jnp.exp(cache_scores - cache_top)
    cache_sum = jnp.sum(cache_exp, -1, keepdims=True)
    cached = jnp.einsum(
        "rhgt,rthd->rhgd",
        cache_exp.astype(jnp.bfloat16),
        kv_cache[:, :, :, hd:],
        preferred_element_type=jnp.float32,
    )
    cache_top = cache_top.reshape(rows, heads, 1)
    cache_sum = cache_sum.reshape(rows, heads, 1)
    cached = cached.reshape(rows, heads, hd)

    mine, meta, rowof, keyed, values, cache_top, cache_sum, cached = lax.optimization_barrier(
        (mine, meta, rowof, keyed, values, cache_top, cache_sum, cached)
    )
    other = lax.ppermute(mine, "tp", swap)

    anywhere = pl.BlockSpec(memory_space=pl.ANY)
    x_scratch = [
        pltpu.VMEM((n * tokens + window, part), jnp.bfloat16),
        pltpu.VMEM((lanes, part), jnp.bfloat16),
    ]
    x_parts = (mine, other, more_mine, more_other)
    row_spec = pl.BlockSpec((1, 1, lanes), lambda k, m: (m[n * n] ^ k, 0, 0))
    slot_spec = pl.BlockSpec((heads, lanes), lambda k, m: (0, 0))
    slot_shape = jax.ShapeDtypeStruct((heads, lanes), jnp.bfloat16)
    partial_scores = pl.pallas_call(
        functools.partial(score_kernel, n, rows, window),
        grid_spec=pltpu.PrefetchScalarGridSpec(
            num_scalar_prefetch=1,
            grid=(n,),
            in_specs=[
                *[anywhere] * 4,
                pl.BlockSpec((kvh, per, part), lambda k, m: (0, k, 0)),
                row_spec,
            ],
            out_specs=[slot_spec] * n,
            scratch_shapes=[*x_scratch, pltpu.SemaphoreType.DMA((ntp, n))],
        ),
        out_shape=[slot_shape] * n,
        compiler_params=pltpu.CompilerParams(vmem_limit_bytes=20 * MIB),
        name="prompt_scores",
    )(meta, *x_parts, keyed, rowof)

    parts = swap_parts(partial_scores, n)
    my_rows = lax.dynamic_index_in_dim(rowof, me, 0, keepdims=False)
    weights, kept = pl.pallas_call(
        functools.partial(weight_kernel, n, scale),
        out_shape=[slot_shape, jax.ShapeDtypeStruct((rows, heads, hd), jnp.float32)],
        compiler_params=pltpu.CompilerParams(vmem_limit_bytes=16 * MIB),
        name="softmax_weights",
    )(*parts, my_rows, cache_top, cache_sum, cached)

    all_weights = swap_parts([weights] * n, n)
    terms = pl.pallas_call(
        functools.partial(value_kernel, n, rows, window),
        grid_spec=pltpu.PrefetchScalarGridSpec(
            num_scalar_prefetch=1,
            grid=(n,),
            in_specs=[
                *[anywhere] * 4,
                row_spec,
                pl.BlockSpec((kvh, part, hd), lambda k, m: (0, 0, 0)),
                *[slot_spec] * n,
            ],
            out_specs=[pl.BlockSpec((kvh, per, hd), lambda k, m: (0, 0, 0))] * n,
            scratch_shapes=[
                *x_scratch,
                pltpu.VMEM((heads, lanes), jnp.bfloat16),
                pltpu.VMEM((kvh, n * per, part), jnp.bfloat16),
                pltpu.SemaphoreType.DMA((ntp, n)),
            ],
        ),
        out_shape=[jax.ShapeDtypeStruct((kvh, per, hd), jnp.bfloat16)] * n,
        compiler_params=pltpu.CompilerParams(vmem_limit_bytes=24 * MIB),
        name="weighted_values",
    )(meta, *x_parts, rowof, values, *all_weights)

    attended = pl.pallas_call(
        functools.partial(sum_kernel, n),
        out_shape=jax.ShapeDtypeStruct((rows, heads * hd), jnp.bfloat16),
        scratch_shapes=[pltpu.VMEM((kvh * per, hd), jnp.float32)],
        compiler_params=pltpu.CompilerParams(vmem_limit_bytes=16 * MIB),
        name="attended_sum",
    )(*swap_parts(terms, n), kept)

    everyone = jnp.concatenate(swap_parts([attended] * n, n))
    product = jnp.dot(everyone, out_weight, preferred_element_type=jnp.float32)
    cols = out_weight.shape[1] // ntp
    own = lax.dynamic_slice_in_dim(product, core * cols, cols, 1)
    away = lax.dynamic_slice_in_dim(product, (1 - core) * cols, cols, 1)
    got = lax.ppermute(away, "tp", swap)
    return pl.pallas_call(
        functools.partial(order_kernel, n),
        grid_spec=pltpu.PrefetchScalarGridSpec(
            num_scalar_prefetch=1,
            grid=(1,),
            in_specs=[pl.BlockSpec((n * rows, cols), lambda i, m: (0, 0))] * 2,
            out_specs=pl.BlockSpec((n * rows, cols), lambda i, m: (0, 0)),
        ),
        out_shape=jax.ShapeDtypeStruct((n * rows, cols), jnp.bfloat16),
        compiler_params=pltpu.CompilerParams(vmem_limit_bytes=16 * MIB),
        name="order_rows",
    )(me.reshape(1), own, got)


def solution(mesh):
    in_specs = (
        P(("groups", "pool"), None),
        P("pool", "tp", None),
        P("groups", None),
        P("groups"),
        P("groups"),
        P(("groups", "pool"), "tp", None),
        P(("groups", "pool"), None, "tp", None),
        P(("groups", "pool")),
        P("tp", "pool"),
    )
    out_specs = P("groups", ("pool", "tp"))
    return jax.shard_map(local, mesh=mesh, in_specs=in_specs, out_specs=out_specs, check_vma=False)
```

```python
import functools

import jax
import jax.numpy as jnp
from jax import lax
from jax.experimental import pallas as pl
from jax.experimental.pallas import tpu as pltpu
from jax.sharding import PartitionSpec as P

BLK = 8
MIB = 1 << 20


def pack_kernel(base, at_ref, fill_ref, dest_ref, x_ref, out_ref, held, packed, count, in_sem, out_sem):
    n, tokens, part = held.shape
    size = packed.shape[1]
    blocks = tokens // BLK

    def load(q):
        return pltpu.make_async_copy(
            x_ref.at[:, pl.ds(q * part, part)], held.at[q], in_sem.at[q]
        )

    def store(q):
        return pltpu.make_async_copy(packed.at[q], out_ref.at[q], out_sem.at[q])

    for q in range(n):
        load(q).start()
    first = at_ref[0] * blocks
    for q in range(n):
        count[q] = 0

    @pl.loop(0, blocks)
    def _(b):
        owner = dest_ref[first + b]
        count[owner] = count[owner] + fill_ref[first + b]

    def starts(q, total):
        here = count[q]
        count[q] = total
        return total + here

    lax.fori_loop(0, n, starts, jnp.int32(0))
    token = lax.broadcasted_iota(jnp.int32, (1, tokens), 1)

    def place(b, ranks):
        owner = dest_ref[first + b]
        fill = fill_ref[first + b]
        start = count[owner]
        count[owner] = start + fill
        inner = token - b * BLK
        return jnp.where((inner >= 0) & (inner < fill), start + inner, ranks)

    ranks = lax.fori_loop(0, blocks, place, jnp.full((1, tokens), -1, jnp.int32))
    wanted = base + at_ref[1] * size + lax.broadcasted_iota(jnp.int32, (size, tokens), 0)
    pick = (wanted == ranks).astype(jnp.bfloat16)
    for q in range(n):
        load(q).wait()
        packed[q] = jnp.dot(pick, held[q], preferred_element_type=jnp.float32).astype(
            packed.dtype
        )
        store(q).start()
    for q in range(n):
        store(q).wait()


def pack(x_prompt, fill, dest, at, n, base, size):
    tokens, width = x_prompt.shape
    part = width // n
    return pl.pallas_call(
        functools.partial(pack_kernel, base),
        grid_spec=pltpu.PrefetchScalarGridSpec(
            num_scalar_prefetch=3,
            grid=(1,),
            in_specs=[pl.BlockSpec(memory_space=pl.ANY)],
            out_specs=pl.BlockSpec(memory_space=pl.ANY),
            scratch_shapes=[
                pltpu.VMEM((n, tokens, part), jnp.bfloat16),
                pltpu.VMEM((n, size, part), jnp.bfloat16),
                pltpu.SMEM((n,), jnp.int32),
                pltpu.SemaphoreType.DMA((n,)),
                pltpu.SemaphoreType.DMA((n,)),
            ],
        ),
        out_shape=jax.ShapeDtypeStruct((n, size, part), jnp.bfloat16),
        compiler_params=pltpu.CompilerParams(vmem_limit_bytes=56 * MIB),
        name="pack_live_tokens",
    )(at, fill, dest, x_prompt)


def tile_cuts(lanes):
    return [0] + list(range(min(256, lanes), lanes, 128)) + [lanes]


def load_tokens(n, core, over, x_refs, held, more, wide, sem):
    size, extra = held.shape[1] // n, more.shape[1] // n
    tokens = 2 * (size + extra)
    part = wide.shape[1]
    cuts = sem.shape[1]

    def copies(refs, buffer):
        span = buffer.shape[1] // cuts
        return [
            [
                pltpu.make_async_copy(
                    ref.at[pl.ds(i * span, span)], buffer.at[j, pl.ds(i * span, span)], sem.at[j, i]
                )
                for j, ref in enumerate(refs)
            ]
            for i in range(cuts)
        ]

    def widen(buffer, base, first, last):
        length = buffer.shape[1] // n

        @pl.loop(first, last)
        def _(s):
            for j in range(2):
                side = core if j == 0 else 1 - core
                to = pl.multiple_of(s * tokens + base + side * length, BLK)
                wide[pl.ds(to, length), :] = buffer[
                    j, pl.ds(pl.multiple_of(s * length, length), length), :
                ].astype(wide.dtype)

    main = copies(x_refs[:2], held)
    for pair in main:
        for copy in pair:
            copy.start()

    @pl.loop(0, n)
    def _(s):
        at = pl.multiple_of(s * tokens + 2 * size, BLK)
        wide[pl.ds(at, 2 * extra), :] = jnp.zeros((2 * extra, part), wide.dtype)

    wide[n * tokens :, :] = jnp.zeros((wide.shape[0] - n * tokens, part), wide.dtype)
    for i, pair in enumerate(main):
        for copy in pair:
            copy.wait()
        widen(held, 0, i * n // cuts, (i + 1) * n // cuts)

    @pl.when(over != 0)
    def _():
        rest = copies(x_refs[2:], more)
        for pair in rest:
            for copy in pair:
                copy.start()
        for pair in rest:
            for copy in pair:
                copy.wait()
        widen(more, 2 * size, 0, n)


def score_kernel(n, rows, window, meta_ref, *refs):
    x_refs, (keyed_ref, row_ref), (out_ref, low_ref, high_ref) = refs[:4], refs[4:6], refs[6:9]
    held, more, wide, line, low, high, in_sem, out_sem = refs[9:]
    q = pl.program_id(0)
    pairs = n * n
    part = wide.shape[1]
    lanes = out_ref.shape[2]
    cuts = tile_cuts(lanes)

    @pl.when(q == 0)
    def _():
        load_tokens(
            n, meta_ref[3 * pairs + n + 1], meta_ref[3 * pairs + n + 2], x_refs, held, more, wide, in_sem
        )

        @pl.loop(0, line.shape[0] // BLK)
        def _(i):
            line[pl.ds(pl.multiple_of(i * BLK, BLK), BLK), :] = jnp.zeros((BLK, part), line.dtype)

    usual = min(32, window)
    for s in range(n):
        source = pl.multiple_of(meta_ref[q * n + s], BLK)
        target = pl.multiple_of(meta_ref[pairs + q * n + s], BLK)
        line[pl.ds(target, usual), :] = wide[pl.ds(source, usual), :]
        if window > usual:

            @pl.when(meta_ref[2 * pairs + q * n + s] > usual)
            def _(source=source, target=target):
                line[pl.ds(target + usual, window - usual), :] = wide[
                    pl.ds(source + usual, window - usual), :
                ]

    kvh, per, _ = keyed_ref.shape
    group = per // rows

    def copy(o, t):
        if t == 0:
            return pltpu.make_async_copy(low.at[o], low_ref.at[o], out_sem.at[o, 0])
        here = pl.ds(cuts[t] - cuts[1], cuts[t + 1] - cuts[t])
        return pltpu.make_async_copy(
            high.at[o, here], high_ref.at[o, here], out_sem.at[o, t]
        )

    def one(t):
        here = slice(cuts[t], cuts[t + 1])
        tile = line[here, :].astype(low.dtype)
        if t == 0:
            low[q] = tile
        else:
            high[q, cuts[t] - cuts[1] : cuts[t + 1] - cuts[1], :] = tile
        copy(q, t).start()
        raw = lax.dot_general(
            keyed_ref[...].reshape(kvh * per, part),
            tile,
            (((1,), (1,)), ((), ())),
            preferred_element_type=jnp.float32,
        ).reshape(kvh, rows, group, cuts[t + 1] - cuts[t])
        owner_row = row_ref[0, :, here]
        picked = jnp.zeros((kvh, group, cuts[t + 1] - cuts[t]), jnp.float32)
        for r in range(rows):
            picked = picked + jnp.where((owner_row == r)[None], raw[:, r], 0.0)
        out_ref[0, :, here] = picked.reshape(kvh * group, -1).astype(out_ref.dtype)

    one(0)
    for t in range(1, len(cuts) - 1):
        pl.when(meta_ref[3 * pairs + q] > cuts[t])(functools.partial(one, t))

    @pl.when(q == n - 1)
    def _():
        for o in range(n):
            copy(o, 0).wait()
            for t in range(1, len(cuts) - 1):
                pl.when(meta_ref[3 * pairs + o] > cuts[t])(lambda o=o, t=t: copy(o, t).wait())


def weight_kernel(scale, parts_ref, row_ref, top_ref, sum_ref, cached_ref, w_ref, kept_ref):
    n = parts_ref.shape[0]
    scores = parts_ref[0].astype(jnp.float32)
    for i in range(1, n):
        scores = scores + parts_ref[i].astype(jnp.float32)
    scores = scores * scale
    owner_row = row_ref[...]
    weights = jnp.zeros(scores.shape, jnp.float32)
    for r in range(top_ref.shape[0]):
        own = jnp.where(owner_row == r, scores, -jnp.inf)
        cache_top = top_ref[r]
        top = jnp.maximum(jnp.max(own, 1, keepdims=True), cache_top)
        held = jnp.exp(own - top)
        fade = jnp.exp(cache_top - top)
        total = jnp.sum(held, 1, keepdims=True) + sum_ref[r] * fade
        weights = weights + held / total
        kept_ref[r] = cached_ref[r] * (fade / total)
    weights = weights.astype(w_ref.dtype)
    for i in range(n):
        w_ref[i] = weights


def value_kernel(
    rows, size_ref, w_ref, row_ref, low_ref, high_ref, value_ref, out_ref, low, high, acc, mixed, sem
):
    q = pl.program_id(0)
    n = low.shape[0]
    kvh = value_ref.shape[0]
    _, heads, lanes = w_ref.shape
    per = rows * heads // kvh
    cuts = tile_cuts(lanes)

    def copy(o, t):
        if t == 0:
            return pltpu.make_async_copy(low_ref.at[o], low.at[o], sem.at[o, 0])
        here = pl.ds(cuts[t] - cuts[1], cuts[t + 1] - cuts[t])
        return pltpu.make_async_copy(high_ref.at[o, here], high.at[o, here], sem.at[o, t])

    @pl.when(q == 0)
    def _():
        for o in range(n):
            copy(o, 0).start()
            for t in range(1, len(cuts) - 1):
                pl.when(size_ref[o] > cuts[t])(lambda o=o, t=t: copy(o, t).start())

    def one(t):
        copy(q, t).wait()
        here = slice(cuts[t], cuts[t + 1])
        width = cuts[t + 1] - cuts[t]
        weights = w_ref[0, :, here].astype(jnp.float32).reshape(kvh, 1, heads // kvh, width)
        owner_row = row_ref[0, :, here]
        spread = jnp.concatenate(
            [jnp.where((owner_row == r)[None, None], weights, 0.0) for r in range(rows)], 1
        ).reshape(kvh * per, width)
        tile = low[q] if t == 0 else high[q, cuts[t] - cuts[1] : cuts[t + 1] - cuts[1], :]
        got = jnp.dot(spread.astype(jnp.bfloat16), tile, preferred_element_type=jnp.float32)
        if t:
            acc[...] += got
        else:
            acc[...] = got

    one(0)
    for t in range(1, len(cuts) - 1):
        pl.when(size_ref[q] > cuts[t])(functools.partial(one, t))
    for h in range(kvh):
        mixed[h, pl.ds(pl.multiple_of(q * per, per), per), :] = acc[
            h * per : (h + 1) * per, :
        ].astype(mixed.dtype)

    @pl.when(q == n - 1)
    def _():
        for h in range(kvh):
            done = jnp.dot(mixed[h], value_ref[h], preferred_element_type=jnp.float32)
            out_ref[:, h] = done.reshape(n, per, done.shape[1]).astype(out_ref.dtype)


def sum_kernel(parts_ref, kept_ref, out_ref, total):
    n, kvh, per, hd = parts_ref.shape
    rows, heads = kept_ref.shape[:2]
    group = heads // kvh
    for h in range(kvh):
        terms = parts_ref[0, h].astype(jnp.float32)
        for i in range(1, n):
            terms = terms + parts_ref[i, h].astype(jnp.float32)
        for r in range(rows):
            here = slice((h * rows + r) * group, (h * rows + r + 1) * group)
            total[here, :] = (
                terms[r * group : (r + 1) * group] + kept_ref[r, h * group : (h + 1) * group, :]
            )
    pieces = [
        total[pl.ds(h * per + g, rows, stride=group), :]
        for h in range(kvh)
        for g in range(group)
    ]
    out_ref[...] = jnp.concatenate(pieces, 1).astype(out_ref.dtype)


def project_kernel(n, core_ref, *refs):
    row_refs, (weight_ref, own_ref, away_ref, gathered) = refs[:n], refs[n:]
    rows = row_refs[0].shape[0]
    cols = own_ref.shape[1]
    for k in range(0, n, 2):
        pair = [row_refs[k + j][...].astype(jnp.float32) for j in range(2)]
        gathered[k * rows : (k + 2) * rows, :] = jnp.concatenate(pair).astype(gathered.dtype)
    step = min(256, cols)
    for i in range(0, 2 * cols, step):
        done = jnp.dot(
            gathered[...], weight_ref[:, i : i + step], preferred_element_type=jnp.float32
        )
        here = slice(i % cols, i % cols + step)

        @pl.when(core_ref[0] == i // cols)
        def _(done=done, here=here):
            own_ref[:, here] = done

        @pl.when(core_ref[0] != i // cols)
        def _(done=done, here=here):
            away_ref[:, here] = done


def order_kernel(n, me_ref, own_ref, got_ref, out_ref):
    rows = own_ref.shape[0] // n
    for q in range(0, n, 2):
        pair = []
        for j in range(2):
            here = pl.ds(pl.multiple_of((me_ref[0] ^ (q + j)) * rows, rows), rows)
            pair.append(own_ref[here, :] + got_ref[here, :])
        out_ref[q * rows : (q + 2) * rows, :] = jnp.concatenate(pair).astype(out_ref.dtype)


def with_partner(x, k, n):
    return lax.ppermute(x, "pool", [(i, i ^ k) for i in range(n)])


def from_rest(held, n):
    k = n // 4
    while k >= 1:
        held = jnp.concatenate([held, with_partner(held, k, n)])
        k //= 2
    return held


def reversed_bits(k, n):
    out, bit = 0, 1
    while bit < n:
        out = out + (k // bit) % 2 * (n // 2 // bit)
        bit *= 2
    return out


def far_first(n):
    return sorted(range(1, n), reverse=True)


def swap_parts(parts, n):
    got = [parts[0]] + [None] * (n - 1)
    for k in far_first(n):
        got[k] = with_partner(parts[k], k, n)
    return got


def local(
    x_prompt, kv_weight, block_dest, block_row, block_fill, queries, kv_cache, cache_len, out_weight
):
    n = lax.axis_size("pool")
    ntp = lax.axis_size("tp")
    me = lax.axis_index("pool").astype(jnp.int32)
    core = lax.axis_index("tp").astype(jnp.int32)
    tokens, width = x_prompt.shape
    part = width // n
    kvh = kv_weight.shape[1]
    hd = kv_weight.shape[2] // 2
    rows, heads = queries.shape[0], queries.shape[1]
    group = heads // kvh
    per = rows * group
    cache_slots = kv_cache.shape[1]
    blocks = tokens // BLK
    cap = max(2, 2 * blocks // n)
    window = cap * BLK + BLK
    lanes = -(-n * window // 128) * 128
    half = tokens // ntp
    scale = 1.0 / hd**0.5
    swap = [(i, (i + 1) % ntp) for i in range(ntp)]

    size = half * 3 // 4
    extra = half - size
    at = jnp.stack([me, core])
    dest = block_dest[:, 0]
    packed = pack(x_prompt, block_fill, dest, at, n, 0, size)
    far = with_partner(queries, n // 2, n)
    packed, far = lax.optimization_barrier((packed, far))
    mine = lax.all_to_all(packed, "pool", 0, 0, tiled=True).reshape(n * size, part)

    index = jnp.arange(n * blocks, dtype=jnp.int32)
    sender = index // blocks
    kin = sender[None, :] == sender[:, None]
    lower = kin & (dest[None, :] < dest[:, None])
    level = kin & (dest[None, :] == dest[:, None]) & (index[None, :] < index[:, None])
    before = jnp.sum(jnp.where(lower, block_fill[None, :], 0), 1)
    within = jnp.sum(jnp.where(level, block_fill[None, :], 0), 1)
    pair = jnp.arange(n * n, dtype=jnp.int32)
    to, by = pair // n, pair % n
    owned = dest[None, :] == to[:, None]
    sent = sender[None, :] == by[:, None]
    earlier = sent & (dest[None, :] < to[:, None])
    offset = jnp.sum(jnp.where(earlier, block_fill[None, :], 0), 1)
    amount = jnp.sum(jnp.where(sent & owned, block_fill[None, :], 0), 1)
    runs = jnp.where(amount > 0, (offset % BLK + amount + BLK - 1) // BLK * BLK, 0)
    runs_by = runs.reshape(n, n)
    prior = jnp.arange(n)[:, None] < jnp.arange(n)[None, :]
    targets = jnp.sum(jnp.where(prior[None], runs_by[:, :, None], 0), 1)
    list_rows = jnp.sum(runs_by, 1)
    targets = targets.reshape(-1)
    mine_pair = (dest * n + sender)[:, None] == pair[None, :]
    start = (
        dest * lanes
        + jnp.sum(jnp.where(mine_pair, targets[None, :], 0), 1)
        + before % BLK
        + within
    )
    spot = jnp.arange(n * lanes, dtype=jnp.int32)[:, None]
    inside = (spot >= start[None, :]) & (spot < (start + block_fill)[None, :])
    rowof = jnp.sum(jnp.where(inside, (block_row + 1)[None, :], 0), 1) - 1
    rowof = rowof.reshape(n, 1, lanes)
    sources = by * tokens + offset // BLK * BLK

    most = jnp.max(jnp.sum(block_fill.reshape(n, blocks), 1))
    groups = lax.axis_size("groups")
    k = 1
    while k < groups:
        most = jnp.maximum(
            most, lax.ppermute(most, "groups", [(i, i ^ k) for i in range(groups)])
        )
        k *= 2
    over = most > ntp * size

    def exchange_rest():
        rest = pack(x_prompt, block_fill, dest, at, n, ntp * size, extra)
        rest = lax.all_to_all(rest, "pool", 0, 0, tiled=True).reshape(n * extra, part)
        return rest, lax.ppermute(rest, "tp", swap)

    def no_rest():
        return (jnp.zeros((n * extra, part), jnp.bfloat16),) * 2

    more_mine, more_other = lax.cond(over, exchange_rest, no_rest)
    meta = jnp.concatenate(
        [sources, targets, runs, list_rows, jnp.stack([me, core, over.astype(jnp.int32)])]
    )

    allq = from_rest(jnp.stack([queries, far]), n).reshape(n, rows, kvh, group, hd)
    keyed = jnp.einsum(
        "qrhgd,phd->hqrgp", allq, kv_weight[:, :, :hd], preferred_element_type=jnp.float32
    ).astype(jnp.bfloat16)
    keyed = keyed.reshape(kvh, n * per, part)
    values = kv_weight[:, :, hd:].transpose(1, 0, 2)

    query = queries.reshape(rows, kvh, group, hd)
    cache_scores = (
        jnp.einsum(
            "rhgd,rthd->rhgt", query, kv_cache[:, :, :, :hd], preferred_element_type=jnp.float32
        )
        * scale
    )
    cache_live = jnp.arange(cache_slots, dtype=jnp.int32)[None, :] < cache_len[:, None]
    cache_scores = jnp.where(cache_live[:, None, None, :], cache_scores, -jnp.inf)
    cache_top = jnp.max(cache_scores, -1, keepdims=True)
    cache_exp = jnp.exp(cache_scores - cache_top)
    cache_sum = jnp.sum(cache_exp, -1, keepdims=True)
    cached = jnp.einsum(
        "rhgt,rthd->rhgd",
        cache_exp.astype(jnp.bfloat16),
        kv_cache[:, :, :, hd:],
        preferred_element_type=jnp.float32,
    )
    cache_top = cache_top.reshape(rows, heads, 1)
    cache_sum = cache_sum.reshape(rows, heads, 1)
    cached = cached.reshape(rows, heads, hd)

    mine, meta, list_rows, rowof, keyed, values, cache_top, cache_sum, cached = (
        lax.optimization_barrier(
            (mine, meta, list_rows, rowof, keyed, values, cache_top, cache_sum, cached)
        )
    )
    other = lax.ppermute(mine, "tp", swap)

    anywhere = pl.BlockSpec(memory_space=pl.ANY)
    row_spec = pl.BlockSpec((1, 1, lanes), lambda q, m: (q, 0, 0))
    slot_spec = pl.BlockSpec((1, heads, lanes), lambda q, m: (q, 0, 0))
    slot_shape = jax.ShapeDtypeStruct((n, heads, lanes), jnp.bfloat16)
    cuts = tile_cuts(lanes)
    list_shapes = [(n, cuts[1], part), (n, lanes - cuts[1], part)]
    list_scratch = [pltpu.VMEM(shape, jnp.bfloat16) for shape in list_shapes]
    at_me = 3 * n * n + n
    partial_scores, low, high = pl.pallas_call(
        functools.partial(score_kernel, n, rows, window),
        grid_spec=pltpu.PrefetchScalarGridSpec(
            num_scalar_prefetch=1,
            grid=(n,),
            in_specs=[
                *[anywhere] * 4,
                pl.BlockSpec(
                    (kvh, per, part), lambda q, m: (0, reversed_bits(m[at_me] ^ q, n), 0)
                ),
                row_spec,
            ],
            out_specs=[slot_spec, anywhere, anywhere],
            scratch_shapes=[
                pltpu.VMEM((ntp, n * size, part), jnp.bfloat16),
                pltpu.VMEM((ntp, n * extra, part), jnp.bfloat16),
                pltpu.VMEM((n * tokens + window, part), jnp.float32),
                pltpu.VMEM((lanes + window, part), jnp.float32),
                *list_scratch,
                pltpu.SemaphoreType.DMA((ntp, 4)),
                pltpu.SemaphoreType.DMA((n, len(cuts) - 1)),
            ],
        ),
        out_shape=[
            slot_shape,
            *[jax.ShapeDtypeStruct(shape, jnp.bfloat16) for shape in list_shapes],
        ],
        compiler_params=pltpu.CompilerParams(vmem_limit_bytes=34 * MIB),
        name="prompt_scores",
    )(meta, mine, other, more_mine, more_other, keyed, rowof)

    parts = lax.all_to_all(partial_scores, "pool", 0, 0, tiled=True)
    my_rows = lax.dynamic_index_in_dim(rowof, me, 0, keepdims=False)
    weights, kept = pl.pallas_call(
        functools.partial(weight_kernel, scale),
        out_shape=[slot_shape, jax.ShapeDtypeStruct((rows, heads, hd), jnp.float32)],
        compiler_params=pltpu.CompilerParams(vmem_limit_bytes=8 * MIB),
        name="softmax_weights",
    )(parts, my_rows, cache_top, cache_sum, cached)

    all_weights = lax.all_to_all(weights, "pool", 0, 0, tiled=True)
    terms = pl.pallas_call(
        functools.partial(value_kernel, rows),
        grid_spec=pltpu.PrefetchScalarGridSpec(
            num_scalar_prefetch=1,
            grid=(n,),
            in_specs=[
                slot_spec,
                row_spec,
                anywhere,
                anywhere,
                pl.BlockSpec((kvh, part, hd), lambda q, m: (0, 0, 0)),
            ],
            out_specs=pl.BlockSpec((n, kvh, per, hd), lambda q, m: (0, 0, 0, 0)),
            scratch_shapes=[
                *list_scratch,
                pltpu.VMEM((kvh * per, part), jnp.float32),
                pltpu.VMEM((kvh, n * per, part), jnp.bfloat16),
                pltpu.SemaphoreType.DMA((n, len(cuts) - 1)),
            ],
        ),
        out_shape=jax.ShapeDtypeStruct((n, kvh, per, hd), jnp.bfloat16),
        compiler_params=pltpu.CompilerParams(vmem_limit_bytes=24 * MIB),
        name="weighted_values",
    )(list_rows, all_weights, rowof, low, high, values)

    term_parts = lax.all_to_all(terms, "pool", 0, 0, tiled=True)
    attended = pl.pallas_call(
        sum_kernel,
        out_shape=jax.ShapeDtypeStruct((rows, heads * hd), jnp.bfloat16),
        scratch_shapes=[pltpu.VMEM((kvh * per, hd), jnp.float32)],
        compiler_params=pltpu.CompilerParams(vmem_limit_bytes=8 * MIB),
        name="attended_sum",
    )(term_parts, kept)

    cols = out_weight.shape[1] // ntp
    half_shape = jax.ShapeDtypeStruct((n * rows, cols), jnp.float32)
    half_spec = pl.BlockSpec((n * rows, cols), lambda i, m: (0, 0))
    own, away = pl.pallas_call(
        functools.partial(project_kernel, n),
        grid_spec=pltpu.PrefetchScalarGridSpec(
            num_scalar_prefetch=1,
            grid=(1,),
            in_specs=[
                *[pl.BlockSpec((rows, heads * hd), lambda i, m: (0, 0))] * n,
                pl.BlockSpec(out_weight.shape, lambda i, m: (0, 0)),
            ],
            out_specs=[half_spec] * 2,
            scratch_shapes=[pltpu.VMEM((n * rows, heads * hd), jnp.bfloat16)],
        ),
        out_shape=[half_shape] * 2,
        compiler_params=pltpu.CompilerParams(vmem_limit_bytes=26 * MIB),
        name="output_projection",
    )(core.reshape(1), *swap_parts([attended] * n, n), out_weight)
    got = lax.ppermute(away, "tp", swap)
    return pl.pallas_call(
        functools.partial(order_kernel, n),
        grid_spec=pltpu.PrefetchScalarGridSpec(
            num_scalar_prefetch=1,
            grid=(1,),
            in_specs=[half_spec] * 2,
            out_specs=half_spec,
        ),
        out_shape=jax.ShapeDtypeStruct((n * rows, cols), jnp.bfloat16),
        compiler_params=pltpu.CompilerParams(vmem_limit_bytes=4 * MIB),
        name="order_rows",
    )(me.reshape(1), own, got)


def solution(mesh):
    in_specs = (
        P(("groups", "pool"), None),
        P("pool", "tp", None),
        P("groups", None),
        P("groups"),
        P("groups"),
        P(("groups", "pool"), "tp", None),
        P(("groups", "pool"), None, "tp", None),
        P(("groups", "pool")),
        P("tp", "pool"),
    )
    out_specs = P("groups", ("pool", "tp"))
    return jax.shard_map(local, mesh=mesh, in_specs=in_specs, out_specs=out_specs, check_vma=False)
```

```python
import functools

import jax
import jax.numpy as jnp
from jax import lax
from jax.experimental import pallas as pl
from jax.experimental.pallas import tpu as pltpu
from jax.sharding import PartitionSpec as P

BLK = 8
MIB = 1 << 20


def pack_kernel(base, at_ref, fill_ref, dest_ref, x_ref, out_ref, held, packed, count, in_sem, out_sem):
    n, tokens, part = held.shape
    size = packed.shape[1]
    blocks = tokens // BLK

    def load(q):
        return pltpu.make_async_copy(
            x_ref.at[:, pl.ds(q * part, part)], held.at[q], in_sem.at[q]
        )

    def store(q):
        return pltpu.make_async_copy(packed.at[q], out_ref.at[q], out_sem.at[q])

    for q in range(n):
        load(q).start()
    first = at_ref[0] * blocks
    for q in range(n):
        count[q] = 0

    @pl.loop(0, blocks)
    def _(b):
        owner = dest_ref[first + b]
        count[owner] = count[owner] + fill_ref[first + b]

    def starts(q, total):
        here = count[q]
        count[q] = total
        return total + here

    lax.fori_loop(0, n, starts, jnp.int32(0))
    token = lax.broadcasted_iota(jnp.int32, (1, tokens), 1)

    def place(b, ranks):
        owner = dest_ref[first + b]
        fill = fill_ref[first + b]
        start = count[owner]
        count[owner] = start + fill
        inner = token - b * BLK
        return jnp.where((inner >= 0) & (inner < fill), start + inner, ranks)

    ranks = lax.fori_loop(0, blocks, place, jnp.full((1, tokens), -1, jnp.int32))
    wanted = base + at_ref[1] * size + lax.broadcasted_iota(jnp.int32, (size, tokens), 0)
    pick = (wanted == ranks).astype(jnp.bfloat16)
    for q in range(n):
        load(q).wait()
        packed[q] = jnp.dot(pick, held[q], preferred_element_type=jnp.float32).astype(
            packed.dtype
        )
        store(q).start()
    for q in range(n):
        store(q).wait()


def pack(x_prompt, fill, dest, at, n, base, size):
    tokens, width = x_prompt.shape
    part = width // n
    return pl.pallas_call(
        functools.partial(pack_kernel, base),
        grid_spec=pltpu.PrefetchScalarGridSpec(
            num_scalar_prefetch=3,
            grid=(1,),
            in_specs=[pl.BlockSpec(memory_space=pl.ANY)],
            out_specs=pl.BlockSpec(memory_space=pl.ANY),
            scratch_shapes=[
                pltpu.VMEM((n, tokens, part), jnp.bfloat16),
                pltpu.VMEM((n, size, part), jnp.bfloat16),
                pltpu.SMEM((n,), jnp.int32),
                pltpu.SemaphoreType.DMA((n,)),
                pltpu.SemaphoreType.DMA((n,)),
            ],
        ),
        out_shape=jax.ShapeDtypeStruct((n, size, part), jnp.bfloat16),
        compiler_params=pltpu.CompilerParams(vmem_limit_bytes=56 * MIB),
        name="pack_live_tokens",
    )(at, fill, dest, x_prompt)


def tile_cuts(lanes):
    return [0] + list(range(min(256, lanes), lanes, 128)) + [lanes]


def load_tokens(n, core, over, x_refs, held, more, wide, sem):
    size, extra = held.shape[1] // n, more.shape[1] // n
    tokens = 2 * (size + extra)
    part = wide.shape[1]
    cuts = sem.shape[1]

    def copies(refs, buffer):
        span = buffer.shape[1] // cuts
        return [
            [
                pltpu.make_async_copy(
                    ref.at[pl.ds(i * span, span)], buffer.at[j, pl.ds(i * span, span)], sem.at[j, i]
                )
                for j, ref in enumerate(refs)
            ]
            for i in range(cuts)
        ]

    def widen(buffer, base, first, last):
        length = buffer.shape[1] // n

        @pl.loop(first, last)
        def _(s):
            for j in range(2):
                side = core if j == 0 else 1 - core
                to = pl.multiple_of(s * tokens + base + side * length, BLK)
                wide[pl.ds(to, length), :] = buffer[
                    j, pl.ds(pl.multiple_of(s * length, length), length), :
                ].astype(wide.dtype)

    main = copies(x_refs[:2], held)
    for pair in main:
        for copy in pair:
            copy.start()
    for i, pair in enumerate(main):
        for copy in pair:
            copy.wait()
        widen(held, 0, i * n // cuts, (i + 1) * n // cuts)

    @pl.when(over != 0)
    def _():
        rest = copies(x_refs[2:], more)
        for pair in rest:
            for copy in pair:
                copy.start()
        for pair in rest:
            for copy in pair:
                copy.wait()
        widen(more, 2 * size, 0, n)


def score_kernel(n, rows, meta_ref, *refs):
    x_refs, (near_ref, far_ref, row_ref), (out_ref, low_ref, high_ref) = refs[:4], refs[4:7], refs[7:10]
    held, more, wide, low, high, in_sem, out_sem = refs[10:]
    step = pl.program_id(0)
    part = wide.shape[1]
    lanes = out_ref.shape[2]
    cuts = tile_cuts(lanes)
    groups = lanes // BLK
    at_size = n * groups
    q = meta_ref[at_size + n] ^ reversed_bits(step, n)

    @pl.when(step == 0)
    def _():
        load_tokens(
            n, meta_ref[at_size + n + 1], meta_ref[at_size + n + 2], x_refs, held, more, wide, in_sem
        )

    kvh, per, _ = near_ref.shape
    group = per // rows
    keyed = jnp.where(step < n // 2, near_ref[...], far_ref[...]).reshape(kvh * per, part)

    def copy(o, t):
        if t == 0:
            return pltpu.make_async_copy(low.at[o], low_ref.at[o], out_sem.at[o, 0])
        here = pl.ds(cuts[t] - cuts[1], cuts[t + 1] - cuts[t])
        return pltpu.make_async_copy(
            high.at[o, here], high_ref.at[o, here], out_sem.at[o, t]
        )

    def one(t):
        here = slice(cuts[t], cuts[t + 1])
        buffer, base = (low, 0) if t == 0 else (high, cuts[1])
        for i in range(cuts[t], cuts[t + 1], 2 * BLK):
            pair = [
                wide[pl.ds(pl.multiple_of(meta_ref[q * groups + i // BLK + j], BLK), BLK), :]
                for j in range(2)
            ]
            buffer[q, i - base : i - base + 2 * BLK, :] = jnp.concatenate(pair).astype(low.dtype)
        copy(q, t).start()
        raw = lax.dot_general(
            keyed,
            buffer[q, cuts[t] - base : cuts[t + 1] - base, :],
            (((1,), (1,)), ((), ())),
            preferred_element_type=jnp.float32,
        ).reshape(kvh, rows, group, cuts[t + 1] - cuts[t])
        owner_row = row_ref[0, :, here]
        picked = jnp.zeros((kvh, group, cuts[t + 1] - cuts[t]), jnp.float32)
        for r in range(rows):
            picked = picked + jnp.where((owner_row == r)[None], raw[:, r], 0.0)
        out_ref[0, :, here] = picked.reshape(kvh * group, -1).astype(out_ref.dtype)

    one(0)
    for t in range(1, len(cuts) - 1):
        pl.when(meta_ref[at_size + q] > cuts[t])(functools.partial(one, t))

    @pl.when(step == n - 1)
    def _():
        for o in range(n):
            copy(o, 0).wait()
            for t in range(1, len(cuts) - 1):
                pl.when(meta_ref[at_size + o] > cuts[t])(lambda o=o, t=t: copy(o, t).wait())


def weight_kernel(scale, parts_ref, row_ref, top_ref, sum_ref, cached_ref, w_ref, kept_ref):
    n = parts_ref.shape[0]
    scores = parts_ref[0].astype(jnp.float32)
    for i in range(1, n):
        scores = scores + parts_ref[i].astype(jnp.float32)
    scores = scores * scale
    owner_row = row_ref[...]
    weights = jnp.zeros(scores.shape, jnp.float32)
    for r in range(top_ref.shape[0]):
        own = jnp.where(owner_row == r, scores, -jnp.inf)
        cache_top = top_ref[r]
        top = jnp.maximum(jnp.max(own, 1, keepdims=True), cache_top)
        held = jnp.exp(own - top)
        fade = jnp.exp(cache_top - top)
        total = jnp.sum(held, 1, keepdims=True) + sum_ref[r] * fade
        weights = weights + held / total
        kept_ref[r] = cached_ref[r] * (fade / total)
    weights = weights.astype(w_ref.dtype)
    for i in range(n):
        w_ref[i] = weights


def value_kernel(
    rows, size_ref, w_ref, row_ref, low_ref, high_ref, value_ref, out_ref, low, high, acc, mixed, sem
):
    q = pl.program_id(0)
    n = low.shape[0]
    kvh = value_ref.shape[0]
    _, heads, lanes = w_ref.shape
    per = rows * heads // kvh
    cuts = tile_cuts(lanes)

    def copy(o, t):
        if t == 0:
            return pltpu.make_async_copy(low_ref.at[o], low.at[o], sem.at[o, 0])
        here = pl.ds(cuts[t] - cuts[1], cuts[t + 1] - cuts[t])
        return pltpu.make_async_copy(high_ref.at[o, here], high.at[o, here], sem.at[o, t])

    @pl.when(q == 0)
    def _():
        for o in range(n):
            copy(o, 0).start()
            for t in range(1, len(cuts) - 1):
                pl.when(size_ref[o] > cuts[t])(lambda o=o, t=t: copy(o, t).start())

    def one(t):
        copy(q, t).wait()
        here = slice(cuts[t], cuts[t + 1])
        width = cuts[t + 1] - cuts[t]
        weights = w_ref[0, :, here].astype(jnp.float32).reshape(kvh, 1, heads // kvh, width)
        owner_row = row_ref[0, :, here]
        spread = jnp.concatenate(
            [jnp.where((owner_row == r)[None, None], weights, 0.0) for r in range(rows)], 1
        ).reshape(kvh * per, width)
        tile = low[q] if t == 0 else high[q, cuts[t] - cuts[1] : cuts[t + 1] - cuts[1], :]
        got = jnp.dot(spread.astype(jnp.bfloat16), tile, preferred_element_type=jnp.float32)
        if t:
            acc[...] += got
        else:
            acc[...] = got

    one(0)
    for t in range(1, len(cuts) - 1):
        pl.when(size_ref[q] > cuts[t])(functools.partial(one, t))
    for h in range(kvh):
        mixed[h, pl.ds(pl.multiple_of(q * per, per), per), :] = acc[
            h * per : (h + 1) * per, :
        ].astype(mixed.dtype)

    @pl.when(q == n - 1)
    def _():
        for h in range(kvh):
            done = jnp.dot(mixed[h], value_ref[h], preferred_element_type=jnp.float32)
            out_ref[:, h] = done.reshape(n, per, done.shape[1]).astype(out_ref.dtype)


def sum_kernel(parts_ref, kept_ref, out_ref, total):
    n, kvh, per, hd = parts_ref.shape
    rows, heads = kept_ref.shape[:2]
    group = heads // kvh
    for h in range(kvh):
        terms = parts_ref[0, h].astype(jnp.float32)
        for i in range(1, n):
            terms = terms + parts_ref[i, h].astype(jnp.float32)
        for r in range(rows):
            here = slice((h * rows + r) * group, (h * rows + r + 1) * group)
            total[here, :] = (
                terms[r * group : (r + 1) * group] + kept_ref[r, h * group : (h + 1) * group, :]
            )
    pieces = [
        total[pl.ds(h * per + g, rows, stride=group), :]
        for h in range(kvh)
        for g in range(group)
    ]
    out_ref[...] = jnp.concatenate(pieces, 1).astype(out_ref.dtype)


def project_kernel(n, core_ref, *refs):
    row_refs, (weight_ref, own_ref, away_ref, gathered) = refs[:n], refs[n:]
    rows = row_refs[0].shape[0]
    cols = own_ref.shape[1]
    for k in range(0, n, 2):
        pair = [row_refs[k + j][...].astype(jnp.float32) for j in range(2)]
        gathered[k * rows : (k + 2) * rows, :] = jnp.concatenate(pair).astype(gathered.dtype)
    step = min(256, cols)
    for i in range(0, 2 * cols, step):
        done = jnp.dot(
            gathered[...], weight_ref[:, i : i + step], preferred_element_type=jnp.float32
        )
        here = slice(i % cols, i % cols + step)

        @pl.when(core_ref[0] == i // cols)
        def _(done=done, here=here):
            own_ref[:, here] = done

        @pl.when(core_ref[0] != i // cols)
        def _(done=done, here=here):
            away_ref[:, here] = done


def order_kernel(n, me_ref, own_ref, got_ref, out_ref):
    rows = own_ref.shape[0] // n
    for q in range(0, n, 2):
        pair = []
        for j in range(2):
            here = pl.ds(pl.multiple_of((me_ref[0] ^ (q + j)) * rows, rows), rows)
            pair.append(own_ref[here, :] + got_ref[here, :])
        out_ref[q * rows : (q + 2) * rows, :] = jnp.concatenate(pair).astype(out_ref.dtype)


def with_partner(x, k, n):
    return lax.ppermute(x, "pool", [(i, i ^ k) for i in range(n)])


def from_rest(held, n):
    k = n // 4
    while k >= 2:
        held = jnp.concatenate([held, with_partner(held, k, n)])
        k //= 2
    return held


def reversed_bits(k, n):
    out, bit = 0, 1
    while bit < n:
        out = out + (k // bit) % 2 * (n // 2 // bit)
        bit *= 2
    return out


def far_first(n):
    return sorted(range(1, n), reverse=True)


def swap_parts(parts, n):
    got = [parts[0]] + [None] * (n - 1)
    for k in far_first(n):
        got[k] = with_partner(parts[k], k, n)
    return got


def local(
    x_prompt, kv_weight, block_dest, block_row, block_fill, queries, kv_cache, cache_len, out_weight
):
    n = lax.axis_size("pool")
    ntp = lax.axis_size("tp")
    me = lax.axis_index("pool").astype(jnp.int32)
    core = lax.axis_index("tp").astype(jnp.int32)
    tokens, width = x_prompt.shape
    part = width // n
    kvh = kv_weight.shape[1]
    hd = kv_weight.shape[2] // 2
    rows, heads = queries.shape[0], queries.shape[1]
    group = heads // kvh
    per = rows * group
    cache_slots = kv_cache.shape[1]
    blocks = tokens // BLK
    cap = max(2, 2 * blocks // n)
    window = cap * BLK + BLK
    lanes = -(-n * window // 128) * 128
    half = tokens // ntp
    scale = 1.0 / hd**0.5
    swap = [(i, (i + 1) % ntp) for i in range(ntp)]

    size = half * 3 // 4
    extra = half - size
    at = jnp.stack([me, core])
    pack_fill, pack_dest = block_fill, block_dest[:, 0]
    packed = pack(x_prompt, pack_fill, pack_dest, at, n, 0, size)
    dest = pack_dest
    far = with_partner(queries, n // 2, n)
    packed, far, dest, block_row, block_fill, query, kv_cache, kv_weight = (
        lax.optimization_barrier(
            (packed, far, dest, block_row, block_fill, queries, kv_cache, kv_weight)
        )
    )
    mine = lax.all_to_all(packed, "pool", 0, 0, tiled=True).reshape(n * size, part)

    index = jnp.arange(n * blocks, dtype=jnp.int32)
    sender = index // blocks
    kin = sender[None, :] == sender[:, None]
    lower = kin & (dest[None, :] < dest[:, None])
    level = kin & (dest[None, :] == dest[:, None]) & (index[None, :] < index[:, None])
    before = jnp.sum(jnp.where(lower, block_fill[None, :], 0), 1)
    within = jnp.sum(jnp.where(level, block_fill[None, :], 0), 1)
    pair = jnp.arange(n * n, dtype=jnp.int32)
    to, by = pair // n, pair % n
    owned = dest[None, :] == to[:, None]
    sent = sender[None, :] == by[:, None]
    earlier = sent & (dest[None, :] < to[:, None])
    offset = jnp.sum(jnp.where(earlier, block_fill[None, :], 0), 1)
    amount = jnp.sum(jnp.where(sent & owned, block_fill[None, :], 0), 1)
    runs = jnp.where(amount > 0, (offset % BLK + amount + BLK - 1) // BLK * BLK, 0)
    runs_by = runs.reshape(n, n)
    prior = jnp.arange(n)[:, None] < jnp.arange(n)[None, :]
    targets = jnp.sum(jnp.where(prior[None], runs_by[:, :, None], 0), 1)
    list_rows = jnp.sum(runs_by, 1)
    targets = targets.reshape(-1)
    sources = by * tokens + offset // BLK * BLK
    group_at = jnp.arange(n * lanes // BLK, dtype=jnp.int32) * BLK
    skip = group_at[:, None] - (to * lanes + targets)[None, :]
    group_rows = jnp.sum(
        jnp.where((skip >= 0) & (skip < runs[None, :]), sources[None, :] + skip, 0), 1
    )
    mine_pair = (dest * n + sender)[:, None] == pair[None, :]
    start = (
        dest * lanes
        + jnp.sum(jnp.where(mine_pair, targets[None, :], 0), 1)
        + before % BLK
        + within
    )
    spot = jnp.arange(n * lanes, dtype=jnp.int32)[:, None]
    inside = (spot >= start[None, :]) & (spot < (start + block_fill)[None, :])
    rowof = jnp.sum(jnp.where(inside, (block_row + 1)[None, :], 0), 1) - 1
    rowof = rowof.reshape(n, 1, lanes)

    most = jnp.max(jnp.sum(block_fill.reshape(n, blocks), 1))
    groups = lax.axis_size("groups")
    k = 1
    while k < groups:
        most = jnp.maximum(
            most, lax.ppermute(most, "groups", [(i, i ^ k) for i in range(groups)])
        )
        k *= 2
    over = most > ntp * size

    def exchange_rest():
        rest = pack(x_prompt, pack_fill, pack_dest, at, n, ntp * size, extra)
        rest = lax.all_to_all(rest, "pool", 0, 0, tiled=True).reshape(n * extra, part)
        return rest, lax.ppermute(rest, "tp", swap)

    def no_rest():
        return (jnp.zeros((n * extra, part), jnp.bfloat16),) * 2

    more_mine, more_other = lax.cond(over, exchange_rest, no_rest)
    meta = jnp.concatenate(
        [group_rows, list_rows, jnp.stack([me, core, over.astype(jnp.int32)])]
    )

    keys = kv_weight[:, :, :hd]

    def through_keys(held):
        held = held.reshape(n // 2, rows, kvh, group, hd)
        return (
            jnp.einsum("qrhgd,phd->hqrgp", held, keys, preferred_element_type=jnp.float32)
            .astype(jnp.bfloat16)
            .reshape(kvh, n // 2 * per, part)
        )

    even = from_rest(jnp.stack([queries, far]), n)
    keyed_even = through_keys(even)
    keyed_odd = through_keys(with_partner(even, 1, n))
    values = kv_weight[:, :, hd:].transpose(1, 0, 2)

    query = query.reshape(rows, kvh, group, hd)
    cache_scores = (
        jnp.einsum(
            "rhgd,rthd->rhgt", query, kv_cache[:, :, :, :hd], preferred_element_type=jnp.float32
        )
        * scale
    )
    cache_live = jnp.arange(cache_slots, dtype=jnp.int32)[None, :] < cache_len[:, None]
    cache_scores = jnp.where(cache_live[:, None, None, :], cache_scores, -jnp.inf)
    cache_top = jnp.max(cache_scores, -1, keepdims=True)
    cache_exp = jnp.exp(cache_scores - cache_top)
    cache_sum = jnp.sum(cache_exp, -1, keepdims=True)
    cached = jnp.einsum(
        "rhgt,rthd->rhgd",
        cache_exp.astype(jnp.bfloat16),
        kv_cache[:, :, :, hd:],
        preferred_element_type=jnp.float32,
    )
    cache_top = cache_top.reshape(rows, heads, 1)
    cache_sum = cache_sum.reshape(rows, heads, 1)
    cached = cached.reshape(rows, heads, hd)

    mine, meta, list_rows, rowof, keyed_even, values, cache_top, cache_sum, cached = (
        lax.optimization_barrier(
            (mine, meta, list_rows, rowof, keyed_even, values, cache_top, cache_sum, cached)
        )
    )
    other = lax.ppermute(mine, "tp", swap)

    in_hbm = pl.BlockSpec(memory_space=pltpu.HBM)
    row_spec = pl.BlockSpec((1, 1, lanes), lambda q, m: (q, 0, 0))
    slot_spec = pl.BlockSpec((1, heads, lanes), lambda q, m: (q, 0, 0))
    slot_shape = jax.ShapeDtypeStruct((n, heads, lanes), jnp.bfloat16)
    cuts = tile_cuts(lanes)
    list_shapes = [(n, cuts[1], part), (n, lanes - cuts[1], part)]
    list_scratch = [pltpu.VMEM(shape, jnp.bfloat16) for shape in list_shapes]
    at_me = n * lanes // BLK + n

    def owner(i, m):
        return m[at_me] ^ reversed_bits(i, n)

    partial_scores, low, high = pl.pallas_call(
        functools.partial(score_kernel, n, rows),
        grid_spec=pltpu.PrefetchScalarGridSpec(
            num_scalar_prefetch=1,
            grid=(n,),
            in_specs=[
                *[in_hbm] * 4,
                pl.BlockSpec((kvh, per, part), lambda i, m: (0, jnp.minimum(i, n // 2 - 1), 0)),
                pl.BlockSpec((kvh, per, part), lambda i, m: (0, jnp.maximum(i - n // 2, 0), 0)),
                pl.BlockSpec((1, 1, lanes), lambda i, m: (owner(i, m), 0, 0)),
            ],
            out_specs=[
                pl.BlockSpec((1, heads, lanes), lambda i, m: (owner(i, m), 0, 0)),
                in_hbm,
                in_hbm,
            ],
            scratch_shapes=[
                pltpu.VMEM((ntp, n * size, part), jnp.bfloat16),
                pltpu.VMEM((ntp, n * extra, part), jnp.bfloat16),
                pltpu.VMEM((n * tokens, part), jnp.float32),
                *list_scratch,
                pltpu.SemaphoreType.DMA((ntp, 4)),
                pltpu.SemaphoreType.DMA((n, len(cuts) - 1)),
            ],
        ),
        out_shape=[
            slot_shape,
            *[jax.ShapeDtypeStruct(shape, jnp.bfloat16) for shape in list_shapes],
        ],
        compiler_params=pltpu.CompilerParams(vmem_limit_bytes=32 * MIB),
        name="prompt_scores",
    )(meta, mine, other, more_mine, more_other, keyed_even, keyed_odd, rowof)

    parts = lax.all_to_all(partial_scores, "pool", 0, 0, tiled=True)
    my_rows = lax.dynamic_index_in_dim(rowof, me, 0, keepdims=False)
    weights, kept = pl.pallas_call(
        functools.partial(weight_kernel, scale),
        out_shape=[slot_shape, jax.ShapeDtypeStruct((rows, heads, hd), jnp.float32)],
        compiler_params=pltpu.CompilerParams(vmem_limit_bytes=8 * MIB),
        name="softmax_weights",
    )(parts, my_rows, cache_top, cache_sum, cached)

    all_weights = lax.all_to_all(weights, "pool", 0, 0, tiled=True)
    terms = pl.pallas_call(
        functools.partial(value_kernel, rows),
        grid_spec=pltpu.PrefetchScalarGridSpec(
            num_scalar_prefetch=1,
            grid=(n,),
            in_specs=[
                slot_spec,
                row_spec,
                in_hbm,
                in_hbm,
                pl.BlockSpec((kvh, part, hd), lambda q, m: (0, 0, 0)),
            ],
            out_specs=pl.BlockSpec((n, kvh, per, hd), lambda q, m: (0, 0, 0, 0)),
            scratch_shapes=[
                *list_scratch,
                pltpu.VMEM((kvh * per, part), jnp.float32),
                pltpu.VMEM((kvh, n * per, part), jnp.bfloat16),
                pltpu.SemaphoreType.DMA((n, len(cuts) - 1)),
            ],
        ),
        out_shape=jax.ShapeDtypeStruct((n, kvh, per, hd), jnp.bfloat16),
        compiler_params=pltpu.CompilerParams(vmem_limit_bytes=24 * MIB),
        name="weighted_values",
    )(list_rows, all_weights, rowof, low, high, values)

    term_parts = lax.all_to_all(terms, "pool", 0, 0, tiled=True)
    attended = pl.pallas_call(
        sum_kernel,
        out_shape=jax.ShapeDtypeStruct((rows, heads * hd), jnp.bfloat16),
        scratch_shapes=[pltpu.VMEM((kvh * per, hd), jnp.float32)],
        compiler_params=pltpu.CompilerParams(vmem_limit_bytes=8 * MIB),
        name="attended_sum",
    )(term_parts, kept)

    cols = out_weight.shape[1] // ntp
    half_shape = jax.ShapeDtypeStruct((n * rows, cols), jnp.float32)
    half_spec = pl.BlockSpec((n * rows, cols), lambda i, m: (0, 0))
    own, away = pl.pallas_call(
        functools.partial(project_kernel, n),
        grid_spec=pltpu.PrefetchScalarGridSpec(
            num_scalar_prefetch=1,
            grid=(1,),
            in_specs=[
                *[pl.BlockSpec((rows, heads * hd), lambda i, m: (0, 0))] * n,
                pl.BlockSpec(out_weight.shape, lambda i, m: (0, 0)),
            ],
            out_specs=[half_spec] * 2,
            scratch_shapes=[pltpu.VMEM((n * rows, heads * hd), jnp.bfloat16)],
        ),
        out_shape=[half_shape] * 2,
        compiler_params=pltpu.CompilerParams(vmem_limit_bytes=26 * MIB),
        name="output_projection",
    )(core.reshape(1), *swap_parts([attended] * n, n), out_weight)
    got = lax.ppermute(away, "tp", swap)
    return pl.pallas_call(
        functools.partial(order_kernel, n),
        grid_spec=pltpu.PrefetchScalarGridSpec(
            num_scalar_prefetch=1,
            grid=(1,),
            in_specs=[half_spec] * 2,
            out_specs=half_spec,
        ),
        out_shape=jax.ShapeDtypeStruct((n * rows, cols), jnp.bfloat16),
        compiler_params=pltpu.CompilerParams(vmem_limit_bytes=4 * MIB),
        name="order_rows",
    )(me.reshape(1), own, got)


def solution(mesh):
    in_specs = (
        P(("groups", "pool"), None),
        P("pool", "tp", None),
        P("groups", None),
        P("groups"),
        P("groups"),
        P(("groups", "pool"), "tp", None),
        P(("groups", "pool"), None, "tp", None),
        P(("groups", "pool")),
        P("tp", "pool"),
    )
    out_specs = P("groups", ("pool", "tp"))
    return jax.shard_map(local, mesh=mesh, in_specs=in_specs, out_specs=out_specs, check_vma=False)
```

```python
import functools

import jax
import jax.numpy as jnp
from jax import lax
from jax.experimental import pallas as pl
from jax.experimental.pallas import tpu as pltpu
from jax.sharding import PartitionSpec as P

BLK = 8
MIB = 1 << 20


def pack_kernel(base, at_ref, fill_ref, dest_ref, x_ref, out_ref, held, packed, count, in_sem, out_sem):
    n, tokens, part = held.shape
    size = packed.shape[1]
    blocks = tokens // BLK

    def load(q):
        return pltpu.make_async_copy(
            x_ref.at[:, pl.ds(q * part, part)], held.at[q], in_sem.at[q]
        )

    def store(q):
        return pltpu.make_async_copy(packed.at[q], out_ref.at[q], out_sem.at[q])

    for q in range(n):
        load(q).start()
    first = at_ref[0] * blocks
    for q in range(n):
        count[q] = 0

    @pl.loop(0, blocks)
    def _(b):
        owner = dest_ref[first + b]
        count[owner] = count[owner] + fill_ref[first + b]

    def starts(q, total):
        here = count[q]
        count[q] = total
        return total + here

    lax.fori_loop(0, n, starts, jnp.int32(0))
    token = lax.broadcasted_iota(jnp.int32, (1, tokens), 1)

    def place(b, ranks):
        owner = dest_ref[first + b]
        fill = fill_ref[first + b]
        start = count[owner]
        count[owner] = start + fill
        inner = token - b * BLK
        return jnp.where((inner >= 0) & (inner < fill), start + inner, ranks)

    ranks = lax.fori_loop(0, blocks, place, jnp.full((1, tokens), -1, jnp.int32))
    wanted = base + at_ref[1] * size + lax.broadcasted_iota(jnp.int32, (size, tokens), 0)
    pick = (wanted == ranks).astype(jnp.bfloat16)
    for q in range(n):
        load(q).wait()
        packed[q] = jnp.dot(pick, held[q], preferred_element_type=jnp.float32).astype(
            packed.dtype
        )
        store(q).start()
    for q in range(n):
        store(q).wait()


def pack(x_prompt, fill, dest, at, n, base, size):
    tokens, width = x_prompt.shape
    part = width // n
    return pl.pallas_call(
        functools.partial(pack_kernel, base),
        grid_spec=pltpu.PrefetchScalarGridSpec(
            num_scalar_prefetch=3,
            grid=(1,),
            in_specs=[pl.BlockSpec(memory_space=pl.ANY)],
            out_specs=pl.BlockSpec(memory_space=pl.ANY),
            scratch_shapes=[
                pltpu.VMEM((n, tokens, part), jnp.bfloat16),
                pltpu.VMEM((n, size, part), jnp.bfloat16),
                pltpu.SMEM((n,), jnp.int32),
                pltpu.SemaphoreType.DMA((n,)),
                pltpu.SemaphoreType.DMA((n,)),
            ],
        ),
        out_shape=jax.ShapeDtypeStruct((n, size, part), jnp.bfloat16),
        compiler_params=pltpu.CompilerParams(vmem_limit_bytes=56 * MIB),
        name="pack_live_tokens",
    )(at, fill, dest, x_prompt)


def tile_cuts(lanes):
    return [0] + list(range(min(256, lanes), lanes, 128)) + [lanes]


def load_tokens(n, core, over, x_refs, held, more, wide, sem):
    size, extra = held.shape[1] // n, more.shape[1] // n
    tokens = 2 * (size + extra)
    part = wide.shape[1]
    cuts = sem.shape[1]

    def copies(refs, buffer):
        span = buffer.shape[1] // cuts
        return [
            [
                pltpu.make_async_copy(
                    ref.at[pl.ds(i * span, span)], buffer.at[j, pl.ds(i * span, span)], sem.at[j, i]
                )
                for j, ref in enumerate(refs)
            ]
            for i in range(cuts)
        ]

    def widen(buffer, base, first, last):
        length = buffer.shape[1] // n

        @pl.loop(first, last)
        def _(s):
            for j in range(2):
                side = core if j == 0 else 1 - core
                to = pl.multiple_of(s * tokens + base + side * length, BLK)
                wide[pl.ds(to, length), :] = buffer[
                    j, pl.ds(pl.multiple_of(s * length, length), length), :
                ].astype(wide.dtype)

    main = copies(x_refs[:2], held)
    for pair in main:
        for copy in pair:
            copy.start()
    for i, pair in enumerate(main):
        for copy in pair:
            copy.wait()
        widen(held, 0, i * n // cuts, (i + 1) * n // cuts)

    @pl.when(over != 0)
    def _():
        rest = copies(x_refs[2:], more)
        for pair in rest:
            for copy in pair:
                copy.start()
        for pair in rest:
            for copy in pair:
                copy.wait()
        widen(more, 2 * size, 0, n)


def score_kernel(n, rows, meta_ref, *refs):
    x_refs, (near_ref, far_ref, row_ref), (out_ref, low_ref, high_ref) = refs[:4], refs[4:7], refs[7:10]
    held, more, wide, low, high, in_sem, out_sem = refs[10:]
    step = pl.program_id(0)
    part = wide.shape[1]
    lanes = out_ref.shape[2]
    cuts = tile_cuts(lanes)
    groups = lanes // BLK
    at_size = n * groups
    q = meta_ref[at_size + n] ^ reversed_bits(step, n)

    @pl.when(step == 0)
    def _():
        load_tokens(
            n, meta_ref[at_size + n + 1], meta_ref[at_size + n + 2], x_refs, held, more, wide, in_sem
        )

    kvh, per, _ = near_ref.shape
    group = per // rows
    keyed = jnp.where(step < n // 2, near_ref[...], far_ref[...]).reshape(kvh * per, part)

    def copy(o, t):
        if t == 0:
            return pltpu.make_async_copy(low.at[o], low_ref.at[o], out_sem.at[o, 0])
        here = pl.ds(cuts[t] - cuts[1], cuts[t + 1] - cuts[t])
        return pltpu.make_async_copy(
            high.at[o, here], high_ref.at[o, here], out_sem.at[o, t]
        )

    def one(t):
        here = slice(cuts[t], cuts[t + 1])
        buffer, base = (low, 0) if t == 0 else (high, cuts[1])
        for i in range(cuts[t], cuts[t + 1], 2 * BLK):
            pair = [
                wide[pl.ds(pl.multiple_of(meta_ref[q * groups + i // BLK + j], BLK), BLK), :]
                for j in range(2)
            ]
            buffer[q, i - base : i - base + 2 * BLK, :] = jnp.concatenate(pair).astype(low.dtype)
        copy(q, t).start()
        raw = lax.dot_general(
            keyed,
            buffer[q, cuts[t] - base : cuts[t + 1] - base, :],
            (((1,), (1,)), ((), ())),
            preferred_element_type=jnp.float32,
        ).reshape(kvh, rows, group, cuts[t + 1] - cuts[t])
        owner_row = row_ref[0, :, here]
        picked = jnp.zeros((kvh, group, cuts[t + 1] - cuts[t]), jnp.float32)
        for r in range(rows):
            picked = picked + jnp.where((owner_row == r)[None], raw[:, r], 0.0)
        out_ref[0, :, here] = picked.reshape(kvh * group, -1).astype(out_ref.dtype)

    one(0)
    for t in range(1, len(cuts) - 1):
        pl.when(meta_ref[at_size + q] > cuts[t])(functools.partial(one, t))

    @pl.when(step == n - 1)
    def _():
        for o in range(n):
            copy(o, 0).wait()
            for t in range(1, len(cuts) - 1):
                pl.when(meta_ref[at_size + o] > cuts[t])(lambda o=o, t=t: copy(o, t).wait())


def weight_kernel(scale, parts_ref, row_ref, top_ref, sum_ref, cached_ref, w_ref, kept_ref):
    n = parts_ref.shape[0]
    scores = parts_ref[0].astype(jnp.float32)
    for i in range(1, n):
        scores = scores + parts_ref[i].astype(jnp.float32)
    scores = scores * scale
    owner_row = row_ref[...]
    weights = jnp.zeros(scores.shape, jnp.float32)
    for r in range(top_ref.shape[0]):
        own = jnp.where(owner_row == r, scores, -jnp.inf)
        cache_top = top_ref[r]
        top = jnp.maximum(jnp.max(own, 1, keepdims=True), cache_top)
        held = jnp.exp(own - top)
        fade = jnp.exp(cache_top - top)
        total = jnp.sum(held, 1, keepdims=True) + sum_ref[r] * fade
        weights = weights + held / total
        kept_ref[r] = cached_ref[r] * (fade / total)
    weights = weights.astype(w_ref.dtype)
    for i in range(n):
        w_ref[i] = weights


def value_kernel(
    rows, size_ref, w_ref, row_ref, low_ref, high_ref, value_ref, out_ref, low, high, acc, mixed, sem
):
    q = pl.program_id(0)
    n = low.shape[0]
    kvh = value_ref.shape[0]
    _, heads, lanes = w_ref.shape
    per = rows * heads // kvh
    cuts = tile_cuts(lanes)

    def copy(o, t):
        if t == 0:
            return pltpu.make_async_copy(low_ref.at[o], low.at[o], sem.at[o, 0])
        here = pl.ds(cuts[t] - cuts[1], cuts[t + 1] - cuts[t])
        return pltpu.make_async_copy(high_ref.at[o, here], high.at[o, here], sem.at[o, t])

    @pl.when(q == 0)
    def _():
        for o in range(n):
            copy(o, 0).start()
            for t in range(1, len(cuts) - 1):
                pl.when(size_ref[o] > cuts[t])(lambda o=o, t=t: copy(o, t).start())

    def one(t):
        copy(q, t).wait()
        here = slice(cuts[t], cuts[t + 1])
        width = cuts[t + 1] - cuts[t]
        weights = w_ref[0, :, here].astype(jnp.float32).reshape(kvh, 1, heads // kvh, width)
        owner_row = row_ref[0, :, here]
        spread = jnp.concatenate(
            [jnp.where((owner_row == r)[None, None], weights, 0.0) for r in range(rows)], 1
        ).reshape(kvh * per, width)
        tile = low[q] if t == 0 else high[q, cuts[t] - cuts[1] : cuts[t + 1] - cuts[1], :]
        got = jnp.dot(spread.astype(jnp.bfloat16), tile, preferred_element_type=jnp.float32)
        if t:
            acc[...] += got
        else:
            acc[...] = got

    one(0)
    for t in range(1, len(cuts) - 1):
        pl.when(size_ref[q] > cuts[t])(functools.partial(one, t))
    for h in range(kvh):
        mixed[h, pl.ds(pl.multiple_of(q * per, per), per), :] = acc[
            h * per : (h + 1) * per, :
        ].astype(mixed.dtype)

    @pl.when(q == n - 1)
    def _():
        for h in range(kvh):
            done = jnp.dot(mixed[h], value_ref[h], preferred_element_type=jnp.float32)
            out_ref[:, h] = done.reshape(n, per, done.shape[1]).astype(out_ref.dtype)


def sum_kernel(parts_ref, kept_ref, out_ref, total):
    n, kvh, per, hd = parts_ref.shape
    rows, heads = kept_ref.shape[:2]
    group = heads // kvh
    for h in range(kvh):
        terms = parts_ref[0, h].astype(jnp.float32)
        for i in range(1, n):
            terms = terms + parts_ref[i, h].astype(jnp.float32)
        for r in range(rows):
            here = slice((h * rows + r) * group, (h * rows + r + 1) * group)
            total[here, :] = (
                terms[r * group : (r + 1) * group] + kept_ref[r, h * group : (h + 1) * group, :]
            )
    pieces = [
        total[pl.ds(h * per + g, rows, stride=group), :]
        for h in range(kvh)
        for g in range(group)
    ]
    out_ref[...] = jnp.concatenate(pieces, 1).astype(out_ref.dtype)


def project_kernel(n, core_ref, *refs):
    row_refs, (weight_ref, own_ref, away_ref, gathered) = refs[:n], refs[n:]
    rows = row_refs[0].shape[0]
    cols = own_ref.shape[1]
    for k in range(0, n, 2):
        pair = [row_refs[k + j][...].astype(jnp.float32) for j in range(2)]
        gathered[k * rows : (k + 2) * rows, :] = jnp.concatenate(pair).astype(gathered.dtype)
    step = min(256, cols)
    for i in range(0, 2 * cols, step):
        done = jnp.dot(
            gathered[...], weight_ref[:, i : i + step], preferred_element_type=jnp.float32
        )
        here = slice(i % cols, i % cols + step)

        @pl.when(core_ref[0] == i // cols)
        def _(done=done, here=here):
            own_ref[:, here] = done

        @pl.when(core_ref[0] != i // cols)
        def _(done=done, here=here):
            away_ref[:, here] = done


def order_kernel(n, me_ref, own_ref, got_ref, out_ref):
    rows = own_ref.shape[0] // n
    for q in range(0, n, 2):
        pair = []
        for j in range(2):
            here = pl.ds(pl.multiple_of((me_ref[0] ^ (q + j)) * rows, rows), rows)
            pair.append(own_ref[here, :] + got_ref[here, :])
        out_ref[q * rows : (q + 2) * rows, :] = jnp.concatenate(pair).astype(out_ref.dtype)


def with_partner(x, k, n):
    return lax.ppermute(x, "pool", [(i, i ^ k) for i in range(n)])


def from_rest(held, n):
    k = n // 4
    while k >= 2:
        held = jnp.concatenate([held, with_partner(held, k, n)])
        k //= 2
    return held


def reversed_bits(k, n):
    out, bit = 0, 1
    while bit < n:
        out = out + (k // bit) % 2 * (n // 2 // bit)
        bit *= 2
    return out


def far_first(n):
    return sorted(range(1, n), reverse=True)


def swap_parts(parts, n):
    got = [parts[0]] + [None] * (n - 1)
    for k in far_first(n):
        got[k] = with_partner(parts[k], k, n)
    return got


def local(
    x_prompt, kv_weight, block_dest, block_row, block_fill, queries, kv_cache, cache_len, out_weight
):
    n = lax.axis_size("pool")
    ntp = lax.axis_size("tp")
    me = lax.axis_index("pool").astype(jnp.int32)
    core = lax.axis_index("tp").astype(jnp.int32)
    tokens, width = x_prompt.shape
    part = width // n
    kvh = kv_weight.shape[1]
    hd = kv_weight.shape[2] // 2
    rows, heads = queries.shape[0], queries.shape[1]
    group = heads // kvh
    per = rows * group
    cache_slots = kv_cache.shape[1]
    blocks = tokens // BLK
    cap = max(2, 2 * blocks // n)
    window = cap * BLK + BLK
    lanes = -(-n * window // 128) * 128
    half = tokens // ntp
    scale = 1.0 / hd**0.5
    swap = [(i, (i + 1) % ntp) for i in range(ntp)]

    size = half * 3 // 4
    extra = half - size
    at = jnp.stack([me, core])
    pack_fill, pack_dest = block_fill, block_dest[:, 0]
    packed = pack(x_prompt, pack_fill, pack_dest, at, n, 0, size)
    dest = pack_dest
    far = with_partner(queries, n // 2, n)
    packed, far, dest, block_row, block_fill, query = lax.optimization_barrier(
        (packed, far, dest, block_row, block_fill, queries)
    )
    mine = lax.all_to_all(packed, "pool", 0, 0, tiled=True).reshape(n * size, part)

    index = jnp.arange(n * blocks, dtype=jnp.int32)
    sender = index // blocks
    kin = sender[None, :] == sender[:, None]
    lower = kin & (dest[None, :] < dest[:, None])
    level = kin & (dest[None, :] == dest[:, None]) & (index[None, :] < index[:, None])
    before = jnp.sum(jnp.where(lower, block_fill[None, :], 0), 1)
    within = jnp.sum(jnp.where(level, block_fill[None, :], 0), 1)
    pair = jnp.arange(n * n, dtype=jnp.int32)
    to, by = pair // n, pair % n
    owned = dest[None, :] == to[:, None]
    sent = sender[None, :] == by[:, None]
    earlier = sent & (dest[None, :] < to[:, None])
    offset = jnp.sum(jnp.where(earlier, block_fill[None, :], 0), 1)
    amount = jnp.sum(jnp.where(sent & owned, block_fill[None, :], 0), 1)
    runs = jnp.where(amount > 0, (offset % BLK + amount + BLK - 1) // BLK * BLK, 0)
    runs_by = runs.reshape(n, n)
    prior = jnp.arange(n)[:, None] < jnp.arange(n)[None, :]
    targets = jnp.sum(jnp.where(prior[None], runs_by[:, :, None], 0), 1)
    list_rows = jnp.sum(runs_by, 1)
    targets = targets.reshape(-1)
    sources = by * tokens + offset // BLK * BLK
    group_at = jnp.arange(n * lanes // BLK, dtype=jnp.int32) * BLK
    skip = group_at[:, None] - (to * lanes + targets)[None, :]
    group_rows = jnp.sum(
        jnp.where((skip >= 0) & (skip < runs[None, :]), sources[None, :] + skip, 0), 1
    )
    mine_pair = (dest * n + sender)[:, None] == pair[None, :]
    start = (
        dest * lanes
        + jnp.sum(jnp.where(mine_pair, targets[None, :], 0), 1)
        + before % BLK
        + within
    )
    spot = jnp.arange(n * lanes, dtype=jnp.int32)[:, None]
    inside = (spot >= start[None, :]) & (spot < (start + block_fill)[None, :])
    rowof = jnp.sum(jnp.where(inside, (block_row + 1)[None, :], 0), 1) - 1
    rowof = rowof.reshape(n, 1, lanes)

    most = jnp.max(jnp.sum(block_fill.reshape(n, blocks), 1))
    groups = lax.axis_size("groups")
    k = 1
    while k < groups:
        most = jnp.maximum(
            most, lax.ppermute(most, "groups", [(i, i ^ k) for i in range(groups)])
        )
        k *= 2
    over = most > ntp * size

    def exchange_rest():
        rest = pack(x_prompt, pack_fill, pack_dest, at, n, ntp * size, extra)
        rest = lax.all_to_all(rest, "pool", 0, 0, tiled=True).reshape(n * extra, part)
        return rest, lax.ppermute(rest, "tp", swap)

    def no_rest():
        return (jnp.zeros((n * extra, part), jnp.bfloat16),) * 2

    more_mine, more_other = lax.cond(over, exchange_rest, no_rest)
    meta = jnp.concatenate(
        [group_rows, list_rows, jnp.stack([me, core, over.astype(jnp.int32)])]
    )

    keys = kv_weight[:, :, :hd]

    def through_keys(held):
        held = held.reshape(n // 2, rows, kvh, group, hd)
        return (
            jnp.einsum("qrhgd,phd->hqrgp", held, keys, preferred_element_type=jnp.float32)
            .astype(jnp.bfloat16)
            .reshape(kvh, n // 2 * per, part)
        )

    even = from_rest(jnp.stack([queries, far]), n)
    keyed_even = through_keys(even)
    odd = with_partner(even, 1, n)
    values = kv_weight[:, :, hd:].transpose(1, 0, 2)

    query = query.reshape(rows, kvh, group, hd)
    cache_scores = (
        jnp.einsum(
            "rhgd,rthd->rhgt", query, kv_cache[:, :, :, :hd], preferred_element_type=jnp.float32
        )
        * scale
    )
    cache_live = jnp.arange(cache_slots, dtype=jnp.int32)[None, :] < cache_len[:, None]
    cache_scores = jnp.where(cache_live[:, None, None, :], cache_scores, -jnp.inf)
    cache_top = jnp.max(cache_scores, -1, keepdims=True)
    cache_exp = jnp.exp(cache_scores - cache_top)
    cache_sum = jnp.sum(cache_exp, -1, keepdims=True)
    cached = jnp.einsum(
        "rhgt,rthd->rhgd",
        cache_exp.astype(jnp.bfloat16),
        kv_cache[:, :, :, hd:],
        preferred_element_type=jnp.float32,
    )
    cache_top = cache_top.reshape(rows, heads, 1)
    cache_sum = cache_sum.reshape(rows, heads, 1)
    cached = cached.reshape(rows, heads, hd)

    mine, odd, meta, list_rows, rowof, keyed_even, values, cache_top, cache_sum, cached = (
        lax.optimization_barrier(
            (mine, odd, meta, list_rows, rowof, keyed_even, values, cache_top, cache_sum, cached)
        )
    )
    other = lax.ppermute(mine, "tp", swap)
    keyed_odd = through_keys(odd)

    in_hbm = pl.BlockSpec(memory_space=pltpu.HBM)
    row_spec = pl.BlockSpec((1, 1, lanes), lambda q, m: (q, 0, 0))
    slot_spec = pl.BlockSpec((1, heads, lanes), lambda q, m: (q, 0, 0))
    slot_shape = jax.ShapeDtypeStruct((n, heads, lanes), jnp.bfloat16)
    cuts = tile_cuts(lanes)
    list_shapes = [(n, cuts[1], part), (n, lanes - cuts[1], part)]
    list_scratch = [pltpu.VMEM(shape, jnp.bfloat16) for shape in list_shapes]
    at_me = n * lanes // BLK + n

    def owner(i, m):
        return m[at_me] ^ reversed_bits(i, n)

    partial_scores, low, high = pl.pallas_call(
        functools.partial(score_kernel, n, rows),
        grid_spec=pltpu.PrefetchScalarGridSpec(
            num_scalar_prefetch=1,
            grid=(n,),
            in_specs=[
                *[in_hbm] * 4,
                pl.BlockSpec((kvh, per, part), lambda i, m: (0, jnp.minimum(i, n // 2 - 1), 0)),
                pl.BlockSpec((kvh, per, part), lambda i, m: (0, jnp.maximum(i - n // 2, 0), 0)),
                pl.BlockSpec((1, 1, lanes), lambda i, m: (owner(i, m), 0, 0)),
            ],
            out_specs=[
                pl.BlockSpec((1, heads, lanes), lambda i, m: (owner(i, m), 0, 0)),
                in_hbm,
                in_hbm,
            ],
            scratch_shapes=[
                pltpu.VMEM((ntp, n * size, part), jnp.bfloat16),
                pltpu.VMEM((ntp, n * extra, part), jnp.bfloat16),
                pltpu.VMEM((n * tokens, part), jnp.float32),
                *list_scratch,
                pltpu.SemaphoreType.DMA((ntp, 4)),
                pltpu.SemaphoreType.DMA((n, len(cuts) - 1)),
            ],
        ),
        out_shape=[
            slot_shape,
            *[jax.ShapeDtypeStruct(shape, jnp.bfloat16) for shape in list_shapes],
        ],
        compiler_params=pltpu.CompilerParams(vmem_limit_bytes=56 * MIB),
        name="prompt_scores",
    )(meta, mine, other, more_mine, more_other, keyed_even, keyed_odd, rowof)

    parts = lax.all_to_all(partial_scores, "pool", 0, 0, tiled=True)
    my_rows = lax.dynamic_index_in_dim(rowof, me, 0, keepdims=False)
    weights, kept = pl.pallas_call(
        functools.partial(weight_kernel, scale),
        out_shape=[slot_shape, jax.ShapeDtypeStruct((rows, heads, hd), jnp.float32)],
        compiler_params=pltpu.CompilerParams(vmem_limit_bytes=8 * MIB),
        name="softmax_weights",
    )(parts, my_rows, cache_top, cache_sum, cached)

    all_weights = lax.all_to_all(weights, "pool", 0, 0, tiled=True)
    terms = pl.pallas_call(
        functools.partial(value_kernel, rows),
        grid_spec=pltpu.PrefetchScalarGridSpec(
            num_scalar_prefetch=1,
            grid=(n,),
            in_specs=[
                slot_spec,
                row_spec,
                in_hbm,
                in_hbm,
                pl.BlockSpec((kvh, part, hd), lambda q, m: (0, 0, 0)),
            ],
            out_specs=pl.BlockSpec((n, kvh, per, hd), lambda q, m: (0, 0, 0, 0)),
            scratch_shapes=[
                *list_scratch,
                pltpu.VMEM((kvh * per, part), jnp.float32),
                pltpu.VMEM((kvh, n * per, part), jnp.bfloat16),
                pltpu.SemaphoreType.DMA((n, len(cuts) - 1)),
            ],
        ),
        out_shape=jax.ShapeDtypeStruct((n, kvh, per, hd), jnp.bfloat16),
        compiler_params=pltpu.CompilerParams(vmem_limit_bytes=56 * MIB),
        name="weighted_values",
    )(list_rows, all_weights, rowof, low, high, values)

    term_parts = lax.all_to_all(terms, "pool", 0, 0, tiled=True)
    attended = pl.pallas_call(
        sum_kernel,
        out_shape=jax.ShapeDtypeStruct((rows, heads * hd), jnp.bfloat16),
        scratch_shapes=[pltpu.VMEM((kvh * per, hd), jnp.float32)],
        compiler_params=pltpu.CompilerParams(vmem_limit_bytes=8 * MIB),
        name="attended_sum",
    )(term_parts, kept)

    cols = out_weight.shape[1] // ntp
    half_shape = jax.ShapeDtypeStruct((n * rows, cols), jnp.float32)
    half_spec = pl.BlockSpec((n * rows, cols), lambda i, m: (0, 0))
    own, away = pl.pallas_call(
        functools.partial(project_kernel, n),
        grid_spec=pltpu.PrefetchScalarGridSpec(
            num_scalar_prefetch=1,
            grid=(1,),
            in_specs=[
                *[pl.BlockSpec((rows, heads * hd), lambda i, m: (0, 0))] * n,
                pl.BlockSpec(out_weight.shape, lambda i, m: (0, 0)),
            ],
            out_specs=[half_spec] * 2,
            scratch_shapes=[pltpu.VMEM((n * rows, heads * hd), jnp.bfloat16)],
        ),
        out_shape=[half_shape] * 2,
        compiler_params=pltpu.CompilerParams(vmem_limit_bytes=26 * MIB),
        name="output_projection",
    )(core.reshape(1), *swap_parts([attended] * n, n), out_weight)
    got = lax.ppermute(away, "tp", swap)
    return pl.pallas_call(
        functools.partial(order_kernel, n),
        grid_spec=pltpu.PrefetchScalarGridSpec(
            num_scalar_prefetch=1,
            grid=(1,),
            in_specs=[half_spec] * 2,
            out_specs=half_spec,
        ),
        out_shape=jax.ShapeDtypeStruct((n * rows, cols), jnp.bfloat16),
        compiler_params=pltpu.CompilerParams(vmem_limit_bytes=4 * MIB),
        name="order_rows",
    )(me.reshape(1), own, got)


def solution(mesh):
    in_specs = (
        P(("groups", "pool"), None),
        P("pool", "tp", None),
        P("groups", None),
        P("groups"),
        P("groups"),
        P(("groups", "pool"), "tp", None),
        P(("groups", "pool"), None, "tp", None),
        P(("groups", "pool")),
        P("tp", "pool"),
    )
    out_specs = P("groups", ("pool", "tp"))
    return jax.shard_map(local, mesh=mesh, in_specs=in_specs, out_specs=out_specs, check_vma=False)
```

```python
import functools

import jax
import jax.numpy as jnp
from jax import lax
from jax.experimental import pallas as pl
from jax.experimental.pallas import tpu as pltpu
from jax.sharding import PartitionSpec as P

BLK = 8
MIB = 1 << 20


def pack_kernel(base, at_ref, fill_ref, dest_ref, x_ref, out_ref, held, packed, count, in_sem, out_sem):
    n, tokens, part = held.shape
    size = packed.shape[1]
    blocks = tokens // BLK

    def load(q):
        return pltpu.make_async_copy(
            x_ref.at[:, pl.ds(q * part, part)], held.at[q], in_sem.at[q]
        )

    def store(q):
        return pltpu.make_async_copy(packed.at[q], out_ref.at[q], out_sem.at[q])

    for q in range(n):
        load(q).start()
    first = at_ref[0] * blocks
    for q in range(n):
        count[q] = 0

    @pl.loop(0, blocks)
    def _(b):
        owner = dest_ref[first + b]
        count[owner] = count[owner] + fill_ref[first + b]

    def starts(q, total):
        here = count[q]
        count[q] = total
        return total + here

    lax.fori_loop(0, n, starts, jnp.int32(0))
    token = lax.broadcasted_iota(jnp.int32, (1, tokens), 1)

    def place(b, ranks):
        owner = dest_ref[first + b]
        fill = fill_ref[first + b]
        start = count[owner]
        count[owner] = start + fill
        inner = token - b * BLK
        return jnp.where((inner >= 0) & (inner < fill), start + inner, ranks)

    ranks = lax.fori_loop(0, blocks, place, jnp.full((1, tokens), -1, jnp.int32))
    wanted = base + at_ref[1] * size + lax.broadcasted_iota(jnp.int32, (size, tokens), 0)
    pick = (wanted == ranks).astype(jnp.bfloat16)
    for q in range(n):
        load(q).wait()
        packed[q] = jnp.dot(pick, held[q], preferred_element_type=jnp.float32).astype(
            packed.dtype
        )
        store(q).start()
    for q in range(n):
        store(q).wait()


def pack(x_prompt, fill, dest, at, n, base, size):
    tokens, width = x_prompt.shape
    part = width // n
    return pl.pallas_call(
        functools.partial(pack_kernel, base),
        grid_spec=pltpu.PrefetchScalarGridSpec(
            num_scalar_prefetch=3,
            grid=(1,),
            in_specs=[pl.BlockSpec(memory_space=pl.ANY)],
            out_specs=pl.BlockSpec(memory_space=pl.ANY),
            scratch_shapes=[
                pltpu.VMEM((n, tokens, part), jnp.bfloat16),
                pltpu.VMEM((n, size, part), jnp.bfloat16),
                pltpu.SMEM((n,), jnp.int32),
                pltpu.SemaphoreType.DMA((n,)),
                pltpu.SemaphoreType.DMA((n,)),
            ],
        ),
        out_shape=jax.ShapeDtypeStruct((n, size, part), jnp.bfloat16),
        compiler_params=pltpu.CompilerParams(vmem_limit_bytes=56 * MIB),
        cost_estimate=pl.CostEstimate(
            flops=2 * size * tokens * width, bytes_accessed=64 * MIB, transcendentals=0
        ),
        name="pack_live_tokens",
    )(at, fill, dest, x_prompt)


def tile_cuts(lanes):
    return [0] + list(range(min(256, lanes), lanes, 128)) + [lanes]


def near_lanes(lanes):
    return min(lanes, -(-lanes * 3 // 5 // 128) * 128)


def load_tokens(n, core, over, x_refs, held, more, wide, sem, others):
    size, extra = held.shape[1] // n, more.shape[1] // n
    tokens = 2 * (size + extra)
    part = wide.shape[1]
    cuts = sem.shape[1]

    def copies(refs, buffer):
        span = buffer.shape[1] // cuts
        return [
            [
                pltpu.make_async_copy(
                    ref.at[pl.ds(i * span, span)], buffer.at[j, pl.ds(i * span, span)], sem.at[j, i]
                )
                for j, ref in enumerate(refs)
            ]
            for i in range(cuts)
        ]

    def widen(buffer, base, first, last):
        length = buffer.shape[1] // n

        @pl.loop(first, last)
        def _(s):
            for j in range(2):
                side = core if j == 0 else 1 - core
                to = pl.multiple_of(s * tokens + base + side * length, BLK)
                wide[pl.ds(to, length), :] = buffer[
                    j, pl.ds(pl.multiple_of(s * length, length), length), :
                ].astype(wide.dtype)

    main = copies(x_refs[:2], held)
    for pair in main:
        for copy in pair:
            copy.start()
    for copy in others:
        copy.start()
    for i, pair in enumerate(main):
        for copy in pair:
            copy.wait()
        widen(held, 0, i * n // cuts, (i + 1) * n // cuts)

    @pl.when(over != 0)
    def _():
        rest = copies(x_refs[2:], more)
        for pair in rest:
            for copy in pair:
                copy.start()
        for pair in rest:
            for copy in pair:
                copy.wait()
        widen(more, 2 * size, 0, n)


def score_kernel(n, rows, meta_ref, *refs):
    x_refs, keyed_refs, (row_ref, near_ref, rest_ref, low_ref, high_ref) = (
        refs[:4], refs[4:6], refs[6:11]
    )
    held, more, wide, keyed, low, high, in_sem, keyed_sem, out_sem = refs[11:]
    step = pl.program_id(0)
    part = wide.shape[1]
    near = near_ref.shape[2]
    lanes = near + rest_ref.shape[2]
    cuts = tile_cuts(lanes)
    groups = lanes // BLK
    at_size = n * groups
    q = meta_ref[at_size + n] ^ reversed_bits(step, n)
    kvh, per = keyed.shape[0], keyed.shape[1] // n
    group = per // rows

    @pl.when(step == 0)
    def _():
        loads = [
            pltpu.make_async_copy(
                ref.at[h], keyed.at[h, pl.ds(i * n // 2 * per, n // 2 * per)], keyed_sem.at[i, h]
            )
            for i, ref in enumerate(keyed_refs)
            for h in range(kvh)
        ]
        load_tokens(
            n,
            meta_ref[at_size + n + 1],
            meta_ref[at_size + n + 2],
            x_refs,
            held,
            more,
            wide,
            in_sem,
            loads,
        )
        for load in loads:
            load.wait()

    def copy(o, t):
        if t == 0:
            return pltpu.make_async_copy(low.at[o], low_ref.at[o], out_sem.at[o, 0])
        here = pl.ds(cuts[t] - cuts[1], cuts[t + 1] - cuts[t])
        return pltpu.make_async_copy(
            high.at[o, here], high_ref.at[o, here], out_sem.at[o, t]
        )

    def one(t):
        here = slice(cuts[t], cuts[t + 1])
        buffer, base = (low, 0) if t == 0 else (high, cuts[1])
        for i in range(cuts[t], cuts[t + 1], 2 * BLK):
            pair = [
                wide[pl.ds(pl.multiple_of(meta_ref[q * groups + i // BLK + j], BLK), BLK), :]
                for j in range(2)
            ]
            buffer[q, i - base : i - base + 2 * BLK, :] = jnp.concatenate(pair).astype(low.dtype)
        copy(q, t).start()
        raw = lax.dot_general(
            keyed[:, pl.ds(pl.multiple_of(step * per, per), per), :].reshape(kvh * per, part),
            buffer[q, cuts[t] - base : cuts[t + 1] - base, :],
            (((1,), (1,)), ((), ())),
            preferred_element_type=jnp.float32,
        ).reshape(kvh, rows, group, cuts[t + 1] - cuts[t])
        owner_row = row_ref[0, :, here]
        picked = jnp.zeros((kvh, group, cuts[t + 1] - cuts[t]), jnp.float32)
        for r in range(rows):
            picked = picked + jnp.where((owner_row == r)[None], raw[:, r], 0.0)
        picked = picked.reshape(kvh * group, -1).astype(near_ref.dtype)
        if cuts[t] < near:
            near_ref[0, :, here] = picked
        else:
            rest_ref[0, :, cuts[t] - near : cuts[t + 1] - near] = picked

    one(0)
    for t in range(1, len(cuts) - 1):
        pl.when(meta_ref[at_size + q] > cuts[t])(functools.partial(one, t))

    @pl.when(step == n - 1)
    def _():
        for o in range(n):
            copy(o, 0).wait()
            for t in range(1, len(cuts) - 1):
                pl.when(meta_ref[at_size + o] > cuts[t])(lambda o=o, t=t: copy(o, t).wait())


def weight_kernel(scale, count, *refs):
    part_refs, row_refs = refs[:count], refs[count : 2 * count]
    top_ref, sum_ref, cached_ref = refs[2 * count : 2 * count + 3]
    w_refs, kept_ref = refs[2 * count + 3 : -1], refs[-1]
    n = part_refs[0].shape[0]
    scores, owner_rows = [], []
    for part_ref, row_ref in zip(part_refs, row_refs):
        got = part_ref[0].astype(jnp.float32)
        for i in range(1, n):
            got = got + part_ref[i].astype(jnp.float32)
        scores.append(got * scale)
        owner_rows.append(row_ref[...])
    weights = [jnp.zeros(s.shape, jnp.float32) for s in scores]
    for r in range(top_ref.shape[0]):
        own = [jnp.where(o == r, s, -jnp.inf) for o, s in zip(owner_rows, scores)]
        cache_top = top_ref[r]
        top = cache_top
        for o in own:
            top = jnp.maximum(top, jnp.max(o, 1, keepdims=True))
        held = [jnp.exp(o - top) for o in own]
        fade = jnp.exp(cache_top - top)
        total = sum_ref[r] * fade
        for h in held:
            total = total + jnp.sum(h, 1, keepdims=True)
        weights = [w + h / total for w, h in zip(weights, held)]
        kept_ref[r] = cached_ref[r] * (fade / total)
    for w, w_ref in zip(weights, w_refs):
        for i in range(n):
            w_ref[i] = w.astype(w_ref.dtype)


def value_kernel(
    rows, size_ref, near_ref, rest_ref, row_ref, low_ref, high_ref, value_ref, out_ref,
    low, high, values, acc, mixed, sem, value_sem,
):
    q = pl.program_id(0)
    n = low.shape[0]
    kvh = values.shape[0]
    _, heads, near = near_ref.shape
    lanes = near + rest_ref.shape[2]
    per = rows * heads // kvh
    cuts = tile_cuts(lanes)
    load_values = pltpu.make_async_copy(value_ref, values, value_sem)

    def copy(o, t):
        if t == 0:
            return pltpu.make_async_copy(low_ref.at[o], low.at[o], sem.at[o, 0])
        here = pl.ds(cuts[t] - cuts[1], cuts[t + 1] - cuts[t])
        return pltpu.make_async_copy(high_ref.at[o, here], high.at[o, here], sem.at[o, t])

    @pl.when(q == 0)
    def _():
        for o in range(n):
            copy(o, 0).start()
            for t in range(1, len(cuts) - 1):
                pl.when(size_ref[o] > cuts[t])(lambda o=o, t=t: copy(o, t).start())
        load_values.start()

    def one(t):
        copy(q, t).wait()
        here = slice(cuts[t], cuts[t + 1])
        width = cuts[t + 1] - cuts[t]
        if cuts[t] < near:
            weights = near_ref[0, :, here]
        else:
            weights = rest_ref[0, :, cuts[t] - near : cuts[t + 1] - near]
        weights = weights.astype(jnp.float32).reshape(kvh, 1, heads // kvh, width)
        owner_row = row_ref[0, :, here]
        spread = jnp.concatenate(
            [jnp.where((owner_row == r)[None, None], weights, 0.0) for r in range(rows)], 1
        ).reshape(kvh * per, width)
        tile = low[q] if t == 0 else high[q, cuts[t] - cuts[1] : cuts[t + 1] - cuts[1], :]
        got = jnp.dot(spread.astype(jnp.bfloat16), tile, preferred_element_type=jnp.float32)
        if t:
            acc[...] += got
        else:
            acc[...] = got

    one(0)
    for t in range(1, len(cuts) - 1):
        pl.when(size_ref[q] > cuts[t])(functools.partial(one, t))
    for h in range(kvh):
        mixed[h, pl.ds(pl.multiple_of(q * per, per), per), :] = acc[
            h * per : (h + 1) * per, :
        ].astype(mixed.dtype)

    @pl.when(q == n - 1)
    def _():
        load_values.wait()
        for h in range(kvh):
            done = jnp.dot(mixed[h], values[h], preferred_element_type=jnp.float32)
            out_ref[:, h] = done.reshape(n, per, done.shape[1]).astype(out_ref.dtype)


def sum_kernel(parts_ref, kept_ref, out_ref, total):
    n, kvh, per, hd = parts_ref.shape
    rows, heads = kept_ref.shape[:2]
    group = heads // kvh
    for h in range(kvh):
        terms = parts_ref[0, h].astype(jnp.float32)
        for i in range(1, n):
            terms = terms + parts_ref[i, h].astype(jnp.float32)
        for r in range(rows):
            here = slice((h * rows + r) * group, (h * rows + r + 1) * group)
            total[here, :] = (
                terms[r * group : (r + 1) * group] + kept_ref[r, h * group : (h + 1) * group, :]
            )
    pieces = [
        total[pl.ds(h * per + g, rows, stride=group), :]
        for h in range(kvh)
        for g in range(group)
    ]
    out_ref[...] = jnp.concatenate(pieces, 1).astype(out_ref.dtype)


def project_kernel(n, core_ref, *refs):
    row_refs, (weight_ref, own_ref, away_ref, gathered, weight, sem) = refs[:n], refs[n:]
    rows, cols = row_refs[0].shape[0], own_ref.shape[1]
    cuts = sem.shape[0]
    span = weight.shape[0] // cuts
    loads = [
        pltpu.make_async_copy(
            weight_ref.at[pl.ds(i * span, span)], weight.at[pl.ds(i * span, span)], sem.at[i]
        )
        for i in range(cuts)
    ]
    for load in loads:
        load.start()
    for k in range(0, n, 2):
        pair = [row_refs[k + j][...].astype(jnp.float32) for j in range(2)]
        gathered[k * rows : (k + 2) * rows, :] = jnp.concatenate(pair).astype(gathered.dtype)
    done = jnp.zeros((n * rows, 2 * cols), jnp.float32)
    for i, load in enumerate(loads):
        load.wait()
        here = slice(i * span, (i + 1) * span)
        done = done + jnp.dot(
            gathered[:, here], weight[here, :], preferred_element_type=jnp.float32
        )
    first = core_ref[0] == 0
    own_ref[...] = jnp.where(first, done[:, :cols], done[:, cols:])
    away_ref[...] = jnp.where(first, done[:, cols:], done[:, :cols])


def order_kernel(n, me_ref, own_ref, got_ref, out_ref):
    rows = own_ref.shape[0] // n
    for q in range(0, n, 2):
        pair = []
        for j in range(2):
            here = pl.ds(pl.multiple_of((me_ref[0] ^ (q + j)) * rows, rows), rows)
            pair.append(own_ref[here, :] + got_ref[here, :])
        out_ref[q * rows : (q + 2) * rows, :] = jnp.concatenate(pair).astype(out_ref.dtype)


def with_partner(x, k, n):
    return lax.ppermute(x, "pool", [(i, i ^ k) for i in range(n)])


def from_rest(held, n):
    k = n // 4
    while k >= 2:
        held = jnp.concatenate([held, with_partner(held, k, n)])
        k //= 2
    return held


def reversed_bits(k, n):
    out, bit = 0, 1
    while bit < n:
        out = out + (k // bit) % 2 * (n // 2 // bit)
        bit *= 2
    return out


def far_first(n):
    return sorted(range(1, n), reverse=True)


def swap_parts(parts, n):
    got = [parts[0]] + [None] * (n - 1)
    for k in far_first(n):
        got[k] = with_partner(parts[k], k, n)
    return got


def local(
    x_prompt, kv_weight, block_dest, block_row, block_fill, queries, kv_cache, cache_len, out_weight
):
    n = lax.axis_size("pool")
    ntp = lax.axis_size("tp")
    me = lax.axis_index("pool").astype(jnp.int32)
    core = lax.axis_index("tp").astype(jnp.int32)
    tokens, width = x_prompt.shape
    part = width // n
    kvh = kv_weight.shape[1]
    hd = kv_weight.shape[2] // 2
    rows, heads = queries.shape[0], queries.shape[1]
    group = heads // kvh
    per = rows * group
    cache_slots = kv_cache.shape[1]
    blocks = tokens // BLK
    cap = max(2, 2 * blocks // n)
    window = cap * BLK + BLK
    lanes = -(-n * window // 128) * 128
    half = tokens // ntp
    scale = 1.0 / hd**0.5
    swap = [(i, (i + 1) % ntp) for i in range(ntp)]

    size = half * 3 // 4
    extra = half - size
    at = jnp.stack([me, core])
    pack_fill, pack_dest = block_fill, block_dest[:, 0]
    packed = pack(x_prompt, pack_fill, pack_dest, at, n, 0, size)
    dest = pack_dest
    far = with_partner(queries, n // 2, n)
    packed, far, dest, block_row, block_fill, query = lax.optimization_barrier(
        (packed, far, dest, block_row, block_fill, queries)
    )
    mine = lax.all_to_all(packed, "pool", 0, 0, tiled=True).reshape(n * size, part)

    index = jnp.arange(n * blocks, dtype=jnp.int32)
    sender = index // blocks
    kin = sender[None, :] == sender[:, None]
    lower = kin & (dest[None, :] < dest[:, None])
    level = kin & (dest[None, :] == dest[:, None]) & (index[None, :] < index[:, None])
    before = jnp.sum(jnp.where(lower, block_fill[None, :], 0), 1)
    within = jnp.sum(jnp.where(level, block_fill[None, :], 0), 1)
    pair = jnp.arange(n * n, dtype=jnp.int32)
    to, by = pair // n, pair % n
    owned = dest[None, :] == to[:, None]
    sent = sender[None, :] == by[:, None]
    earlier = sent & (dest[None, :] < to[:, None])
    offset = jnp.sum(jnp.where(earlier, block_fill[None, :], 0), 1)
    amount = jnp.sum(jnp.where(sent & owned, block_fill[None, :], 0), 1)
    runs = jnp.where(amount > 0, (offset % BLK + amount + BLK - 1) // BLK * BLK, 0)
    runs_by = runs.reshape(n, n)
    prior = jnp.arange(n)[:, None] < jnp.arange(n)[None, :]
    targets = jnp.sum(jnp.where(prior[None], runs_by[:, :, None], 0), 1)
    list_rows = jnp.sum(runs_by, 1)
    targets = targets.reshape(-1)
    sources = by * tokens + offset // BLK * BLK
    group_at = jnp.arange(n * lanes // BLK, dtype=jnp.int32) * BLK
    skip = group_at[:, None] - (to * lanes + targets)[None, :]
    group_rows = jnp.sum(
        jnp.where((skip >= 0) & (skip < runs[None, :]), sources[None, :] + skip, 0), 1
    )
    mine_pair = (dest * n + sender)[:, None] == pair[None, :]
    start = (
        dest * lanes
        + jnp.sum(jnp.where(mine_pair, targets[None, :], 0), 1)
        + before % BLK
        + within
    )
    spot = jnp.arange(n * lanes, dtype=jnp.int32)[:, None]
    inside = (spot >= start[None, :]) & (spot < (start + block_fill)[None, :])
    rowof = jnp.sum(jnp.where(inside, (block_row + 1)[None, :], 0), 1) - 1
    rowof = rowof.reshape(n, 1, lanes)

    near = near_lanes(lanes)
    most = jnp.stack([jnp.max(jnp.sum(block_fill.reshape(n, blocks), 1)), jnp.max(list_rows)])
    groups = lax.axis_size("groups")
    k = 1
    while k < groups:
        most = jnp.maximum(
            most, lax.ppermute(most, "groups", [(i, i ^ k) for i in range(groups)])
        )
        k *= 2
    over, longer = most[0] > ntp * size, most[1] > near

    def exchange_rest():
        rest = pack(x_prompt, pack_fill, pack_dest, at, n, ntp * size, extra)
        rest = lax.all_to_all(rest, "pool", 0, 0, tiled=True).reshape(n * extra, part)
        return rest, lax.ppermute(rest, "tp", swap)

    def no_rest():
        return (jnp.zeros((n * extra, part), jnp.bfloat16),) * 2

    more_mine, more_other = lax.cond(over, exchange_rest, no_rest)
    meta = jnp.concatenate(
        [group_rows, list_rows, jnp.stack([me, core, over.astype(jnp.int32)])]
    )

    keys = kv_weight[:, :, :hd]

    def through_keys(held):
        held = held.reshape(n // 2, rows, kvh, group, hd)
        return (
            jnp.einsum("qrhgd,phd->hqrgp", held, keys, preferred_element_type=jnp.float32)
            .astype(jnp.bfloat16)
            .reshape(kvh, n // 2 * per, part)
        )

    even = from_rest(jnp.stack([queries, far]), n)
    keyed_even = through_keys(even)
    keyed_odd = through_keys(with_partner(even, 1, n))
    values = kv_weight[:, :, hd:].transpose(1, 0, 2)

    query = query.reshape(rows, kvh, group, hd)
    cache_scores = (
        jnp.einsum(
            "rhgd,rthd->rhgt", query, kv_cache[:, :, :, :hd], preferred_element_type=jnp.float32
        )
        * scale
    )
    cache_live = jnp.arange(cache_slots, dtype=jnp.int32)[None, :] < cache_len[:, None]
    cache_scores = jnp.where(cache_live[:, None, None, :], cache_scores, -jnp.inf)
    cache_top = jnp.max(cache_scores, -1, keepdims=True)
    cache_exp = jnp.exp(cache_scores - cache_top)
    cache_sum = jnp.sum(cache_exp, -1, keepdims=True)
    cached = jnp.einsum(
        "rhgt,rthd->rhgd",
        cache_exp.astype(jnp.bfloat16),
        kv_cache[:, :, :, hd:],
        preferred_element_type=jnp.float32,
    )
    cache_top = cache_top.reshape(rows, heads, 1)
    cache_sum = cache_sum.reshape(rows, heads, 1)
    cached = cached.reshape(rows, heads, hd)

    mine, meta, list_rows, rowof, keyed_even, keyed_odd, values, cache_top, cache_sum, cached = (
        lax.optimization_barrier(
            (
                mine, meta, list_rows, rowof, keyed_even, keyed_odd, values,
                cache_top, cache_sum, cached,
            )
        )
    )
    other = lax.ppermute(mine, "tp", swap)

    in_hbm = pl.BlockSpec(memory_space=pltpu.HBM)
    row_spec = pl.BlockSpec((1, 1, lanes), lambda q, m: (q, 0, 0))
    slot_specs = [
        pl.BlockSpec((1, heads, length), lambda q, m: (q, 0, 0)) for length in (near, lanes - near)
    ]
    slot_shapes = [
        jax.ShapeDtypeStruct((n, heads, length), jnp.bfloat16) for length in (near, lanes - near)
    ]
    cuts = tile_cuts(lanes)
    list_shapes = [(n, cuts[1], part), (n, lanes - cuts[1], part)]
    list_scratch = [pltpu.VMEM(shape, jnp.bfloat16) for shape in list_shapes]
    at_me = n * lanes // BLK + n

    def owner(i, m):
        return m[at_me] ^ reversed_bits(i, n)

    score_near, score_rest, low, high = pl.pallas_call(
        functools.partial(score_kernel, n, rows),
        grid_spec=pltpu.PrefetchScalarGridSpec(
            num_scalar_prefetch=1,
            grid=(n,),
            in_specs=[
                *[in_hbm] * 6,
                pl.BlockSpec((1, 1, lanes), lambda i, m: (owner(i, m), 0, 0)),
            ],
            out_specs=[
                *[
                    pl.BlockSpec((1, heads, length), lambda i, m: (owner(i, m), 0, 0))
                    for length in (near, lanes - near)
                ],
                in_hbm,
                in_hbm,
            ],
            scratch_shapes=[
                pltpu.VMEM((ntp, n * size, part), jnp.bfloat16),
                pltpu.VMEM((ntp, n * extra, part), jnp.bfloat16),
                pltpu.VMEM((n * tokens, part), jnp.float32),
                pltpu.VMEM((kvh, n * per, part), jnp.bfloat16),
                *list_scratch,
                pltpu.SemaphoreType.DMA((ntp, 4)),
                pltpu.SemaphoreType.DMA((2, kvh)),
                pltpu.SemaphoreType.DMA((n, len(cuts) - 1)),
            ],
        ),
        out_shape=[
            *slot_shapes,
            *[jax.ShapeDtypeStruct(shape, jnp.bfloat16) for shape in list_shapes],
        ],
        compiler_params=pltpu.CompilerParams(vmem_limit_bytes=56 * MIB),
        name="prompt_scores",
    )(meta, mine, other, more_mine, more_other, keyed_even, keyed_odd, rowof)

    my_rows = lax.dynamic_index_in_dim(rowof, me, 0, keepdims=False)

    def exchange_weights(*scores):
        count = len(scores)
        parts = [lax.all_to_all(s, "pool", 0, 0, tiled=True) for s in scores]
        row_parts = [my_rows[:, :near], my_rows[:, near:]][:count]
        *weights, kept = pl.pallas_call(
            functools.partial(weight_kernel, scale, count),
            out_shape=[*slot_shapes[:count], jax.ShapeDtypeStruct((rows, heads, hd), jnp.float32)],
            compiler_params=pltpu.CompilerParams(vmem_limit_bytes=8 * MIB),
            name="softmax_weights",
        )(*parts, *row_parts, cache_top, cache_sum, cached)
        return *[lax.all_to_all(w, "pool", 0, 0, tiled=True) for w in weights], kept

    def near_only():
        weights, kept = exchange_weights(score_near)
        return weights, jnp.zeros(slot_shapes[1].shape, jnp.bfloat16), kept

    weight_near, weight_rest, kept = lax.cond(
        longer, lambda: exchange_weights(score_near, score_rest), near_only
    )
    terms = pl.pallas_call(
        functools.partial(value_kernel, rows),
        grid_spec=pltpu.PrefetchScalarGridSpec(
            num_scalar_prefetch=1,
            grid=(n,),
            in_specs=[*slot_specs, row_spec, in_hbm, in_hbm, in_hbm],
            out_specs=pl.BlockSpec((n, kvh, per, hd), lambda q, m: (0, 0, 0, 0)),
            scratch_shapes=[
                *list_scratch,
                pltpu.VMEM((kvh, part, hd), jnp.bfloat16),
                pltpu.VMEM((kvh * per, part), jnp.float32),
                pltpu.VMEM((kvh, n * per, part), jnp.bfloat16),
                pltpu.SemaphoreType.DMA((n, len(cuts) - 1)),
                pltpu.SemaphoreType.DMA,
            ],
        ),
        out_shape=jax.ShapeDtypeStruct((n, kvh, per, hd), jnp.bfloat16),
        compiler_params=pltpu.CompilerParams(vmem_limit_bytes=56 * MIB),
        name="weighted_values",
    )(list_rows, weight_near, weight_rest, rowof, low, high, values)

    term_parts = lax.all_to_all(terms, "pool", 0, 0, tiled=True)
    attended = pl.pallas_call(
        sum_kernel,
        out_shape=jax.ShapeDtypeStruct((rows, heads * hd), jnp.bfloat16),
        scratch_shapes=[pltpu.VMEM((kvh * per, hd), jnp.float32)],
        compiler_params=pltpu.CompilerParams(vmem_limit_bytes=8 * MIB),
        name="attended_sum",
    )(term_parts, kept)

    cols = out_weight.shape[1] // ntp
    half_shape = jax.ShapeDtypeStruct((n * rows, cols), jnp.float32)
    half_spec = pl.BlockSpec((n * rows, cols), lambda i, m: (0, 0))
    own, away = pl.pallas_call(
        functools.partial(project_kernel, n),
        grid_spec=pltpu.PrefetchScalarGridSpec(
            num_scalar_prefetch=1,
            grid=(1,),
            in_specs=[
                *[pl.BlockSpec((rows, heads * hd), lambda i, m: (0, 0))] * n,
                in_hbm,
            ],
            out_specs=[half_spec] * 2,
            scratch_shapes=[
                pltpu.VMEM((n * rows, heads * hd), jnp.bfloat16),
                pltpu.VMEM(out_weight.shape, jnp.bfloat16),
                pltpu.SemaphoreType.DMA((8,)),
            ],
        ),
        out_shape=[half_shape] * 2,
        compiler_params=pltpu.CompilerParams(vmem_limit_bytes=56 * MIB),
        name="output_projection",
    )(core.reshape(1), *swap_parts([attended] * n, n), out_weight)
    got = lax.ppermute(away, "tp", swap)
    return pl.pallas_call(
        functools.partial(order_kernel, n),
        grid_spec=pltpu.PrefetchScalarGridSpec(
            num_scalar_prefetch=1,
            grid=(1,),
            in_specs=[half_spec] * 2,
            out_specs=half_spec,
        ),
        out_shape=jax.ShapeDtypeStruct((n * rows, cols), jnp.bfloat16),
        compiler_params=pltpu.CompilerParams(vmem_limit_bytes=4 * MIB),
        name="order_rows",
    )(me.reshape(1), own, got)


def solution(mesh):
    in_specs = (
        P(("groups", "pool"), None),
        P("pool", "tp", None),
        P("groups", None),
        P("groups"),
        P("groups"),
        P(("groups", "pool"), "tp", None),
        P(("groups", "pool"), None, "tp", None),
        P(("groups", "pool")),
        P("tp", "pool"),
    )
    out_specs = P("groups", ("pool", "tp"))
    return jax.shard_map(local, mesh=mesh, in_specs=in_specs, out_specs=out_specs, check_vma=False)
```

```python
import functools

import jax
import jax.numpy as jnp
from jax import lax
from jax.experimental import pallas as pl
from jax.experimental.pallas import tpu as pltpu
from jax.sharding import PartitionSpec as P

BLK = 8
MIB = 1 << 20


def pack_kernel(base, at_ref, fill_ref, dest_ref, x_ref, out_ref, held, packed, count, in_sem, out_sem):
    n, tokens, part = held.shape
    size = packed.shape[1]
    blocks = tokens // BLK

    def load(q):
        return pltpu.make_async_copy(
            x_ref.at[:, pl.ds(q * part, part)], held.at[q], in_sem.at[q]
        )

    def store(q):
        return pltpu.make_async_copy(packed.at[q], out_ref.at[q], out_sem.at[q])

    for q in range(n):
        load(q).start()
    first = at_ref[0] * blocks
    for q in range(n):
        count[q] = 0

    @pl.loop(0, blocks)
    def _(b):
        owner = dest_ref[first + b]
        count[owner] = count[owner] + fill_ref[first + b]

    def starts(q, total):
        here = count[q]
        count[q] = total
        return total + here

    lax.fori_loop(0, n, starts, jnp.int32(0))
    token = lax.broadcasted_iota(jnp.int32, (1, tokens), 1)

    def place(b, ranks):
        owner = dest_ref[first + b]
        fill = fill_ref[first + b]
        start = count[owner]
        count[owner] = start + fill
        inner = token - b * BLK
        return jnp.where((inner >= 0) & (inner < fill), start + inner, ranks)

    ranks = lax.fori_loop(0, blocks, place, jnp.full((1, tokens), -1, jnp.int32))
    wanted = base + at_ref[1] * size + lax.broadcasted_iota(jnp.int32, (size, tokens), 0)
    pick = (wanted == ranks).astype(jnp.bfloat16)
    for q in range(n):
        load(q).wait()
        packed[q] = jnp.dot(pick, held[q], preferred_element_type=jnp.float32).astype(
            packed.dtype
        )
        store(q).start()
    for q in range(n):
        store(q).wait()


def pack(x_prompt, fill, dest, at, n, base, size):
    tokens, width = x_prompt.shape
    part = width // n
    return pl.pallas_call(
        functools.partial(pack_kernel, base),
        grid_spec=pltpu.PrefetchScalarGridSpec(
            num_scalar_prefetch=3,
            grid=(1,),
            in_specs=[pl.BlockSpec(memory_space=pl.ANY)],
            out_specs=pl.BlockSpec(memory_space=pl.ANY),
            scratch_shapes=[
                pltpu.VMEM((n, tokens, part), jnp.bfloat16),
                pltpu.VMEM((n, size, part), jnp.bfloat16),
                pltpu.SMEM((n,), jnp.int32),
                pltpu.SemaphoreType.DMA((n,)),
                pltpu.SemaphoreType.DMA((n,)),
            ],
        ),
        out_shape=jax.ShapeDtypeStruct((n, size, part), jnp.bfloat16),
        compiler_params=pltpu.CompilerParams(vmem_limit_bytes=56 * MIB),
        cost_estimate=pl.CostEstimate(
            flops=2 * size * tokens * width, bytes_accessed=64 * MIB, transcendentals=0
        ),
        name="pack_live_tokens",
    )(at, fill, dest, x_prompt)


def tile_cuts(lanes):
    return [0] + list(range(min(256, lanes), lanes, 128)) + [lanes]


def near_lanes(lanes):
    return min(lanes, -(-lanes * 3 // 5 // 128) * 128)


def load_tokens(n, core, over, x_refs, held, more, wide, sem):
    size, extra = held.shape[1] // n, more.shape[1] // n
    tokens = 2 * (size + extra)
    cuts = sem.shape[1]

    def copies(refs, buffer):
        span = buffer.shape[1] // cuts
        return [
            [
                pltpu.make_async_copy(
                    ref.at[pl.ds(i * span, span)], buffer.at[j, pl.ds(i * span, span)], sem.at[j, i]
                )
                for j, ref in enumerate(refs)
            ]
            for i in range(cuts)
        ]

    def widen(buffer, base, first, last):
        length = buffer.shape[1] // n

        @pl.loop(first, last)
        def _(s):
            for j in range(2):
                side = core if j == 0 else 1 - core
                to = pl.multiple_of(s * tokens + base + side * length, BLK)
                wide[pl.ds(to, length), :] = buffer[
                    j, pl.ds(pl.multiple_of(s * length, length), length), :
                ].astype(wide.dtype)

    main = copies(x_refs[:2], held)
    for pair in main:
        for copy in pair:
            copy.start()
    for i, pair in enumerate(main):
        for copy in pair:
            copy.wait()
        widen(held, 0, i * n // cuts, (i + 1) * n // cuts)

    @pl.when(over != 0)
    def _():
        rest = copies(x_refs[2:], more)
        for pair in rest:
            for copy in pair:
                copy.start()
        for pair in rest:
            for copy in pair:
                copy.wait()
        widen(more, 2 * size, 0, n)


def list_tile(meta_ref, first, count, wide, tile):
    for i in range(0, count, 2):
        pair = [
            wide[pl.ds(pl.multiple_of(meta_ref[first + i + j], BLK), BLK), :] for j in range(2)
        ]
        tile[i * BLK : (i + 2) * BLK, :] = jnp.concatenate(pair).astype(tile.dtype)
    return tile[: count * BLK, :]


def score_kernel(n, rows, meta_ref, *refs):
    x_refs, (even_ref, odd_ref, row_ref), (near_ref, rest_ref) = refs[:4], refs[4:7], refs[7:9]
    held, more, wide, tile, sem = refs[9:]
    step = pl.program_id(0)
    part = wide.shape[1]
    near = near_ref.shape[2]
    lanes = near + rest_ref.shape[2]
    cuts = tile_cuts(lanes)
    groups = lanes // BLK
    at_size = n * groups
    q = meta_ref[at_size + n] ^ reversed_bits(step, n)
    kvh, per = even_ref.shape[0], even_ref.shape[1] * 2 // n
    group = per // rows

    @pl.when(step == 0)
    def _():
        load_tokens(
            n, meta_ref[at_size + n + 1], meta_ref[at_size + n + 2], x_refs, held, more, wide, sem
        )

    def one(keyed_ref, at, t):
        here = slice(cuts[t], cuts[t + 1])
        count = (cuts[t + 1] - cuts[t]) // BLK
        raw = lax.dot_general(
            keyed_ref[:, pl.ds(pl.multiple_of(at * per, per), per), :].reshape(kvh * per, part),
            list_tile(meta_ref, q * groups + cuts[t] // BLK, count, wide, tile),
            (((1,), (1,)), ((), ())),
            preferred_element_type=jnp.float32,
        ).reshape(kvh, rows, group, count * BLK)
        owner_row = row_ref[0, :, here]
        picked = jnp.zeros((kvh, group, count * BLK), jnp.float32)
        for r in range(rows):
            picked = picked + jnp.where((owner_row == r)[None], raw[:, r], 0.0)
        picked = picked.reshape(kvh * group, -1).astype(near_ref.dtype)
        if cuts[t] < near:
            near_ref[0, :, here] = picked
        else:
            rest_ref[0, :, cuts[t] - near : cuts[t + 1] - near] = picked

    def whole(keyed_ref, at):
        one(keyed_ref, at, 0)
        for t in range(1, len(cuts) - 1):
            pl.when(meta_ref[at_size + q] > cuts[t])(functools.partial(one, keyed_ref, at, t))

    pl.when(step < n // 2)(lambda: whole(even_ref, step))
    pl.when(step >= n // 2)(lambda: whole(odd_ref, step - n // 2))


def weight_kernel(scale, count, *refs):
    part_refs, row_refs = refs[:count], refs[count : 2 * count]
    top_ref, sum_ref, cached_ref = refs[2 * count : 2 * count + 3]
    w_refs, kept_ref = refs[2 * count + 3 : -1], refs[-1]
    n = part_refs[0].shape[0]
    scores, owner_rows = [], []
    for part_ref, row_ref in zip(part_refs, row_refs):
        got = part_ref[0].astype(jnp.float32)
        for i in range(1, n):
            got = got + part_ref[i].astype(jnp.float32)
        scores.append(got * scale)
        owner_rows.append(row_ref[...])
    weights = [jnp.zeros(s.shape, jnp.float32) for s in scores]
    for r in range(top_ref.shape[0]):
        own = [jnp.where(o == r, s, -jnp.inf) for o, s in zip(owner_rows, scores)]
        cache_top = top_ref[r]
        top = cache_top
        for o in own:
            top = jnp.maximum(top, jnp.max(o, 1, keepdims=True))
        held = [jnp.exp(o - top) for o in own]
        fade = jnp.exp(cache_top - top)
        total = sum_ref[r] * fade
        for h in held:
            total = total + jnp.sum(h, 1, keepdims=True)
        weights = [w + h / total for w, h in zip(weights, held)]
        kept_ref[r] = cached_ref[r] * (fade / total)
    for w, w_ref in zip(weights, w_refs):
        for i in range(n):
            w_ref[i] = w.astype(w_ref.dtype)


def value_kernel(n, rows, meta_ref, *refs):
    x_refs, (near_ref, rest_ref, row_ref, value_ref, out_ref) = refs[:4], refs[4:9]
    held, more, wide, tile, acc, mixed, sem = refs[9:]
    q = pl.program_id(0)
    kvh = value_ref.shape[0]
    _, heads, near = near_ref.shape
    lanes = near + rest_ref.shape[2]
    per = rows * heads // kvh
    cuts = tile_cuts(lanes)
    groups = lanes // BLK
    at_size = n * groups

    @pl.when(q == 0)
    def _():
        load_tokens(
            n, meta_ref[at_size + n + 1], meta_ref[at_size + n + 2], x_refs, held, more, wide, sem
        )

    def one(t):
        here = slice(cuts[t], cuts[t + 1])
        width = cuts[t + 1] - cuts[t]
        if cuts[t] < near:
            weights = near_ref[0, :, here]
        else:
            weights = rest_ref[0, :, cuts[t] - near : cuts[t + 1] - near]
        weights = weights.astype(jnp.float32).reshape(kvh, 1, heads // kvh, width)
        owner_row = row_ref[0, :, here]
        spread = jnp.concatenate(
            [jnp.where((owner_row == r)[None, None], weights, 0.0) for r in range(rows)], 1
        ).reshape(kvh * per, width)
        got = jnp.dot(
            spread.astype(jnp.bfloat16),
            list_tile(meta_ref, q * groups + cuts[t] // BLK, width // BLK, wide, tile),
            preferred_element_type=jnp.float32,
        )
        if t:
            acc[...] += got
        else:
            acc[...] = got

    one(0)
    for t in range(1, len(cuts) - 1):
        pl.when(meta_ref[at_size + q] > cuts[t])(functools.partial(one, t))
    for h in range(kvh):
        mixed[h, pl.ds(pl.multiple_of(q * per, per), per), :] = acc[
            h * per : (h + 1) * per, :
        ].astype(mixed.dtype)

    @pl.when(q == n - 1)
    def _():
        for h in range(kvh):
            done = jnp.dot(mixed[h], value_ref[h], preferred_element_type=jnp.float32)
            out_ref[:, h] = done.reshape(n, per, done.shape[1]).astype(out_ref.dtype)


def sum_kernel(parts_ref, kept_ref, out_ref, total):
    n, kvh, per, hd = parts_ref.shape
    rows, heads = kept_ref.shape[:2]
    group = heads // kvh
    for h in range(kvh):
        terms = parts_ref[0, h].astype(jnp.float32)
        for i in range(1, n):
            terms = terms + parts_ref[i, h].astype(jnp.float32)
        for r in range(rows):
            here = slice((h * rows + r) * group, (h * rows + r + 1) * group)
            total[here, :] = (
                terms[r * group : (r + 1) * group] + kept_ref[r, h * group : (h + 1) * group, :]
            )
    pieces = [
        total[pl.ds(h * per + g, rows, stride=group), :]
        for h in range(kvh)
        for g in range(group)
    ]
    out_ref[...] = jnp.concatenate(pieces, 1).astype(out_ref.dtype)


def project_kernel(n, core_ref, *refs):
    row_refs, (weight_ref, own_ref, away_ref, gathered) = refs[:n], refs[n:]
    rows = row_refs[0].shape[0]
    cols = own_ref.shape[1]
    for k in range(0, n, 2):
        pair = [row_refs[k + j][...].astype(jnp.float32) for j in range(2)]
        gathered[k * rows : (k + 2) * rows, :] = jnp.concatenate(pair).astype(gathered.dtype)
    step = min(256, cols)
    for i in range(0, 2 * cols, step):
        done = jnp.dot(
            gathered[...], weight_ref[:, i : i + step], preferred_element_type=jnp.float32
        )
        here = slice(i % cols, i % cols + step)

        @pl.when(core_ref[0] == i // cols)
        def _(done=done, here=here):
            own_ref[:, here] = done

        @pl.when(core_ref[0] != i // cols)
        def _(done=done, here=here):
            away_ref[:, here] = done


def order_kernel(n, me_ref, own_ref, got_ref, out_ref):
    rows = own_ref.shape[0] // n
    for q in range(0, n, 2):
        pair = []
        for j in range(2):
            here = pl.ds(pl.multiple_of((me_ref[0] ^ (q + j)) * rows, rows), rows)
            pair.append(own_ref[here, :] + got_ref[here, :])
        out_ref[q * rows : (q + 2) * rows, :] = jnp.concatenate(pair).astype(out_ref.dtype)


def with_partner(x, k, n):
    return lax.ppermute(x, "pool", [(i, i ^ k) for i in range(n)])


def from_rest(held, n):
    k = n // 4
    while k >= 2:
        held = jnp.concatenate([held, with_partner(held, k, n)])
        k //= 2
    return held


def reversed_bits(k, n):
    out, bit = 0, 1
    while bit < n:
        out = out + (k // bit) % 2 * (n // 2 // bit)
        bit *= 2
    return out


def far_first(n):
    return sorted(range(1, n), reverse=True)


def swap_parts(parts, n):
    got = [parts[0]] + [None] * (n - 1)
    for k in far_first(n):
        got[k] = with_partner(parts[k], k, n)
    return got


def local(
    x_prompt, kv_weight, block_dest, block_row, block_fill, queries, kv_cache, cache_len, out_weight
):
    n = lax.axis_size("pool")
    ntp = lax.axis_size("tp")
    me = lax.axis_index("pool").astype(jnp.int32)
    core = lax.axis_index("tp").astype(jnp.int32)
    tokens, width = x_prompt.shape
    part = width // n
    kvh = kv_weight.shape[1]
    hd = kv_weight.shape[2] // 2
    rows, heads = queries.shape[0], queries.shape[1]
    group = heads // kvh
    per = rows * group
    cache_slots = kv_cache.shape[1]
    blocks = tokens // BLK
    cap = max(2, 2 * blocks // n)
    window = cap * BLK + BLK
    lanes = -(-n * window // 128) * 128
    half = tokens // ntp
    scale = 1.0 / hd**0.5
    swap = [(i, (i + 1) % ntp) for i in range(ntp)]

    size = half * 3 // 4
    extra = half - size
    at = jnp.stack([me, core])
    pack_fill, pack_dest = block_fill, block_dest[:, 0]
    packed = pack(x_prompt, pack_fill, pack_dest, at, n, 0, size)
    dest = pack_dest
    far = with_partner(queries, n // 2, n)
    packed, far, dest, block_row, block_fill, query, cache_len, kv_weight = (
        lax.optimization_barrier(
            (packed, far, dest, block_row, block_fill, queries, cache_len, kv_weight)
        )
    )
    mine = lax.all_to_all(packed, "pool", 0, 0, tiled=True).reshape(n * size, part)

    index = jnp.arange(n * blocks, dtype=jnp.int32)
    sender = index // blocks
    kin = sender[None, :] == sender[:, None]
    lower = kin & (dest[None, :] < dest[:, None])
    level = kin & (dest[None, :] == dest[:, None]) & (index[None, :] < index[:, None])
    before = jnp.sum(jnp.where(lower, block_fill[None, :], 0), 1)
    within = jnp.sum(jnp.where(level, block_fill[None, :], 0), 1)
    pair = jnp.arange(n * n, dtype=jnp.int32)
    to, by = pair // n, pair % n
    owned = dest[None, :] == to[:, None]
    sent = sender[None, :] == by[:, None]
    earlier = sent & (dest[None, :] < to[:, None])
    offset = jnp.sum(jnp.where(earlier, block_fill[None, :], 0), 1)
    amount = jnp.sum(jnp.where(sent & owned, block_fill[None, :], 0), 1)
    runs = jnp.where(amount > 0, (offset % BLK + amount + BLK - 1) // BLK * BLK, 0)
    runs_by = runs.reshape(n, n)
    prior = jnp.arange(n)[:, None] < jnp.arange(n)[None, :]
    targets = jnp.sum(jnp.where(prior[None], runs_by[:, :, None], 0), 1)
    list_rows = jnp.sum(runs_by, 1)
    targets = targets.reshape(-1)
    sources = by * tokens + offset // BLK * BLK
    group_at = jnp.arange(n * lanes // BLK, dtype=jnp.int32) * BLK
    skip = group_at[:, None] - (to * lanes + targets)[None, :]
    group_rows = jnp.sum(
        jnp.where((skip >= 0) & (skip < runs[None, :]), sources[None, :] + skip, 0), 1
    )
    mine_pair = (dest * n + sender)[:, None] == pair[None, :]
    start = (
        dest * lanes
        + jnp.sum(jnp.where(mine_pair, targets[None, :], 0), 1)
        + before % BLK
        + within
    )
    spot = jnp.arange(n * lanes, dtype=jnp.int32)[:, None]
    inside = (spot >= start[None, :]) & (spot < (start + block_fill)[None, :])
    rowof = jnp.sum(jnp.where(inside, (block_row + 1)[None, :], 0), 1) - 1
    rowof = rowof.reshape(n, 1, lanes)

    near = near_lanes(lanes)
    most = jnp.stack([jnp.max(jnp.sum(block_fill.reshape(n, blocks), 1)), jnp.max(list_rows)])
    groups = lax.axis_size("groups")
    k = 1
    while k < groups:
        most = jnp.maximum(
            most, lax.ppermute(most, "groups", [(i, i ^ k) for i in range(groups)])
        )
        k *= 2
    over, longer = most[0] > ntp * size, most[1] > near

    def exchange_rest():
        rest = pack(x_prompt, pack_fill, pack_dest, at, n, ntp * size, extra)
        rest = lax.all_to_all(rest, "pool", 0, 0, tiled=True).reshape(n * extra, part)
        return rest, lax.ppermute(rest, "tp", swap)

    def no_rest():
        return (jnp.zeros((n * extra, part), jnp.bfloat16),) * 2

    more_mine, more_other = lax.cond(over, exchange_rest, no_rest)
    meta = jnp.concatenate(
        [group_rows, list_rows, jnp.stack([me, core, over.astype(jnp.int32)])]
    )

    keys = kv_weight[:, :, :hd]

    def through_keys(held):
        held = held.reshape(n // 2, rows, kvh, group, hd)
        return (
            jnp.einsum("qrhgd,phd->hqrgp", held, keys, preferred_element_type=jnp.float32)
            .astype(jnp.bfloat16)
            .reshape(kvh, n // 2 * per, part)
        )

    even = from_rest(jnp.stack([queries, far]), n)
    keyed_even = through_keys(even)
    keyed_odd = through_keys(with_partner(even, 1, n))
    values = kv_weight[:, :, hd:].transpose(1, 0, 2)

    query = query.reshape(rows, kvh, group, hd)
    cache_live = jnp.arange(cache_slots, dtype=jnp.int32)[None, :] < cache_len[:, None]
    cached_keys, cached_values = (
        jnp.where(cache_live[:, :, None, None], kv_cache[:, :, :, at : at + hd], 0)
        for at in (0, hd)
    )
    cache_scores = (
        jnp.einsum("rhgd,rthd->rhgt", query, cached_keys, preferred_element_type=jnp.float32)
        * scale
    )
    cache_scores = jnp.where(cache_live[:, None, None, :], cache_scores, -jnp.inf)
    cache_top = jnp.max(cache_scores, -1, keepdims=True)
    cache_exp = jnp.exp(cache_scores - cache_top)
    cache_sum = jnp.sum(cache_exp, -1, keepdims=True)
    cached = jnp.einsum(
        "rhgt,rthd->rhgd",
        cache_exp.astype(jnp.bfloat16),
        cached_values,
        preferred_element_type=jnp.float32,
    )
    cache_top = cache_top.reshape(rows, heads, 1)
    cache_sum = cache_sum.reshape(rows, heads, 1)
    cached = cached.reshape(rows, heads, hd)

    mine, meta, rowof, keyed_even, keyed_odd, values, cache_top, cache_sum, cached = (
        lax.optimization_barrier(
            (mine, meta, rowof, keyed_even, keyed_odd, values, cache_top, cache_sum, cached)
        )
    )
    other = lax.ppermute(mine, "tp", swap)

    in_hbm = pl.BlockSpec(memory_space=pltpu.HBM)
    row_spec = pl.BlockSpec((1, 1, lanes), lambda q, m: (q, 0, 0))
    slot_specs = [
        pl.BlockSpec((1, heads, length), lambda q, m: (q, 0, 0)) for length in (near, lanes - near)
    ]
    slot_shapes = [
        jax.ShapeDtypeStruct((n, heads, length), jnp.bfloat16) for length in (near, lanes - near)
    ]
    in_vmem = pl.BlockSpec(memory_space=pltpu.VMEM)
    x_parts = (mine, other, more_mine, more_other)
    x_scratch = [
        pltpu.VMEM((ntp, n * size, part), jnp.bfloat16),
        pltpu.VMEM((ntp, n * extra, part), jnp.bfloat16),
        pltpu.VMEM((n * tokens, part), jnp.float32),
        pltpu.VMEM((tile_cuts(lanes)[1], part), jnp.bfloat16),
    ]
    at_me = n * lanes // BLK + n

    def owner(i, m):
        return m[at_me] ^ reversed_bits(i, n)

    score_near, score_rest = pl.pallas_call(
        functools.partial(score_kernel, n, rows),
        grid_spec=pltpu.PrefetchScalarGridSpec(
            num_scalar_prefetch=1,
            grid=(n,),
            in_specs=[
                *[in_hbm] * 4,
                in_vmem,
                in_vmem,
                pl.BlockSpec((1, 1, lanes), lambda i, m: (owner(i, m), 0, 0)),
            ],
            out_specs=[
                pl.BlockSpec((1, heads, length), lambda i, m: (owner(i, m), 0, 0))
                for length in (near, lanes - near)
            ],
            scratch_shapes=[*x_scratch, pltpu.SemaphoreType.DMA((ntp, 4))],
        ),
        out_shape=slot_shapes,
        compiler_params=pltpu.CompilerParams(vmem_limit_bytes=20 * MIB),
        name="prompt_scores",
    )(meta, *x_parts, keyed_even, keyed_odd, rowof)

    my_rows = lax.dynamic_index_in_dim(rowof, me, 0, keepdims=False)

    def exchange_weights(*scores):
        count = len(scores)
        parts = [lax.all_to_all(s, "pool", 0, 0, tiled=True) for s in scores]
        row_parts = [my_rows[:, :near], my_rows[:, near:]][:count]
        *weights, kept = pl.pallas_call(
            functools.partial(weight_kernel, scale, count),
            out_shape=[*slot_shapes[:count], jax.ShapeDtypeStruct((rows, heads, hd), jnp.float32)],
            compiler_params=pltpu.CompilerParams(vmem_limit_bytes=8 * MIB),
            name="softmax_weights",
        )(*parts, *row_parts, cache_top, cache_sum, cached)
        return *[lax.all_to_all(w, "pool", 0, 0, tiled=True) for w in weights], kept

    def near_only():
        weights, kept = exchange_weights(score_near)
        return weights, jnp.zeros(slot_shapes[1].shape, jnp.bfloat16), kept

    weight_near, weight_rest, kept = lax.cond(
        longer, lambda: exchange_weights(score_near, score_rest), near_only
    )
    terms = pl.pallas_call(
        functools.partial(value_kernel, n, rows),
        grid_spec=pltpu.PrefetchScalarGridSpec(
            num_scalar_prefetch=1,
            grid=(n,),
            in_specs=[*[in_hbm] * 4, *slot_specs, row_spec, in_vmem],
            out_specs=pl.BlockSpec((n, kvh, per, hd), lambda q, m: (0, 0, 0, 0)),
            scratch_shapes=[
                *x_scratch,
                pltpu.VMEM((kvh * per, part), jnp.float32),
                pltpu.VMEM((kvh, n * per, part), jnp.bfloat16),
                pltpu.SemaphoreType.DMA((ntp, 4)),
            ],
        ),
        out_shape=jax.ShapeDtypeStruct((n, kvh, per, hd), jnp.bfloat16),
        compiler_params=pltpu.CompilerParams(vmem_limit_bytes=26 * MIB),
        name="weighted_values",
    )(meta, *x_parts, weight_near, weight_rest, rowof, values)

    term_parts = lax.all_to_all(terms, "pool", 0, 0, tiled=True)
    attended = pl.pallas_call(
        sum_kernel,
        out_shape=jax.ShapeDtypeStruct((rows, heads * hd), jnp.bfloat16),
        scratch_shapes=[pltpu.VMEM((kvh * per, hd), jnp.float32)],
        compiler_params=pltpu.CompilerParams(vmem_limit_bytes=8 * MIB),
        name="attended_sum",
    )(term_parts, kept)

    cols = out_weight.shape[1] // ntp
    half_shape = jax.ShapeDtypeStruct((n * rows, cols), jnp.float32)
    half_spec = pl.BlockSpec((n * rows, cols), lambda i, m: (0, 0))
    own, away = pl.pallas_call(
        functools.partial(project_kernel, n),
        grid_spec=pltpu.PrefetchScalarGridSpec(
            num_scalar_prefetch=1,
            grid=(1,),
            in_specs=[
                *[pl.BlockSpec((rows, heads * hd), lambda i, m: (0, 0))] * n,
                pl.BlockSpec(out_weight.shape, lambda i, m: (0, 0)),
            ],
            out_specs=[half_spec] * 2,
            scratch_shapes=[pltpu.VMEM((n * rows, heads * hd), jnp.bfloat16)],
        ),
        out_shape=[half_shape] * 2,
        compiler_params=pltpu.CompilerParams(vmem_limit_bytes=26 * MIB),
        name="output_projection",
    )(core.reshape(1), *swap_parts([attended] * n, n), out_weight)
    got = lax.ppermute(away, "tp", swap)
    return pl.pallas_call(
        functools.partial(order_kernel, n),
        grid_spec=pltpu.PrefetchScalarGridSpec(
            num_scalar_prefetch=1,
            grid=(1,),
            in_specs=[half_spec] * 2,
            out_specs=half_spec,
        ),
        out_shape=jax.ShapeDtypeStruct((n * rows, cols), jnp.bfloat16),
        compiler_params=pltpu.CompilerParams(vmem_limit_bytes=4 * MIB),
        name="order_rows",
    )(me.reshape(1), own, got)


def solution(mesh):
    in_specs = (
        P(("groups", "pool"), None),
        P("pool", "tp", None),
        P("groups", None),
        P("groups"),
        P("groups"),
        P(("groups", "pool"), "tp", None),
        P(("groups", "pool"), None, "tp", None),
        P(("groups", "pool")),
        P("tp", "pool"),
    )
    out_specs = P("groups", ("pool", "tp"))
    return jax.shard_map(local, mesh=mesh, in_specs=in_specs, out_specs=out_specs, check_vma=False)
```

```python
import functools

import jax
import jax.numpy as jnp
from jax import lax
from jax.experimental import pallas as pl
from jax.experimental.pallas import tpu as pltpu
from jax.sharding import PartitionSpec as P

BLK = 8
MIB = 1 << 20


def pack_kernel(base, at_ref, fill_ref, dest_ref, x_ref, out_ref, held, packed, count, in_sem, out_sem):
    n, tokens, part = held.shape
    size = packed.shape[1]
    blocks = tokens // BLK

    def load(q):
        return pltpu.make_async_copy(
            x_ref.at[:, pl.ds(q * part, part)], held.at[q], in_sem.at[q]
        )

    def store(q):
        return pltpu.make_async_copy(packed.at[q], out_ref.at[q], out_sem.at[q])

    for q in range(n):
        load(q).start()
    first = at_ref[0] * blocks
    for q in range(n):
        count[q] = 0

    @pl.loop(0, blocks)
    def _(b):
        owner = dest_ref[first + b]
        count[owner] = count[owner] + fill_ref[first + b]

    def starts(q, total):
        here = count[q]
        count[q] = total
        return total + here

    lax.fori_loop(0, n, starts, jnp.int32(0))
    token = lax.broadcasted_iota(jnp.int32, (1, tokens), 1)

    def place(b, ranks):
        owner = dest_ref[first + b]
        fill = fill_ref[first + b]
        start = count[owner]
        count[owner] = start + fill
        inner = token - b * BLK
        return jnp.where((inner >= 0) & (inner < fill), start + inner, ranks)

    ranks = lax.fori_loop(0, blocks, place, jnp.full((1, tokens), -1, jnp.int32))
    wanted = base + at_ref[1] * size + lax.broadcasted_iota(jnp.int32, (size, tokens), 0)
    pick = (wanted == ranks).astype(jnp.bfloat16)
    for q in range(n):
        load(q).wait()
        packed[q] = jnp.dot(pick, held[q], preferred_element_type=jnp.float32).astype(
            packed.dtype
        )
        store(q).start()
    for q in range(n):
        store(q).wait()


def pack(x_prompt, fill, dest, at, n, base, size):
    tokens, width = x_prompt.shape
    part = width // n
    return pl.pallas_call(
        functools.partial(pack_kernel, base),
        grid_spec=pltpu.PrefetchScalarGridSpec(
            num_scalar_prefetch=3,
            grid=(1,),
            in_specs=[pl.BlockSpec(memory_space=pl.ANY)],
            out_specs=pl.BlockSpec(memory_space=pl.ANY),
            scratch_shapes=[
                pltpu.VMEM((n, tokens, part), jnp.bfloat16),
                pltpu.VMEM((n, size, part), jnp.bfloat16),
                pltpu.SMEM((n,), jnp.int32),
                pltpu.SemaphoreType.DMA((n,)),
                pltpu.SemaphoreType.DMA((n,)),
            ],
        ),
        out_shape=jax.ShapeDtypeStruct((n, size, part), jnp.bfloat16),
        compiler_params=pltpu.CompilerParams(vmem_limit_bytes=56 * MIB),
        cost_estimate=pl.CostEstimate(
            flops=2 * size * tokens * width, bytes_accessed=64 * MIB, transcendentals=0
        ),
        name="pack_live_tokens",
    )(at, fill, dest, x_prompt)


def tile_cuts(lanes):
    return [0] + list(range(min(256, lanes), lanes, 128)) + [lanes]


def near_lanes(lanes):
    return min(lanes, -(-lanes * 3 // 5 // 128) * 128)


def load_tokens(n, core, over, x_refs, held, more, wide, sem, others=()):
    size, extra = held.shape[1] // n, more.shape[1] // n
    tokens = 2 * (size + extra)
    cuts = sem.shape[1]

    def copies(refs, buffer):
        span = buffer.shape[1] // cuts
        return [
            [
                pltpu.make_async_copy(
                    ref.at[pl.ds(i * span, span)], buffer.at[j, pl.ds(i * span, span)], sem.at[j, i]
                )
                for j, ref in enumerate(refs)
            ]
            for i in range(cuts)
        ]

    def widen(buffer, base, first, last):
        length = buffer.shape[1] // n

        @pl.loop(first, last)
        def _(s):
            for j in range(2):
                side = core if j == 0 else 1 - core
                to = pl.multiple_of(s * tokens + base + side * length, BLK)
                wide[pl.ds(to, length), :] = buffer[
                    j, pl.ds(pl.multiple_of(s * length, length), length), :
                ].astype(wide.dtype)

    main = copies(x_refs[:2], held)
    for pair in main:
        for copy in pair:
            copy.start()
    for copy in others:
        copy.start()
    for i, pair in enumerate(main):
        for copy in pair:
            copy.wait()
        widen(held, 0, i * n // cuts, (i + 1) * n // cuts)

    @pl.when(over != 0)
    def _():
        rest = copies(x_refs[2:], more)
        for pair in rest:
            for copy in pair:
                copy.start()
        for pair in rest:
            for copy in pair:
                copy.wait()
        widen(more, 2 * size, 0, n)


def list_tile(meta_ref, first, count, wide, tile):
    for i in range(0, count, 2):
        pair = [
            wide[pl.ds(pl.multiple_of(meta_ref[first + i + j], BLK), BLK), :] for j in range(2)
        ]
        tile[i * BLK : (i + 2) * BLK, :] = jnp.concatenate(pair).astype(tile.dtype)
    return tile[: count * BLK, :]


def score_kernel(n, rows, meta_ref, *refs):
    x_refs, keyed_refs, (row_ref, near_ref, rest_ref) = refs[:4], refs[4:6], refs[6:9]
    held, more, wide, tile, keyed, sem, keyed_sem = refs[9:]
    step = pl.program_id(0)
    part = wide.shape[1]
    near = near_ref.shape[2]
    lanes = near + rest_ref.shape[2]
    cuts = tile_cuts(lanes)
    groups = lanes // BLK
    at_size = n * groups
    q = meta_ref[at_size + n] ^ reversed_bits(step, n)
    kvh, per = keyed.shape[0], keyed.shape[1] // n
    group = per // rows

    @pl.when(step == 0)
    def _():
        span = n // 2 * per
        loads = [
            pltpu.make_async_copy(
                ref.at[h], keyed.at[h, pl.ds(i * span, span)], keyed_sem.at[i, h]
            )
            for i, ref in enumerate(keyed_refs)
            for h in range(kvh)
        ]
        load_tokens(
            n, meta_ref[at_size + n + 1], meta_ref[at_size + n + 2], x_refs, held, more, wide, sem,
            loads,
        )
        for load in loads:
            load.wait()

    def one(t):
        here = slice(cuts[t], cuts[t + 1])
        count = (cuts[t + 1] - cuts[t]) // BLK
        raw = lax.dot_general(
            keyed[:, pl.ds(pl.multiple_of(step * per, per), per), :].reshape(kvh * per, part),
            list_tile(meta_ref, q * groups + cuts[t] // BLK, count, wide, tile),
            (((1,), (1,)), ((), ())),
            preferred_element_type=jnp.float32,
        ).reshape(kvh, rows, group, count * BLK)
        owner_row = row_ref[0, :, here]
        picked = jnp.zeros((kvh, group, count * BLK), jnp.float32)
        for r in range(rows):
            picked = picked + jnp.where((owner_row == r)[None], raw[:, r], 0.0)
        picked = picked.reshape(kvh * group, -1).astype(near_ref.dtype)
        if cuts[t] < near:
            near_ref[0, :, here] = picked
        else:
            rest_ref[0, :, cuts[t] - near : cuts[t + 1] - near] = picked

    one(0)
    for t in range(1, len(cuts) - 1):
        pl.when(meta_ref[at_size + q] > cuts[t])(functools.partial(one, t))


def weight_kernel(scale, count, *refs):
    part_refs, row_refs = refs[:count], refs[count : 2 * count]
    top_ref, sum_ref, cached_ref = refs[2 * count : 2 * count + 3]
    w_refs, kept_ref = refs[2 * count + 3 : -1], refs[-1]
    n = part_refs[0].shape[0]
    scores, owner_rows = [], []
    for part_ref, row_ref in zip(part_refs, row_refs):
        got = part_ref[0].astype(jnp.float32)
        for i in range(1, n):
            got = got + part_ref[i].astype(jnp.float32)
        scores.append(got * scale)
        owner_rows.append(row_ref[...])
    weights = [jnp.zeros(s.shape, jnp.float32) for s in scores]
    for r in range(top_ref.shape[0]):
        own = [jnp.where(o == r, s, -jnp.inf) for o, s in zip(owner_rows, scores)]
        cache_top = top_ref[r]
        top = cache_top
        for o in own:
            top = jnp.maximum(top, jnp.max(o, 1, keepdims=True))
        held = [jnp.exp(o - top) for o in own]
        fade = jnp.exp(cache_top - top)
        total = sum_ref[r] * fade
        for h in held:
            total = total + jnp.sum(h, 1, keepdims=True)
        weights = [w + h / total for w, h in zip(weights, held)]
        kept_ref[r] = cached_ref[r] * (fade / total)
    for w, w_ref in zip(weights, w_refs):
        for i in range(n):
            w_ref[i] = w.astype(w_ref.dtype)


def value_kernel(n, rows, meta_ref, *refs):
    x_refs, (near_ref, rest_ref, row_ref, value_ref, out_ref) = refs[:4], refs[4:9]
    held, more, wide, tile, values, acc, mixed, sem, value_sem = refs[9:]
    q = pl.program_id(0)
    kvh = values.shape[0]
    load_values = pltpu.make_async_copy(value_ref, values, value_sem)
    _, heads, near = near_ref.shape
    lanes = near + rest_ref.shape[2]
    per = rows * heads // kvh
    cuts = tile_cuts(lanes)
    groups = lanes // BLK
    at_size = n * groups

    @pl.when(q == 0)
    def _():
        load_tokens(
            n, meta_ref[at_size + n + 1], meta_ref[at_size + n + 2], x_refs, held, more, wide, sem,
            [load_values],
        )

    def one(t):
        here = slice(cuts[t], cuts[t + 1])
        width = cuts[t + 1] - cuts[t]
        if cuts[t] < near:
            weights = near_ref[0, :, here]
        else:
            weights = rest_ref[0, :, cuts[t] - near : cuts[t + 1] - near]
        weights = weights.astype(jnp.float32).reshape(kvh, 1, heads // kvh, width)
        owner_row = row_ref[0, :, here]
        spread = jnp.concatenate(
            [jnp.where((owner_row == r)[None, None], weights, 0.0) for r in range(rows)], 1
        ).reshape(kvh * per, width)
        got = jnp.dot(
            spread.astype(jnp.bfloat16),
            list_tile(meta_ref, q * groups + cuts[t] // BLK, width // BLK, wide, tile),
            preferred_element_type=jnp.float32,
        )
        if t:
            acc[...] += got
        else:
            acc[...] = got

    one(0)
    for t in range(1, len(cuts) - 1):
        pl.when(meta_ref[at_size + q] > cuts[t])(functools.partial(one, t))
    for h in range(kvh):
        mixed[h, pl.ds(pl.multiple_of(q * per, per), per), :] = acc[
            h * per : (h + 1) * per, :
        ].astype(mixed.dtype)

    @pl.when(q == n - 1)
    def _():
        load_values.wait()
        for h in range(kvh):
            done = jnp.dot(mixed[h], values[h], preferred_element_type=jnp.float32)
            done = done.reshape(2, n // 2, per, done.shape[1]).astype(out_ref.dtype)
            for side in range(2):
                out_ref[:, side, h] = done[side]


def half_sum_kernel(side_ref, parts_ref, kept_ref, send_ref, mine_ref):
    half, sides, kvh, per, hd = parts_ref.shape
    rows, heads = kept_ref.shape[:2]
    group = heads // kvh
    for side in range(sides):
        own = side_ref[0] == side
        for h in range(kvh):
            terms = parts_ref[0, side, h].astype(jnp.float32)
            for i in range(1, half):
                terms = terms + parts_ref[i, side, h].astype(jnp.float32)
            kept = jnp.concatenate(
                [kept_ref[r, h * group : (h + 1) * group, :] for r in range(rows)]
            )
            terms = terms + jnp.where(own, kept, 0.0)
            mine_ref[side, h] = terms
            send_ref[side, h] = terms.astype(send_ref.dtype)


def whole_sum_kernel(mine_ref, got_ref, out_ref, total):
    sides, kvh, per, _ = mine_ref.shape
    rows = out_ref.shape[0] // sides
    group = per // rows
    total[...] = mine_ref[...] + got_ref[...].astype(jnp.float32)
    for h in range(kvh):
        for g in range(group):
            column = [
                total[side, h, pl.ds(g, rows, stride=group), :] for side in range(sides)
            ]
            head = h * group + g
            hd = column[0].shape[1]
            out_ref[:, head * hd : (head + 1) * hd] = jnp.concatenate(column).astype(
                out_ref.dtype
            )


def order_kernel(n, me_ref, own_ref, got_ref, out_ref):
    half = n // 2
    rows = own_ref.shape[0] // n
    for q in range(0, n, 2):
        pair = []
        for owner in (q, q + 1):
            block = ((me_ref[0] % half) ^ (owner % half)) * 2 + owner // half
            here = pl.ds(pl.multiple_of(block * rows, rows), rows)
            pair.append(own_ref[here, :] + got_ref[here, :])
        out_ref[q * rows : (q + 2) * rows, :] = jnp.concatenate(pair).astype(out_ref.dtype)


def with_partner(x, k, n):
    return lax.ppermute(x, "pool", [(i, i ^ k) for i in range(n)])


def from_rest(held, n):
    k = n // 4
    while k >= 2:
        held = jnp.concatenate([held, with_partner(held, k, n)])
        k //= 2
    return held


def reversed_bits(k, n):
    out, bit = 0, 1
    while bit < n:
        out = out + (k // bit) % 2 * (n // 2 // bit)
        bit *= 2
    return out


def local(
    x_prompt, kv_weight, block_dest, block_row, block_fill, queries, kv_cache, cache_len, out_weight
):
    n = lax.axis_size("pool")
    ntp = lax.axis_size("tp")
    me = lax.axis_index("pool").astype(jnp.int32)
    core = lax.axis_index("tp").astype(jnp.int32)
    tokens, width = x_prompt.shape
    part = width // n
    kvh = kv_weight.shape[1]
    hd = kv_weight.shape[2] // 2
    rows, heads = queries.shape[0], queries.shape[1]
    group = heads // kvh
    per = rows * group
    cache_slots = kv_cache.shape[1]
    blocks = tokens // BLK
    cap = max(2, 2 * blocks // n)
    window = cap * BLK + BLK
    lanes = -(-n * window // 128) * 128
    half = tokens // ntp
    scale = 1.0 / hd**0.5
    swap = [(i, (i + 1) % ntp) for i in range(ntp)]

    size = half * 3 // 4
    extra = half - size
    at = jnp.stack([me, core])
    pack_fill, pack_dest = block_fill, block_dest[:, 0]
    packed = pack(x_prompt, pack_fill, pack_dest, at, n, 0, size)
    dest = pack_dest
    even = from_rest(jnp.stack([queries, with_partner(queries, n // 2, n)]), n)
    packed, even, dest, block_row, block_fill, query, kv_weight, ready = (
        lax.optimization_barrier(
            (
                packed, even, dest, block_row, block_fill, queries, kv_weight,
                jnp.ones((), jnp.bool_),
            )
        )
    )
    mine = lax.all_to_all(packed, "pool", 0, 0, tiled=True).reshape(n * size, part)

    index = jnp.arange(n * blocks, dtype=jnp.int32)
    sender = index // blocks
    kin = sender[None, :] == sender[:, None]
    lower = kin & (dest[None, :] < dest[:, None])
    level = kin & (dest[None, :] == dest[:, None]) & (index[None, :] < index[:, None])
    before = jnp.sum(jnp.where(lower, block_fill[None, :], 0), 1)
    within = jnp.sum(jnp.where(level, block_fill[None, :], 0), 1)
    pair = jnp.arange(n * n, dtype=jnp.int32)
    to, by = pair // n, pair % n
    owned = dest[None, :] == to[:, None]
    sent = sender[None, :] == by[:, None]
    earlier = sent & (dest[None, :] < to[:, None])
    offset = jnp.sum(jnp.where(earlier, block_fill[None, :], 0), 1)
    amount = jnp.sum(jnp.where(sent & owned, block_fill[None, :], 0), 1)
    runs = jnp.where(amount > 0, (offset % BLK + amount + BLK - 1) // BLK * BLK, 0)
    runs_by = runs.reshape(n, n)
    prior = jnp.arange(n)[:, None] < jnp.arange(n)[None, :]
    targets = jnp.sum(jnp.where(prior[None], runs_by[:, :, None], 0), 1)
    list_rows = jnp.sum(runs_by, 1)
    targets = targets.reshape(-1)
    sources = by * tokens + offset // BLK * BLK
    group_at = jnp.arange(n * lanes // BLK, dtype=jnp.int32) * BLK
    skip = group_at[:, None] - (to * lanes + targets)[None, :]
    group_rows = jnp.sum(
        jnp.where((skip >= 0) & (skip < runs[None, :]), sources[None, :] + skip, 0), 1
    )
    mine_pair = (dest * n + sender)[:, None] == pair[None, :]
    start = (
        dest * lanes
        + jnp.sum(jnp.where(mine_pair, targets[None, :], 0), 1)
        + before % BLK
        + within
    )
    spot = jnp.arange(n * lanes, dtype=jnp.int32)[:, None]
    inside = (spot >= start[None, :]) & (spot < (start + block_fill)[None, :])
    rowof = jnp.sum(jnp.where(inside, (block_row + 1)[None, :], 0), 1) - 1
    rowof = rowof.reshape(n, 1, lanes)

    near = near_lanes(lanes)
    most = jnp.stack([jnp.max(jnp.sum(block_fill.reshape(n, blocks), 1)), jnp.max(list_rows)])
    groups = lax.axis_size("groups")
    k = 1
    while k < groups:
        most = jnp.maximum(
            most, lax.ppermute(most, "groups", [(i, i ^ k) for i in range(groups)])
        )
        k *= 2
    over, longer = most[0] > ntp * size, most[1] > near

    def exchange_rest():
        rest = pack(x_prompt, pack_fill, pack_dest, at, n, ntp * size, extra)
        rest = lax.all_to_all(rest, "pool", 0, 0, tiled=True).reshape(n * extra, part)
        return rest, lax.ppermute(rest, "tp", swap)

    def no_rest():
        return (jnp.zeros((n * extra, part), jnp.bfloat16),) * 2

    more_mine, more_other = lax.cond(over, exchange_rest, no_rest)
    meta = jnp.concatenate(
        [group_rows, list_rows, jnp.stack([me, core, over.astype(jnp.int32)])]
    )

    keys = kv_weight[:, :, :hd]

    def through_keys(held):
        held = held.reshape(n // 2, rows, kvh, group, hd)
        return (
            jnp.einsum("qrhgd,phd->hqrgp", held, keys, preferred_element_type=jnp.float32)
            .astype(jnp.bfloat16)
            .reshape(kvh, n // 2 * per, part)
        )

    keyed_even = through_keys(even)
    keyed_odd = through_keys(with_partner(even, 1, n))
    values = kv_weight[:, :, hd:].transpose(1, 0, 2)

    query = query.reshape(rows, kvh, group, hd)
    cache_live = jnp.arange(cache_slots, dtype=jnp.int32)[None, :] < cache_len[:, None]
    cached_keys, cached_values = (
        jnp.where(ready, kv_cache[:, :, :, at : at + hd], 0)
        for at in (0, hd)
    )
    cache_scores = (
        jnp.einsum("rhgd,rthd->rhgt", query, cached_keys, preferred_element_type=jnp.float32)
        * scale
    )
    cache_scores = jnp.where(cache_live[:, None, None, :], cache_scores, -jnp.inf)
    cache_top = jnp.max(cache_scores, -1, keepdims=True)
    cache_exp = jnp.exp(cache_scores - cache_top)
    cache_sum = jnp.sum(cache_exp, -1, keepdims=True)
    cached = jnp.einsum(
        "rhgt,rthd->rhgd",
        cache_exp.astype(jnp.bfloat16),
        cached_values,
        preferred_element_type=jnp.float32,
    )
    cache_top = cache_top.reshape(rows, heads, 1)
    cache_sum = cache_sum.reshape(rows, heads, 1)
    cached = cached.reshape(rows, heads, hd)

    mine, meta, rowof, keyed_even, keyed_odd, values, cache_top, cache_sum, cached = (
        lax.optimization_barrier(
            (mine, meta, rowof, keyed_even, keyed_odd, values, cache_top, cache_sum, cached)
        )
    )
    other = lax.ppermute(mine, "tp", swap)

    in_hbm = pl.BlockSpec(memory_space=pltpu.HBM)
    row_spec = pl.BlockSpec((1, 1, lanes), lambda q, m: (q, 0, 0))
    slot_specs = [
        pl.BlockSpec((1, heads, length), lambda q, m: (q, 0, 0)) for length in (near, lanes - near)
    ]
    slot_shapes = [
        jax.ShapeDtypeStruct((n, heads, length), jnp.bfloat16) for length in (near, lanes - near)
    ]
    in_vmem = pl.BlockSpec(memory_space=pltpu.VMEM)
    x_parts = (mine, other, more_mine, more_other)
    x_scratch = [
        pltpu.VMEM((ntp, n * size, part), jnp.bfloat16),
        pltpu.VMEM((ntp, n * extra, part), jnp.bfloat16),
        pltpu.VMEM((n * tokens, part), jnp.float32),
        pltpu.VMEM((tile_cuts(lanes)[1], part), jnp.bfloat16),
    ]
    at_me = n * lanes // BLK + n

    def owner(i, m):
        return m[at_me] ^ reversed_bits(i, n)

    score_near, score_rest = pl.pallas_call(
        functools.partial(score_kernel, n, rows),
        grid_spec=pltpu.PrefetchScalarGridSpec(
            num_scalar_prefetch=1,
            grid=(n,),
            in_specs=[
                *[in_hbm] * 6,
                pl.BlockSpec((1, 1, lanes), lambda i, m: (owner(i, m), 0, 0)),
            ],
            out_specs=[
                pl.BlockSpec((1, heads, length), lambda i, m: (owner(i, m), 0, 0))
                for length in (near, lanes - near)
            ],
            scratch_shapes=[
                *x_scratch,
                pltpu.VMEM((kvh, n * per, part), jnp.bfloat16),
                pltpu.SemaphoreType.DMA((ntp, 4)),
                pltpu.SemaphoreType.DMA((2, kvh)),
            ],
        ),
        out_shape=slot_shapes,
        compiler_params=pltpu.CompilerParams(vmem_limit_bytes=56 * MIB),
        name="prompt_scores",
    )(meta, *x_parts, keyed_even, keyed_odd, rowof)

    my_rows = lax.dynamic_index_in_dim(rowof, me, 0, keepdims=False)

    def exchange_weights(*scores):
        count = len(scores)
        parts = [lax.all_to_all(s, "pool", 0, 0, tiled=True) for s in scores]
        row_parts = [my_rows[:, :near], my_rows[:, near:]][:count]
        *weights, kept = pl.pallas_call(
            functools.partial(weight_kernel, scale, count),
            out_shape=[*slot_shapes[:count], jax.ShapeDtypeStruct((rows, heads, hd), jnp.float32)],
            compiler_params=pltpu.CompilerParams(vmem_limit_bytes=8 * MIB),
            name="softmax_weights",
        )(*parts, *row_parts, cache_top, cache_sum, cached)
        return *[lax.all_to_all(w, "pool", 0, 0, tiled=True) for w in weights], kept

    def near_only():
        weights, kept = exchange_weights(score_near)
        return weights, jnp.zeros(slot_shapes[1].shape, jnp.bfloat16), kept

    weight_near, weight_rest, kept = lax.cond(
        longer, lambda: exchange_weights(score_near, score_rest), near_only
    )
    terms = pl.pallas_call(
        functools.partial(value_kernel, n, rows),
        grid_spec=pltpu.PrefetchScalarGridSpec(
            num_scalar_prefetch=1,
            grid=(n,),
            in_specs=[*[in_hbm] * 4, *slot_specs, row_spec, in_hbm],
            out_specs=pl.BlockSpec((n // 2, 2, kvh, per, hd), lambda q, m: (0, 0, 0, 0, 0)),
            scratch_shapes=[
                *x_scratch,
                pltpu.VMEM((kvh, part, hd), jnp.bfloat16),
                pltpu.VMEM((kvh * per, part), jnp.float32),
                pltpu.VMEM((kvh, n * per, part), jnp.bfloat16),
                pltpu.SemaphoreType.DMA((ntp, 4)),
                pltpu.SemaphoreType.DMA,
            ],
        ),
        out_shape=jax.ShapeDtypeStruct((n // 2, 2, kvh, per, hd), jnp.bfloat16),
        compiler_params=pltpu.CompilerParams(vmem_limit_bytes=56 * MIB),
        name="weighted_values",
    )(meta, *x_parts, weight_near, weight_rest, rowof, values)

    halves = [list(range(n // 2)), list(range(n // 2, n))]
    term_parts = lax.all_to_all(
        terms, "pool", 0, 0, axis_index_groups=halves, tiled=True
    )
    pair_shape = (2, kvh, per, hd)
    send, held = pl.pallas_call(
        half_sum_kernel,
        in_specs=[pl.BlockSpec(memory_space=pltpu.SMEM), in_vmem, in_vmem],
        out_shape=[
            jax.ShapeDtypeStruct(pair_shape, jnp.bfloat16),
            jax.ShapeDtypeStruct(pair_shape, jnp.float32),
        ],
        compiler_params=pltpu.CompilerParams(vmem_limit_bytes=8 * MIB),
        name="half_pool_sum",
    )((me // (n // 2)).reshape(1), term_parts, kept)
    attended = pl.pallas_call(
        whole_sum_kernel,
        out_shape=jax.ShapeDtypeStruct((2 * rows, heads * hd), jnp.bfloat16),
        scratch_shapes=[pltpu.VMEM(pair_shape, jnp.float32)],
        compiler_params=pltpu.CompilerParams(vmem_limit_bytes=8 * MIB),
        name="attended_sum",
    )(held, with_partner(send, n // 2, n))

    everyone = [attended] + [with_partner(attended, k, n) for k in range(1, n // 2)]
    product = jnp.dot(
        jnp.concatenate(everyone), out_weight, preferred_element_type=jnp.float32
    )
    cols = out_weight.shape[1] // ntp
    half_spec = pl.BlockSpec((n * rows, cols), lambda i, m: (0, 0))
    own = lax.dynamic_slice_in_dim(product, core * cols, cols, 1)
    away = lax.dynamic_slice_in_dim(product, (1 - core) * cols, cols, 1)
    got = lax.ppermute(away, "tp", swap)
    return pl.pallas_call(
        functools.partial(order_kernel, n),
        grid_spec=pltpu.PrefetchScalarGridSpec(
            num_scalar_prefetch=1,
            grid=(1,),
            in_specs=[half_spec] * 2,
            out_specs=half_spec,
        ),
        out_shape=jax.ShapeDtypeStruct((n * rows, cols), jnp.bfloat16),
        compiler_params=pltpu.CompilerParams(vmem_limit_bytes=4 * MIB),
        name="order_rows",
    )(me.reshape(1), own, got)


def solution(mesh):
    in_specs = (
        P(("groups", "pool"), None),
        P("pool", "tp", None),
        P("groups", None),
        P("groups"),
        P("groups"),
        P(("groups", "pool"), "tp", None),
        P(("groups", "pool"), None, "tp", None),
        P(("groups", "pool")),
        P("tp", "pool"),
    )
    out_specs = P("groups", ("pool", "tp"))
    return jax.shard_map(local, mesh=mesh, in_specs=in_specs, out_specs=out_specs, check_vma=False)
```

```python
import functools

import jax
import jax.numpy as jnp
from jax import lax
from jax.experimental import pallas as pl
from jax.experimental.pallas import tpu as pltpu
from jax.sharding import PartitionSpec as P

BLK = 8
MIB = 1 << 20


def pack_kernel(base, at_ref, fill_ref, dest_ref, x_ref, out_ref, packed, count, out_sem):
    n, size, part = packed.shape
    tokens = x_ref.shape[0]
    blocks = tokens // BLK

    def store(q):
        return pltpu.make_async_copy(packed.at[q], out_ref.at[q], out_sem.at[q])

    first = at_ref[0] * blocks
    for q in range(n):
        count[q] = 0

    @pl.loop(0, blocks)
    def _(b):
        owner = dest_ref[first + b]
        count[owner] = count[owner] + fill_ref[first + b]

    def starts(q, total):
        here = count[q]
        count[q] = total
        return total + here

    lax.fori_loop(0, n, starts, jnp.int32(0))
    token = lax.broadcasted_iota(jnp.int32, (1, tokens), 1)

    def place(b, ranks):
        owner = dest_ref[first + b]
        fill = fill_ref[first + b]
        start = count[owner]
        count[owner] = start + fill
        inner = token - b * BLK
        return jnp.where((inner >= 0) & (inner < fill), start + inner, ranks)

    ranks = lax.fori_loop(0, blocks, place, jnp.full((1, tokens), -1, jnp.int32))
    wanted = base + at_ref[1] * size + lax.broadcasted_iota(jnp.int32, (size, tokens), 0)
    pick = (wanted == ranks).astype(jnp.bfloat16)
    for q in range(n):
        packed[q] = jnp.dot(
            pick, x_ref[:, q * part : (q + 1) * part], preferred_element_type=jnp.float32
        ).astype(packed.dtype)
        store(q).start()
    for q in range(n):
        store(q).wait()


def pack(x_prompt, fill, dest, at, n, base, size):
    tokens, width = x_prompt.shape
    part = width // n
    return pl.pallas_call(
        functools.partial(pack_kernel, base),
        grid_spec=pltpu.PrefetchScalarGridSpec(
            num_scalar_prefetch=3,
            grid=(1,),
            in_specs=[pl.BlockSpec(memory_space=pltpu.VMEM)],
            out_specs=pl.BlockSpec(memory_space=pl.ANY),
            scratch_shapes=[
                pltpu.VMEM((n, size, part), jnp.bfloat16),
                pltpu.SMEM((n,), jnp.int32),
                pltpu.SemaphoreType.DMA((n,)),
            ],
        ),
        out_shape=jax.ShapeDtypeStruct((n, size, part), jnp.bfloat16),
        compiler_params=pltpu.CompilerParams(vmem_limit_bytes=16 * MIB),
        cost_estimate=pl.CostEstimate(
            flops=2 * size * tokens * width, bytes_accessed=64 * MIB, transcendentals=0
        ),
        name="pack_live_tokens",
    )(at, fill, dest, x_prompt)


def tile_cuts(lanes):
    return [0] + list(range(min(256, lanes), lanes, 128)) + [lanes]


def near_lanes(lanes):
    return min(lanes, -(-lanes * 3 // 5 // 128) * 128)


def widen(core, n, refs, wide, base, first, last):
    length = refs[0].shape[0] // n
    tokens = wide.shape[0] // n

    @pl.loop(first, last)
    def _(s):
        for j, ref in enumerate(refs):
            side = core if j == 0 else 1 - core
            to = pl.multiple_of(s * tokens + base + side * length, BLK)
            wide[pl.ds(to, length), :] = ref[
                pl.ds(pl.multiple_of(s * length, length), length), :
            ].astype(wide.dtype)


def span_copies(refs, buffer, sem):
    cuts = sem.shape[1]
    span = buffer.shape[1] // cuts
    return [
        [
            pltpu.make_async_copy(
                ref.at[pl.ds(i * span, span)], buffer.at[j, pl.ds(i * span, span)], sem.at[j, i]
            )
            for j, ref in enumerate(refs)
        ]
        for i in range(cuts)
    ]


def widen_rest(core, over, n, refs, more, wide, sem):
    @pl.when(over != 0)
    def _():
        rest = span_copies(refs, more, sem)
        for pair in rest:
            for copy in pair:
                copy.start()
        for pair in rest:
            for copy in pair:
                copy.wait()
        base = wide.shape[0] // n - 2 * more.shape[1] // n
        widen(core, n, [more.at[0], more.at[1]], wide, base, 0, n)


def list_tile(meta_ref, first, count, wide, tile):
    for i in range(0, count, 2):
        pair = [
            wide[pl.ds(pl.multiple_of(meta_ref[first + i + j], BLK), BLK), :] for j in range(2)
        ]
        tile[i * BLK : (i + 2) * BLK, :] = jnp.concatenate(pair).astype(tile.dtype)
    return tile[: count * BLK, :]


def score_kernel(n, rows, meta_ref, *refs):
    x_refs, keyed_refs, (row_ref, near_ref, rest_ref) = refs[:4], refs[4:6], refs[6:9]
    more, wide, tile, keyed, sem, keyed_sem = refs[9:]
    step = pl.program_id(0)
    part = wide.shape[1]
    near = near_ref.shape[2]
    lanes = near + rest_ref.shape[2]
    cuts = tile_cuts(lanes)
    groups = lanes // BLK
    at_size = n * groups
    q = meta_ref[at_size + n] ^ reversed_bits(step, n)
    kvh, per = keyed.shape[0], keyed.shape[1] // n
    group = per // rows

    def load(i):
        span = n // 2 * per
        return [
            pltpu.make_async_copy(
                keyed_refs[i].at[h], keyed.at[h, pl.ds(i * span, span)], keyed_sem.at[i, h]
            )
            for h in range(kvh)
        ]

    @pl.when(step == 0)
    def _():
        for i in range(2):
            for copy in load(i):
                copy.start()
        core = meta_ref[at_size + n + 1]
        widen(core, n, x_refs[:2], wide, 0, 0, n)
        widen_rest(core, meta_ref[at_size + n + 2], n, x_refs[2:], more, wide, sem)

    for i in range(2):

        @pl.when(step == i * (n // 2))
        def _(i=i):
            for copy in load(i):
                copy.wait()

    def one(t):
        here = slice(cuts[t], cuts[t + 1])
        count = (cuts[t + 1] - cuts[t]) // BLK
        raw = lax.dot_general(
            keyed[:, pl.ds(pl.multiple_of(step * per, per), per), :].reshape(kvh * per, part),
            list_tile(meta_ref, q * groups + cuts[t] // BLK, count, wide, tile),
            (((1,), (1,)), ((), ())),
            preferred_element_type=jnp.float32,
        ).reshape(kvh, rows, group, count * BLK)
        owner_row = row_ref[0, :, here]
        picked = jnp.zeros((kvh, group, count * BLK), jnp.float32)
        for r in range(rows):
            picked = picked + jnp.where((owner_row == r)[None], raw[:, r], 0.0)
        picked = picked.reshape(kvh * group, -1).astype(near_ref.dtype)
        if cuts[t] < near:
            near_ref[0, :, here] = picked
        else:
            rest_ref[0, :, cuts[t] - near : cuts[t + 1] - near] = picked

    one(0)
    for t in range(1, len(cuts) - 1):
        pl.when(meta_ref[at_size + q] > cuts[t])(functools.partial(one, t))


def weight_kernel(scale, count, *refs):
    part_refs, row_refs = refs[:count], refs[count : 2 * count]
    top_ref, sum_ref = refs[2 * count : 2 * count + 2]
    w_refs, share_ref = refs[2 * count + 2 : -1], refs[-1]
    n = part_refs[0].shape[0]
    scores, owner_rows = [], []
    for part_ref, row_ref in zip(part_refs, row_refs):
        got = part_ref[0].astype(jnp.float32)
        for i in range(1, n):
            got = got + part_ref[i].astype(jnp.float32)
        scores.append(got * scale)
        owner_rows.append(row_ref[...])
    weights = [jnp.zeros(s.shape, jnp.float32) for s in scores]
    for r in range(top_ref.shape[0]):
        own = [jnp.where(o == r, s, -jnp.inf) for o, s in zip(owner_rows, scores)]
        cache_top = top_ref[r]
        top = cache_top
        for o in own:
            top = jnp.maximum(top, jnp.max(o, 1, keepdims=True))
        held = [jnp.exp(o - top) for o in own]
        fade = jnp.exp(cache_top - top)
        total = sum_ref[r] * fade
        for h in held:
            total = total + jnp.sum(h, 1, keepdims=True)
        weights = [w + h / total for w, h in zip(weights, held)]
        share_ref[r] = fade / total
    for w, w_ref in zip(weights, w_refs):
        for i in range(n):
            w_ref[i] = w.astype(w_ref.dtype)


def value_kernel(n, rows, meta_ref, *refs):
    x_refs, (near_ref, rest_ref, row_ref, value_ref, out_ref) = refs[:4], refs[4:9]
    held, more, wide, tile, values, acc, mixed, sem, value_sem = refs[9:]
    q = pl.program_id(0)
    kvh = values.shape[0]
    load_values = pltpu.make_async_copy(value_ref, values, value_sem)
    _, heads, near = near_ref.shape
    lanes = near + rest_ref.shape[2]
    per = rows * heads // kvh
    cuts = tile_cuts(lanes)
    groups = lanes // BLK
    at_size = n * groups

    @pl.when(q == 0)
    def _():
        core = meta_ref[at_size + n + 1]
        main = span_copies(x_refs[:2], held, sem)
        for pair in main:
            for copy in pair:
                copy.start()
        load_values.start()
        for i, pair in enumerate(main):
            for copy in pair:
                copy.wait()
            parts = [held.at[0], held.at[1]]
            widen(core, n, parts, wide, 0, i * n // len(main), (i + 1) * n // len(main))
        widen_rest(core, meta_ref[at_size + n + 2], n, x_refs[2:], more, wide, sem)

    def one(t):
        here = slice(cuts[t], cuts[t + 1])
        width = cuts[t + 1] - cuts[t]
        if cuts[t] < near:
            weights = near_ref[0, :, here]
        else:
            weights = rest_ref[0, :, cuts[t] - near : cuts[t + 1] - near]
        weights = weights.astype(jnp.float32).reshape(kvh, 1, heads // kvh, width)
        owner_row = row_ref[0, :, here]
        spread = jnp.concatenate(
            [jnp.where((owner_row == r)[None, None], weights, 0.0) for r in range(rows)], 1
        ).reshape(kvh * per, width)
        got = jnp.dot(
            spread.astype(jnp.bfloat16),
            list_tile(meta_ref, q * groups + cuts[t] // BLK, width // BLK, wide, tile),
            preferred_element_type=jnp.float32,
        )
        if t:
            acc[...] += got
        else:
            acc[...] = got

    one(0)
    for t in range(1, len(cuts) - 1):
        pl.when(meta_ref[at_size + q] > cuts[t])(functools.partial(one, t))
    for h in range(kvh):
        mixed[h, pl.ds(pl.multiple_of(q * per, per), per), :] = acc[
            h * per : (h + 1) * per, :
        ].astype(mixed.dtype)

    @pl.when(q == n - 1)
    def _():
        load_values.wait()
        for h in range(kvh):
            done = jnp.dot(mixed[h], values[h], preferred_element_type=jnp.float32)
            done = done.reshape(2, n // 2, per, done.shape[1]).astype(out_ref.dtype)
            for side in range(2):
                out_ref[:, side, h] = done[side]


def half_sum_kernel(side_ref, parts_ref, kept_ref, send_ref, mine_ref):
    half, sides, kvh, per, hd = parts_ref.shape
    rows, heads = kept_ref.shape[:2]
    group = heads // kvh
    for side in range(sides):
        own = side_ref[0] == side
        for h in range(kvh):
            terms = parts_ref[0, side, h].astype(jnp.float32)
            for i in range(1, half):
                terms = terms + parts_ref[i, side, h].astype(jnp.float32)
            kept = jnp.concatenate(
                [kept_ref[r, h * group : (h + 1) * group, :] for r in range(rows)]
            )
            terms = terms + jnp.where(own, kept, 0.0)
            mine_ref[side, h] = terms
            send_ref[side, h] = terms.astype(send_ref.dtype)


def whole_sum_kernel(mine_ref, got_ref, out_ref, total):
    sides, kvh, per, _ = mine_ref.shape
    rows = out_ref.shape[0] // sides
    group = per // rows
    total[...] = mine_ref[...] + got_ref[...].astype(jnp.float32)
    for h in range(kvh):
        for g in range(group):
            column = [
                total[side, h, pl.ds(g, rows, stride=group), :] for side in range(sides)
            ]
            head = h * group + g
            hd = column[0].shape[1]
            out_ref[:, head * hd : (head + 1) * hd] = jnp.concatenate(column).astype(
                out_ref.dtype
            )


def order_kernel(n, me_ref, own_ref, got_ref, out_ref):
    half = n // 2
    rows = own_ref.shape[0] // n
    for q in range(0, n, 2):
        pair = []
        for owner in (q, q + 1):
            block = ((me_ref[0] % half) ^ (owner % half)) * 2 + owner // half
            here = pl.ds(pl.multiple_of(block * rows, rows), rows)
            pair.append(own_ref[here, :] + got_ref[here, :])
        out_ref[q * rows : (q + 2) * rows, :] = jnp.concatenate(pair).astype(out_ref.dtype)


def with_partner(x, k, n):
    return lax.ppermute(x, "pool", [(i, i ^ k) for i in range(n)])


def from_rest(held, n):
    k = n // 4
    while k >= 2:
        held = jnp.concatenate([held, with_partner(held, k, n)])
        k //= 2
    return held


def reversed_bits(k, n):
    out, bit = 0, 1
    while bit < n:
        out = out + (k // bit) % 2 * (n // 2 // bit)
        bit *= 2
    return out


def local(
    x_prompt, kv_weight, block_dest, block_row, block_fill, queries, kv_cache, cache_len, out_weight
):
    n = lax.axis_size("pool")
    ntp = lax.axis_size("tp")
    me = lax.axis_index("pool").astype(jnp.int32)
    core = lax.axis_index("tp").astype(jnp.int32)
    tokens, width = x_prompt.shape
    part = width // n
    kvh = kv_weight.shape[1]
    hd = kv_weight.shape[2] // 2
    rows, heads = queries.shape[0], queries.shape[1]
    group = heads // kvh
    per = rows * group
    cache_slots = kv_cache.shape[1]
    blocks = tokens // BLK
    cap = max(2, 2 * blocks // n)
    window = cap * BLK + BLK
    lanes = -(-n * window // 128) * 128
    half = tokens // ntp
    scale = 1.0 / hd**0.5
    swap = [(i, (i + 1) % ntp) for i in range(ntp)]

    size = half * 3 // 4
    extra = half - size
    at = jnp.stack([me, core])
    pack_fill, pack_dest = block_fill, block_dest[:, 0]
    packed = pack(x_prompt, pack_fill, pack_dest, at, n, 0, size)
    dest = pack_dest
    even = from_rest(jnp.stack([queries, with_partner(queries, n // 2, n)]), n)
    packed, even, dest, block_row, block_fill, kv_weight = lax.optimization_barrier(
        (packed, even, dest, block_row, block_fill, kv_weight)
    )
    mine = lax.all_to_all(packed, "pool", 0, 0, tiled=True).reshape(n * size, part)

    index = jnp.arange(n * blocks, dtype=jnp.int32)
    sender = index // blocks
    kin = sender[None, :] == sender[:, None]
    lower = kin & (dest[None, :] < dest[:, None])
    level = kin & (dest[None, :] == dest[:, None]) & (index[None, :] < index[:, None])
    before = jnp.sum(jnp.where(lower, block_fill[None, :], 0), 1)
    within = jnp.sum(jnp.where(level, block_fill[None, :], 0), 1)
    pair = jnp.arange(n * n, dtype=jnp.int32)
    to, by = pair // n, pair % n
    owned = dest[None, :] == to[:, None]
    sent = sender[None, :] == by[:, None]
    earlier = sent & (dest[None, :] < to[:, None])
    offset = jnp.sum(jnp.where(earlier, block_fill[None, :], 0), 1)
    amount = jnp.sum(jnp.where(sent & owned, block_fill[None, :], 0), 1)
    runs = jnp.where(amount > 0, (offset % BLK + amount + BLK - 1) // BLK * BLK, 0)
    runs_by = runs.reshape(n, n)
    prior = jnp.arange(n)[:, None] < jnp.arange(n)[None, :]
    targets = jnp.sum(jnp.where(prior[None], runs_by[:, :, None], 0), 1)
    list_rows = jnp.sum(runs_by, 1)
    targets = targets.reshape(-1)
    sources = by * tokens + offset // BLK * BLK
    group_at = jnp.arange(n * lanes // BLK, dtype=jnp.int32) * BLK
    skip = group_at[:, None] - (to * lanes + targets)[None, :]
    group_rows = jnp.sum(
        jnp.where((skip >= 0) & (skip < runs[None, :]), sources[None, :] + skip, 0), 1
    )
    mine_pair = (dest * n + sender)[:, None] == pair[None, :]
    start = (
        dest * lanes
        + jnp.sum(jnp.where(mine_pair, targets[None, :], 0), 1)
        + before % BLK
        + within
    )
    spot = jnp.arange(n * lanes, dtype=jnp.int32)[:, None]
    inside = (spot >= start[None, :]) & (spot < (start + block_fill)[None, :])
    rowof = jnp.sum(jnp.where(inside, (block_row + 1)[None, :], 0), 1) - 1
    rowof = rowof.reshape(n, 1, lanes)

    near = near_lanes(lanes)
    most = jnp.stack([jnp.max(jnp.sum(block_fill.reshape(n, blocks), 1)), jnp.max(list_rows)])
    groups = lax.axis_size("groups")
    k = 1
    while k < groups:
        most = jnp.maximum(
            most, lax.ppermute(most, "groups", [(i, i ^ k) for i in range(groups)])
        )
        k *= 2
    over, longer = most[0] > ntp * size, most[1] > near

    def exchange_rest():
        rest = pack(x_prompt, pack_fill, pack_dest, at, n, ntp * size, extra)
        rest = lax.all_to_all(rest, "pool", 0, 0, tiled=True).reshape(n * extra, part)
        return rest, lax.ppermute(rest, "tp", swap)

    def no_rest():
        return (jnp.zeros((n * extra, part), jnp.bfloat16),) * 2

    more_mine, more_other = lax.cond(over, exchange_rest, no_rest)
    meta = jnp.concatenate(
        [group_rows, list_rows, jnp.stack([me, core, over.astype(jnp.int32)])]
    )

    keys = kv_weight[:, :, :hd]

    def through_keys(held):
        held = held.reshape(n // 2, rows, kvh, group, hd)
        return (
            jnp.einsum("qrhgd,phd->hqrgp", held, keys, preferred_element_type=jnp.float32)
            .astype(jnp.bfloat16)
            .reshape(kvh, n // 2 * per, part)
        )

    keyed_even = through_keys(even)
    keyed_odd = through_keys(with_partner(even, 1, n))
    values = kv_weight[:, :, hd:].transpose(1, 0, 2)

    mine, meta, rowof, keyed_even, keyed_odd, values = lax.optimization_barrier(
        (mine, meta, rowof, keyed_even, keyed_odd, values)
    )
    other = lax.ppermute(mine, "tp", swap)

    in_hbm = pl.BlockSpec(memory_space=pltpu.HBM)
    row_spec = pl.BlockSpec((1, 1, lanes), lambda q, m: (q, 0, 0))
    slot_specs = [
        pl.BlockSpec((1, heads, length), lambda q, m: (q, 0, 0)) for length in (near, lanes - near)
    ]
    slot_shapes = [
        jax.ShapeDtypeStruct((n, heads, length), jnp.bfloat16) for length in (near, lanes - near)
    ]
    in_vmem = pl.BlockSpec(memory_space=pltpu.VMEM)
    x_parts = (mine, other, more_mine, more_other)
    x_scratch = [
        pltpu.VMEM((ntp, n * extra, part), jnp.bfloat16),
        pltpu.VMEM((n * tokens, part), jnp.float32),
        pltpu.VMEM((tile_cuts(lanes)[1], part), jnp.bfloat16),
    ]
    at_me = n * lanes // BLK + n

    def owner(i, m):
        return m[at_me] ^ reversed_bits(i, n)

    score_near, score_rest = pl.pallas_call(
        functools.partial(score_kernel, n, rows),
        grid_spec=pltpu.PrefetchScalarGridSpec(
            num_scalar_prefetch=1,
            grid=(n,),
            in_specs=[
                *[in_vmem] * 2,
                *[in_hbm] * 4,
                pl.BlockSpec((1, 1, lanes), lambda i, m: (owner(i, m), 0, 0)),
            ],
            out_specs=[
                pl.BlockSpec((1, heads, length), lambda i, m: (owner(i, m), 0, 0))
                for length in (near, lanes - near)
            ],
            scratch_shapes=[
                *x_scratch,
                pltpu.VMEM((kvh, n * per, part), jnp.bfloat16),
                pltpu.SemaphoreType.DMA((ntp, 4)),
                pltpu.SemaphoreType.DMA((2, kvh)),
            ],
        ),
        out_shape=slot_shapes,
        compiler_params=pltpu.CompilerParams(vmem_limit_bytes=20 * MIB),
        name="prompt_scores",
    )(meta, *x_parts, keyed_even, keyed_odd, rowof)

    my_rows = lax.dynamic_index_in_dim(rowof, me, 0, keepdims=False)

    def exchange_weights(*scores):
        count = len(scores)
        parts = [lax.all_to_all(s, "pool", 0, 0, tiled=True) for s in scores]
        query = queries.reshape(rows, kvh, group, hd)
        cache_scores = (
            jnp.einsum(
                "rhgd,rthd->rhgt", query, kv_cache[:, :, :, :hd], preferred_element_type=jnp.float32
            )
            * scale
        )
        cache_live = jnp.arange(cache_slots, dtype=jnp.int32)[None, :] < cache_len[:, None]
        cache_scores = jnp.where(cache_live[:, None, None, :], cache_scores, -jnp.inf)
        cache_top = jnp.max(cache_scores, -1, keepdims=True)
        cache_exp = jnp.exp(cache_scores - cache_top)
        cache_sum = jnp.sum(cache_exp, -1, keepdims=True)
        row_parts = [my_rows[:, :near], my_rows[:, near:]][:count]
        *weights, share = pl.pallas_call(
            functools.partial(weight_kernel, scale, count),
            out_shape=[*slot_shapes[:count], jax.ShapeDtypeStruct((rows, heads, 1), jnp.float32)],
            compiler_params=pltpu.CompilerParams(vmem_limit_bytes=8 * MIB),
            name="softmax_weights",
        )(
            *parts,
            *row_parts,
            cache_top.reshape(rows, heads, 1),
            cache_sum.reshape(rows, heads, 1),
        )
        weights = [lax.all_to_all(w, "pool", 0, 0, tiled=True) for w in weights]
        cached = jnp.einsum(
            "rhgt,rthd->rhgd",
            cache_exp.astype(jnp.bfloat16),
            kv_cache[:, :, :, hd:],
            preferred_element_type=jnp.float32,
        )
        return *weights, cached.reshape(rows, heads, hd) * share

    def near_only():
        weights, kept = exchange_weights(score_near)
        return weights, jnp.zeros(slot_shapes[1].shape, jnp.bfloat16), kept

    weight_near, weight_rest, kept = lax.cond(
        longer, lambda: exchange_weights(score_near, score_rest), near_only
    )
    terms = pl.pallas_call(
        functools.partial(value_kernel, n, rows),
        grid_spec=pltpu.PrefetchScalarGridSpec(
            num_scalar_prefetch=1,
            grid=(n,),
            in_specs=[*[in_hbm] * 4, *slot_specs, row_spec, in_hbm],
            out_specs=pl.BlockSpec((n // 2, 2, kvh, per, hd), lambda q, m: (0, 0, 0, 0, 0)),
            scratch_shapes=[
                pltpu.VMEM((ntp, n * size, part), jnp.bfloat16),
                *x_scratch,
                pltpu.VMEM((kvh, part, hd), jnp.bfloat16),
                pltpu.VMEM((kvh * per, part), jnp.float32),
                pltpu.VMEM((kvh, n * per, part), jnp.bfloat16),
                pltpu.SemaphoreType.DMA((ntp, 4)),
                pltpu.SemaphoreType.DMA,
            ],
        ),
        out_shape=jax.ShapeDtypeStruct((n // 2, 2, kvh, per, hd), jnp.bfloat16),
        compiler_params=pltpu.CompilerParams(vmem_limit_bytes=56 * MIB),
        name="weighted_values",
    )(meta, *x_parts, weight_near, weight_rest, rowof, values)

    halves = [list(range(n // 2)), list(range(n // 2, n))]
    term_parts = lax.all_to_all(
        terms, "pool", 0, 0, axis_index_groups=halves, tiled=True
    )
    pair_shape = (2, kvh, per, hd)
    send, held = pl.pallas_call(
        half_sum_kernel,
        in_specs=[pl.BlockSpec(memory_space=pltpu.SMEM), in_vmem, in_vmem],
        out_shape=[
            jax.ShapeDtypeStruct(pair_shape, jnp.bfloat16),
            jax.ShapeDtypeStruct(pair_shape, jnp.float32),
        ],
        compiler_params=pltpu.CompilerParams(vmem_limit_bytes=8 * MIB),
        name="half_pool_sum",
    )((me // (n // 2)).reshape(1), term_parts, kept)
    attended = pl.pallas_call(
        whole_sum_kernel,
        out_shape=jax.ShapeDtypeStruct((2 * rows, heads * hd), jnp.bfloat16),
        scratch_shapes=[pltpu.VMEM(pair_shape, jnp.float32)],
        compiler_params=pltpu.CompilerParams(vmem_limit_bytes=8 * MIB),
        name="attended_sum",
    )(held, with_partner(send, n // 2, n))

    everyone = [attended] + [with_partner(attended, k, n) for k in range(1, n // 2)]
    product = jnp.dot(
        jnp.concatenate(everyone), out_weight, preferred_element_type=jnp.float32
    )
    cols = out_weight.shape[1] // ntp
    half_spec = pl.BlockSpec((n * rows, cols), lambda i, m: (0, 0))
    own = lax.dynamic_slice_in_dim(product, core * cols, cols, 1)
    away = lax.dynamic_slice_in_dim(product, (1 - core) * cols, cols, 1)
    got = lax.ppermute(away, "tp", swap)
    return pl.pallas_call(
        functools.partial(order_kernel, n),
        grid_spec=pltpu.PrefetchScalarGridSpec(
            num_scalar_prefetch=1,
            grid=(1,),
            in_specs=[half_spec] * 2,
            out_specs=half_spec,
        ),
        out_shape=jax.ShapeDtypeStruct((n * rows, cols), jnp.bfloat16),
        compiler_params=pltpu.CompilerParams(vmem_limit_bytes=4 * MIB),
        name="order_rows",
    )(me.reshape(1), own, got)


def solution(mesh):
    in_specs = (
        P(("groups", "pool"), None),
        P("pool", "tp", None),
        P("groups", None),
        P("groups"),
        P("groups"),
        P(("groups", "pool"), "tp", None),
        P(("groups", "pool"), None, "tp", None),
        P(("groups", "pool")),
        P("tp", "pool"),
    )
    out_specs = P("groups", ("pool", "tp"))
    return jax.shard_map(local, mesh=mesh, in_specs=in_specs, out_specs=out_specs, check_vma=False)
```

```python
import functools

import jax
import jax.numpy as jnp
from jax import lax
from jax.experimental import pallas as pl
from jax.experimental.pallas import tpu as pltpu
from jax.sharding import PartitionSpec as P

BLK = 8
MIB = 1 << 20


def pack_kernel(base, at_ref, fill_ref, dest_ref, x_ref, out_ref, packed, count, out_sem):
    n, size, part = packed.shape
    tokens = x_ref.shape[0]
    blocks = tokens // BLK

    def store(q):
        return pltpu.make_async_copy(packed.at[q], out_ref.at[q], out_sem.at[q])

    first = at_ref[0] * blocks
    for q in range(n):
        count[q] = 0

    @pl.loop(0, blocks)
    def _(b):
        owner = dest_ref[first + b]
        count[owner] = count[owner] + fill_ref[first + b]

    def starts(q, total):
        here = count[q]
        count[q] = total
        return total + here

    lax.fori_loop(0, n, starts, jnp.int32(0))
    token = lax.broadcasted_iota(jnp.int32, (1, tokens), 1)

    def place(b, ranks):
        owner = dest_ref[first + b]
        fill = fill_ref[first + b]
        start = count[owner]
        count[owner] = start + fill
        inner = token - b * BLK
        return jnp.where((inner >= 0) & (inner < fill), start + inner, ranks)

    ranks = lax.fori_loop(0, blocks, place, jnp.full((1, tokens), -1, jnp.int32))
    wanted = base + at_ref[1] * size + lax.broadcasted_iota(jnp.int32, (size, tokens), 0)
    pick = (wanted == ranks).astype(jnp.bfloat16)
    for q in range(n):
        packed[q] = jnp.dot(
            pick, x_ref[:, q * part : (q + 1) * part], preferred_element_type=jnp.float32
        ).astype(packed.dtype)
        store(q).start()
    for q in range(n):
        store(q).wait()


def pack(x_prompt, fill, dest, at, n, base, size):
    tokens, width = x_prompt.shape
    part = width // n
    return pl.pallas_call(
        functools.partial(pack_kernel, base),
        grid_spec=pltpu.PrefetchScalarGridSpec(
            num_scalar_prefetch=3,
            grid=(1,),
            in_specs=[pl.BlockSpec(memory_space=pltpu.VMEM)],
            out_specs=pl.BlockSpec(memory_space=pl.ANY),
            scratch_shapes=[
                pltpu.VMEM((n, size, part), jnp.bfloat16),
                pltpu.SMEM((n,), jnp.int32),
                pltpu.SemaphoreType.DMA((n,)),
            ],
        ),
        out_shape=jax.ShapeDtypeStruct((n, size, part), jnp.bfloat16),
        compiler_params=pltpu.CompilerParams(vmem_limit_bytes=16 * MIB),
        cost_estimate=pl.CostEstimate(
            flops=2 * size * tokens * width, bytes_accessed=64 * MIB, transcendentals=0
        ),
        name="pack_live_tokens",
    )(at, fill, dest, x_prompt)


def tile_cuts(lanes):
    return [0] + list(range(min(256, lanes), lanes, 128)) + [lanes]


def near_lanes(lanes):
    return min(lanes, -(-lanes * 3 // 5 // 128) * 128)


def widen(core, n, refs, wide, base, first, last):
    length = refs[0].shape[0] // n
    tokens = wide.shape[0] // n

    @pl.loop(first, last)
    def _(s):
        for j, ref in enumerate(refs):
            side = core if j == 0 else 1 - core
            to = pl.multiple_of(s * tokens + base + side * length, BLK)
            wide[pl.ds(to, length), :] = ref[
                pl.ds(pl.multiple_of(s * length, length), length), :
            ].astype(wide.dtype)


def span_copies(refs, buffer, sem):
    cuts = sem.shape[1]
    span = buffer.shape[1] // cuts
    return [
        [
            pltpu.make_async_copy(
                ref.at[pl.ds(i * span, span)], buffer.at[j, pl.ds(i * span, span)], sem.at[j, i]
            )
            for j, ref in enumerate(refs)
        ]
        for i in range(cuts)
    ]


def load_tokens(n, core, over, x_refs, held, more, wide, sem, others):
    main = span_copies(x_refs[:2], held, sem)
    for pair in main:
        for copy in pair:
            copy.start()
    for copy in others:
        copy.start()
    for i, pair in enumerate(main):
        for copy in pair:
            copy.wait()
        parts = [held.at[0], held.at[1]]
        widen(core, n, parts, wide, 0, i * n // len(main), (i + 1) * n // len(main))

    @pl.when(over != 0)
    def _():
        rest = span_copies(x_refs[2:], more, sem)
        for pair in rest:
            for copy in pair:
                copy.start()
        for pair in rest:
            for copy in pair:
                copy.wait()
        base = wide.shape[0] // n - 2 * more.shape[1] // n
        widen(core, n, [more.at[0], more.at[1]], wide, base, 0, n)


def list_tile(meta_ref, first, count, wide, tile):
    for i in range(0, count, 2):
        pair = [
            wide[pl.ds(pl.multiple_of(meta_ref[first + i + j], BLK), BLK), :] for j in range(2)
        ]
        tile[i * BLK : (i + 2) * BLK, :] = jnp.concatenate(pair).astype(tile.dtype)
    return tile[: count * BLK, :]


def key_kernel(query_ref, weight_ref, out_ref):
    group = out_ref.shape[1] // query_ref.shape[0]
    hd = query_ref.shape[2]
    h = pl.program_id(0)
    for i in range(query_ref.shape[1] // group):

        @pl.when(h == i)
        def _(i=i):
            query = query_ref[:, i * group : (i + 1) * group, :].astype(jnp.float32)
            out_ref[0] = lax.dot_general(
                query.reshape(-1, hd).astype(jnp.bfloat16),
                weight_ref[0, :, :hd],
                (((1,), (1,)), ((), ())),
                preferred_element_type=jnp.float32,
            ).astype(out_ref.dtype)


def score_kernel(n, rows, meta_ref, *refs):
    x_refs, keyed_refs, (row_ref, near_ref, rest_ref) = refs[:4], refs[4:6], refs[6:9]
    held, more, wide, tile, keyed, sem, keyed_sem = refs[9:]
    step = pl.program_id(0)
    part = wide.shape[1]
    near = near_ref.shape[2]
    lanes = near + rest_ref.shape[2]
    cuts = tile_cuts(lanes)
    groups = lanes // BLK
    at_size = n * groups
    q = meta_ref[at_size + n] ^ reversed_bits(step, n)
    kvh, per = keyed.shape[0], keyed.shape[1] // n
    group = per // rows

    def load(i):
        span = n // 2 * per
        return [
            pltpu.make_async_copy(
                keyed_refs[i].at[h], keyed.at[h, pl.ds(i * span, span)], keyed_sem.at[i, h]
            )
            for h in range(kvh)
        ]

    @pl.when(step == 0)
    def _():
        load_tokens(
            n, meta_ref[at_size + n + 1], meta_ref[at_size + n + 2], x_refs, held, more, wide, sem,
            load(0) + load(1),
        )

    for i in range(2):

        @pl.when(step == i * (n // 2))
        def _(i=i):
            for copy in load(i):
                copy.wait()

    def one(t):
        here = slice(cuts[t], cuts[t + 1])
        count = (cuts[t + 1] - cuts[t]) // BLK
        raw = lax.dot_general(
            keyed[:, pl.ds(pl.multiple_of(step * per, per), per), :].reshape(kvh * per, part),
            list_tile(meta_ref, q * groups + cuts[t] // BLK, count, wide, tile),
            (((1,), (1,)), ((), ())),
            preferred_element_type=jnp.float32,
        ).reshape(kvh, rows, group, count * BLK)
        owner_row = row_ref[0, :, here]
        picked = jnp.zeros((kvh, group, count * BLK), jnp.float32)
        for r in range(rows):
            picked = picked + jnp.where((owner_row == r)[None], raw[:, r], 0.0)
        picked = picked.reshape(kvh * group, -1).astype(near_ref.dtype)
        if cuts[t] < near:
            near_ref[0, :, here] = picked
        else:
            rest_ref[0, :, cuts[t] - near : cuts[t + 1] - near] = picked

    one(0)
    for t in range(1, len(cuts) - 1):
        pl.when(meta_ref[at_size + q] > cuts[t])(functools.partial(one, t))


def weight_kernel(scale, count, *refs):
    part_refs, row_refs = refs[:count], refs[count : 2 * count]
    top_ref, sum_ref = refs[2 * count : 2 * count + 2]
    w_refs, share_ref = refs[2 * count + 2 : -1], refs[-1]
    n = part_refs[0].shape[0]
    scores, owner_rows = [], []
    for part_ref, row_ref in zip(part_refs, row_refs):
        got = part_ref[0].astype(jnp.float32)
        for i in range(1, n):
            got = got + part_ref[i].astype(jnp.float32)
        scores.append(got * scale)
        owner_rows.append(row_ref[...])
    weights = [jnp.zeros(s.shape, jnp.float32) for s in scores]
    for r in range(top_ref.shape[0]):
        own = [jnp.where(o == r, s, -jnp.inf) for o, s in zip(owner_rows, scores)]
        cache_top = top_ref[r]
        top = cache_top
        for o in own:
            top = jnp.maximum(top, jnp.max(o, 1, keepdims=True))
        held = [jnp.exp(o - top) for o in own]
        fade = jnp.exp(cache_top - top)
        total = sum_ref[r] * fade
        for h in held:
            total = total + jnp.sum(h, 1, keepdims=True)
        weights = [w + h / total for w, h in zip(weights, held)]
        share_ref[r] = fade / total
    for w, w_ref in zip(weights, w_refs):
        for i in range(n):
            w_ref[i] = w.astype(w_ref.dtype)


def value_kernel(n, rows, meta_ref, *refs):
    x_refs, (near_ref, rest_ref, row_ref, weight_ref, out_ref) = refs[:4], refs[4:9]
    held, more, wide, tile, values, acc, mixed, sem, value_sem = refs[9:]
    q = pl.program_id(0)
    kvh = values.shape[0]
    hd = values.shape[2]
    load_values = [
        pltpu.make_async_copy(
            weight_ref.at[h, :, pl.ds(hd, hd)], values.at[h], value_sem.at[h]
        )
        for h in range(kvh)
    ]
    _, heads, near = near_ref.shape
    lanes = near + rest_ref.shape[2]
    per = rows * heads // kvh
    cuts = tile_cuts(lanes)
    groups = lanes // BLK
    at_size = n * groups

    @pl.when(q == 0)
    def _():
        load_tokens(
            n, meta_ref[at_size + n + 1], meta_ref[at_size + n + 2], x_refs, held, more, wide, sem,
            load_values,
        )

    def one(t):
        here = slice(cuts[t], cuts[t + 1])
        width = cuts[t + 1] - cuts[t]
        if cuts[t] < near:
            weights = near_ref[0, :, here]
        else:
            weights = rest_ref[0, :, cuts[t] - near : cuts[t + 1] - near]
        weights = weights.astype(jnp.float32).reshape(kvh, 1, heads // kvh, width)
        owner_row = row_ref[0, :, here]
        spread = jnp.concatenate(
            [jnp.where((owner_row == r)[None, None], weights, 0.0) for r in range(rows)], 1
        ).reshape(kvh * per, width)
        got = jnp.dot(
            spread.astype(jnp.bfloat16),
            list_tile(meta_ref, q * groups + cuts[t] // BLK, width // BLK, wide, tile),
            preferred_element_type=jnp.float32,
        )
        if t:
            acc[...] += got
        else:
            acc[...] = got

    one(0)
    for t in range(1, len(cuts) - 1):
        pl.when(meta_ref[at_size + q] > cuts[t])(functools.partial(one, t))
    for h in range(kvh):
        mixed[h, pl.ds(pl.multiple_of(q * per, per), per), :] = acc[
            h * per : (h + 1) * per, :
        ].astype(mixed.dtype)

    @pl.when(q == n - 1)
    def _():
        for load in load_values:
            load.wait()
        for h in range(kvh):
            done = jnp.dot(mixed[h], values[h], preferred_element_type=jnp.float32)
            done = done.reshape(2, n // 2, per, done.shape[1]).astype(out_ref.dtype)
            for side in range(2):
                out_ref[:, side, h] = done[side]


def half_sum_kernel(side_ref, parts_ref, kept_ref, send_ref, mine_ref):
    half, sides, kvh, per, hd = parts_ref.shape
    rows, heads = kept_ref.shape[:2]
    group = heads // kvh
    for side in range(sides):
        own = side_ref[0] == side
        for h in range(kvh):
            terms = parts_ref[0, side, h].astype(jnp.float32)
            for i in range(1, half):
                terms = terms + parts_ref[i, side, h].astype(jnp.float32)
            kept = jnp.concatenate(
                [kept_ref[r, h * group : (h + 1) * group, :] for r in range(rows)]
            )
            terms = terms + jnp.where(own, kept, 0.0)
            mine_ref[side, h] = terms
            send_ref[side, h] = terms.astype(send_ref.dtype)


def whole_sum_kernel(mine_ref, got_ref, out_ref, total):
    sides, kvh, per, _ = mine_ref.shape
    rows = out_ref.shape[0] // sides
    group = per // rows
    total[...] = mine_ref[...] + got_ref[...].astype(jnp.float32)
    for h in range(kvh):
        for g in range(group):
            column = [
                total[side, h, pl.ds(g, rows, stride=group), :] for side in range(sides)
            ]
            head = h * group + g
            hd = column[0].shape[1]
            out_ref[:, head * hd : (head + 1) * hd] = jnp.concatenate(column).astype(
                out_ref.dtype
            )


def order_kernel(n, me_ref, own_ref, got_ref, out_ref):
    half = n // 2
    rows = own_ref.shape[0] // n
    for q in range(0, n, 2):
        pair = []
        for owner in (q, q + 1):
            block = ((me_ref[0] % half) ^ (owner % half)) * 2 + owner // half
            here = pl.ds(pl.multiple_of(block * rows, rows), rows)
            pair.append(own_ref[here, :] + got_ref[here, :])
        out_ref[q * rows : (q + 2) * rows, :] = jnp.concatenate(pair).astype(out_ref.dtype)


def with_partner(x, k, n):
    return lax.ppermute(x, "pool", [(i, i ^ k) for i in range(n)])


def from_rest(held, n):
    k = n // 4
    while k >= 2:
        held = jnp.concatenate([held, with_partner(held, k, n)])
        k //= 2
    return held


def reversed_bits(k, n):
    out, bit = 0, 1
    while bit < n:
        out = out + (k // bit) % 2 * (n // 2 // bit)
        bit *= 2
    return out


def local(
    x_prompt, kv_weight, block_dest, block_row, block_fill, queries, kv_cache, cache_len, out_weight
):
    n = lax.axis_size("pool")
    ntp = lax.axis_size("tp")
    me = lax.axis_index("pool").astype(jnp.int32)
    core = lax.axis_index("tp").astype(jnp.int32)
    tokens, width = x_prompt.shape
    part = width // n
    kvh = kv_weight.shape[1]
    hd = kv_weight.shape[2] // 2
    rows, heads = queries.shape[0], queries.shape[1]
    group = heads // kvh
    per = rows * group
    cache_slots = kv_cache.shape[1]
    blocks = tokens // BLK
    cap = max(2, 2 * blocks // n)
    window = cap * BLK + BLK
    lanes = -(-n * window // 128) * 128
    half = tokens // ntp
    scale = 1.0 / hd**0.5
    swap = [(i, (i + 1) % ntp) for i in range(ntp)]

    size = half * 3 // 4
    extra = half - size
    at = jnp.stack([me, core])
    pack_fill, pack_dest = block_fill, block_dest[:, 0]
    packed = pack(x_prompt, pack_fill, pack_dest, at, n, 0, size)
    dest = pack_dest
    far = with_partner(queries, n // 2, n)
    packed, far, dest, block_row, block_fill, kv_weight = lax.optimization_barrier(
        (packed, far, dest, block_row, block_fill, kv_weight)
    )
    kv_weight = kv_weight.transpose(1, 0, 2)
    even = from_rest(jnp.stack([queries, far]), n)
    packed, even = lax.optimization_barrier((packed, even))
    mine = lax.all_to_all(packed, "pool", 0, 0, tiled=True).reshape(n * size, part)

    index = jnp.arange(n * blocks, dtype=jnp.int32)
    sender = index // blocks
    kin = sender[None, :] == sender[:, None]
    lower = kin & (dest[None, :] < dest[:, None])
    level = kin & (dest[None, :] == dest[:, None]) & (index[None, :] < index[:, None])
    before = jnp.sum(jnp.where(lower, block_fill[None, :], 0), 1)
    within = jnp.sum(jnp.where(level, block_fill[None, :], 0), 1)
    pair = jnp.arange(n * n, dtype=jnp.int32)
    to, by = pair // n, pair % n
    owned = dest[None, :] == to[:, None]
    sent = sender[None, :] == by[:, None]
    earlier = sent & (dest[None, :] < to[:, None])
    offset = jnp.sum(jnp.where(earlier, block_fill[None, :], 0), 1)
    amount = jnp.sum(jnp.where(sent & owned, block_fill[None, :], 0), 1)
    runs = jnp.where(amount > 0, (offset % BLK + amount + BLK - 1) // BLK * BLK, 0)
    runs_by = runs.reshape(n, n)
    prior = jnp.arange(n)[:, None] < jnp.arange(n)[None, :]
    targets = jnp.sum(jnp.where(prior[None], runs_by[:, :, None], 0), 1)
    list_rows = jnp.sum(runs_by, 1)
    targets = targets.reshape(-1)
    sources = by * tokens + offset // BLK * BLK
    group_at = jnp.arange(n * lanes // BLK, dtype=jnp.int32) * BLK
    skip = group_at[:, None] - (to * lanes + targets)[None, :]
    group_rows = jnp.sum(
        jnp.where((skip >= 0) & (skip < runs[None, :]), sources[None, :] + skip, 0), 1
    )
    mine_pair = (dest * n + sender)[:, None] == pair[None, :]
    start = (
        dest * lanes
        + jnp.sum(jnp.where(mine_pair, targets[None, :], 0), 1)
        + before % BLK
        + within
    )
    spot = jnp.arange(n * lanes, dtype=jnp.int32)[:, None]
    inside = (spot >= start[None, :]) & (spot < (start + block_fill)[None, :])
    rowof = jnp.sum(jnp.where(inside, (block_row + 1)[None, :], 0), 1) - 1
    rowof = rowof.reshape(n, 1, lanes)

    near = near_lanes(lanes)
    most = jnp.stack([jnp.max(jnp.sum(block_fill.reshape(n, blocks), 1)), jnp.max(list_rows)])
    groups = lax.axis_size("groups")
    k = 1
    while k < groups:
        most = jnp.maximum(
            most, lax.ppermute(most, "groups", [(i, i ^ k) for i in range(groups)])
        )
        k *= 2
    over, longer = most[0] > ntp * size, most[1] > near

    def exchange_rest():
        rest = pack(x_prompt, pack_fill, pack_dest, at, n, ntp * size, extra)
        rest = lax.all_to_all(rest, "pool", 0, 0, tiled=True).reshape(n * extra, part)
        return rest, lax.ppermute(rest, "tp", swap)

    def no_rest():
        return (jnp.zeros((n * extra, part), jnp.bfloat16),) * 2

    more_mine, more_other = lax.cond(over, exchange_rest, no_rest)
    meta = jnp.concatenate(
        [group_rows, list_rows, jnp.stack([me, core, over.astype(jnp.int32)])]
    )

    def through_keys(held):
        held = held.reshape(n // 2 * rows, heads, hd)
        return pl.pallas_call(
            key_kernel,
            grid=(kvh,),
            in_specs=[
                pl.BlockSpec(held.shape, lambda h: (0, 0, 0)),
                pl.BlockSpec((1, part, 2 * hd), lambda h: (h, 0, 0)),
            ],
            out_specs=pl.BlockSpec((1, n // 2 * per, part), lambda h: (h, 0, 0)),
            out_shape=jax.ShapeDtypeStruct((kvh, n // 2 * per, part), jnp.bfloat16),
            compiler_params=pltpu.CompilerParams(vmem_limit_bytes=16 * MIB),
            cost_estimate=pl.CostEstimate(flops=0, bytes_accessed=1024, transcendentals=0),
            name="key_projection",
        )(held, kv_weight)

    keyed_even = through_keys(even)
    keyed_odd = through_keys(with_partner(even, 1, n))

    mine, meta, rowof, keyed_even, keyed_odd = lax.optimization_barrier(
        (mine, meta, rowof, keyed_even, keyed_odd)
    )
    other = lax.ppermute(mine, "tp", swap)

    in_hbm = pl.BlockSpec(memory_space=pltpu.HBM)
    row_spec = pl.BlockSpec((1, 1, lanes), lambda q, m: (q, 0, 0))
    slot_specs = [
        pl.BlockSpec((1, heads, length), lambda q, m: (q, 0, 0)) for length in (near, lanes - near)
    ]
    slot_shapes = [
        jax.ShapeDtypeStruct((n, heads, length), jnp.bfloat16) for length in (near, lanes - near)
    ]
    in_vmem = pl.BlockSpec(memory_space=pltpu.VMEM)
    x_parts = (mine, other, more_mine, more_other)
    x_scratch = [
        pltpu.VMEM((ntp, n * size, part), jnp.bfloat16),
        pltpu.VMEM((ntp, n * extra, part), jnp.bfloat16),
        pltpu.VMEM((n * tokens, part), jnp.float32),
        pltpu.VMEM((tile_cuts(lanes)[1], part), jnp.bfloat16),
    ]
    at_me = n * lanes // BLK + n

    def owner(i, m):
        return m[at_me] ^ reversed_bits(i, n)

    score_near, score_rest = pl.pallas_call(
        functools.partial(score_kernel, n, rows),
        grid_spec=pltpu.PrefetchScalarGridSpec(
            num_scalar_prefetch=1,
            grid=(n,),
            in_specs=[
                *[in_hbm] * 6,
                pl.BlockSpec((1, 1, lanes), lambda i, m: (owner(i, m), 0, 0)),
            ],
            out_specs=[
                pl.BlockSpec((1, heads, length), lambda i, m: (owner(i, m), 0, 0))
                for length in (near, lanes - near)
            ],
            scratch_shapes=[
                *x_scratch,
                pltpu.VMEM((kvh, n * per, part), jnp.bfloat16),
                pltpu.SemaphoreType.DMA((ntp, 4)),
                pltpu.SemaphoreType.DMA((2, kvh)),
            ],
        ),
        out_shape=slot_shapes,
        compiler_params=pltpu.CompilerParams(vmem_limit_bytes=24 * MIB),
        name="prompt_scores",
    )(meta, *x_parts, keyed_even, keyed_odd, rowof)

    my_rows = lax.dynamic_index_in_dim(rowof, me, 0, keepdims=False)

    def exchange_weights(*scores):
        count = len(scores)
        parts = [lax.all_to_all(s, "pool", 0, 0, tiled=True) for s in scores]
        query = queries.reshape(rows, kvh, group, hd)
        cache_scores = (
            jnp.einsum(
                "rhgd,rthd->rhgt", query, kv_cache[:, :, :, :hd], preferred_element_type=jnp.float32
            )
            * scale
        )
        cache_live = jnp.arange(cache_slots, dtype=jnp.int32)[None, :] < cache_len[:, None]
        cache_scores = jnp.where(cache_live[:, None, None, :], cache_scores, -jnp.inf)
        cache_top = jnp.max(cache_scores, -1, keepdims=True)
        cache_exp = jnp.exp(cache_scores - cache_top)
        cache_sum = jnp.sum(cache_exp, -1, keepdims=True)
        row_parts = [my_rows[:, :near], my_rows[:, near:]][:count]
        *weights, share = pl.pallas_call(
            functools.partial(weight_kernel, scale, count),
            out_shape=[*slot_shapes[:count], jax.ShapeDtypeStruct((rows, heads, 1), jnp.float32)],
            compiler_params=pltpu.CompilerParams(vmem_limit_bytes=8 * MIB),
            name="softmax_weights",
        )(
            *parts,
            *row_parts,
            cache_top.reshape(rows, heads, 1),
            cache_sum.reshape(rows, heads, 1),
        )
        weights = [lax.all_to_all(w, "pool", 0, 0, tiled=True) for w in weights]
        cached = jnp.einsum(
            "rhgt,rthd->rhgd",
            cache_exp.astype(jnp.bfloat16),
            kv_cache[:, :, :, hd:],
            preferred_element_type=jnp.float32,
        )
        return *weights, cached.reshape(rows, heads, hd) * share

    def near_only():
        weights, kept = exchange_weights(score_near)
        return weights, jnp.zeros(slot_shapes[1].shape, jnp.bfloat16), kept

    weight_near, weight_rest, kept = lax.cond(
        longer, lambda: exchange_weights(score_near, score_rest), near_only
    )
    terms = pl.pallas_call(
        functools.partial(value_kernel, n, rows),
        grid_spec=pltpu.PrefetchScalarGridSpec(
            num_scalar_prefetch=1,
            grid=(n,),
            in_specs=[*[in_hbm] * 4, *slot_specs, row_spec, in_hbm],
            out_specs=pl.BlockSpec((n // 2, 2, kvh, per, hd), lambda q, m: (0, 0, 0, 0, 0)),
            scratch_shapes=[
                *x_scratch,
                pltpu.VMEM((kvh, part, hd), jnp.bfloat16),
                pltpu.VMEM((kvh * per, part), jnp.float32),
                pltpu.VMEM((kvh, n * per, part), jnp.bfloat16),
                pltpu.SemaphoreType.DMA((ntp, 4)),
                pltpu.SemaphoreType.DMA((kvh,)),
            ],
        ),
        out_shape=jax.ShapeDtypeStruct((n // 2, 2, kvh, per, hd), jnp.bfloat16),
        compiler_params=pltpu.CompilerParams(vmem_limit_bytes=56 * MIB),
        name="weighted_values",
    )(meta, *x_parts, weight_near, weight_rest, rowof, kv_weight)

    halves = [list(range(n // 2)), list(range(n // 2, n))]
    term_parts = lax.all_to_all(
        terms, "pool", 0, 0, axis_index_groups=halves, tiled=True
    )
    pair_shape = (2, kvh, per, hd)
    send, held = pl.pallas_call(
        half_sum_kernel,
        in_specs=[pl.BlockSpec(memory_space=pltpu.SMEM), in_vmem, in_vmem],
        out_shape=[
            jax.ShapeDtypeStruct(pair_shape, jnp.bfloat16),
            jax.ShapeDtypeStruct(pair_shape, jnp.float32),
        ],
        compiler_params=pltpu.CompilerParams(vmem_limit_bytes=8 * MIB),
        name="half_pool_sum",
    )((me // (n // 2)).reshape(1), term_parts, kept)
    attended = pl.pallas_call(
        whole_sum_kernel,
        out_shape=jax.ShapeDtypeStruct((2 * rows, heads * hd), jnp.bfloat16),
        scratch_shapes=[pltpu.VMEM(pair_shape, jnp.float32)],
        compiler_params=pltpu.CompilerParams(vmem_limit_bytes=8 * MIB),
        name="attended_sum",
    )(held, with_partner(send, n // 2, n))

    everyone = [attended] + [with_partner(attended, k, n) for k in range(1, n // 2)]
    product = jnp.dot(
        jnp.concatenate(everyone), out_weight, preferred_element_type=jnp.float32
    )
    cols = out_weight.shape[1] // ntp
    half_spec = pl.BlockSpec((n * rows, cols), lambda i, m: (0, 0))
    own = lax.dynamic_slice_in_dim(product, core * cols, cols, 1)
    away = lax.dynamic_slice_in_dim(product, (1 - core) * cols, cols, 1)
    got = lax.ppermute(away, "tp", swap)
    return pl.pallas_call(
        functools.partial(order_kernel, n),
        grid_spec=pltpu.PrefetchScalarGridSpec(
            num_scalar_prefetch=1,
            grid=(1,),
            in_specs=[half_spec] * 2,
            out_specs=half_spec,
        ),
        out_shape=jax.ShapeDtypeStruct((n * rows, cols), jnp.bfloat16),
        compiler_params=pltpu.CompilerParams(vmem_limit_bytes=4 * MIB),
        name="order_rows",
    )(me.reshape(1), own, got)


def solution(mesh):
    in_specs = (
        P(("groups", "pool"), None),
        P("pool", "tp", None),
        P("groups", None),
        P("groups"),
        P("groups"),
        P(("groups", "pool"), "tp", None),
        P(("groups", "pool"), None, "tp", None),
        P(("groups", "pool")),
        P("tp", "pool"),
    )
    out_specs = P("groups", ("pool", "tp"))
    return jax.shard_map(local, mesh=mesh, in_specs=in_specs, out_specs=out_specs, check_vma=False)
```

```python
import functools

import jax
import jax.numpy as jnp
from jax import lax
from jax.experimental import pallas as pl
from jax.experimental.pallas import tpu as pltpu
from jax.sharding import PartitionSpec as P

BLK = 8
MIB = 1 << 20


def pack_kernel(base, at_ref, fill_ref, dest_ref, x_ref, out_ref, packed, count, out_sem):
    n, size, part = packed.shape
    tokens = x_ref.shape[0]
    blocks = tokens // BLK

    def store(q):
        return pltpu.make_async_copy(packed.at[q], out_ref.at[q], out_sem.at[q])

    first = at_ref[0] * blocks
    for q in range(n):
        count[q] = 0

    @pl.loop(0, blocks)
    def _(b):
        owner = dest_ref[first + b]
        count[owner] = count[owner] + fill_ref[first + b]

    def starts(q, total):
        here = count[q]
        count[q] = total
        return total + here

    lax.fori_loop(0, n, starts, jnp.int32(0))
    token = lax.broadcasted_iota(jnp.int32, (1, tokens), 1)

    def place(b, ranks):
        owner = dest_ref[first + b]
        fill = fill_ref[first + b]
        start = count[owner]
        count[owner] = start + fill
        inner = token - b * BLK
        return jnp.where((inner >= 0) & (inner < fill), start + inner, ranks)

    ranks = lax.fori_loop(0, blocks, place, jnp.full((1, tokens), -1, jnp.int32))
    wanted = base + at_ref[1] * size + lax.broadcasted_iota(jnp.int32, (size, tokens), 0)
    pick = (wanted == ranks).astype(jnp.bfloat16)
    for q in range(n):
        packed[q] = jnp.dot(
            pick, x_ref[:, q * part : (q + 1) * part], preferred_element_type=jnp.float32
        ).astype(packed.dtype)
        store(q).start()
    for q in range(n):
        store(q).wait()


def pack(x_prompt, fill, dest, at, n, base, size):
    tokens, width = x_prompt.shape
    part = width // n
    return pl.pallas_call(
        functools.partial(pack_kernel, base),
        grid_spec=pltpu.PrefetchScalarGridSpec(
            num_scalar_prefetch=3,
            grid=(1,),
            in_specs=[pl.BlockSpec(memory_space=pltpu.VMEM)],
            out_specs=pl.BlockSpec(memory_space=pl.ANY),
            scratch_shapes=[
                pltpu.VMEM((n, size, part), jnp.bfloat16),
                pltpu.SMEM((n,), jnp.int32),
                pltpu.SemaphoreType.DMA((n,)),
            ],
        ),
        out_shape=jax.ShapeDtypeStruct((n, size, part), jnp.bfloat16),
        compiler_params=pltpu.CompilerParams(vmem_limit_bytes=16 * MIB),
        cost_estimate=pl.CostEstimate(
            flops=2 * size * tokens * width, bytes_accessed=64 * MIB, transcendentals=0
        ),
        name="pack_live_tokens",
    )(at, fill, dest, x_prompt)


def tile_cuts(lanes):
    return [0] + list(range(min(256, lanes), lanes, 128)) + [lanes]


def near_lanes(lanes):
    return min(lanes, -(-lanes * 3 // 5 // 128) * 128)


def widen(core, n, refs, wide, base, first, last):
    length = refs[0].shape[0] // n
    tokens = wide.shape[0] // n

    @pl.loop(first, last)
    def _(s):
        for j, ref in enumerate(refs):
            side = core if j == 0 else 1 - core
            to = pl.multiple_of(s * tokens + base + side * length, BLK)
            wide[pl.ds(to, length), :] = ref[
                pl.ds(pl.multiple_of(s * length, length), length), :
            ].astype(wide.dtype)


def span_copies(refs, buffer, sem):
    cuts = sem.shape[1]
    span = buffer.shape[1] // cuts
    return [
        [
            pltpu.make_async_copy(
                ref.at[pl.ds(i * span, span)], buffer.at[j, pl.ds(i * span, span)], sem.at[j, i]
            )
            for j, ref in enumerate(refs)
        ]
        for i in range(cuts)
    ]


def load_tokens(n, core, over, x_refs, held, more, wide, sem, others):
    main = span_copies(x_refs[:2], held, sem)
    for pair in main:
        for copy in pair:
            copy.start()
    for copy in others:
        copy.start()
    for i, pair in enumerate(main):
        for copy in pair:
            copy.wait()
        parts = [held.at[0], held.at[1]]
        widen(core, n, parts, wide, 0, i * n // len(main), (i + 1) * n // len(main))

    @pl.when(over != 0)
    def _():
        rest = span_copies(x_refs[2:], more, sem)
        for pair in rest:
            for copy in pair:
                copy.start()
        for pair in rest:
            for copy in pair:
                copy.wait()
        base = wide.shape[0] // n - 2 * more.shape[1] // n
        widen(core, n, [more.at[0], more.at[1]], wide, base, 0, n)


def list_tile(meta_ref, first, count, wide, tile):
    for i in range(0, count, 2):
        pair = [
            wide[pl.ds(pl.multiple_of(meta_ref[first + i + j], BLK), BLK), :] for j in range(2)
        ]
        tile[i * BLK : (i + 2) * BLK, :] = jnp.concatenate(pair).astype(tile.dtype)
    return tile[: count * BLK, :]


def key_kernel(query_ref, weight_ref, out_ref):
    group = out_ref.shape[1] // query_ref.shape[0]
    hd = query_ref.shape[2]
    h = pl.program_id(0)
    for i in range(query_ref.shape[1] // group):

        @pl.when(h == i)
        def _(i=i):
            query = query_ref[:, i * group : (i + 1) * group, :].astype(jnp.float32)
            out_ref[0] = lax.dot_general(
                query.reshape(-1, hd).astype(jnp.bfloat16),
                weight_ref[0, :, :hd],
                (((1,), (1,)), ((), ())),
                preferred_element_type=jnp.float32,
            ).astype(out_ref.dtype)


def score_kernel(n, rows, meta_ref, *refs):
    x_refs, keyed_refs, (row_ref, near_ref, rest_ref) = refs[:4], refs[4:6], refs[6:9]
    held, more, wide, tile, keyed, sem, keyed_sem = refs[9:]
    step = pl.program_id(0)
    part = wide.shape[1]
    near = near_ref.shape[2]
    lanes = near + rest_ref.shape[2]
    cuts = tile_cuts(lanes)
    groups = lanes // BLK
    at_size = n * groups
    q = meta_ref[at_size + n] ^ reversed_bits(step, n)
    kvh, per = keyed.shape[0], keyed.shape[1] // n
    group = per // rows

    def load(i):
        span = n // 2 * per
        return [
            pltpu.make_async_copy(
                keyed_refs[i].at[h], keyed.at[h, pl.ds(i * span, span)], keyed_sem.at[i, h]
            )
            for h in range(kvh)
        ]

    @pl.when(step == 0)
    def _():
        load_tokens(
            n, meta_ref[at_size + n + 1], meta_ref[at_size + n + 2], x_refs, held, more, wide, sem,
            load(0) + load(1),
        )

    for i in range(2):

        @pl.when(step == i * (n // 2))
        def _(i=i):
            for copy in load(i):
                copy.wait()

    def one(t):
        here = slice(cuts[t], cuts[t + 1])
        count = (cuts[t + 1] - cuts[t]) // BLK
        raw = lax.dot_general(
            keyed[:, pl.ds(pl.multiple_of(step * per, per), per), :].reshape(kvh * per, part),
            list_tile(meta_ref, q * groups + cuts[t] // BLK, count, wide, tile),
            (((1,), (1,)), ((), ())),
            preferred_element_type=jnp.float32,
        ).reshape(kvh, rows, group, count * BLK)
        owner_row = row_ref[0, :, here]
        picked = jnp.zeros((kvh, group, count * BLK), jnp.float32)
        for r in range(rows):
            picked = picked + jnp.where((owner_row == r)[None], raw[:, r], 0.0)
        picked = picked.reshape(kvh * group, -1).astype(near_ref.dtype)
        if cuts[t] < near:
            near_ref[0, :, here] = picked
        else:
            rest_ref[0, :, cuts[t] - near : cuts[t + 1] - near] = picked

    one(0)
    for t in range(1, len(cuts) - 1):
        pl.when(meta_ref[at_size + q] > cuts[t])(functools.partial(one, t))


def weight_kernel(scale, count, *refs):
    part_refs, row_refs = refs[:count], refs[count : 2 * count]
    top_ref, sum_ref = refs[2 * count : 2 * count + 2]
    w_refs, share_ref = refs[2 * count + 2 : -1], refs[-1]
    n = part_refs[0].shape[0]
    scores, owner_rows = [], []
    for part_ref, row_ref in zip(part_refs, row_refs):
        got = part_ref[0].astype(jnp.float32)
        for i in range(1, n):
            got = got + part_ref[i].astype(jnp.float32)
        scores.append(got * scale)
        owner_rows.append(row_ref[...])
    weights = [jnp.zeros(s.shape, jnp.float32) for s in scores]
    for r in range(top_ref.shape[0]):
        own = [jnp.where(o == r, s, -jnp.inf) for o, s in zip(owner_rows, scores)]
        cache_top = top_ref[r]
        top = cache_top
        for o in own:
            top = jnp.maximum(top, jnp.max(o, 1, keepdims=True))
        held = [jnp.exp(o - top) for o in own]
        fade = jnp.exp(cache_top - top)
        total = sum_ref[r] * fade
        for h in held:
            total = total + jnp.sum(h, 1, keepdims=True)
        weights = [w + h / total for w, h in zip(weights, held)]
        share_ref[r] = fade / total
    for w, w_ref in zip(weights, w_refs):
        for i in range(n):
            w_ref[i] = w.astype(w_ref.dtype)


def value_kernel(n, rows, meta_ref, *refs):
    x_refs, (near_ref, rest_ref, row_ref, weight_ref, out_ref) = refs[:4], refs[4:9]
    held, more, wide, tile, values, acc, mixed, sem, value_sem = refs[9:]
    q = pl.program_id(0)
    kvh = values.shape[0]
    hd = values.shape[2]
    load_values = [
        pltpu.make_async_copy(
            weight_ref.at[h, :, pl.ds(hd, hd)], values.at[h], value_sem.at[h]
        )
        for h in range(kvh)
    ]
    _, heads, near = near_ref.shape
    lanes = near + rest_ref.shape[2]
    per = rows * heads // kvh
    cuts = tile_cuts(lanes)
    groups = lanes // BLK
    at_size = n * groups

    @pl.when(q == 0)
    def _():
        load_tokens(
            n, meta_ref[at_size + n + 1], meta_ref[at_size + n + 2], x_refs, held, more, wide, sem,
            load_values,
        )

    def one(t):
        here = slice(cuts[t], cuts[t + 1])
        width = cuts[t + 1] - cuts[t]
        if cuts[t] < near:
            weights = near_ref[0, :, here]
        else:
            weights = rest_ref[0, :, cuts[t] - near : cuts[t + 1] - near]
        weights = weights.astype(jnp.float32).reshape(kvh, 1, heads // kvh, width)
        owner_row = row_ref[0, :, here]
        spread = jnp.concatenate(
            [jnp.where((owner_row == r)[None, None], weights, 0.0) for r in range(rows)], 1
        ).reshape(kvh * per, width)
        got = jnp.dot(
            spread.astype(jnp.bfloat16),
            list_tile(meta_ref, q * groups + cuts[t] // BLK, width // BLK, wide, tile),
            preferred_element_type=jnp.float32,
        )
        if t == 0:
            first = got
            pl.when(size <= cuts[1])(lambda: keep(first))

            @pl.when(size > cuts[1])
            def _():
                acc[...] = first

        else:
            acc[...] += got

    size = meta_ref[at_size + q]

    def keep(sums):
        for h in range(kvh):
            mixed[h, pl.ds(pl.multiple_of(q * per, per), per), :] = sums[
                h * per : (h + 1) * per
            ].astype(mixed.dtype)

    one(0)
    for t in range(1, len(cuts) - 1):
        pl.when(size > cuts[t])(functools.partial(one, t))
    pl.when(size > cuts[1])(lambda: keep(acc[...]))

    @pl.when(q == n - 1)
    def _():
        for load in load_values:
            load.wait()
        for h in range(kvh):
            done = jnp.dot(mixed[h], values[h], preferred_element_type=jnp.float32)
            done = done.reshape(2, n // 2, per, done.shape[1]).astype(out_ref.dtype)
            for side in range(2):
                out_ref[:, side, h] = done[side]


def half_sum_kernel(side_ref, parts_ref, kept_ref, send_ref, mine_ref):
    half, sides, kvh, per, hd = parts_ref.shape
    rows, heads = kept_ref.shape[:2]
    group = heads // kvh
    for side in range(sides):
        own = side_ref[0] == side
        for h in range(kvh):
            terms = parts_ref[0, side, h].astype(jnp.float32)
            for i in range(1, half):
                terms = terms + parts_ref[i, side, h].astype(jnp.float32)
            kept = jnp.concatenate(
                [kept_ref[r, h * group : (h + 1) * group, :] for r in range(rows)]
            )
            terms = terms + jnp.where(own, kept, 0.0)
            mine_ref[side, h] = terms
            send_ref[side, h] = terms.astype(send_ref.dtype)


def whole_sum_kernel(mine_ref, got_ref, out_ref, total):
    sides, kvh, per, _ = mine_ref.shape
    rows = out_ref.shape[0] // sides
    group = per // rows
    total[...] = mine_ref[...] + got_ref[...].astype(jnp.float32)
    for h in range(kvh):
        for g in range(group):
            column = [
                total[side, h, pl.ds(g, rows, stride=group), :] for side in range(sides)
            ]
            head = h * group + g
            hd = column[0].shape[1]
            out_ref[:, head * hd : (head + 1) * hd] = jnp.concatenate(column).astype(
                out_ref.dtype
            )


def stage_kernel(after_ref, weight_ref, out_ref, sem):
    cuts = sem.shape[0]
    span = out_ref.shape[0] // cuts
    copies = [
        pltpu.make_async_copy(
            weight_ref.at[pl.ds(i * span, span)], out_ref.at[pl.ds(i * span, span)], sem.at[i]
        )
        for i in range(cuts)
    ]
    for copy in copies:
        copy.start()
    for copy in copies:
        copy.wait()


def order_kernel(n, me_ref, own_ref, got_ref, out_ref):
    half = n // 2
    rows = own_ref.shape[0] // n
    for q in range(0, n, 2):
        pair = []
        for owner in (q, q + 1):
            block = ((me_ref[0] % half) ^ (owner % half)) * 2 + owner // half
            here = pl.ds(pl.multiple_of(block * rows, rows), rows)
            pair.append(own_ref[here, :] + got_ref[here, :])
        out_ref[q * rows : (q + 2) * rows, :] = jnp.concatenate(pair).astype(out_ref.dtype)


def with_partner(x, k, n):
    return lax.ppermute(x, "pool", [(i, i ^ k) for i in range(n)])


def from_rest(held, n):
    k = n // 4
    while k >= 2:
        held = jnp.concatenate([held, with_partner(held, k, n)])
        k //= 2
    return held


def reversed_bits(k, n):
    out, bit = 0, 1
    while bit < n:
        out = out + (k // bit) % 2 * (n // 2 // bit)
        bit *= 2
    return out


def local(
    x_prompt, kv_weight, block_dest, block_row, block_fill, queries, kv_cache, cache_len, out_weight
):
    n = lax.axis_size("pool")
    ntp = lax.axis_size("tp")
    me = lax.axis_index("pool").astype(jnp.int32)
    core = lax.axis_index("tp").astype(jnp.int32)
    tokens, width = x_prompt.shape
    part = width // n
    kvh = kv_weight.shape[1]
    hd = kv_weight.shape[2] // 2
    rows, heads = queries.shape[0], queries.shape[1]
    group = heads // kvh
    per = rows * group
    cache_slots = kv_cache.shape[1]
    blocks = tokens // BLK
    cap = max(2, 2 * blocks // n)
    window = cap * BLK + BLK
    lanes = -(-n * window // 128) * 128
    half = tokens // ntp
    scale = 1.0 / hd**0.5
    swap = [(i, (i + 1) % ntp) for i in range(ntp)]

    size = half * 3 // 4
    extra = half - size
    at = jnp.stack([me, core])
    pack_fill, pack_dest = block_fill, block_dest[:, 0]
    packed = pack(x_prompt, pack_fill, pack_dest, at, n, 0, size)
    dest = pack_dest
    far = with_partner(queries, n // 2, n)
    packed, far, dest, block_row, block_fill, kv_weight = lax.optimization_barrier(
        (packed, far, dest, block_row, block_fill, kv_weight)
    )
    kv_weight = kv_weight.transpose(1, 0, 2)
    even = from_rest(jnp.stack([queries, far]), n)
    mine = lax.all_to_all(packed, "pool", 0, 0, tiled=True).reshape(n * size, part)

    index = jnp.arange(n * blocks, dtype=jnp.int32)
    sender = index // blocks
    kin = sender[None, :] == sender[:, None]
    lower = kin & (dest[None, :] < dest[:, None])
    level = kin & (dest[None, :] == dest[:, None]) & (index[None, :] < index[:, None])
    before = jnp.sum(jnp.where(lower, block_fill[None, :], 0), 1)
    within = jnp.sum(jnp.where(level, block_fill[None, :], 0), 1)
    pair = jnp.arange(n * n, dtype=jnp.int32)
    to, by = pair // n, pair % n
    owned = dest[None, :] == to[:, None]
    sent = sender[None, :] == by[:, None]
    earlier = sent & (dest[None, :] < to[:, None])
    offset = jnp.sum(jnp.where(earlier, block_fill[None, :], 0), 1)
    amount = jnp.sum(jnp.where(sent & owned, block_fill[None, :], 0), 1)
    runs = jnp.where(amount > 0, (offset % BLK + amount + BLK - 1) // BLK * BLK, 0)
    runs_by = runs.reshape(n, n)
    prior = jnp.arange(n)[:, None] < jnp.arange(n)[None, :]
    targets = jnp.sum(jnp.where(prior[None], runs_by[:, :, None], 0), 1)
    list_rows = jnp.sum(runs_by, 1)
    targets = targets.reshape(-1)
    sources = by * tokens + offset // BLK * BLK
    group_at = jnp.arange(n * lanes // BLK, dtype=jnp.int32) * BLK
    skip = group_at[:, None] - (to * lanes + targets)[None, :]
    group_rows = jnp.sum(
        jnp.where((skip >= 0) & (skip < runs[None, :]), sources[None, :] + skip, 0), 1
    )
    mine_pair = (dest * n + sender)[:, None] == pair[None, :]
    start = (
        dest * lanes
        + jnp.sum(jnp.where(mine_pair, targets[None, :], 0), 1)
        + before % BLK
        + within
    )
    spot = jnp.arange(n * lanes, dtype=jnp.int32)[:, None]
    inside = (spot >= start[None, :]) & (spot < (start + block_fill)[None, :])
    rowof = jnp.sum(jnp.where(inside, (block_row + 1)[None, :], 0), 1) - 1
    rowof = rowof.reshape(n, 1, lanes)

    near = near_lanes(lanes)
    most = jnp.stack([jnp.max(jnp.sum(block_fill.reshape(n, blocks), 1)), jnp.max(list_rows)])
    groups = lax.axis_size("groups")
    k = 1
    while k < groups:
        most = jnp.maximum(
            most, lax.ppermute(most, "groups", [(i, i ^ k) for i in range(groups)])
        )
        k *= 2
    over, longer = most[0] > ntp * size, most[1] > near

    def exchange_rest():
        rest = pack(x_prompt, pack_fill, pack_dest, at, n, ntp * size, extra)
        rest = lax.all_to_all(rest, "pool", 0, 0, tiled=True).reshape(n * extra, part)
        return rest, lax.ppermute(rest, "tp", swap)

    def no_rest():
        return (jnp.zeros((n * extra, part), jnp.bfloat16),) * 2

    more_mine, more_other = lax.cond(over, exchange_rest, no_rest)
    meta = jnp.concatenate(
        [group_rows, list_rows, jnp.stack([me, core, over.astype(jnp.int32)])]
    )

    def through_keys(held):
        held = held.reshape(n // 2 * rows, heads, hd)
        return pl.pallas_call(
            key_kernel,
            grid=(kvh,),
            in_specs=[
                pl.BlockSpec(held.shape, lambda h: (0, 0, 0)),
                pl.BlockSpec((1, part, 2 * hd), lambda h: (h, 0, 0)),
            ],
            out_specs=pl.BlockSpec((1, n // 2 * per, part), lambda h: (h, 0, 0)),
            out_shape=jax.ShapeDtypeStruct((kvh, n // 2 * per, part), jnp.bfloat16),
            compiler_params=pltpu.CompilerParams(vmem_limit_bytes=16 * MIB),
            cost_estimate=pl.CostEstimate(flops=0, bytes_accessed=1024, transcendentals=0),
            name="key_projection",
        )(held, kv_weight)

    keyed_even = through_keys(even)
    keyed_odd = through_keys(with_partner(even, 1, n))

    mine, meta, rowof, keyed_even, keyed_odd = lax.optimization_barrier(
        (mine, meta, rowof, keyed_even, keyed_odd)
    )
    other = lax.ppermute(mine, "tp", swap)

    anywhere = pl.BlockSpec(memory_space=pl.ANY)
    row_spec = pl.BlockSpec((1, 1, lanes), lambda q, m: (q, 0, 0))
    slot_specs = [
        pl.BlockSpec((1, heads, length), lambda q, m: (q, 0, 0)) for length in (near, lanes - near)
    ]
    slot_shapes = [
        jax.ShapeDtypeStruct((n, heads, length), jnp.bfloat16) for length in (near, lanes - near)
    ]
    in_vmem = pl.BlockSpec(memory_space=pltpu.VMEM)
    x_parts = (mine, other, more_mine, more_other)
    x_scratch = [
        pltpu.VMEM((ntp, n * size, part), jnp.bfloat16),
        pltpu.VMEM((ntp, n * extra, part), jnp.bfloat16),
        pltpu.VMEM((n * tokens, part), jnp.float32),
        pltpu.VMEM((tile_cuts(lanes)[1], part), jnp.bfloat16),
    ]
    at_me = n * lanes // BLK + n

    def owner(i, m):
        return m[at_me] ^ reversed_bits(i, n)

    score_near, score_rest = pl.pallas_call(
        functools.partial(score_kernel, n, rows),
        grid_spec=pltpu.PrefetchScalarGridSpec(
            num_scalar_prefetch=1,
            grid=(n,),
            in_specs=[
                *[anywhere] * 6,
                pl.BlockSpec((1, 1, lanes), lambda i, m: (owner(i, m), 0, 0)),
            ],
            out_specs=[
                pl.BlockSpec((1, heads, length), lambda i, m: (owner(i, m), 0, 0))
                for length in (near, lanes - near)
            ],
            scratch_shapes=[
                *x_scratch,
                pltpu.VMEM((kvh, n * per, part), jnp.bfloat16),
                pltpu.SemaphoreType.DMA((ntp, 4)),
                pltpu.SemaphoreType.DMA((2, kvh)),
            ],
        ),
        out_shape=slot_shapes,
        compiler_params=pltpu.CompilerParams(vmem_limit_bytes=24 * MIB),
        name="prompt_scores",
    )(meta, *x_parts, keyed_even, keyed_odd, rowof)

    my_rows = lax.dynamic_index_in_dim(rowof, me, 0, keepdims=False)

    def exchange_weights(*scores):
        count = len(scores)
        parts = [lax.all_to_all(s, "pool", 0, 0, tiled=True) for s in scores]
        query = queries.reshape(rows, kvh, group, hd)
        cache_scores = (
            jnp.einsum(
                "rhgd,rthd->rhgt", query, kv_cache[:, :, :, :hd], preferred_element_type=jnp.float32
            )
            * scale
        )
        cache_live = jnp.arange(cache_slots, dtype=jnp.int32)[None, :] < cache_len[:, None]
        cache_scores = jnp.where(cache_live[:, None, None, :], cache_scores, -jnp.inf)
        cache_top = jnp.max(cache_scores, -1, keepdims=True)
        cache_exp = jnp.exp(cache_scores - cache_top)
        cache_sum = jnp.sum(cache_exp, -1, keepdims=True)
        row_parts = [my_rows[:, :near], my_rows[:, near:]][:count]
        *weights, share = pl.pallas_call(
            functools.partial(weight_kernel, scale, count),
            out_shape=[*slot_shapes[:count], jax.ShapeDtypeStruct((rows, heads, 1), jnp.float32)],
            compiler_params=pltpu.CompilerParams(vmem_limit_bytes=8 * MIB),
            name="softmax_weights",
        )(
            *parts,
            *row_parts,
            cache_top.reshape(rows, heads, 1),
            cache_sum.reshape(rows, heads, 1),
        )
        weights = [lax.all_to_all(w, "pool", 0, 0, tiled=True) for w in weights]
        cached = jnp.einsum(
            "rhgt,rthd->rhgd",
            cache_exp.astype(jnp.bfloat16),
            kv_cache[:, :, :, hd:],
            preferred_element_type=jnp.float32,
        )
        return *weights, cached.reshape(rows, heads, hd) * share

    def near_only():
        weights, kept = exchange_weights(score_near)
        return weights, jnp.zeros(slot_shapes[1].shape, jnp.bfloat16), kept

    weight_near, weight_rest, kept = lax.cond(
        longer, lambda: exchange_weights(score_near, score_rest), near_only
    )
    terms = pl.pallas_call(
        functools.partial(value_kernel, n, rows),
        grid_spec=pltpu.PrefetchScalarGridSpec(
            num_scalar_prefetch=1,
            grid=(n,),
            in_specs=[*[anywhere] * 4, *slot_specs, row_spec, anywhere],
            out_specs=pl.BlockSpec((n // 2, 2, kvh, per, hd), lambda q, m: (0, 0, 0, 0, 0)),
            scratch_shapes=[
                *x_scratch,
                pltpu.VMEM((kvh, part, hd), jnp.bfloat16),
                pltpu.VMEM((kvh * per, part), jnp.float32),
                pltpu.VMEM((kvh, n * per, part), jnp.bfloat16),
                pltpu.SemaphoreType.DMA((ntp, 4)),
                pltpu.SemaphoreType.DMA((kvh,)),
            ],
        ),
        out_shape=jax.ShapeDtypeStruct((n // 2, 2, kvh, per, hd), jnp.bfloat16),
        compiler_params=pltpu.CompilerParams(vmem_limit_bytes=56 * MIB),
        name="weighted_values",
    )(meta, *x_parts, weight_near, weight_rest, rowof, kv_weight)

    halves = [list(range(n // 2)), list(range(n // 2, n))]
    term_parts = lax.all_to_all(
        terms, "pool", 0, 0, axis_index_groups=halves, tiled=True
    )
    pair_shape = (2, kvh, per, hd)
    send, held = pl.pallas_call(
        half_sum_kernel,
        in_specs=[pl.BlockSpec(memory_space=pltpu.SMEM), in_vmem, in_vmem],
        out_shape=[
            jax.ShapeDtypeStruct(pair_shape, jnp.bfloat16),
            jax.ShapeDtypeStruct(pair_shape, jnp.float32),
        ],
        compiler_params=pltpu.CompilerParams(vmem_limit_bytes=8 * MIB),
        name="half_pool_sum",
    )((me // (n // 2)).reshape(1), term_parts, kept)
    attended = pl.pallas_call(
        whole_sum_kernel,
        out_shape=jax.ShapeDtypeStruct((2 * rows, heads * hd), jnp.bfloat16),
        scratch_shapes=[pltpu.VMEM(pair_shape, jnp.float32)],
        compiler_params=pltpu.CompilerParams(vmem_limit_bytes=8 * MIB),
        name="attended_sum",
    )(held, with_partner(send, n // 2, n))

    staged = pl.pallas_call(
        stage_kernel,
        in_specs=[anywhere, pl.BlockSpec(memory_space=pltpu.HBM)],
        out_specs=in_vmem,
        out_shape=jax.ShapeDtypeStruct(out_weight.shape, jnp.bfloat16),
        scratch_shapes=[pltpu.SemaphoreType.DMA((8,))],
        compiler_params=pltpu.CompilerParams(vmem_limit_bytes=16 * MIB),
        cost_estimate=pl.CostEstimate(
            flops=0, bytes_accessed=2 * out_weight.size * 2, transcendentals=0
        ),
        name="stage_out_weight",
    )(send, out_weight)

    everyone = [attended] + [with_partner(attended, k, n) for k in range(1, n // 2)]
    product = jnp.dot(
        jnp.concatenate(everyone), staged, preferred_element_type=jnp.float32
    )
    cols = out_weight.shape[1] // ntp
    half_spec = pl.BlockSpec((n * rows, cols), lambda i, m: (0, 0))
    own = lax.dynamic_slice_in_dim(product, core * cols, cols, 1)
    away = lax.dynamic_slice_in_dim(product, (1 - core) * cols, cols, 1)
    got = lax.ppermute(away, "tp", swap)
    return pl.pallas_call(
        functools.partial(order_kernel, n),
        grid_spec=pltpu.PrefetchScalarGridSpec(
            num_scalar_prefetch=1,
            grid=(1,),
            in_specs=[half_spec] * 2,
            out_specs=half_spec,
        ),
        out_shape=jax.ShapeDtypeStruct((n * rows, cols), jnp.bfloat16),
        compiler_params=pltpu.CompilerParams(vmem_limit_bytes=4 * MIB),
        name="order_rows",
    )(me.reshape(1), own, got)


def solution(mesh):
    in_specs = (
        P(("groups", "pool"), None),
        P("pool", "tp", None),
        P("groups", None),
        P("groups"),
        P("groups"),
        P(("groups", "pool"), "tp", None),
        P(("groups", "pool"), None, "tp", None),
        P(("groups", "pool")),
        P("tp", "pool"),
    )
    out_specs = P("groups", ("pool", "tp"))
    return jax.shard_map(local, mesh=mesh, in_specs=in_specs, out_specs=out_specs, check_vma=False)
```

```python
import functools

import jax
import jax.numpy as jnp
from jax import lax
from jax.experimental import pallas as pl
from jax.experimental.pallas import tpu as pltpu
from jax.sharding import PartitionSpec as P

BLK = 8
MIB = 1 << 20


def pack_kernel(base, at_ref, fill_ref, dest_ref, x_ref, out_ref, packed, count, out_sem):
    n, size, part = packed.shape
    tokens = x_ref.shape[0]
    blocks = tokens // BLK

    def store(q):
        return pltpu.make_async_copy(packed.at[q], out_ref.at[q], out_sem.at[q])

    first = at_ref[0] * blocks
    for q in range(n):
        count[q] = 0

    @pl.loop(0, blocks)
    def _(b):
        owner = dest_ref[first + b]
        count[owner] = count[owner] + fill_ref[first + b]

    def starts(q, total):
        here = count[q]
        count[q] = total
        return total + here

    lax.fori_loop(0, n, starts, jnp.int32(0))
    token = lax.broadcasted_iota(jnp.int32, (1, tokens), 1)

    def place(b, ranks):
        owner = dest_ref[first + b]
        fill = fill_ref[first + b]
        start = count[owner]
        count[owner] = start + fill
        inner = token - b * BLK
        return jnp.where((inner >= 0) & (inner < fill), start + inner, ranks)

    ranks = lax.fori_loop(0, blocks, place, jnp.full((1, tokens), -1, jnp.int32))
    wanted = base + at_ref[1] * size + lax.broadcasted_iota(jnp.int32, (size, tokens), 0)
    pick = (wanted == ranks).astype(jnp.bfloat16)
    for q in range(n):
        packed[q] = jnp.dot(
            pick, x_ref[:, q * part : (q + 1) * part], preferred_element_type=jnp.float32
        ).astype(packed.dtype)
        store(q).start()
    for q in range(n):
        store(q).wait()


def pack(x_prompt, fill, dest, at, n, base, size):
    tokens, width = x_prompt.shape
    part = width // n
    return pl.pallas_call(
        functools.partial(pack_kernel, base),
        grid_spec=pltpu.PrefetchScalarGridSpec(
            num_scalar_prefetch=3,
            grid=(1,),
            in_specs=[pl.BlockSpec(memory_space=pltpu.VMEM)],
            out_specs=pl.BlockSpec(memory_space=pl.ANY),
            scratch_shapes=[
                pltpu.VMEM((n, size, part), jnp.bfloat16),
                pltpu.SMEM((n,), jnp.int32),
                pltpu.SemaphoreType.DMA((n,)),
            ],
        ),
        out_shape=jax.ShapeDtypeStruct((n, size, part), jnp.bfloat16),
        compiler_params=pltpu.CompilerParams(vmem_limit_bytes=16 * MIB),
        cost_estimate=pl.CostEstimate(
            flops=2 * size * tokens * width, bytes_accessed=64 * MIB, transcendentals=0
        ),
        name="pack_live_tokens",
    )(at, fill, dest, x_prompt)


def tile_cuts(lanes):
    return [0] + list(range(min(256, lanes), lanes, 128)) + [lanes]


def near_lanes(lanes):
    return min(lanes, -(-lanes * 3 // 5 // 128) * 128)


def widen(core, n, refs, wide, base, first, last):
    length = refs[0].shape[0] // n
    tokens = wide.shape[0] // n

    @pl.loop(first, last)
    def _(s):
        for j, ref in enumerate(refs):
            side = core if j == 0 else 1 - core
            to = pl.multiple_of(s * tokens + base + side * length, BLK)
            wide[pl.ds(to, length), :] = ref[
                pl.ds(pl.multiple_of(s * length, length), length), :
            ].astype(wide.dtype)


def span_copies(refs, buffer, sem):
    cuts = sem.shape[1]
    span = buffer.shape[1] // cuts
    return [
        [
            pltpu.make_async_copy(
                ref.at[pl.ds(i * span, span)], buffer.at[j, pl.ds(i * span, span)], sem.at[j, i]
            )
            for j, ref in enumerate(refs)
        ]
        for i in range(cuts)
    ]


def load_tokens(n, core, over, x_refs, there, held, more, wide, sem, others):
    main = span_copies(x_refs[: 2 - len(there)], held, sem)
    for pair in main:
        for copy in pair:
            copy.start()
    for copy in others:
        copy.start()
    for i, pair in enumerate(main):
        for copy in pair:
            copy.wait()
        parts = [held.at[j] for j in range(2 - len(there))] + there
        widen(core, n, parts, wide, 0, i * n // len(main), (i + 1) * n // len(main))

    @pl.when(over != 0)
    def _():
        rest = span_copies(x_refs[2:], more, sem)
        for pair in rest:
            for copy in pair:
                copy.start()
        for pair in rest:
            for copy in pair:
                copy.wait()
        base = wide.shape[0] // n - 2 * more.shape[1] // n
        widen(core, n, [more.at[0], more.at[1]], wide, base, 0, n)


def list_tile(meta_ref, first, count, wide, tile):
    for i in range(0, count, 2):
        pair = [
            wide[pl.ds(pl.multiple_of(meta_ref[first + i + j], BLK), BLK), :] for j in range(2)
        ]
        tile[i * BLK : (i + 2) * BLK, :] = jnp.concatenate(pair).astype(tile.dtype)
    return tile[: count * BLK, :]


def key_kernel(query_ref, weight_ref, out_ref):
    group = out_ref.shape[1] // query_ref.shape[0]
    hd = query_ref.shape[2]
    h = pl.program_id(0)
    for i in range(query_ref.shape[1] // group):

        @pl.when(h == i)
        def _(i=i):
            query = query_ref[:, i * group : (i + 1) * group, :].astype(jnp.float32)
            out_ref[0] = lax.dot_general(
                query.reshape(-1, hd).astype(jnp.bfloat16),
                weight_ref[0, :, :hd],
                (((1,), (1,)), ((), ())),
                preferred_element_type=jnp.float32,
            ).astype(out_ref.dtype)


def score_kernel(n, rows, meta_ref, *refs):
    x_refs, keyed_refs, (row_ref, near_ref, rest_ref) = refs[:4], refs[4:6], refs[6:9]
    held, more, wide, tile, keyed, sem, keyed_sem = refs[9:]
    step = pl.program_id(0)
    part = wide.shape[1]
    near = near_ref.shape[2]
    lanes = near + rest_ref.shape[2]
    cuts = tile_cuts(lanes)
    groups = lanes // BLK
    at_size = n * groups
    q = meta_ref[at_size + n] ^ reversed_bits(step, n)
    kvh, per = keyed.shape[0], keyed.shape[1] * 2 // n
    group = per // rows

    even_ref, odd_ref = keyed_refs
    load = [
        pltpu.make_async_copy(even_ref.at[h], keyed.at[h], keyed_sem.at[h]) for h in range(kvh)
    ]

    @pl.when(step == 0)
    def _():
        load_tokens(
            n, meta_ref[at_size + n + 1], meta_ref[at_size + n + 2], x_refs, [x_refs[1]], held, more,
            wide, sem, load,
        )
        for copy in load:
            copy.wait()

    at = pl.ds(pl.multiple_of(step % (n // 2) * per, per), per)
    query = jnp.where(step < n // 2, keyed[:, at, :], odd_ref[:, at, :])

    def one(t):
        here = slice(cuts[t], cuts[t + 1])
        count = (cuts[t + 1] - cuts[t]) // BLK
        raw = lax.dot_general(
            query.reshape(kvh * per, part),
            list_tile(meta_ref, q * groups + cuts[t] // BLK, count, wide, tile),
            (((1,), (1,)), ((), ())),
            preferred_element_type=jnp.float32,
        ).reshape(kvh, rows, group, count * BLK)
        owner_row = row_ref[0, :, here]
        picked = jnp.zeros((kvh, group, count * BLK), jnp.float32)
        for r in range(rows):
            picked = picked + jnp.where((owner_row == r)[None], raw[:, r], 0.0)
        picked = picked.reshape(kvh * group, -1).astype(near_ref.dtype)
        if cuts[t] < near:
            near_ref[0, :, here] = picked
        else:
            rest_ref[0, :, cuts[t] - near : cuts[t + 1] - near] = picked

    one(0)
    for t in range(1, len(cuts) - 1):
        pl.when(meta_ref[at_size + q] > cuts[t])(functools.partial(one, t))


def weight_kernel(scale, count, *refs):
    part_refs, row_refs = refs[:count], refs[count : 2 * count]
    top_ref, sum_ref = refs[2 * count : 2 * count + 2]
    w_refs, share_ref = refs[2 * count + 2 : -1], refs[-1]
    n = part_refs[0].shape[0]
    scores, owner_rows = [], []
    for part_ref, row_ref in zip(part_refs, row_refs):
        got = part_ref[0].astype(jnp.float32)
        for i in range(1, n):
            got = got + part_ref[i].astype(jnp.float32)
        scores.append(got * scale)
        owner_rows.append(row_ref[...])
    weights = [jnp.zeros(s.shape, jnp.float32) for s in scores]
    for r in range(top_ref.shape[0]):
        own = [jnp.where(o == r, s, -jnp.inf) for o, s in zip(owner_rows, scores)]
        cache_top = top_ref[r]
        top = cache_top
        for o in own:
            top = jnp.maximum(top, jnp.max(o, 1, keepdims=True))
        held = [jnp.exp(o - top) for o in own]
        fade = jnp.exp(cache_top - top)
        total = sum_ref[r] * fade
        for h in held:
            total = total + jnp.sum(h, 1, keepdims=True)
        weights = [w + h / total for w, h in zip(weights, held)]
        share_ref[r] = fade / total
    for w, w_ref in zip(weights, w_refs):
        for i in range(n):
            w_ref[i] = w.astype(w_ref.dtype)


def list_kernel(n, meta_ref, *refs):
    x_refs, (_, out_ref, held, more, wide, sem) = refs[:4], refs[4:]
    q = pl.program_id(0)
    lanes = out_ref.shape[1]
    cuts = tile_cuts(lanes)
    groups = lanes // BLK
    at_size = n * groups

    @pl.when(q == 0)
    def _():
        load_tokens(
            n, meta_ref[at_size + n + 1], meta_ref[at_size + n + 2], x_refs, [], held, more, wide,
            sem, [],
        )

    def one(t):
        list_tile(
            meta_ref, q * groups + cuts[t] // BLK, (cuts[t + 1] - cuts[t]) // BLK, wide,
            out_ref.at[q, cuts[t] : cuts[t + 1]],
        )

    one(0)
    for t in range(1, len(cuts) - 1):
        pl.when(meta_ref[at_size + q] > cuts[t])(functools.partial(one, t))


def value_kernel(n, rows, count, meta_ref, *refs):
    w_refs, (row_ref, list_ref, weight_ref, out_ref) = refs[:count], refs[count : count + 4]
    values, acc, mixed, value_sem = refs[count + 4 :]
    q = pl.program_id(0)
    kvh, _, hd = values.shape
    load_values = [
        pltpu.make_async_copy(
            weight_ref.at[h, :, pl.ds(hd, hd)], values.at[h], value_sem.at[h]
        )
        for h in range(kvh)
    ]
    _, heads, near = w_refs[0].shape
    lanes = list_ref.shape[1]
    per = rows * heads // kvh
    cuts = tile_cuts(lanes)
    size = meta_ref[n * lanes // BLK + q]

    @pl.when(q == 0)
    def _():
        for load in load_values:
            load.start()

    def one(t):
        here = slice(cuts[t], cuts[t + 1])
        width = cuts[t + 1] - cuts[t]
        piece = 0 if cuts[t] < near else 1
        weights = w_refs[piece][0, :, cuts[t] - piece * near : cuts[t + 1] - piece * near]
        weights = weights.astype(jnp.float32).reshape(kvh, 1, heads // kvh, width)
        owner_row = row_ref[0, :, here]
        spread = jnp.concatenate(
            [jnp.where((owner_row == r)[None, None], weights, 0.0) for r in range(rows)], 1
        ).reshape(kvh * per, width)
        got = jnp.dot(
            spread.astype(jnp.bfloat16), list_ref[q, here, :], preferred_element_type=jnp.float32
        )
        if t == 0:
            pl.when(size <= cuts[1])(lambda: keep(got))

            @pl.when(size > cuts[1])
            def _():
                acc[...] = got

        else:
            acc[...] += got

    def keep(sums):
        for h in range(kvh):
            mixed[h, pl.ds(pl.multiple_of(q * per, per), per), :] = sums[
                h * per : (h + 1) * per
            ].astype(mixed.dtype)

    one(0)
    for t in range(1, len(cuts) - 1):
        if cuts[t] < near or count > 1:
            pl.when(size > cuts[t])(functools.partial(one, t))
    pl.when(size > cuts[1])(lambda: keep(acc[...]))

    @pl.when(q == n - 1)
    def _():
        for load in load_values:
            load.wait()
        for h in range(kvh):
            done = jnp.dot(mixed[h], values[h], preferred_element_type=jnp.float32)
            done = done.reshape(2, n // 2, per, done.shape[1]).astype(out_ref.dtype)
            for side in range(2):
                out_ref[:, side, h] = done[side]


def half_sum_kernel(side_ref, parts_ref, kept_ref, send_ref, mine_ref):
    half, sides, kvh, per, hd = parts_ref.shape
    rows, heads = kept_ref.shape[:2]
    group = heads // kvh
    for side in range(sides):
        own = side_ref[0] == side
        for h in range(kvh):
            terms = parts_ref[0, side, h].astype(jnp.float32)
            for i in range(1, half):
                terms = terms + parts_ref[i, side, h].astype(jnp.float32)
            kept = jnp.concatenate(
                [kept_ref[r, h * group : (h + 1) * group, :] for r in range(rows)]
            )
            terms = terms + jnp.where(own, kept, 0.0)
            mine_ref[side, h] = terms
            send_ref[side, h] = terms.astype(send_ref.dtype)


def whole_sum_kernel(mine_ref, got_ref, out_ref, total):
    sides, kvh, per, _ = mine_ref.shape
    rows = out_ref.shape[0] // sides
    group = per // rows
    total[...] = mine_ref[...] + got_ref[...].astype(jnp.float32)
    for h in range(kvh):
        for g in range(group):
            column = [
                total[side, h, pl.ds(g, rows, stride=group), :] for side in range(sides)
            ]
            head = h * group + g
            hd = column[0].shape[1]
            out_ref[:, head * hd : (head + 1) * hd] = jnp.concatenate(column).astype(
                out_ref.dtype
            )


def stage_kernel(after_ref, weight_ref, out_ref, sem):
    cuts = sem.shape[0]
    span = out_ref.shape[0] // cuts
    copies = [
        pltpu.make_async_copy(
            weight_ref.at[pl.ds(i * span, span)], out_ref.at[pl.ds(i * span, span)], sem.at[i]
        )
        for i in range(cuts)
    ]
    for copy in copies:
        copy.start()
    for copy in copies:
        copy.wait()


def order_kernel(n, me_ref, own_ref, got_ref, out_ref):
    half = n // 2
    rows = own_ref.shape[0] // n
    for q in range(0, n, 2):
        pair = []
        for owner in (q, q + 1):
            block = ((me_ref[0] % half) ^ (owner % half)) * 2 + owner // half
            here = pl.ds(pl.multiple_of(block * rows, rows), rows)
            pair.append(own_ref[here, :] + got_ref[here, :])
        out_ref[q * rows : (q + 2) * rows, :] = jnp.concatenate(pair).astype(out_ref.dtype)


def with_partner(x, k, n):
    return lax.ppermute(x, "pool", [(i, i ^ k) for i in range(n)])


def from_rest(held, n):
    k = n // 4
    while k >= 2:
        held = jnp.concatenate([held, with_partner(held, k, n)])
        k //= 2
    return held


def reversed_bits(k, n):
    out, bit = 0, 1
    while bit < n:
        out = out + (k // bit) % 2 * (n // 2 // bit)
        bit *= 2
    return out


def local(
    x_prompt, kv_weight, block_dest, block_row, block_fill, queries, kv_cache, cache_len, out_weight
):
    n = lax.axis_size("pool")
    ntp = lax.axis_size("tp")
    me = lax.axis_index("pool").astype(jnp.int32)
    core = lax.axis_index("tp").astype(jnp.int32)
    tokens, width = x_prompt.shape
    part = width // n
    kvh = kv_weight.shape[1]
    hd = kv_weight.shape[2] // 2
    rows, heads = queries.shape[0], queries.shape[1]
    group = heads // kvh
    per = rows * group
    cache_slots = kv_cache.shape[1]
    blocks = tokens // BLK
    cap = max(2, 2 * blocks // n)
    window = cap * BLK + BLK
    lanes = -(-n * window // 128) * 128
    half = tokens // ntp
    scale = 1.0 / hd**0.5
    swap = [(i, (i + 1) % ntp) for i in range(ntp)]

    size = half * 3 // 4
    extra = half - size
    at = jnp.stack([me, core])
    pack_fill, pack_dest = block_fill, block_dest[:, 0]
    packed = pack(x_prompt, pack_fill, pack_dest, at, n, 0, size)
    dest = pack_dest
    far = with_partner(queries, n // 2, n)
    packed, far, dest, block_row, block_fill, kv_weight = lax.optimization_barrier(
        (packed, far, dest, block_row, block_fill, kv_weight)
    )
    kv_weight = kv_weight.transpose(1, 0, 2)
    even = from_rest(jnp.stack([queries, far]), n)
    mine = lax.all_to_all(packed, "pool", 0, 0, tiled=True).reshape(n * size, part)

    index = jnp.arange(n * blocks, dtype=jnp.int32)
    sender = index // blocks
    kin = sender[None, :] == sender[:, None]
    lower = kin & (dest[None, :] < dest[:, None])
    level = kin & (dest[None, :] == dest[:, None]) & (index[None, :] < index[:, None])
    before = jnp.sum(jnp.where(lower, block_fill[None, :], 0), 1)
    within = jnp.sum(jnp.where(level, block_fill[None, :], 0), 1)
    pair = jnp.arange(n * n, dtype=jnp.int32)
    to, by = pair // n, pair % n
    owned = dest[None, :] == to[:, None]
    sent = sender[None, :] == by[:, None]
    earlier = sent & (dest[None, :] < to[:, None])
    offset = jnp.sum(jnp.where(earlier, block_fill[None, :], 0), 1)
    amount = jnp.sum(jnp.where(sent & owned, block_fill[None, :], 0), 1)
    runs = jnp.where(amount > 0, (offset % BLK + amount + BLK - 1) // BLK * BLK, 0)
    runs_by = runs.reshape(n, n)
    prior = jnp.arange(n)[:, None] < jnp.arange(n)[None, :]
    targets = jnp.sum(jnp.where(prior[None], runs_by[:, :, None], 0), 1)
    list_rows = jnp.sum(runs_by, 1)
    targets = targets.reshape(-1)
    sources = by * tokens + offset // BLK * BLK
    group_at = jnp.arange(n * lanes // BLK, dtype=jnp.int32) * BLK
    skip = group_at[:, None] - (to * lanes + targets)[None, :]
    group_rows = jnp.sum(
        jnp.where((skip >= 0) & (skip < runs[None, :]), sources[None, :] + skip, 0), 1
    )
    mine_pair = (dest * n + sender)[:, None] == pair[None, :]
    start = (
        dest * lanes
        + jnp.sum(jnp.where(mine_pair, targets[None, :], 0), 1)
        + before % BLK
        + within
    )
    spot = jnp.arange(n * lanes, dtype=jnp.int32)[:, None]
    inside = (spot >= start[None, :]) & (spot < (start + block_fill)[None, :])
    rowof = jnp.sum(jnp.where(inside, (block_row + 1)[None, :], 0), 1) - 1
    rowof = rowof.reshape(n, 1, lanes)

    near = near_lanes(lanes)
    most = jnp.stack([jnp.max(jnp.sum(block_fill.reshape(n, blocks), 1)), jnp.max(list_rows)])
    groups = lax.axis_size("groups")
    k = 1
    while k < groups:
        most = jnp.maximum(
            most, lax.ppermute(most, "groups", [(i, i ^ k) for i in range(groups)])
        )
        k *= 2
    over, longer = most[0] > ntp * size, most[1] > near

    def exchange_rest():
        rest = pack(x_prompt, pack_fill, pack_dest, at, n, ntp * size, extra)
        rest = lax.all_to_all(rest, "pool", 0, 0, tiled=True).reshape(n * extra, part)
        return rest, lax.ppermute(rest, "tp", swap)

    def no_rest():
        return (jnp.zeros((n * extra, part), jnp.bfloat16),) * 2

    more_mine, more_other = lax.cond(over, exchange_rest, no_rest)
    meta = jnp.concatenate(
        [group_rows, list_rows, jnp.stack([me, core, over.astype(jnp.int32)])]
    )

    def through_keys(held):
        held = held.reshape(n // 2 * rows, heads, hd)
        return pl.pallas_call(
            key_kernel,
            grid=(kvh,),
            in_specs=[
                pl.BlockSpec(held.shape, lambda h: (0, 0, 0)),
                pl.BlockSpec((1, part, 2 * hd), lambda h: (h, 0, 0)),
            ],
            out_specs=pl.BlockSpec((1, n // 2 * per, part), lambda h: (h, 0, 0)),
            out_shape=jax.ShapeDtypeStruct((kvh, n // 2 * per, part), jnp.bfloat16),
            compiler_params=pltpu.CompilerParams(vmem_limit_bytes=16 * MIB),
            cost_estimate=pl.CostEstimate(flops=0, bytes_accessed=1024, transcendentals=0),
            name="key_projection",
        )(held, kv_weight)

    keyed_even = through_keys(even)
    keyed_odd = through_keys(with_partner(even, 1, n))

    mine, meta, rowof, keyed_even, keyed_odd = lax.optimization_barrier(
        (mine, meta, rowof, keyed_even, keyed_odd)
    )
    other = lax.ppermute(mine, "tp", swap)

    anywhere = pl.BlockSpec(memory_space=pl.ANY)
    row_spec = pl.BlockSpec((1, 1, lanes), lambda q, m: (q, 0, 0))
    slot_specs = [
        pl.BlockSpec((1, heads, length), lambda q, m: (q, 0, 0)) for length in (near, lanes - near)
    ]
    slot_shapes = [
        jax.ShapeDtypeStruct((n, heads, length), jnp.bfloat16) for length in (near, lanes - near)
    ]
    in_vmem = pl.BlockSpec(memory_space=pltpu.VMEM)
    x_parts = (mine, other, more_mine, more_other)
    x_scratch = [
        pltpu.VMEM((ntp, n * extra, part), jnp.bfloat16),
        pltpu.VMEM((n * tokens, part), jnp.float32),
    ]
    at_me = n * lanes // BLK + n

    def owner(i, m):
        return m[at_me] ^ reversed_bits(i, n)

    score_near, score_rest = pl.pallas_call(
        functools.partial(score_kernel, n, rows),
        grid_spec=pltpu.PrefetchScalarGridSpec(
            num_scalar_prefetch=1,
            grid=(n,),
            in_specs=[
                anywhere,
                in_vmem,
                anywhere,
                anywhere,
                anywhere,
                in_vmem,
                pl.BlockSpec((1, 1, lanes), lambda i, m: (owner(i, m), 0, 0)),
            ],
            out_specs=[
                pl.BlockSpec((1, heads, length), lambda i, m: (owner(i, m), 0, 0))
                for length in (near, lanes - near)
            ],
            scratch_shapes=[
                pltpu.VMEM((1, n * size, part), jnp.bfloat16),
                *x_scratch,
                pltpu.VMEM((tile_cuts(lanes)[1], part), jnp.bfloat16),
                pltpu.VMEM((kvh, n // 2 * per, part), jnp.bfloat16),
                pltpu.SemaphoreType.DMA((ntp, 4)),
                pltpu.SemaphoreType.DMA((kvh,)),
            ],
        ),
        out_shape=slot_shapes,
        compiler_params=pltpu.CompilerParams(vmem_limit_bytes=24 * MIB),
        name="prompt_scores",
    )(meta, *x_parts, keyed_even, keyed_odd, rowof)

    my_rows = lax.dynamic_index_in_dim(rowof, me, 0, keepdims=False)

    def exchange_weights(*scores):
        count = len(scores)
        parts = [lax.all_to_all(s, "pool", 0, 0, tiled=True) for s in scores]
        query = queries.reshape(rows, kvh, group, hd)
        cache_scores = (
            jnp.einsum(
                "rhgd,rthd->rhgt", query, kv_cache[:, :, :, :hd], preferred_element_type=jnp.float32
            )
            * scale
        )
        cache_live = jnp.arange(cache_slots, dtype=jnp.int32)[None, :] < cache_len[:, None]
        cache_scores = jnp.where(cache_live[:, None, None, :], cache_scores, -jnp.inf)
        cache_top = jnp.max(cache_scores, -1, keepdims=True)
        cache_exp = jnp.exp(cache_scores - cache_top)
        cache_sum = jnp.sum(cache_exp, -1, keepdims=True)
        row_parts = [my_rows[:, :near], my_rows[:, near:]][:count]
        *weights, share = pl.pallas_call(
            functools.partial(weight_kernel, scale, count),
            out_shape=[*slot_shapes[:count], jax.ShapeDtypeStruct((rows, heads, 1), jnp.float32)],
            compiler_params=pltpu.CompilerParams(vmem_limit_bytes=8 * MIB),
            name="softmax_weights",
        )(
            *parts,
            *row_parts,
            cache_top.reshape(rows, heads, 1),
            cache_sum.reshape(rows, heads, 1),
        )
        lists = pl.pallas_call(
            functools.partial(list_kernel, n),
            grid_spec=pltpu.PrefetchScalarGridSpec(
                num_scalar_prefetch=1,
                grid=(n,),
                in_specs=[anywhere] * 5,
                out_specs=in_vmem,
                scratch_shapes=[
                    pltpu.VMEM((ntp, n * size, part), jnp.bfloat16),
                    *x_scratch,
                    pltpu.SemaphoreType.DMA((ntp, 4)),
                ],
            ),
            out_shape=jax.ShapeDtypeStruct((n, lanes, part), jnp.bfloat16),
            compiler_params=pltpu.CompilerParams(vmem_limit_bytes=28 * MIB),
            cost_estimate=pl.CostEstimate(
                flops=0, bytes_accessed=16 * MIB, transcendentals=0
            ),
            name="owner_lists",
        )(meta, *x_parts, weights[0])
        weights = [lax.all_to_all(w, "pool", 0, 0, tiled=True) for w in weights]
        cached = jnp.einsum(
            "rhgt,rthd->rhgd",
            cache_exp.astype(jnp.bfloat16),
            kv_cache[:, :, :, hd:],
            preferred_element_type=jnp.float32,
        )
        terms = pl.pallas_call(
            functools.partial(value_kernel, n, rows, count),
            grid_spec=pltpu.PrefetchScalarGridSpec(
                num_scalar_prefetch=1,
                grid=(n,),
                in_specs=[*slot_specs[:count], row_spec, in_vmem, anywhere],
                out_specs=pl.BlockSpec((n // 2, 2, kvh, per, hd), lambda q, m: (0, 0, 0, 0, 0)),
                scratch_shapes=[
                    pltpu.VMEM((kvh, part, hd), jnp.bfloat16),
                    pltpu.VMEM((kvh * per, part), jnp.float32),
                    pltpu.VMEM((kvh, n * per, part), jnp.bfloat16),
                    pltpu.SemaphoreType.DMA((kvh,)),
                ],
            ),
            out_shape=jax.ShapeDtypeStruct((n // 2, 2, kvh, per, hd), jnp.bfloat16),
            compiler_params=pltpu.CompilerParams(vmem_limit_bytes=16 * MIB),
            name="weighted_values",
        )(meta, *weights, rowof, lists, kv_weight)
        return terms, cached.reshape(rows, heads, hd) * share

    terms, kept = lax.cond(
        longer,
        lambda: exchange_weights(score_near, score_rest),
        lambda: exchange_weights(score_near),
    )

    halves = [list(range(n // 2)), list(range(n // 2, n))]
    term_parts = lax.all_to_all(
        terms, "pool", 0, 0, axis_index_groups=halves, tiled=True
    )
    pair_shape = (2, kvh, per, hd)
    send, held = pl.pallas_call(
        half_sum_kernel,
        in_specs=[pl.BlockSpec(memory_space=pltpu.SMEM), in_vmem, in_vmem],
        out_shape=[
            jax.ShapeDtypeStruct(pair_shape, jnp.bfloat16),
            jax.ShapeDtypeStruct(pair_shape, jnp.float32),
        ],
        compiler_params=pltpu.CompilerParams(vmem_limit_bytes=8 * MIB),
        name="half_pool_sum",
    )((me // (n // 2)).reshape(1), term_parts, kept)
    attended = pl.pallas_call(
        whole_sum_kernel,
        out_shape=jax.ShapeDtypeStruct((2 * rows, heads * hd), jnp.bfloat16),
        scratch_shapes=[pltpu.VMEM(pair_shape, jnp.float32)],
        compiler_params=pltpu.CompilerParams(vmem_limit_bytes=8 * MIB),
        name="attended_sum",
    )(held, with_partner(send, n // 2, n))

    staged = pl.pallas_call(
        stage_kernel,
        in_specs=[anywhere, pl.BlockSpec(memory_space=pltpu.HBM)],
        out_specs=in_vmem,
        out_shape=jax.ShapeDtypeStruct(out_weight.shape, jnp.bfloat16),
        scratch_shapes=[pltpu.SemaphoreType.DMA((8,))],
        compiler_params=pltpu.CompilerParams(vmem_limit_bytes=16 * MIB),
        cost_estimate=pl.CostEstimate(
            flops=0, bytes_accessed=2 * out_weight.size * 2, transcendentals=0
        ),
        name="stage_out_weight",
    )(send, out_weight)

    everyone = [attended] + [with_partner(attended, k, n) for k in range(1, n // 2)]
    product = jnp.dot(
        jnp.concatenate(everyone), staged, preferred_element_type=jnp.float32
    )
    cols = out_weight.shape[1] // ntp
    half_spec = pl.BlockSpec((n * rows, cols), lambda i, m: (0, 0))
    own = lax.dynamic_slice_in_dim(product, core * cols, cols, 1)
    away = lax.dynamic_slice_in_dim(product, (1 - core) * cols, cols, 1)
    got = lax.ppermute(away, "tp", swap)
    return pl.pallas_call(
        functools.partial(order_kernel, n),
        grid_spec=pltpu.PrefetchScalarGridSpec(
            num_scalar_prefetch=1,
            grid=(1,),
            in_specs=[half_spec] * 2,
            out_specs=half_spec,
        ),
        out_shape=jax.ShapeDtypeStruct((n * rows, cols), jnp.bfloat16),
        compiler_params=pltpu.CompilerParams(vmem_limit_bytes=4 * MIB),
        name="order_rows",
    )(me.reshape(1), own, got)


def solution(mesh):
    in_specs = (
        P(("groups", "pool"), None),
        P("pool", "tp", None),
        P("groups", None),
        P("groups"),
        P("groups"),
        P(("groups", "pool"), "tp", None),
        P(("groups", "pool"), None, "tp", None),
        P(("groups", "pool")),
        P("tp", "pool"),
    )
    out_specs = P("groups", ("pool", "tp"))
    return jax.shard_map(local, mesh=mesh, in_specs=in_specs, out_specs=out_specs, check_vma=False)
```

```python
import functools

import jax
import jax.numpy as jnp
from jax import lax
from jax.experimental import pallas as pl
from jax.experimental.pallas import tpu as pltpu
from jax.sharding import PartitionSpec as P

BLK = 8
MIB = 1 << 20


def pack_kernel(base, at_ref, fill_ref, dest_ref, x_ref, out_ref, packed, count, out_sem):
    n, size, part = packed.shape
    tokens = x_ref.shape[0]
    blocks = tokens // BLK

    def store(q):
        return pltpu.make_async_copy(packed.at[q], out_ref.at[q], out_sem.at[q])

    first = at_ref[0] * blocks
    for q in range(n):
        count[q] = 0

    @pl.loop(0, blocks)
    def _(b):
        owner = dest_ref[first + b]
        count[owner] = count[owner] + fill_ref[first + b]

    def starts(q, total):
        here = count[q]
        count[q] = total
        return total + here

    lax.fori_loop(0, n, starts, jnp.int32(0))
    token = lax.broadcasted_iota(jnp.int32, (1, tokens), 1)

    def place(b, ranks):
        owner = dest_ref[first + b]
        fill = fill_ref[first + b]
        start = count[owner]
        count[owner] = start + fill
        inner = token - b * BLK
        return jnp.where((inner >= 0) & (inner < fill), start + inner, ranks)

    ranks = lax.fori_loop(0, blocks, place, jnp.full((1, tokens), -1, jnp.int32))
    wanted = base + at_ref[1] * size + lax.broadcasted_iota(jnp.int32, (size, tokens), 0)
    pick = (wanted == ranks).astype(jnp.bfloat16)
    for q in range(n):
        packed[q] = jnp.dot(
            pick, x_ref[:, q * part : (q + 1) * part], preferred_element_type=jnp.float32
        ).astype(packed.dtype)
        store(q).start()
    for q in range(n):
        store(q).wait()


def pack(x_prompt, fill, dest, at, n, base, size):
    tokens, width = x_prompt.shape
    part = width // n
    return pl.pallas_call(
        functools.partial(pack_kernel, base),
        grid_spec=pltpu.PrefetchScalarGridSpec(
            num_scalar_prefetch=3,
            grid=(1,),
            in_specs=[pl.BlockSpec(memory_space=pltpu.VMEM)],
            out_specs=pl.BlockSpec(memory_space=pl.ANY),
            scratch_shapes=[
                pltpu.VMEM((n, size, part), jnp.bfloat16),
                pltpu.SMEM((n,), jnp.int32),
                pltpu.SemaphoreType.DMA((n,)),
            ],
        ),
        out_shape=jax.ShapeDtypeStruct((n, size, part), jnp.bfloat16),
        compiler_params=pltpu.CompilerParams(vmem_limit_bytes=16 * MIB),
        cost_estimate=pl.CostEstimate(
            flops=2 * size * tokens * width, bytes_accessed=64 * MIB, transcendentals=0
        ),
        name="pack_live_tokens",
    )(at, fill, dest, x_prompt)


def tile_cuts(lanes):
    return [0] + list(range(min(256, lanes), lanes, 128)) + [lanes]


def near_lanes(lanes):
    return min(lanes, -(-lanes * 3 // 5 // 128) * 128)


def widen(core, n, refs, wide, base, first, last):
    length = refs[0].shape[0] // n
    tokens = wide.shape[0] // n

    @pl.loop(first, last)
    def _(s):
        for j, ref in enumerate(refs):
            side = core if j == 0 else 1 - core
            to = pl.multiple_of(s * tokens + base + side * length, BLK)
            wide[pl.ds(to, length), :] = ref[
                pl.ds(pl.multiple_of(s * length, length), length), :
            ].astype(wide.dtype)


def span_copies(refs, buffer, sem):
    cuts = sem.shape[1]
    span = buffer.shape[1] // cuts
    return [
        [
            pltpu.make_async_copy(
                ref.at[pl.ds(i * span, span)], buffer.at[j, pl.ds(i * span, span)], sem.at[j, i]
            )
            for j, ref in enumerate(refs)
        ]
        for i in range(cuts)
    ]


def load_tokens(n, core, over, x_refs, there, held, more, wide, sem, others):
    main = span_copies(x_refs[: 2 - len(there)], held, sem)
    for pair in main:
        for copy in pair:
            copy.start()
    for copy in others:
        copy.start()
    for i, pair in enumerate(main):
        for copy in pair:
            copy.wait()
        parts = [held.at[j] for j in range(2 - len(there))] + there
        widen(core, n, parts, wide, 0, i * n // len(main), (i + 1) * n // len(main))

    @pl.when(over != 0)
    def _():
        rest = span_copies(x_refs[2:], more, sem)
        for pair in rest:
            for copy in pair:
                copy.start()
        for pair in rest:
            for copy in pair:
                copy.wait()
        base = wide.shape[0] // n - 2 * more.shape[1] // n
        widen(core, n, [more.at[0], more.at[1]], wide, base, 0, n)


def list_tile(meta_ref, first, count, wide, tile):
    for i in range(0, count, 2):
        pair = [
            wide[pl.ds(pl.multiple_of(meta_ref[first + i + j], BLK), BLK), :] for j in range(2)
        ]
        tile[i * BLK : (i + 2) * BLK, :] = jnp.concatenate(pair).astype(tile.dtype)
    return tile[: count * BLK, :]


def key_kernel(query_ref, weight_ref, out_ref):
    group = out_ref.shape[1] // query_ref.shape[0]
    hd = query_ref.shape[2]
    h = pl.program_id(0)
    for i in range(query_ref.shape[1] // group):

        @pl.when(h == i)
        def _(i=i):
            query = query_ref[:, i * group : (i + 1) * group, :].astype(jnp.float32)
            out_ref[0] = lax.dot_general(
                query.reshape(-1, hd).astype(jnp.bfloat16),
                weight_ref[0, :, :hd],
                (((1,), (1,)), ((), ())),
                preferred_element_type=jnp.float32,
            ).astype(out_ref.dtype)


def score_kernel(n, rows, meta_ref, *refs):
    x_refs, keyed_refs, (row_ref, near_ref, rest_ref) = refs[:4], refs[4:6], refs[6:9]
    held, more, wide, tile, keyed, sem, keyed_sem = refs[9:]
    step = pl.program_id(0)
    part = wide.shape[1]
    near = near_ref.shape[2]
    lanes = near + rest_ref.shape[2]
    cuts = tile_cuts(lanes)
    groups = lanes // BLK
    at_size = n * groups
    q = meta_ref[at_size + n] ^ reversed_bits(step, n)
    kvh, per = keyed.shape[0], keyed.shape[1] // n
    group = per // rows

    def load(i):
        span = n // 2 * per
        return [
            pltpu.make_async_copy(
                keyed_refs[i].at[h], keyed.at[h, pl.ds(i * span, span)], keyed_sem.at[i, h]
            )
            for h in range(kvh)
        ]

    @pl.when(step == 0)
    def _():
        load_tokens(
            n, meta_ref[at_size + n + 1], meta_ref[at_size + n + 2], x_refs, [], held, more, wide, sem,
            load(0) + load(1),
        )

    for i in range(2):

        @pl.when(step == i * (n // 2))
        def _(i=i):
            for copy in load(i):
                copy.wait()

    def one(t):
        here = slice(cuts[t], cuts[t + 1])
        count = (cuts[t + 1] - cuts[t]) // BLK
        raw = lax.dot_general(
            keyed[:, pl.ds(pl.multiple_of(step * per, per), per), :].reshape(kvh * per, part),
            list_tile(meta_ref, q * groups + cuts[t] // BLK, count, wide, tile),
            (((1,), (1,)), ((), ())),
            preferred_element_type=jnp.float32,
        ).reshape(kvh, rows, group, count * BLK)
        owner_row = row_ref[0, :, here]
        picked = jnp.zeros((kvh, group, count * BLK), jnp.float32)
        for r in range(rows):
            picked = picked + jnp.where((owner_row == r)[None], raw[:, r], 0.0)
        picked = picked.reshape(kvh * group, -1).astype(near_ref.dtype)
        if cuts[t] < near:
            near_ref[0, :, here] = picked
        else:
            rest_ref[0, :, cuts[t] - near : cuts[t + 1] - near] = picked

    one(0)
    for t in range(1, len(cuts) - 1):
        pl.when(meta_ref[at_size + q] > cuts[t])(functools.partial(one, t))


def weight_kernel(scale, count, *refs):
    part_refs, row_refs = refs[:count], refs[count : 2 * count]
    top_ref, sum_ref = refs[2 * count : 2 * count + 2]
    w_refs, share_ref = refs[2 * count + 2 : -1], refs[-1]
    n = part_refs[0].shape[0]
    scores, owner_rows = [], []
    for part_ref, row_ref in zip(part_refs, row_refs):
        got = part_ref[0].astype(jnp.float32)
        for i in range(1, n):
            got = got + part_ref[i].astype(jnp.float32)
        scores.append(got * scale)
        owner_rows.append(row_ref[...])
    weights = [jnp.zeros(s.shape, jnp.float32) for s in scores]
    for r in range(top_ref.shape[0]):
        own = [jnp.where(o == r, s, -jnp.inf) for o, s in zip(owner_rows, scores)]
        cache_top = top_ref[r]
        top = cache_top
        for o in own:
            top = jnp.maximum(top, jnp.max(o, 1, keepdims=True))
        held = [jnp.exp(o - top) for o in own]
        fade = jnp.exp(cache_top - top)
        total = sum_ref[r] * fade
        for h in held:
            total = total + jnp.sum(h, 1, keepdims=True)
        weights = [w + h / total for w, h in zip(weights, held)]
        share_ref[r] = fade / total
    for w, w_ref in zip(weights, w_refs):
        for i in range(n):
            w_ref[i] = w.astype(w_ref.dtype)


def list_copies(n, lanes, sizes, source, target, sem):
    cuts = tile_cuts(lanes)

    def copies(o):
        for t in range(len(cuts) - 1):
            here = pl.ds(cuts[t], cuts[t + 1] - cuts[t])
            copy = pltpu.make_async_copy(source.at[o, here], target.at[o, here], sem.at[o, t])
            yield (True if t == 0 else sizes(o) > cuts[t]), copy

    return copies


def list_kernel(n, meta_ref, *refs):
    x_refs, (_, out_ref, held, more, wide, lists, sem, out_sem) = refs[:4], refs[4:]
    q = pl.program_id(0)
    lanes = lists.shape[1]
    cuts = tile_cuts(lanes)
    groups = lanes // BLK
    at_size = n * groups
    copies = list_copies(n, lanes, lambda o: meta_ref[at_size + o], lists, out_ref, out_sem)

    @pl.when(q == 0)
    def _():
        load_tokens(
            n, meta_ref[at_size + n + 1], meta_ref[at_size + n + 2], x_refs, [], held, more, wide,
            sem, [],
        )

    for t, (used, copy) in enumerate(copies(q)):

        @pl.when(used)
        def _(t=t, copy=copy):
            list_tile(
                meta_ref, q * groups + cuts[t] // BLK, (cuts[t + 1] - cuts[t]) // BLK, wide,
                lists.at[q, cuts[t] : cuts[t + 1]],
            )
            copy.start()

    @pl.when(q == n - 1)
    def _():
        for o in range(n):
            for used, copy in copies(o):
                pl.when(used)(copy.wait)


def value_kernel(n, rows, count, meta_ref, *refs):
    w_refs, (row_ref, list_ref, weight_ref, out_ref) = refs[:count], refs[count : count + 4]
    values, lists, acc, mixed, value_sem, sem = refs[count + 4 :]
    q = pl.program_id(0)
    kvh, _, hd = values.shape
    load_values = [
        pltpu.make_async_copy(
            weight_ref.at[h, :, pl.ds(hd, hd)], values.at[h], value_sem.at[h]
        )
        for h in range(kvh)
    ]
    _, heads, near = w_refs[0].shape
    lanes = lists.shape[1]
    per = rows * heads // kvh
    cuts = tile_cuts(lanes)
    at_size = n * lanes // BLK
    size = meta_ref[at_size + q]
    copies = list_copies(n, lanes, lambda o: meta_ref[at_size + o], list_ref, lists, sem)
    ahead = min(3, n)

    def fetch(o):
        for used, copy in copies(o):
            pl.when(used)(copy.start)

    @pl.when(q == 0)
    def _():
        for o in range(ahead):
            fetch(o)

    pl.when(q + ahead < n)(lambda: fetch(jnp.minimum(q + ahead, n - 1)))

    @pl.when(q == n // 2)
    def _():
        for load in load_values:
            load.start()

    for used, copy in copies(q):
        pl.when(used)(copy.wait)

    def one(t):
        here = slice(cuts[t], cuts[t + 1])
        width = cuts[t + 1] - cuts[t]
        piece = 0 if cuts[t] < near else 1
        weights = w_refs[piece][0, :, cuts[t] - piece * near : cuts[t + 1] - piece * near]
        weights = weights.astype(jnp.float32).reshape(kvh, 1, heads // kvh, width)
        owner_row = row_ref[0, :, here]
        spread = jnp.concatenate(
            [jnp.where((owner_row == r)[None, None], weights, 0.0) for r in range(rows)], 1
        ).reshape(kvh * per, width)
        got = jnp.dot(
            spread.astype(jnp.bfloat16), lists[q, here, :], preferred_element_type=jnp.float32
        )
        if t == 0:
            pl.when(size <= cuts[1])(lambda: keep(got))

            @pl.when(size > cuts[1])
            def _():
                acc[...] = got

        else:
            acc[...] += got

    def keep(sums):
        for h in range(kvh):
            mixed[h, pl.ds(pl.multiple_of(q * per, per), per), :] = sums[
                h * per : (h + 1) * per
            ].astype(mixed.dtype)

    one(0)
    for t in range(1, len(cuts) - 1):
        if cuts[t] < near or count > 1:
            pl.when(size > cuts[t])(functools.partial(one, t))
    pl.when(size > cuts[1])(lambda: keep(acc[...]))

    @pl.when(q == n - 1)
    def _():
        for load in load_values:
            load.wait()
        for h in range(kvh):
            done = jnp.dot(mixed[h], values[h], preferred_element_type=jnp.float32)
            done = done.reshape(2, n // 2, per, done.shape[1]).astype(out_ref.dtype)
            for side in range(2):
                out_ref[:, side, h] = done[side]


def half_sum_kernel(side_ref, parts_ref, kept_ref, send_ref, mine_ref):
    half, sides, kvh, per, hd = parts_ref.shape
    rows, heads = kept_ref.shape[:2]
    group = heads // kvh
    for side in range(sides):
        own = side_ref[0] == side
        for h in range(kvh):
            terms = parts_ref[0, side, h].astype(jnp.float32)
            for i in range(1, half):
                terms = terms + parts_ref[i, side, h].astype(jnp.float32)
            kept = jnp.concatenate(
                [kept_ref[r, h * group : (h + 1) * group, :] for r in range(rows)]
            )
            terms = terms + jnp.where(own, kept, 0.0)
            mine_ref[side, h] = terms
            send_ref[side, h] = terms.astype(send_ref.dtype)


def whole_sum_kernel(mine_ref, got_ref, out_ref, total):
    sides, kvh, per, _ = mine_ref.shape
    rows = out_ref.shape[0] // sides
    group = per // rows
    total[...] = mine_ref[...] + got_ref[...].astype(jnp.float32)
    for h in range(kvh):
        for g in range(group):
            column = [
                total[side, h, pl.ds(g, rows, stride=group), :] for side in range(sides)
            ]
            head = h * group + g
            hd = column[0].shape[1]
            out_ref[:, head * hd : (head + 1) * hd] = jnp.concatenate(column).astype(
                out_ref.dtype
            )


def stage_kernel(after_ref, weight_ref, out_ref, sem):
    cuts = sem.shape[0]
    span = out_ref.shape[0] // cuts
    copies = [
        pltpu.make_async_copy(
            weight_ref.at[pl.ds(i * span, span)], out_ref.at[pl.ds(i * span, span)], sem.at[i]
        )
        for i in range(cuts)
    ]
    for copy in copies:
        copy.start()
    for copy in copies:
        copy.wait()


def order_kernel(n, me_ref, own_ref, got_ref, out_ref):
    half = n // 2
    rows = own_ref.shape[0] // n
    for q in range(0, n, 2):
        pair = []
        for owner in (q, q + 1):
            block = ((me_ref[0] % half) ^ (owner % half)) * 2 + owner // half
            here = pl.ds(pl.multiple_of(block * rows, rows), rows)
            pair.append(own_ref[here, :] + got_ref[here, :])
        out_ref[q * rows : (q + 2) * rows, :] = jnp.concatenate(pair).astype(out_ref.dtype)


def with_partner(x, k, n):
    return lax.ppermute(x, "pool", [(i, i ^ k) for i in range(n)])


def from_rest(held, n):
    k = n // 4
    while k >= 2:
        held = jnp.concatenate([held, with_partner(held, k, n)])
        k //= 2
    return held


def reversed_bits(k, n):
    out, bit = 0, 1
    while bit < n:
        out = out + (k // bit) % 2 * (n // 2 // bit)
        bit *= 2
    return out


def local(
    x_prompt, kv_weight, block_dest, block_row, block_fill, queries, kv_cache, cache_len, out_weight
):
    n = lax.axis_size("pool")
    ntp = lax.axis_size("tp")
    me = lax.axis_index("pool").astype(jnp.int32)
    core = lax.axis_index("tp").astype(jnp.int32)
    tokens, width = x_prompt.shape
    part = width // n
    kvh = kv_weight.shape[1]
    hd = kv_weight.shape[2] // 2
    rows, heads = queries.shape[0], queries.shape[1]
    group = heads // kvh
    per = rows * group
    cache_slots = kv_cache.shape[1]
    blocks = tokens // BLK
    cap = max(2, 2 * blocks // n)
    window = cap * BLK + BLK
    lanes = -(-n * window // 128) * 128
    half = tokens // ntp
    scale = 1.0 / hd**0.5
    swap = [(i, (i + 1) % ntp) for i in range(ntp)]

    size = half * 3 // 4
    extra = half - size
    at = jnp.stack([me, core])
    pack_fill, pack_dest = block_fill, block_dest[:, 0]
    packed = pack(x_prompt, pack_fill, pack_dest, at, n, 0, size)
    dest = pack_dest
    far = with_partner(queries, n // 2, n)
    packed, far, dest, block_row, block_fill, kv_weight = lax.optimization_barrier(
        (packed, far, dest, block_row, block_fill, kv_weight)
    )
    kv_weight = kv_weight.transpose(1, 0, 2)
    even = from_rest(jnp.stack([queries, far]), n)
    mine = lax.all_to_all(packed, "pool", 0, 0, tiled=True).reshape(n * size, part)

    index = jnp.arange(n * blocks, dtype=jnp.int32)
    sender = index // blocks
    kin = sender[None, :] == sender[:, None]
    lower = kin & (dest[None, :] < dest[:, None])
    level = kin & (dest[None, :] == dest[:, None]) & (index[None, :] < index[:, None])
    before = jnp.sum(jnp.where(lower, block_fill[None, :], 0), 1)
    within = jnp.sum(jnp.where(level, block_fill[None, :], 0), 1)
    pair = jnp.arange(n * n, dtype=jnp.int32)
    to, by = pair // n, pair % n
    owned = dest[None, :] == to[:, None]
    sent = sender[None, :] == by[:, None]
    earlier = sent & (dest[None, :] < to[:, None])
    offset = jnp.sum(jnp.where(earlier, block_fill[None, :], 0), 1)
    amount = jnp.sum(jnp.where(sent & owned, block_fill[None, :], 0), 1)
    runs = jnp.where(amount > 0, (offset % BLK + amount + BLK - 1) // BLK * BLK, 0)
    runs_by = runs.reshape(n, n)
    prior = jnp.arange(n)[:, None] < jnp.arange(n)[None, :]
    targets = jnp.sum(jnp.where(prior[None], runs_by[:, :, None], 0), 1)
    list_rows = jnp.sum(runs_by, 1)
    targets = targets.reshape(-1)
    sources = by * tokens + offset // BLK * BLK
    group_at = jnp.arange(n * lanes // BLK, dtype=jnp.int32) * BLK
    skip = group_at[:, None] - (to * lanes + targets)[None, :]
    group_rows = jnp.sum(
        jnp.where((skip >= 0) & (skip < runs[None, :]), sources[None, :] + skip, 0), 1
    )
    mine_pair = (dest * n + sender)[:, None] == pair[None, :]
    start = (
        dest * lanes
        + jnp.sum(jnp.where(mine_pair, targets[None, :], 0), 1)
        + before % BLK
        + within
    )
    spot = jnp.arange(n * lanes, dtype=jnp.int32)[:, None]
    inside = (spot >= start[None, :]) & (spot < (start + block_fill)[None, :])
    rowof = jnp.sum(jnp.where(inside, (block_row + 1)[None, :], 0), 1) - 1
    rowof = rowof.reshape(n, 1, lanes)

    near = near_lanes(lanes)
    most = jnp.stack([jnp.max(jnp.sum(block_fill.reshape(n, blocks), 1)), jnp.max(list_rows)])
    groups = lax.axis_size("groups")
    k = 1
    while k < groups:
        most = jnp.maximum(
            most, lax.ppermute(most, "groups", [(i, i ^ k) for i in range(groups)])
        )
        k *= 2
    over, longer = most[0] > ntp * size, most[1] > near

    def exchange_rest():
        rest = pack(x_prompt, pack_fill, pack_dest, at, n, ntp * size, extra)
        rest = lax.all_to_all(rest, "pool", 0, 0, tiled=True).reshape(n * extra, part)
        return rest, lax.ppermute(rest, "tp", swap)

    def no_rest():
        return (jnp.zeros((n * extra, part), jnp.bfloat16),) * 2

    more_mine, more_other = lax.cond(over, exchange_rest, no_rest)
    meta = jnp.concatenate(
        [group_rows, list_rows, jnp.stack([me, core, over.astype(jnp.int32)])]
    )

    def through_keys(held):
        held = held.reshape(n // 2 * rows, heads, hd)
        return pl.pallas_call(
            key_kernel,
            grid=(kvh,),
            in_specs=[
                pl.BlockSpec(held.shape, lambda h: (0, 0, 0)),
                pl.BlockSpec((1, part, 2 * hd), lambda h: (h, 0, 0)),
            ],
            out_specs=pl.BlockSpec((1, n // 2 * per, part), lambda h: (h, 0, 0)),
            out_shape=jax.ShapeDtypeStruct((kvh, n // 2 * per, part), jnp.bfloat16),
            compiler_params=pltpu.CompilerParams(vmem_limit_bytes=16 * MIB),
            cost_estimate=pl.CostEstimate(flops=0, bytes_accessed=1024, transcendentals=0),
            name="key_projection",
        )(held, kv_weight)

    keyed_even = through_keys(even)
    keyed_odd = through_keys(with_partner(even, 1, n))

    mine, meta, rowof, keyed_even, keyed_odd = lax.optimization_barrier(
        (mine, meta, rowof, keyed_even, keyed_odd)
    )
    other = lax.ppermute(mine, "tp", swap)

    anywhere = pl.BlockSpec(memory_space=pl.ANY)
    row_spec = pl.BlockSpec((1, 1, lanes), lambda q, m: (q, 0, 0))
    slot_specs = [
        pl.BlockSpec((1, heads, length), lambda q, m: (q, 0, 0)) for length in (near, lanes - near)
    ]
    slot_shapes = [
        jax.ShapeDtypeStruct((n, heads, length), jnp.bfloat16) for length in (near, lanes - near)
    ]
    in_vmem = pl.BlockSpec(memory_space=pltpu.VMEM)
    x_parts = (mine, other, more_mine, more_other)
    x_scratch = [
        pltpu.VMEM((ntp, n * size, part), jnp.bfloat16),
        pltpu.VMEM((ntp, n * extra, part), jnp.bfloat16),
        pltpu.VMEM((n * tokens, part), jnp.float32),
    ]
    at_me = n * lanes // BLK + n

    def owner(i, m):
        return m[at_me] ^ reversed_bits(i, n)

    score_near, score_rest = pl.pallas_call(
        functools.partial(score_kernel, n, rows),
        grid_spec=pltpu.PrefetchScalarGridSpec(
            num_scalar_prefetch=1,
            grid=(n,),
            in_specs=[
                *[anywhere] * 6,
                pl.BlockSpec((1, 1, lanes), lambda i, m: (owner(i, m), 0, 0)),
            ],
            out_specs=[
                pl.BlockSpec((1, heads, length), lambda i, m: (owner(i, m), 0, 0))
                for length in (near, lanes - near)
            ],
            scratch_shapes=[
                *x_scratch,
                pltpu.VMEM((tile_cuts(lanes)[1], part), jnp.bfloat16),
                pltpu.VMEM((kvh, n * per, part), jnp.bfloat16),
                pltpu.SemaphoreType.DMA((ntp, 4)),
                pltpu.SemaphoreType.DMA((2, kvh)),
            ],
        ),
        out_shape=slot_shapes,
        compiler_params=pltpu.CompilerParams(vmem_limit_bytes=24 * MIB),
        name="prompt_scores",
    )(meta, *x_parts, keyed_even, keyed_odd, rowof)

    my_rows = lax.dynamic_index_in_dim(rowof, me, 0, keepdims=False)

    def exchange_weights(*scores):
        count = len(scores)
        parts = [lax.all_to_all(s, "pool", 0, 0, tiled=True) for s in scores]
        query = queries.reshape(rows, kvh, group, hd)
        cache_scores = (
            jnp.einsum(
                "rhgd,rthd->rhgt", query, kv_cache[:, :, :, :hd], preferred_element_type=jnp.float32
            )
            * scale
        )
        cache_live = jnp.arange(cache_slots, dtype=jnp.int32)[None, :] < cache_len[:, None]
        cache_scores = jnp.where(cache_live[:, None, None, :], cache_scores, -jnp.inf)
        cache_top = jnp.max(cache_scores, -1, keepdims=True)
        cache_exp = jnp.exp(cache_scores - cache_top)
        cache_sum = jnp.sum(cache_exp, -1, keepdims=True)
        row_parts = [my_rows[:, :near], my_rows[:, near:]][:count]
        *weights, share = pl.pallas_call(
            functools.partial(weight_kernel, scale, count),
            out_shape=[*slot_shapes[:count], jax.ShapeDtypeStruct((rows, heads, 1), jnp.float32)],
            compiler_params=pltpu.CompilerParams(vmem_limit_bytes=8 * MIB),
            name="softmax_weights",
        )(
            *parts,
            *row_parts,
            cache_top.reshape(rows, heads, 1),
            cache_sum.reshape(rows, heads, 1),
        )
        lists = pl.pallas_call(
            functools.partial(list_kernel, n),
            grid_spec=pltpu.PrefetchScalarGridSpec(
                num_scalar_prefetch=1,
                grid=(n,),
                in_specs=[anywhere] * 5,
                out_specs=anywhere,
                scratch_shapes=[
                    *x_scratch,
                    pltpu.VMEM((n, lanes, part), jnp.bfloat16),
                    pltpu.SemaphoreType.DMA((ntp, 4)),
                    pltpu.SemaphoreType.DMA((n, len(tile_cuts(lanes)) - 1)),
                ],
            ),
            out_shape=jax.ShapeDtypeStruct((n, lanes, part), jnp.bfloat16),
            compiler_params=pltpu.CompilerParams(vmem_limit_bytes=56 * MIB),
            cost_estimate=pl.CostEstimate(
                flops=0, bytes_accessed=16 * MIB, transcendentals=0
            ),
            name="owner_lists",
        )(meta, *x_parts, weights[0])
        weights = [lax.all_to_all(w, "pool", 0, 0, tiled=True) for w in weights]
        cached = jnp.einsum(
            "rhgt,rthd->rhgd",
            cache_exp.astype(jnp.bfloat16),
            kv_cache[:, :, :, hd:],
            preferred_element_type=jnp.float32,
        )
        terms = pl.pallas_call(
            functools.partial(value_kernel, n, rows, count),
            grid_spec=pltpu.PrefetchScalarGridSpec(
                num_scalar_prefetch=1,
                grid=(n,),
                in_specs=[*slot_specs[:count], row_spec, anywhere, anywhere],
                out_specs=pl.BlockSpec((n // 2, 2, kvh, per, hd), lambda q, m: (0, 0, 0, 0, 0)),
                scratch_shapes=[
                    pltpu.VMEM((kvh, part, hd), jnp.bfloat16),
                    pltpu.VMEM((n, lanes, part), jnp.bfloat16),
                    pltpu.VMEM((kvh * per, part), jnp.float32),
                    pltpu.VMEM((kvh, n * per, part), jnp.bfloat16),
                    pltpu.SemaphoreType.DMA((kvh,)),
                    pltpu.SemaphoreType.DMA((n, len(tile_cuts(lanes)) - 1)),
                ],
            ),
            out_shape=jax.ShapeDtypeStruct((n // 2, 2, kvh, per, hd), jnp.bfloat16),
            compiler_params=pltpu.CompilerParams(vmem_limit_bytes=56 * MIB),
            name="weighted_values",
        )(meta, *weights, rowof, lists, kv_weight)
        return terms, cached.reshape(rows, heads, hd) * share

    terms, kept = lax.cond(
        longer,
        lambda: exchange_weights(score_near, score_rest),
        lambda: exchange_weights(score_near),
    )

    halves = [list(range(n // 2)), list(range(n // 2, n))]
    term_parts = lax.all_to_all(
        terms, "pool", 0, 0, axis_index_groups=halves, tiled=True
    )
    pair_shape = (2, kvh, per, hd)
    send, held = pl.pallas_call(
        half_sum_kernel,
        in_specs=[pl.BlockSpec(memory_space=pltpu.SMEM), in_vmem, in_vmem],
        out_shape=[
            jax.ShapeDtypeStruct(pair_shape, jnp.bfloat16),
            jax.ShapeDtypeStruct(pair_shape, jnp.float32),
        ],
        compiler_params=pltpu.CompilerParams(vmem_limit_bytes=8 * MIB),
        name="half_pool_sum",
    )((me // (n // 2)).reshape(1), term_parts, kept)
    attended = pl.pallas_call(
        whole_sum_kernel,
        out_shape=jax.ShapeDtypeStruct((2 * rows, heads * hd), jnp.bfloat16),
        scratch_shapes=[pltpu.VMEM(pair_shape, jnp.float32)],
        compiler_params=pltpu.CompilerParams(vmem_limit_bytes=8 * MIB),
        name="attended_sum",
    )(held, with_partner(send, n // 2, n))

    staged = pl.pallas_call(
        stage_kernel,
        in_specs=[anywhere, pl.BlockSpec(memory_space=pltpu.HBM)],
        out_specs=in_vmem,
        out_shape=jax.ShapeDtypeStruct(out_weight.shape, jnp.bfloat16),
        scratch_shapes=[pltpu.SemaphoreType.DMA((8,))],
        compiler_params=pltpu.CompilerParams(vmem_limit_bytes=16 * MIB),
        cost_estimate=pl.CostEstimate(
            flops=0, bytes_accessed=2 * out_weight.size * 2, transcendentals=0
        ),
        name="stage_out_weight",
    )(send, out_weight)

    everyone = [attended] + [with_partner(attended, k, n) for k in range(1, n // 2)]
    product = jnp.dot(
        jnp.concatenate(everyone), staged, preferred_element_type=jnp.float32
    )
    cols = out_weight.shape[1] // ntp
    half_spec = pl.BlockSpec((n * rows, cols), lambda i, m: (0, 0))
    own = lax.dynamic_slice_in_dim(product, core * cols, cols, 1)
    away = lax.dynamic_slice_in_dim(product, (1 - core) * cols, cols, 1)
    got = lax.ppermute(away, "tp", swap)
    return pl.pallas_call(
        functools.partial(order_kernel, n),
        grid_spec=pltpu.PrefetchScalarGridSpec(
            num_scalar_prefetch=1,
            grid=(1,),
            in_specs=[half_spec] * 2,
            out_specs=half_spec,
        ),
        out_shape=jax.ShapeDtypeStruct((n * rows, cols), jnp.bfloat16),
        compiler_params=pltpu.CompilerParams(vmem_limit_bytes=4 * MIB),
        name="order_rows",
    )(me.reshape(1), own, got)


def solution(mesh):
    in_specs = (
        P(("groups", "pool"), None),
        P("pool", "tp", None),
        P("groups", None),
        P("groups"),
        P("groups"),
        P(("groups", "pool"), "tp", None),
        P(("groups", "pool"), None, "tp", None),
        P(("groups", "pool")),
        P("tp", "pool"),
    )
    out_specs = P("groups", ("pool", "tp"))
    return jax.shard_map(local, mesh=mesh, in_specs=in_specs, out_specs=out_specs, check_vma=False)
```

```python
import functools

import jax
import jax.numpy as jnp
from jax import lax
from jax.experimental import pallas as pl
from jax.experimental.pallas import tpu as pltpu
from jax.sharding import PartitionSpec as P

BLK = 8
MIB = 1 << 20


def pack_kernel(base, at_ref, fill_ref, dest_ref, x_ref, out_ref, packed, count, out_sem):
    n, size, part = packed.shape
    tokens = x_ref.shape[0]
    blocks = tokens // BLK

    def store(q):
        return pltpu.make_async_copy(packed.at[q], out_ref.at[q], out_sem.at[q])

    first = at_ref[0] * blocks
    for q in range(n):
        count[q] = 0

    @pl.loop(0, blocks)
    def _(b):
        owner = dest_ref[first + b]
        count[owner] = count[owner] + fill_ref[first + b]

    def starts(q, total):
        here = count[q]
        count[q] = total
        return total + here

    lax.fori_loop(0, n, starts, jnp.int32(0))
    token = lax.broadcasted_iota(jnp.int32, (1, tokens), 1)

    def place(b, ranks):
        owner = dest_ref[first + b]
        fill = fill_ref[first + b]
        start = count[owner]
        count[owner] = start + fill
        inner = token - b * BLK
        return jnp.where((inner >= 0) & (inner < fill), start + inner, ranks)

    ranks = lax.fori_loop(0, blocks, place, jnp.full((1, tokens), -1, jnp.int32))
    wanted = base + at_ref[1] * size + lax.broadcasted_iota(jnp.int32, (size, tokens), 0)
    pick = (wanted == ranks).astype(jnp.bfloat16)
    for q in range(n):
        packed[q] = jnp.dot(
            pick, x_ref[:, q * part : (q + 1) * part], preferred_element_type=jnp.float32
        ).astype(packed.dtype)
        store(q).start()
    for q in range(n):
        store(q).wait()


def pack(x_prompt, fill, dest, at, n, base, size):
    tokens, width = x_prompt.shape
    part = width // n
    return pl.pallas_call(
        functools.partial(pack_kernel, base),
        grid_spec=pltpu.PrefetchScalarGridSpec(
            num_scalar_prefetch=3,
            grid=(1,),
            in_specs=[pl.BlockSpec(memory_space=pltpu.VMEM)],
            out_specs=pl.BlockSpec(memory_space=pl.ANY),
            scratch_shapes=[
                pltpu.VMEM((n, size, part), jnp.bfloat16),
                pltpu.SMEM((n,), jnp.int32),
                pltpu.SemaphoreType.DMA((n,)),
            ],
        ),
        out_shape=jax.ShapeDtypeStruct((n, size, part), jnp.bfloat16),
        compiler_params=pltpu.CompilerParams(vmem_limit_bytes=16 * MIB),
        cost_estimate=pl.CostEstimate(
            flops=2 * size * tokens * width, bytes_accessed=64 * MIB, transcendentals=0
        ),
        name="pack_live_tokens",
    )(at, fill, dest, x_prompt)


def tile_cuts(lanes):
    return [0] + list(range(min(256, lanes), lanes, 128)) + [lanes]


def near_lanes(lanes):
    return min(lanes, -(-lanes * 3 // 5 // 128) * 128)


def widen(core, n, refs, wide, base, first, last):
    length = refs[0].shape[0] // n
    tokens = wide.shape[0] // n

    @pl.loop(first, last)
    def _(s):
        for j, ref in enumerate(refs):
            side = core if j == 0 else 1 - core
            to = pl.multiple_of(s * tokens + base + side * length, BLK)
            wide[pl.ds(to, length), :] = ref[
                pl.ds(pl.multiple_of(s * length, length), length), :
            ].astype(wide.dtype)


def span_copies(refs, buffer, sem):
    cuts = sem.shape[1]
    span = buffer.shape[1] // cuts
    return [
        [
            pltpu.make_async_copy(
                ref.at[pl.ds(i * span, span)], buffer.at[j, pl.ds(i * span, span)], sem.at[j, i]
            )
            for j, ref in enumerate(refs)
        ]
        for i in range(cuts)
    ]


def load_tokens(n, core, over, x_refs, there, held, more, wide, sem, others):
    main = span_copies(x_refs[: 2 - len(there)], held, sem)
    for pair in main:
        for copy in pair:
            copy.start()
    for copy in others:
        copy.start()
    for i, pair in enumerate(main):
        for copy in pair:
            copy.wait()
        parts = [held.at[j] for j in range(2 - len(there))] + there
        widen(core, n, parts, wide, 0, i * n // len(main), (i + 1) * n // len(main))

    @pl.when(over != 0)
    def _():
        rest = span_copies(x_refs[2:], more, sem)
        for pair in rest:
            for copy in pair:
                copy.start()
        for pair in rest:
            for copy in pair:
                copy.wait()
        base = wide.shape[0] // n - 2 * more.shape[1] // n
        widen(core, n, [more.at[0], more.at[1]], wide, base, 0, n)


def list_tile(meta_ref, first, count, wide, tile):
    for i in range(0, count, 2):
        pair = [
            wide[pl.ds(pl.multiple_of(meta_ref[first + i + j], BLK), BLK), :] for j in range(2)
        ]
        tile[i * BLK : (i + 2) * BLK, :] = jnp.concatenate(pair).astype(tile.dtype)
    return tile[: count * BLK, :]


def key_kernel(query_ref, weight_ref, out_ref):
    group = out_ref.shape[1] // query_ref.shape[0]
    hd = query_ref.shape[2]
    h = pl.program_id(0)
    for i in range(query_ref.shape[1] // group):

        @pl.when(h == i)
        def _(i=i):
            query = query_ref[:, i * group : (i + 1) * group, :].astype(jnp.float32)
            out_ref[0] = lax.dot_general(
                query.reshape(-1, hd).astype(jnp.bfloat16),
                weight_ref[0, :, :hd],
                (((1,), (1,)), ((), ())),
                preferred_element_type=jnp.float32,
            ).astype(out_ref.dtype)


def score_kernel(n, rows, meta_ref, *refs):
    x_refs, keyed_refs, (row_ref, near_ref, rest_ref) = refs[:4], refs[4:6], refs[6:9]
    held, more, wide, tile, keyed, sem, keyed_sem = refs[9:]
    step = pl.program_id(0)
    part = wide.shape[1]
    near = near_ref.shape[2]
    lanes = near + rest_ref.shape[2]
    cuts = tile_cuts(lanes)
    groups = lanes // BLK
    at_size = n * groups
    q = meta_ref[at_size + n] ^ reversed_bits(step, n)
    kvh, per = keyed.shape[0], keyed.shape[1] // n
    group = per // rows

    def load(i):
        span = n // 2 * per
        return [
            pltpu.make_async_copy(
                keyed_refs[i].at[h], keyed.at[h, pl.ds(i * span, span)], keyed_sem.at[i, h]
            )
            for h in range(kvh)
        ]

    @pl.when(step == 0)
    def _():
        load_tokens(
            n, meta_ref[at_size + n + 1], meta_ref[at_size + n + 2], x_refs, [], held, more, wide, sem,
            load(0) + load(1),
        )

    for i in range(2):

        @pl.when(step == i * (n // 2))
        def _(i=i):
            for copy in load(i):
                copy.wait()

    def one(t):
        here = slice(cuts[t], cuts[t + 1])
        count = (cuts[t + 1] - cuts[t]) // BLK
        raw = lax.dot_general(
            keyed[:, pl.ds(pl.multiple_of(step * per, per), per), :].reshape(kvh * per, part),
            list_tile(meta_ref, q * groups + cuts[t] // BLK, count, wide, tile),
            (((1,), (1,)), ((), ())),
            preferred_element_type=jnp.float32,
        ).reshape(kvh, rows, group, count * BLK)
        owner_row = row_ref[0, :, here]
        picked = jnp.zeros((kvh, group, count * BLK), jnp.float32)
        for r in range(rows):
            picked = picked + jnp.where((owner_row == r)[None], raw[:, r], 0.0)
        picked = picked.reshape(kvh * group, -1).astype(near_ref.dtype)
        if cuts[t] < near:
            near_ref[0, :, here] = picked
        else:
            rest_ref[0, :, cuts[t] - near : cuts[t + 1] - near] = picked

    one(0)
    for t in range(1, len(cuts) - 1):
        pl.when(meta_ref[at_size + q] > cuts[t])(functools.partial(one, t))


def weight_kernel(scale, count, *refs):
    part_refs, row_refs = refs[:count], refs[count : 2 * count]
    top_ref, sum_ref = refs[2 * count : 2 * count + 2]
    w_refs, share_ref = refs[2 * count + 2 : -1], refs[-1]
    n = part_refs[0].shape[0]
    scores, owner_rows = [], []
    for part_ref, row_ref in zip(part_refs, row_refs):
        got = part_ref[0].astype(jnp.float32)
        for i in range(1, n):
            got = got + part_ref[i].astype(jnp.float32)
        scores.append(got * scale)
        owner_rows.append(row_ref[...])
    weights = [jnp.zeros(s.shape, jnp.float32) for s in scores]
    for r in range(top_ref.shape[0]):
        own = [jnp.where(o == r, s, -jnp.inf) for o, s in zip(owner_rows, scores)]
        cache_top = top_ref[r]
        top = cache_top
        for o in own:
            top = jnp.maximum(top, jnp.max(o, 1, keepdims=True))
        held = [jnp.exp(o - top) for o in own]
        fade = jnp.exp(cache_top - top)
        total = sum_ref[r] * fade
        for h in held:
            total = total + jnp.sum(h, 1, keepdims=True)
        weights = [w + h / total for w, h in zip(weights, held)]
        share_ref[r] = fade / total
    for w, w_ref in zip(weights, w_refs):
        for i in range(n):
            w_ref[i] = w.astype(w_ref.dtype)


def list_copies(n, lanes, sizes, source, target, sem):
    cuts = tile_cuts(lanes)

    def copies(o):
        for t in range(len(cuts) - 1):
            here = pl.ds(cuts[t], cuts[t + 1] - cuts[t])
            copy = pltpu.make_async_copy(source.at[o, here], target.at[o, here], sem.at[o, t])
            yield (True if t == 0 else sizes(o) > cuts[t]), copy

    return copies


def list_kernel(n, meta_ref, *refs):
    x_refs, (_, out_ref, held, more, wide, lists, sem, out_sem) = refs[:4], refs[4:]
    q = pl.program_id(0)
    lanes = lists.shape[1]
    cuts = tile_cuts(lanes)
    groups = lanes // BLK
    at_size = n * groups
    copies = list_copies(n, lanes, lambda o: meta_ref[at_size + o], lists, out_ref, out_sem)

    @pl.when(q == 0)
    def _():
        load_tokens(
            n, meta_ref[at_size + n + 1], meta_ref[at_size + n + 2], x_refs, [], held, more, wide,
            sem, [],
        )

    for t, (used, copy) in enumerate(copies(q)):

        @pl.when(used)
        def _(t=t, copy=copy):
            list_tile(
                meta_ref, q * groups + cuts[t] // BLK, (cuts[t + 1] - cuts[t]) // BLK, wide,
                lists.at[q, cuts[t] : cuts[t + 1]],
            )
            copy.start()

    @pl.when(q == n - 1)
    def _():
        for o in range(n):
            for used, copy in copies(o):
                pl.when(used)(copy.wait)


def value_kernel(n, rows, count, meta_ref, *refs):
    w_refs, (row_ref, list_ref, weight_ref) = refs[:count], refs[count : count + 3]
    out_refs, scratch = refs[count + 3 : count + 3 + n // 2], refs[count + 3 + n // 2 :]
    values, lists, acc, mixed, value_sem, sem = scratch
    step = pl.program_id(0)
    kvh, _, hd = values.shape
    load_values = [
        pltpu.make_async_copy(
            weight_ref.at[h, :, pl.ds(hd, hd)], values.at[h], value_sem.at[h]
        )
        for h in range(kvh)
    ]
    _, heads, near = w_refs[0].shape
    lanes = lists.shape[1]
    per = rows * heads // kvh
    cuts = tile_cuts(lanes)
    at_size = n * lanes // BLK
    me = meta_ref[at_size + n]
    q = partner_owner(step, me, n)
    size = meta_ref[at_size + q]
    copies = list_copies(n, lanes, lambda o: meta_ref[at_size + o], list_ref, lists, sem)
    ahead = min(3, n)

    def fetch(i):
        for used, copy in copies(partner_owner(i, me, n)):
            pl.when(used)(copy.start)

    @pl.when(step == 0)
    def _():
        for i in range(ahead):
            fetch(i)

    pl.when(step + ahead < n)(lambda: fetch(jnp.minimum(step + ahead, n - 1)))

    @pl.when(step == n // 2)
    def _():
        for load in load_values:
            load.start()

    for used, copy in copies(q):
        pl.when(used)(copy.wait)

    def one(t):
        here = slice(cuts[t], cuts[t + 1])
        width = cuts[t + 1] - cuts[t]
        piece = 0 if cuts[t] < near else 1
        weights = w_refs[piece][0, :, cuts[t] - piece * near : cuts[t + 1] - piece * near]
        weights = weights.astype(jnp.float32).reshape(kvh, 1, heads // kvh, width)
        owner_row = row_ref[0, :, here]
        spread = jnp.concatenate(
            [jnp.where((owner_row == r)[None, None], weights, 0.0) for r in range(rows)], 1
        ).reshape(kvh * per, width)
        got = jnp.dot(
            spread.astype(jnp.bfloat16), lists[q, here, :], preferred_element_type=jnp.float32
        )
        if t == 0:
            pl.when(size <= cuts[1])(lambda: keep(got))

            @pl.when(size > cuts[1])
            def _():
                acc[...] = got

        else:
            acc[...] += got

    def keep(sums):
        for h in range(kvh):
            mixed[h, pl.ds(pl.multiple_of(step * per, per), per), :] = sums[
                h * per : (h + 1) * per
            ].astype(mixed.dtype)

    one(0)
    for t in range(1, len(cuts) - 1):
        if cuts[t] < near or count > 1:
            pl.when(size > cuts[t])(functools.partial(one, t))
    pl.when(size > cuts[1])(lambda: keep(acc[...]))

    @pl.when(step == n - 1)
    def _():
        for load in load_values:
            load.wait()
        for h in range(kvh):
            done = jnp.dot(mixed[h], values[h], preferred_element_type=jnp.float32)
            done = done.astype(jnp.bfloat16)
            for i in range(n):
                out_refs[i // 2][i % 2, h] = done[i * per : (i + 1) * per]


def half_sum_kernel(side_ref, *refs):
    *part_refs, kept_ref, send_ref, mine_ref = refs
    sides, kvh, _, _ = part_refs[0].shape
    rows, heads = kept_ref.shape[:2]
    group = heads // kvh
    for side in range(sides):
        own = side_ref[0] == side
        for h in range(kvh):
            terms = part_refs[0][side, h].astype(jnp.float32)
            for ref in part_refs[1:]:
                terms = terms + ref[side, h].astype(jnp.float32)
            kept = jnp.concatenate(
                [kept_ref[r, h * group : (h + 1) * group, :] for r in range(rows)]
            )
            terms = terms + jnp.where(own, kept, 0.0)
            mine_ref[side, h] = terms
            send_ref[side, h] = terms.astype(send_ref.dtype)


def partner_owner(i, me, n):
    half = n // 2
    return i % 2 * half + ((me % half) ^ (i // 2))


def whole_sum_kernel(mine_ref, got_ref, out_ref, total):
    sides, kvh, per, _ = mine_ref.shape
    rows = out_ref.shape[0] // sides
    group = per // rows
    total[...] = mine_ref[...] + got_ref[...].astype(jnp.float32)
    for h in range(kvh):
        for g in range(group):
            column = [
                total[side, h, pl.ds(g, rows, stride=group), :] for side in range(sides)
            ]
            head = h * group + g
            hd = column[0].shape[1]
            out_ref[:, head * hd : (head + 1) * hd] = jnp.concatenate(column).astype(
                out_ref.dtype
            )


def stage_kernel(after_ref, weight_ref, out_ref, sem):
    cuts = sem.shape[0]
    span = out_ref.shape[0] // cuts
    copies = [
        pltpu.make_async_copy(
            weight_ref.at[pl.ds(i * span, span)], out_ref.at[pl.ds(i * span, span)], sem.at[i]
        )
        for i in range(cuts)
    ]
    for copy in copies:
        copy.start()
    for copy in copies:
        copy.wait()


def order_kernel(n, me_ref, own_ref, got_ref, out_ref):
    half = n // 2
    rows = own_ref.shape[0] // n
    for q in range(0, n, 2):
        pair = []
        for owner in (q, q + 1):
            block = ((me_ref[0] % half) ^ (owner % half)) * 2 + owner // half
            here = pl.ds(pl.multiple_of(block * rows, rows), rows)
            pair.append(own_ref[here, :] + got_ref[here, :])
        out_ref[q * rows : (q + 2) * rows, :] = jnp.concatenate(pair).astype(out_ref.dtype)


def with_partner(x, k, n):
    return lax.ppermute(x, "pool", [(i, i ^ k) for i in range(n)])


def from_rest(held, n):
    k = n // 8
    while k >= 2:
        held = jnp.concatenate([held, with_partner(held, k, n)])
        k //= 2
    return held


def reversed_bits(k, n):
    out, bit = 0, 1
    while bit < n:
        out = out + (k // bit) % 2 * (n // 2 // bit)
        bit *= 2
    return out


def local(
    x_prompt, kv_weight, block_dest, block_row, block_fill, queries, kv_cache, cache_len, out_weight
):
    n = lax.axis_size("pool")
    ntp = lax.axis_size("tp")
    me = lax.axis_index("pool").astype(jnp.int32)
    core = lax.axis_index("tp").astype(jnp.int32)
    tokens, width = x_prompt.shape
    part = width // n
    kvh = kv_weight.shape[1]
    hd = kv_weight.shape[2] // 2
    rows, heads = queries.shape[0], queries.shape[1]
    group = heads // kvh
    per = rows * group
    cache_slots = kv_cache.shape[1]
    blocks = tokens // BLK
    cap = max(2, 2 * blocks // n)
    window = cap * BLK + BLK
    lanes = -(-n * window // 128) * 128
    half = tokens // ntp
    scale = 1.0 / hd**0.5
    swap = [(i, (i + 1) % ntp) for i in range(ntp)]

    size = half * 3 // 4
    extra = half - size
    at = jnp.stack([me, core])
    pack_fill, pack_dest = block_fill, block_dest[:, 0]
    packed = pack(x_prompt, pack_fill, pack_dest, at, n, 0, size)
    dest = pack_dest
    far = [with_partner(queries, k, n) for k in (n // 2, n // 4, n // 2 + n // 4)]
    packed, far, dest, block_row, block_fill, kv_weight = lax.optimization_barrier(
        (packed, far, dest, block_row, block_fill, kv_weight)
    )
    kv_weight = kv_weight.transpose(1, 0, 2)
    even = from_rest(jnp.stack([queries, *far]), n)
    mine = lax.all_to_all(packed, "pool", 0, 0, tiled=True).reshape(n * size, part)

    index = jnp.arange(n * blocks, dtype=jnp.int32)
    sender = index // blocks
    kin = sender[None, :] == sender[:, None]
    lower = kin & (dest[None, :] < dest[:, None])
    level = kin & (dest[None, :] == dest[:, None]) & (index[None, :] < index[:, None])
    before = jnp.sum(jnp.where(lower, block_fill[None, :], 0), 1)
    within = jnp.sum(jnp.where(level, block_fill[None, :], 0), 1)
    pair = jnp.arange(n * n, dtype=jnp.int32)
    to, by = pair // n, pair % n
    owned = dest[None, :] == to[:, None]
    sent = sender[None, :] == by[:, None]
    earlier = sent & (dest[None, :] < to[:, None])
    offset = jnp.sum(jnp.where(earlier, block_fill[None, :], 0), 1)
    amount = jnp.sum(jnp.where(sent & owned, block_fill[None, :], 0), 1)
    runs = jnp.where(amount > 0, (offset % BLK + amount + BLK - 1) // BLK * BLK, 0)
    runs_by = runs.reshape(n, n)
    prior = jnp.arange(n)[:, None] < jnp.arange(n)[None, :]
    targets = jnp.sum(jnp.where(prior[None], runs_by[:, :, None], 0), 1)
    list_rows = jnp.sum(runs_by, 1)
    targets = targets.reshape(-1)
    sources = by * tokens + offset // BLK * BLK
    group_at = jnp.arange(n * lanes // BLK, dtype=jnp.int32) * BLK
    skip = group_at[:, None] - (to * lanes + targets)[None, :]
    group_rows = jnp.sum(
        jnp.where((skip >= 0) & (skip < runs[None, :]), sources[None, :] + skip, 0), 1
    )
    mine_pair = (dest * n + sender)[:, None] == pair[None, :]
    start = (
        dest * lanes
        + jnp.sum(jnp.where(mine_pair, targets[None, :], 0), 1)
        + before % BLK
        + within
    )
    spot = jnp.arange(n * lanes, dtype=jnp.int32)[:, None]
    inside = (spot >= start[None, :]) & (spot < (start + block_fill)[None, :])
    rowof = jnp.sum(jnp.where(inside, (block_row + 1)[None, :], 0), 1) - 1
    rowof = rowof.reshape(n, 1, lanes)

    near = near_lanes(lanes)
    most = jnp.stack([jnp.max(jnp.sum(block_fill.reshape(n, blocks), 1)), jnp.max(list_rows)])
    groups = lax.axis_size("groups")
    k = 1
    while k < groups:
        most = jnp.maximum(
            most, lax.ppermute(most, "groups", [(i, i ^ k) for i in range(groups)])
        )
        k *= 2
    over, longer = most[0] > ntp * size, most[1] > near

    def exchange_rest():
        rest = pack(x_prompt, pack_fill, pack_dest, at, n, ntp * size, extra)
        rest = lax.all_to_all(rest, "pool", 0, 0, tiled=True).reshape(n * extra, part)
        return rest, lax.ppermute(rest, "tp", swap)

    def no_rest():
        return (jnp.zeros((n * extra, part), jnp.bfloat16),) * 2

    more_mine, more_other = lax.cond(over, exchange_rest, no_rest)
    meta = jnp.concatenate(
        [group_rows, list_rows, jnp.stack([me, core, over.astype(jnp.int32)])]
    )

    def through_keys(held):
        held = held.reshape(n // 2 * rows, heads, hd)
        return pl.pallas_call(
            key_kernel,
            grid=(kvh,),
            in_specs=[
                pl.BlockSpec(held.shape, lambda h: (0, 0, 0)),
                pl.BlockSpec((1, part, 2 * hd), lambda h: (h, 0, 0)),
            ],
            out_specs=pl.BlockSpec((1, n // 2 * per, part), lambda h: (h, 0, 0)),
            out_shape=jax.ShapeDtypeStruct((kvh, n // 2 * per, part), jnp.bfloat16),
            compiler_params=pltpu.CompilerParams(vmem_limit_bytes=16 * MIB),
            cost_estimate=pl.CostEstimate(flops=0, bytes_accessed=1024, transcendentals=0),
            name="key_projection",
        )(held, kv_weight)

    keyed_even = through_keys(even)
    keyed_odd = through_keys(with_partner(even, 1, n))

    mine, meta, rowof, keyed_even, keyed_odd = lax.optimization_barrier(
        (mine, meta, rowof, keyed_even, keyed_odd)
    )
    other = lax.ppermute(mine, "tp", swap)

    anywhere = pl.BlockSpec(memory_space=pl.ANY)
    pair_shape = (2, kvh, per, hd)
    slot_shapes = [
        jax.ShapeDtypeStruct((n, heads, length), jnp.bfloat16) for length in (near, lanes - near)
    ]
    in_vmem = pl.BlockSpec(memory_space=pltpu.VMEM)
    x_parts = (mine, other, more_mine, more_other)
    x_scratch = [
        pltpu.VMEM((ntp, n * size, part), jnp.bfloat16),
        pltpu.VMEM((ntp, n * extra, part), jnp.bfloat16),
        pltpu.VMEM((n * tokens, part), jnp.float32),
    ]
    at_me = n * lanes // BLK + n

    def owner(i, m):
        return m[at_me] ^ reversed_bits(i, n)

    score_near, score_rest = pl.pallas_call(
        functools.partial(score_kernel, n, rows),
        grid_spec=pltpu.PrefetchScalarGridSpec(
            num_scalar_prefetch=1,
            grid=(n,),
            in_specs=[
                *[anywhere] * 6,
                pl.BlockSpec((1, 1, lanes), lambda i, m: (owner(i, m), 0, 0)),
            ],
            out_specs=[
                pl.BlockSpec((1, heads, length), lambda i, m: (owner(i, m), 0, 0))
                for length in (near, lanes - near)
            ],
            scratch_shapes=[
                *x_scratch,
                pltpu.VMEM((tile_cuts(lanes)[1], part), jnp.bfloat16),
                pltpu.VMEM((kvh, n * per, part), jnp.bfloat16),
                pltpu.SemaphoreType.DMA((ntp, 4)),
                pltpu.SemaphoreType.DMA((2, kvh)),
            ],
        ),
        out_shape=slot_shapes,
        compiler_params=pltpu.CompilerParams(vmem_limit_bytes=24 * MIB),
        name="prompt_scores",
    )(meta, *x_parts, keyed_even, keyed_odd, rowof)

    my_rows = lax.dynamic_index_in_dim(rowof, me, 0, keepdims=False)

    def exchange_weights(*scores):
        count = len(scores)
        parts = [lax.all_to_all(s, "pool", 0, 0, tiled=True) for s in scores]
        query = queries.reshape(rows, kvh, group, hd)
        cache_scores = (
            jnp.einsum(
                "rhgd,rthd->rhgt", query, kv_cache[:, :, :, :hd], preferred_element_type=jnp.float32
            )
            * scale
        )
        cache_live = jnp.arange(cache_slots, dtype=jnp.int32)[None, :] < cache_len[:, None]
        cache_scores = jnp.where(cache_live[:, None, None, :], cache_scores, -jnp.inf)
        cache_top = jnp.max(cache_scores, -1, keepdims=True)
        cache_exp = jnp.exp(cache_scores - cache_top)
        cache_sum = jnp.sum(cache_exp, -1, keepdims=True)
        row_parts = [my_rows[:, :near], my_rows[:, near:]][:count]
        *weights, share = pl.pallas_call(
            functools.partial(weight_kernel, scale, count),
            out_shape=[*slot_shapes[:count], jax.ShapeDtypeStruct((rows, heads, 1), jnp.float32)],
            compiler_params=pltpu.CompilerParams(vmem_limit_bytes=8 * MIB),
            name="softmax_weights",
        )(
            *parts,
            *row_parts,
            cache_top.reshape(rows, heads, 1),
            cache_sum.reshape(rows, heads, 1),
        )
        lists = pl.pallas_call(
            functools.partial(list_kernel, n),
            grid_spec=pltpu.PrefetchScalarGridSpec(
                num_scalar_prefetch=1,
                grid=(n,),
                in_specs=[anywhere] * 5,
                out_specs=anywhere,
                scratch_shapes=[
                    *x_scratch,
                    pltpu.VMEM((n, lanes, part), jnp.bfloat16),
                    pltpu.SemaphoreType.DMA((ntp, 4)),
                    pltpu.SemaphoreType.DMA((n, len(tile_cuts(lanes)) - 1)),
                ],
            ),
            out_shape=jax.ShapeDtypeStruct((n, lanes, part), jnp.bfloat16),
            compiler_params=pltpu.CompilerParams(vmem_limit_bytes=56 * MIB),
            cost_estimate=pl.CostEstimate(
                flops=0, bytes_accessed=16 * MIB, transcendentals=0
            ),
            name="owner_lists",
        )(meta, *x_parts, weights[0])
        weights = [lax.all_to_all(w, "pool", 0, 0, tiled=True) for w in weights]
        cached = jnp.einsum(
            "rhgt,rthd->rhgd",
            cache_exp.astype(jnp.bfloat16),
            kv_cache[:, :, :, hd:],
            preferred_element_type=jnp.float32,
        )
        terms = pl.pallas_call(
            functools.partial(value_kernel, n, rows, count),
            grid_spec=pltpu.PrefetchScalarGridSpec(
                num_scalar_prefetch=1,
                grid=(n,),
                in_specs=[
                    *[
                        pl.BlockSpec(
                            (1, heads, shape.shape[2]),
                            lambda i, m: (partner_owner(i, m[at_me], n), 0, 0),
                        )
                        for shape in slot_shapes[:count]
                    ],
                    pl.BlockSpec(
                        (1, 1, lanes), lambda i, m: (partner_owner(i, m[at_me], n), 0, 0)
                    ),
                    pl.BlockSpec(memory_space=pltpu.HBM),
                    anywhere,
                ],
                out_specs=[pl.BlockSpec(pair_shape, lambda i, m: (0, 0, 0, 0))] * (n // 2),
                scratch_shapes=[
                    pltpu.VMEM((kvh, part, hd), jnp.bfloat16),
                    pltpu.VMEM((n, lanes, part), jnp.bfloat16),
                    pltpu.VMEM((kvh * per, part), jnp.float32),
                    pltpu.VMEM((kvh, n * per, part), jnp.bfloat16),
                    pltpu.SemaphoreType.DMA((kvh,)),
                    pltpu.SemaphoreType.DMA((n, len(tile_cuts(lanes)) - 1)),
                ],
            ),
            out_shape=[jax.ShapeDtypeStruct(pair_shape, jnp.bfloat16)] * (n // 2),
            compiler_params=pltpu.CompilerParams(vmem_limit_bytes=24 * MIB),
            name="weighted_values",
        )(meta, *weights, rowof, lists, kv_weight)
        return *terms, cached.reshape(rows, heads, hd) * share

    *terms, kept = lax.cond(
        longer,
        lambda: exchange_weights(score_near, score_rest),
        lambda: exchange_weights(score_near),
    )

    term_parts = [terms[0]] + [with_partner(terms[k], k, n) for k in range(1, n // 2)]
    send, held = pl.pallas_call(
        half_sum_kernel,
        in_specs=[pl.BlockSpec(memory_space=pltpu.SMEM), *[in_vmem] * (n // 2 + 1)],
        out_shape=[
            jax.ShapeDtypeStruct(pair_shape, jnp.bfloat16),
            jax.ShapeDtypeStruct(pair_shape, jnp.float32),
        ],
        compiler_params=pltpu.CompilerParams(vmem_limit_bytes=8 * MIB),
        name="half_pool_sum",
    )((me // (n // 2)).reshape(1), *term_parts, kept)
    attended = pl.pallas_call(
        whole_sum_kernel,
        out_shape=jax.ShapeDtypeStruct((2 * rows, heads * hd), jnp.bfloat16),
        scratch_shapes=[pltpu.VMEM(pair_shape, jnp.float32)],
        compiler_params=pltpu.CompilerParams(vmem_limit_bytes=8 * MIB),
        name="attended_sum",
    )(held, with_partner(send, n // 2, n))

    staged = pl.pallas_call(
        stage_kernel,
        in_specs=[anywhere, pl.BlockSpec(memory_space=pltpu.HBM)],
        out_specs=in_vmem,
        out_shape=jax.ShapeDtypeStruct(out_weight.shape, jnp.bfloat16),
        scratch_shapes=[pltpu.SemaphoreType.DMA((8,))],
        compiler_params=pltpu.CompilerParams(vmem_limit_bytes=16 * MIB),
        cost_estimate=pl.CostEstimate(
            flops=0, bytes_accessed=2 * out_weight.size * 2, transcendentals=0
        ),
        name="stage_out_weight",
    )(send, out_weight)

    everyone = [attended] + [with_partner(attended, k, n) for k in range(1, n // 2)]
    product = jnp.dot(
        jnp.concatenate(everyone), staged, preferred_element_type=jnp.float32
    )
    cols = out_weight.shape[1] // ntp
    half_spec = pl.BlockSpec((n * rows, cols), lambda i, m: (0, 0))
    own = lax.dynamic_slice_in_dim(product, core * cols, cols, 1)
    away = lax.dynamic_slice_in_dim(product, (1 - core) * cols, cols, 1)
    got = lax.ppermute(away, "tp", swap)
    return pl.pallas_call(
        functools.partial(order_kernel, n),
        grid_spec=pltpu.PrefetchScalarGridSpec(
            num_scalar_prefetch=1,
            grid=(1,),
            in_specs=[half_spec] * 2,
            out_specs=half_spec,
        ),
        out_shape=jax.ShapeDtypeStruct((n * rows, cols), jnp.bfloat16),
        compiler_params=pltpu.CompilerParams(vmem_limit_bytes=4 * MIB),
        name="order_rows",
    )(me.reshape(1), own, got)


def solution(mesh):
    in_specs = (
        P(("groups", "pool"), None),
        P("pool", "tp", None),
        P("groups", None),
        P("groups"),
        P("groups"),
        P(("groups", "pool"), "tp", None),
        P(("groups", "pool"), None, "tp", None),
        P(("groups", "pool")),
        P("tp", "pool"),
    )
    out_specs = P("groups", ("pool", "tp"))
    return jax.shard_map(local, mesh=mesh, in_specs=in_specs, out_specs=out_specs, check_vma=False)
```

```python
import functools

import jax
import jax.numpy as jnp
from jax import lax
from jax.experimental import pallas as pl
from jax.experimental.pallas import tpu as pltpu
from jax.sharding import PartitionSpec as P

BLK = 8
MIB = 1 << 20


def pack_kernel(base, at_ref, fill_ref, dest_ref, x_ref, out_ref, packed, count, out_sem):
    n, size, part = packed.shape
    tokens = x_ref.shape[0]
    blocks = tokens // BLK

    def store(q):
        return pltpu.make_async_copy(packed.at[q], out_ref.at[q], out_sem.at[q])

    first = at_ref[0] * blocks
    for q in range(n):
        count[q] = 0

    @pl.loop(0, blocks)
    def _(b):
        owner = dest_ref[first + b]
        count[owner] = count[owner] + fill_ref[first + b]

    def starts(q, total):
        here = count[q]
        count[q] = total
        return total + here

    lax.fori_loop(0, n, starts, jnp.int32(0))
    token = lax.broadcasted_iota(jnp.int32, (1, tokens), 1)

    def place(b, ranks):
        owner = dest_ref[first + b]
        fill = fill_ref[first + b]
        start = count[owner]
        count[owner] = start + fill
        inner = token - b * BLK
        return jnp.where((inner >= 0) & (inner < fill), start + inner, ranks)

    ranks = lax.fori_loop(0, blocks, place, jnp.full((1, tokens), -1, jnp.int32))
    wanted = base + at_ref[1] * size + lax.broadcasted_iota(jnp.int32, (size, tokens), 0)
    pick = (wanted == ranks).astype(jnp.bfloat16)
    for q in range(n):
        packed[q] = jnp.dot(
            pick, x_ref[:, q * part : (q + 1) * part], preferred_element_type=jnp.float32
        ).astype(packed.dtype)
        store(q).start()
    for q in range(n):
        store(q).wait()


def pack(x_prompt, fill, dest, at, n, base, size):
    tokens, width = x_prompt.shape
    part = width // n
    return pl.pallas_call(
        functools.partial(pack_kernel, base),
        grid_spec=pltpu.PrefetchScalarGridSpec(
            num_scalar_prefetch=3,
            grid=(1,),
            in_specs=[pl.BlockSpec(memory_space=pltpu.VMEM)],
            out_specs=pl.BlockSpec(memory_space=pl.ANY),
            scratch_shapes=[
                pltpu.VMEM((n, size, part), jnp.bfloat16),
                pltpu.SMEM((n,), jnp.int32),
                pltpu.SemaphoreType.DMA((n,)),
            ],
        ),
        out_shape=jax.ShapeDtypeStruct((n, size, part), jnp.bfloat16),
        compiler_params=pltpu.CompilerParams(vmem_limit_bytes=16 * MIB),
        cost_estimate=pl.CostEstimate(
            flops=2 * size * tokens * width, bytes_accessed=64 * MIB, transcendentals=0
        ),
        name="pack_live_tokens",
    )(at, fill, dest, x_prompt)


def tile_cuts(lanes):
    return [0] + list(range(min(256, lanes), lanes, 128)) + [lanes]


def near_lanes(lanes):
    return min(lanes, -(-lanes * 3 // 5 // 128) * 128)


def widen(core, n, refs, wide, base, first, last):
    length = refs[0].shape[0] // n
    tokens = wide.shape[0] // n

    @pl.loop(first, last)
    def _(s):
        for j, ref in enumerate(refs):
            side = core if j == 0 else 1 - core
            to = pl.multiple_of(s * tokens + base + side * length, BLK)
            wide[pl.ds(to, length), :] = ref[
                pl.ds(pl.multiple_of(s * length, length), length), :
            ].astype(wide.dtype)


def span_copies(refs, buffer, sem):
    cuts = sem.shape[1]
    span = buffer.shape[1] // cuts
    return [
        [
            pltpu.make_async_copy(
                ref.at[pl.ds(i * span, span)], buffer.at[j, pl.ds(i * span, span)], sem.at[j, i]
            )
            for j, ref in enumerate(refs)
        ]
        for i in range(cuts)
    ]


def load_tokens(n, core, over, x_refs, there, held, more, wide, sem, others):
    main = span_copies(x_refs[: 2 - len(there)], held, sem)
    for pair in main:
        for copy in pair:
            copy.start()
    for copy in others:
        copy.start()
    for i, pair in enumerate(main):
        for copy in pair:
            copy.wait()
        parts = [held.at[j] for j in range(2 - len(there))] + there
        widen(core, n, parts, wide, 0, i * n // len(main), (i + 1) * n // len(main))

    @pl.when(over != 0)
    def _():
        rest = span_copies(x_refs[2:], more, sem)
        for pair in rest:
            for copy in pair:
                copy.start()
        for pair in rest:
            for copy in pair:
                copy.wait()
        base = wide.shape[0] // n - 2 * more.shape[1] // n
        widen(core, n, [more.at[0], more.at[1]], wide, base, 0, n)


def list_tile(meta_ref, first, count, wide, tile):
    for i in range(0, count, 2):
        pair = [
            wide[pl.ds(pl.multiple_of(meta_ref[first + i + j], BLK), BLK), :] for j in range(2)
        ]
        tile[i * BLK : (i + 2) * BLK, :] = jnp.concatenate(pair).astype(tile.dtype)
    return tile[: count * BLK, :]


def key_kernel(query_ref, weight_ref, out_ref):
    group = out_ref.shape[1] // query_ref.shape[0]
    hd = query_ref.shape[2]
    h = pl.program_id(0)
    for i in range(query_ref.shape[1] // group):

        @pl.when(h == i)
        def _(i=i):
            query = query_ref[:, i * group : (i + 1) * group, :].astype(jnp.float32)
            out_ref[0] = lax.dot_general(
                query.reshape(-1, hd).astype(jnp.bfloat16),
                weight_ref[0, :, :hd],
                (((1,), (1,)), ((), ())),
                preferred_element_type=jnp.float32,
            ).astype(out_ref.dtype)


def score_kernel(n, rows, meta_ref, *refs):
    x_refs, keyed_refs, (row_ref, near_ref, rest_ref) = refs[:4], refs[4:6], refs[6:9]
    held, more, wide, tile, keyed, sem, keyed_sem = refs[9:]
    step = pl.program_id(0)
    part = wide.shape[1]
    near = near_ref.shape[2]
    lanes = near + rest_ref.shape[2]
    cuts = tile_cuts(lanes)
    groups = lanes // BLK
    at_size = n * groups
    q = meta_ref[at_size + n] ^ reversed_bits(step, n)
    kvh, per = keyed.shape[0], keyed.shape[1] // n
    group = per // rows

    def load(i):
        span = n // 2 * per
        return [
            pltpu.make_async_copy(
                keyed_refs[i].at[h], keyed.at[h, pl.ds(i * span, span)], keyed_sem.at[i, h]
            )
            for h in range(kvh)
        ]

    @pl.when(step == 0)
    def _():
        load_tokens(
            n, meta_ref[at_size + n + 1], meta_ref[at_size + n + 2], x_refs, [], held, more, wide, sem,
            load(0) + load(1),
        )

    for i in range(2):

        @pl.when(step == i * (n // 2))
        def _(i=i):
            for copy in load(i):
                copy.wait()

    def one(t):
        here = slice(cuts[t], cuts[t + 1])
        count = (cuts[t + 1] - cuts[t]) // BLK
        raw = lax.dot_general(
            keyed[:, pl.ds(pl.multiple_of(step * per, per), per), :].reshape(kvh * per, part),
            list_tile(meta_ref, q * groups + cuts[t] // BLK, count, wide, tile),
            (((1,), (1,)), ((), ())),
            preferred_element_type=jnp.float32,
        ).reshape(kvh, rows, group, count * BLK)
        owner_row = row_ref[0, :, here]
        picked = jnp.zeros((kvh, group, count * BLK), jnp.float32)
        for r in range(rows):
            picked = picked + jnp.where((owner_row == r)[None], raw[:, r], 0.0)
        picked = picked.reshape(kvh * group, -1).astype(near_ref.dtype)
        if cuts[t] < near:
            near_ref[0, :, here] = picked
        else:
            rest_ref[0, :, cuts[t] - near : cuts[t + 1] - near] = picked

    one(0)
    for t in range(1, len(cuts) - 1):
        pl.when(meta_ref[at_size + q] > cuts[t])(functools.partial(one, t))


def weight_kernel(scale, count, *refs):
    part_refs, row_refs = refs[:count], refs[count : 2 * count]
    top_ref, sum_ref = refs[2 * count : 2 * count + 2]
    w_refs, share_ref = refs[2 * count + 2 : -1], refs[-1]
    n = part_refs[0].shape[0]
    scores, owner_rows = [], []
    for part_ref, row_ref in zip(part_refs, row_refs):
        got = part_ref[0].astype(jnp.float32)
        for i in range(1, n):
            got = got + part_ref[i].astype(jnp.float32)
        scores.append(got * scale)
        owner_rows.append(row_ref[...])
    rows = range(top_ref.shape[0])
    spread = [jnp.zeros(s.shape, jnp.float32) for s in scores]
    tops = []
    for r in rows:
        top = top_ref[r]
        for o, s in zip(owner_rows, scores):
            top = jnp.maximum(top, jnp.max(jnp.where(o == r, s, -jnp.inf), 1, keepdims=True))
        tops.append(top)
        spread = [jnp.where(o == r, top, t) for o, t in zip(owner_rows, spread)]
    held = [
        jnp.exp(jnp.where(o >= 0, s - t, -jnp.inf))
        for o, s, t in zip(owner_rows, scores, spread)
    ]
    shares = [jnp.zeros(s.shape, jnp.float32) for s in scores]
    for r in rows:
        fade = jnp.exp(top_ref[r] - tops[r])
        total = sum_ref[r] * fade
        for o, h in zip(owner_rows, held):
            total = total + jnp.sum(jnp.where(o == r, h, 0.0), 1, keepdims=True)
        shares = [jnp.where(o == r, 1.0 / total, t) for o, t in zip(owner_rows, shares)]
        share_ref[r] = fade / total
    for h, t, w_ref in zip(held, shares, w_refs):
        weights = (h * t).astype(w_ref.dtype)
        for i in range(n):
            w_ref[i] = weights


def list_copies(n, lanes, sizes, source, target, sem):
    cuts = tile_cuts(lanes)

    def copies(o):
        for t in range(len(cuts) - 1):
            here = pl.ds(cuts[t], cuts[t + 1] - cuts[t])
            copy = pltpu.make_async_copy(source.at[o, here], target.at[o, here], sem.at[o, t])
            yield (True if t == 0 else sizes(o) > cuts[t]), copy

    return copies


def list_kernel(n, lanes, meta_ref, *refs):
    x_refs, (_, out_ref, held, more, wide, lists, sem, out_sem) = refs[:4], refs[4:]
    q = pl.program_id(0)
    length = lists.shape[1]
    cuts = tile_cuts(length)
    groups = lanes // BLK
    at_size = n * groups
    copies = list_copies(n, length, lambda o: meta_ref[at_size + o], lists, out_ref, out_sem)

    @pl.when(q == 0)
    def _():
        load_tokens(
            n, meta_ref[at_size + n + 1], meta_ref[at_size + n + 2], x_refs, [], held, more, wide,
            sem, [],
        )

    for t, (used, copy) in enumerate(copies(q)):

        @pl.when(used)
        def _(t=t, copy=copy):
            list_tile(
                meta_ref, q * groups + cuts[t] // BLK, (cuts[t + 1] - cuts[t]) // BLK, wide,
                lists.at[q, cuts[t] : cuts[t + 1]],
            )
            copy.start()

    @pl.when(q == n - 1)
    def _():
        for o in range(n):
            for used, copy in copies(o):
                pl.when(used)(copy.wait)


def value_kernel(n, rows, lanes, count, meta_ref, *refs):
    w_refs, (row_ref, list_ref, weight_ref) = refs[:count], refs[count : count + 3]
    out_refs, scratch = refs[count + 3 : count + 3 + n // 2], refs[count + 3 + n // 2 :]
    values, lists, acc, mixed, value_sem, sem = scratch
    step = pl.program_id(0)
    kvh, _, hd = values.shape
    load_values = [
        pltpu.make_async_copy(
            weight_ref.at[h, :, pl.ds(hd, hd)], values.at[h], value_sem.at[h]
        )
        for h in range(kvh)
    ]
    _, heads, near = w_refs[0].shape
    length = lists.shape[1]
    per = rows * heads // kvh
    cuts = tile_cuts(length)
    at_size = n * lanes // BLK
    me = meta_ref[at_size + n]
    q = partner_owner(step, me, n)
    size = meta_ref[at_size + q]
    copies = list_copies(n, length, lambda o: meta_ref[at_size + o], list_ref, lists, sem)
    ahead = min(3, n)

    def fetch(i):
        for used, copy in copies(partner_owner(i, me, n)):
            pl.when(used)(copy.start)

    @pl.when(step == 0)
    def _():
        for i in range(ahead):
            fetch(i)

    pl.when(step + ahead < n)(lambda: fetch(jnp.minimum(step + ahead, n - 1)))

    @pl.when(step == n // 2)
    def _():
        for load in load_values:
            load.start()

    for used, copy in copies(q):
        pl.when(used)(copy.wait)

    def one(t):
        here = slice(cuts[t], cuts[t + 1])
        width = cuts[t + 1] - cuts[t]
        piece = 0 if cuts[t] < near else 1
        weights = w_refs[piece][0, :, cuts[t] - piece * near : cuts[t + 1] - piece * near]
        weights = weights.astype(jnp.float32).reshape(kvh, 1, heads // kvh, width)
        owner_row = row_ref[0, :, here]
        spread = jnp.concatenate(
            [jnp.where((owner_row == r)[None, None], weights, 0.0) for r in range(rows)], 1
        ).reshape(kvh * per, width)
        got = jnp.dot(
            spread.astype(jnp.bfloat16), lists[q, here, :], preferred_element_type=jnp.float32
        )
        if t == 0:
            pl.when(size <= cuts[1])(lambda: keep(got))

            @pl.when(size > cuts[1])
            def _():
                acc[...] = got

        else:
            acc[...] += got

    def keep(sums):
        for h in range(kvh):
            mixed[h, pl.ds(pl.multiple_of(step * per, per), per), :] = sums[
                h * per : (h + 1) * per
            ].astype(mixed.dtype)

    one(0)
    for t in range(1, len(cuts) - 1):
        pl.when(size > cuts[t])(functools.partial(one, t))
    pl.when(size > cuts[1])(lambda: keep(acc[...]))

    @pl.when(step == n - 1)
    def _():
        for load in load_values:
            load.wait()
        for h in range(kvh):
            done = jnp.dot(mixed[h], values[h], preferred_element_type=jnp.float32)
            done = done.astype(jnp.bfloat16)
            for i in range(n):
                out_refs[i // 2][i % 2, h] = done[i * per : (i + 1) * per]


def half_sum_kernel(side_ref, *refs):
    *part_refs, kept_ref, send_ref, mine_ref = refs
    sides, kvh, _, _ = part_refs[0].shape
    rows, heads = kept_ref.shape[:2]
    group = heads // kvh
    for side in range(sides):
        own = side_ref[0] == side
        for h in range(kvh):
            terms = part_refs[0][side, h].astype(jnp.float32)
            for ref in part_refs[1:]:
                terms = terms + ref[side, h].astype(jnp.float32)
            kept = jnp.concatenate(
                [kept_ref[r, h * group : (h + 1) * group, :] for r in range(rows)]
            )
            terms = terms + jnp.where(own, kept, 0.0)
            mine_ref[side, h] = terms
            send_ref[side, h] = terms.astype(send_ref.dtype)


def partner_owner(i, me, n):
    half = n // 2
    return i % 2 * half + ((me % half) ^ (i // 2))


def whole_sum_kernel(mine_ref, got_ref, out_ref, total):
    sides, kvh, per, _ = mine_ref.shape
    rows = out_ref.shape[0] // sides
    group = per // rows
    total[...] = mine_ref[...] + got_ref[...].astype(jnp.float32)
    for h in range(kvh):
        for g in range(group):
            column = [
                total[side, h, pl.ds(g, rows, stride=group), :] for side in range(sides)
            ]
            head = h * group + g
            hd = column[0].shape[1]
            out_ref[:, head * hd : (head + 1) * hd] = jnp.concatenate(column).astype(
                out_ref.dtype
            )


def stage_kernel(core_ref, after_ref, weight_ref, own_ref, away_ref, sem):
    cuts = sem.shape[1]
    span, cols = own_ref.shape[0] // cuts, own_ref.shape[1]
    copies = [
        pltpu.make_async_copy(
            weight_ref.at[
                pl.ds(i * span, span), pl.ds(pl.multiple_of(side * cols, 128), cols)
            ],
            ref.at[pl.ds(i * span, span)],
            sem.at[j, i],
        )
        for j, (side, ref) in enumerate(((1 - core_ref[0], away_ref), (core_ref[0], own_ref)))
        for i in range(cuts)
    ]
    for copy in copies:
        copy.start()
    for copy in copies:
        copy.wait()


def order_kernel(n, me_ref, own_ref, got_ref, out_ref):
    half = n // 2
    rows = own_ref.shape[0] // n
    for q in range(0, n, 2):
        pair = []
        for owner in (q, q + 1):
            block = ((me_ref[0] % half) ^ (owner % half)) * 2 + owner // half
            here = pl.ds(pl.multiple_of(block * rows, rows), rows)
            pair.append(own_ref[here, :] + got_ref[here, :])
        out_ref[q * rows : (q + 2) * rows, :] = jnp.concatenate(pair).astype(out_ref.dtype)


def with_partner(x, k, n):
    return lax.ppermute(x, "pool", [(i, i ^ k) for i in range(n)])


def from_rest(held, n):
    k = n // 8
    while k >= 2:
        held = jnp.concatenate([held, with_partner(held, k, n)])
        k //= 2
    return held


def reversed_bits(k, n):
    out, bit = 0, 1
    while bit < n:
        out = out + (k // bit) % 2 * (n // 2 // bit)
        bit *= 2
    return out


def local(
    x_prompt, kv_weight, block_dest, block_row, block_fill, queries, kv_cache, cache_len, out_weight
):
    n = lax.axis_size("pool")
    ntp = lax.axis_size("tp")
    me = lax.axis_index("pool").astype(jnp.int32)
    core = lax.axis_index("tp").astype(jnp.int32)
    tokens, width = x_prompt.shape
    part = width // n
    kvh = kv_weight.shape[1]
    hd = kv_weight.shape[2] // 2
    rows, heads = queries.shape[0], queries.shape[1]
    group = heads // kvh
    per = rows * group
    cache_slots = kv_cache.shape[1]
    blocks = tokens // BLK
    cap = max(2, 2 * blocks // n)
    window = cap * BLK + BLK
    lanes = -(-n * window // 128) * 128
    half = tokens // ntp
    scale = 1.0 / hd**0.5
    swap = [(i, (i + 1) % ntp) for i in range(ntp)]

    size = half * 3 // 4
    extra = half - size
    at = jnp.stack([me, core])
    pack_fill, pack_dest = block_fill, block_dest[:, 0]
    packed = pack(x_prompt, pack_fill, pack_dest, at, n, 0, size)
    dest = pack_dest
    far = [with_partner(queries, k, n) for k in (n // 2, n // 4, n // 2 + n // 4)]
    packed, far, dest, block_row, block_fill, kv_weight = lax.optimization_barrier(
        (packed, far, dest, block_row, block_fill, kv_weight)
    )
    kv_weight = kv_weight.transpose(1, 0, 2)
    even = from_rest(jnp.stack([queries, *far]), n)
    mine = lax.all_to_all(packed, "pool", 0, 0, tiled=True).reshape(n * size, part)

    index = jnp.arange(n * blocks, dtype=jnp.int32)
    sender = index // blocks
    kin = sender[None, :] == sender[:, None]
    lower = kin & (dest[None, :] < dest[:, None])
    level = kin & (dest[None, :] == dest[:, None]) & (index[None, :] < index[:, None])
    before = jnp.sum(jnp.where(lower, block_fill[None, :], 0), 1)
    within = jnp.sum(jnp.where(level, block_fill[None, :], 0), 1)
    pair = jnp.arange(n * n, dtype=jnp.int32)
    to, by = pair // n, pair % n
    owned = dest[None, :] == to[:, None]
    sent = sender[None, :] == by[:, None]
    earlier = sent & (dest[None, :] < to[:, None])
    offset = jnp.sum(jnp.where(earlier, block_fill[None, :], 0), 1)
    amount = jnp.sum(jnp.where(sent & owned, block_fill[None, :], 0), 1)
    runs = jnp.where(amount > 0, (offset % BLK + amount + BLK - 1) // BLK * BLK, 0)
    runs_by = runs.reshape(n, n)
    prior = jnp.arange(n)[:, None] < jnp.arange(n)[None, :]
    targets = jnp.sum(jnp.where(prior[None], runs_by[:, :, None], 0), 1)
    list_rows = jnp.sum(runs_by, 1)
    targets = targets.reshape(-1)
    sources = by * tokens + offset // BLK * BLK
    group_at = jnp.arange(n * lanes // BLK, dtype=jnp.int32) * BLK
    skip = group_at[:, None] - (to * lanes + targets)[None, :]
    group_rows = jnp.sum(
        jnp.where((skip >= 0) & (skip < runs[None, :]), sources[None, :] + skip, 0), 1
    )
    mine_pair = (dest * n + sender)[:, None] == pair[None, :]
    start = (
        dest * lanes
        + jnp.sum(jnp.where(mine_pair, targets[None, :], 0), 1)
        + before % BLK
        + within
    )
    spot = jnp.arange(n * lanes, dtype=jnp.int32)[:, None]
    inside = (spot >= start[None, :]) & (spot < (start + block_fill)[None, :])
    rowof = jnp.sum(jnp.where(inside, (block_row + 1)[None, :], 0), 1) - 1
    rowof = rowof.reshape(n, 1, lanes)

    near = near_lanes(lanes)
    most = jnp.stack([jnp.max(jnp.sum(block_fill.reshape(n, blocks), 1)), jnp.max(list_rows)])
    groups = lax.axis_size("groups")
    k = 1
    while k < groups:
        most = jnp.maximum(
            most, lax.ppermute(most, "groups", [(i, i ^ k) for i in range(groups)])
        )
        k *= 2
    over, longer = most[0] > ntp * size, most[1] > near

    def exchange_rest():
        rest = pack(x_prompt, pack_fill, pack_dest, at, n, ntp * size, extra)
        rest = lax.all_to_all(rest, "pool", 0, 0, tiled=True).reshape(n * extra, part)
        return rest, lax.ppermute(rest, "tp", swap)

    def no_rest():
        return (jnp.zeros((n * extra, part), jnp.bfloat16),) * 2

    more_mine, more_other = lax.cond(over, exchange_rest, no_rest)
    meta = jnp.concatenate(
        [group_rows, list_rows, jnp.stack([me, core, over.astype(jnp.int32)])]
    )

    def through_keys(held):
        held = held.reshape(n // 2 * rows, heads, hd)
        return pl.pallas_call(
            key_kernel,
            grid=(kvh,),
            in_specs=[
                pl.BlockSpec(held.shape, lambda h: (0, 0, 0)),
                pl.BlockSpec((1, part, 2 * hd), lambda h: (h, 0, 0)),
            ],
            out_specs=pl.BlockSpec((1, n // 2 * per, part), lambda h: (h, 0, 0)),
            out_shape=jax.ShapeDtypeStruct((kvh, n // 2 * per, part), jnp.bfloat16),
            compiler_params=pltpu.CompilerParams(vmem_limit_bytes=16 * MIB),
            cost_estimate=pl.CostEstimate(flops=0, bytes_accessed=1024, transcendentals=0),
            name="key_projection",
        )(held, kv_weight)

    keyed_even = through_keys(even)
    keyed_odd = through_keys(with_partner(even, 1, n))

    mine, meta, rowof, keyed_even, keyed_odd = lax.optimization_barrier(
        (mine, meta, rowof, keyed_even, keyed_odd)
    )
    other = lax.ppermute(mine, "tp", swap)

    anywhere = pl.BlockSpec(memory_space=pl.ANY)
    pair_shape = (2, kvh, per, hd)
    slot_shapes = [
        jax.ShapeDtypeStruct((n, heads, length), jnp.bfloat16) for length in (near, lanes - near)
    ]
    in_vmem = pl.BlockSpec(memory_space=pltpu.VMEM)
    x_parts = (mine, other, more_mine, more_other)
    x_scratch = [
        pltpu.VMEM((ntp, n * size, part), jnp.bfloat16),
        pltpu.VMEM((ntp, n * extra, part), jnp.bfloat16),
        pltpu.VMEM((n * tokens, part), jnp.float32),
    ]
    at_me = n * lanes // BLK + n

    def owner(i, m):
        return m[at_me] ^ reversed_bits(i, n)

    score_near, score_rest = pl.pallas_call(
        functools.partial(score_kernel, n, rows),
        grid_spec=pltpu.PrefetchScalarGridSpec(
            num_scalar_prefetch=1,
            grid=(n,),
            in_specs=[
                *[anywhere] * 6,
                pl.BlockSpec((1, 1, lanes), lambda i, m: (owner(i, m), 0, 0)),
            ],
            out_specs=[
                pl.BlockSpec((1, heads, length), lambda i, m: (owner(i, m), 0, 0))
                for length in (near, lanes - near)
            ],
            scratch_shapes=[
                *x_scratch,
                pltpu.VMEM((tile_cuts(lanes)[1], part), jnp.bfloat16),
                pltpu.VMEM((kvh, n * per, part), jnp.bfloat16),
                pltpu.SemaphoreType.DMA((ntp, 4)),
                pltpu.SemaphoreType.DMA((2, kvh)),
            ],
        ),
        out_shape=slot_shapes,
        compiler_params=pltpu.CompilerParams(vmem_limit_bytes=24 * MIB),
        name="prompt_scores",
    )(meta, *x_parts, keyed_even, keyed_odd, rowof)

    my_rows = lax.dynamic_index_in_dim(rowof, me, 0, keepdims=False)

    def exchange_weights(*scores):
        count = len(scores)
        parts = [lax.all_to_all(s, "pool", 0, 0, tiled=True) for s in scores]
        query = queries.reshape(rows, kvh, group, hd)
        cache_scores = (
            jnp.einsum(
                "rhgd,rthd->rhgt", query, kv_cache[:, :, :, :hd], preferred_element_type=jnp.float32
            )
            * scale
        )
        cache_live = jnp.arange(cache_slots, dtype=jnp.int32)[None, :] < cache_len[:, None]
        cache_scores = jnp.where(cache_live[:, None, None, :], cache_scores, -jnp.inf)
        cache_top = jnp.max(cache_scores, -1, keepdims=True)
        cache_exp = jnp.exp(cache_scores - cache_top)
        cache_sum = jnp.sum(cache_exp, -1, keepdims=True)
        row_parts = [my_rows[:, :near], my_rows[:, near:]][:count]
        *weights, share = pl.pallas_call(
            functools.partial(weight_kernel, scale, count),
            out_shape=[*slot_shapes[:count], jax.ShapeDtypeStruct((rows, heads, 1), jnp.float32)],
            compiler_params=pltpu.CompilerParams(vmem_limit_bytes=8 * MIB),
            name="softmax_weights",
        )(
            *parts,
            *row_parts,
            cache_top.reshape(rows, heads, 1),
            cache_sum.reshape(rows, heads, 1),
        )
        length = near if count == 1 else lanes
        lists = pl.pallas_call(
            functools.partial(list_kernel, n, lanes),
            grid_spec=pltpu.PrefetchScalarGridSpec(
                num_scalar_prefetch=1,
                grid=(n,),
                in_specs=[anywhere] * 5,
                out_specs=anywhere,
                scratch_shapes=[
                    *x_scratch,
                    pltpu.VMEM((n, length, part), jnp.bfloat16),
                    pltpu.SemaphoreType.DMA((ntp, 4)),
                    pltpu.SemaphoreType.DMA((n, len(tile_cuts(length)) - 1)),
                ],
            ),
            out_shape=jax.ShapeDtypeStruct((n, length, part), jnp.bfloat16),
            compiler_params=pltpu.CompilerParams(vmem_limit_bytes=56 * MIB),
            cost_estimate=pl.CostEstimate(
                flops=0, bytes_accessed=16 * MIB, transcendentals=0
            ),
            name="owner_lists",
        )(meta, *x_parts, weights[0])
        weights = [lax.all_to_all(w, "pool", 0, 0, tiled=True) for w in weights]
        cached = jnp.einsum(
            "rhgt,rthd->rhgd",
            cache_exp.astype(jnp.bfloat16),
            kv_cache[:, :, :, hd:],
            preferred_element_type=jnp.float32,
        )
        terms = pl.pallas_call(
            functools.partial(value_kernel, n, rows, lanes, count),
            grid_spec=pltpu.PrefetchScalarGridSpec(
                num_scalar_prefetch=1,
                grid=(n,),
                in_specs=[
                    *[
                        pl.BlockSpec(
                            (1, heads, shape.shape[2]),
                            lambda i, m: (partner_owner(i, m[at_me], n), 0, 0),
                        )
                        for shape in slot_shapes[:count]
                    ],
                    pl.BlockSpec(
                        (1, 1, lanes), lambda i, m: (partner_owner(i, m[at_me], n), 0, 0)
                    ),
                    pl.BlockSpec(memory_space=pltpu.HBM),
                    anywhere,
                ],
                out_specs=[pl.BlockSpec(pair_shape, lambda i, m: (0, 0, 0, 0))] * (n // 2),
                scratch_shapes=[
                    pltpu.VMEM((kvh, part, hd), jnp.bfloat16),
                    pltpu.VMEM((n, length, part), jnp.bfloat16),
                    pltpu.VMEM((kvh * per, part), jnp.float32),
                    pltpu.VMEM((kvh, n * per, part), jnp.bfloat16),
                    pltpu.SemaphoreType.DMA((kvh,)),
                    pltpu.SemaphoreType.DMA((n, len(tile_cuts(length)) - 1)),
                ],
            ),
            out_shape=[jax.ShapeDtypeStruct(pair_shape, jnp.bfloat16)] * (n // 2),
            compiler_params=pltpu.CompilerParams(vmem_limit_bytes=24 * MIB),
            name="weighted_values",
        )(meta, *weights, rowof, lists, kv_weight)
        return *terms, cached.reshape(rows, heads, hd) * share

    *terms, kept = lax.cond(
        longer,
        lambda: exchange_weights(score_near, score_rest),
        lambda: exchange_weights(score_near),
    )

    term_parts = [terms[0]] + [with_partner(terms[k], k, n) for k in range(1, n // 2)]
    send, held = pl.pallas_call(
        half_sum_kernel,
        in_specs=[pl.BlockSpec(memory_space=pltpu.SMEM), *[in_vmem] * (n // 2 + 1)],
        out_shape=[
            jax.ShapeDtypeStruct(pair_shape, jnp.bfloat16),
            jax.ShapeDtypeStruct(pair_shape, jnp.float32),
        ],
        compiler_params=pltpu.CompilerParams(vmem_limit_bytes=8 * MIB),
        name="half_pool_sum",
    )((me // (n // 2)).reshape(1), *term_parts, kept)
    attended = pl.pallas_call(
        whole_sum_kernel,
        out_shape=jax.ShapeDtypeStruct((2 * rows, heads * hd), jnp.bfloat16),
        scratch_shapes=[pltpu.VMEM(pair_shape, jnp.float32)],
        compiler_params=pltpu.CompilerParams(vmem_limit_bytes=8 * MIB),
        name="attended_sum",
    )(held, with_partner(send, n // 2, n))

    cols = out_weight.shape[1] // ntp
    own_weight, away_weight = pl.pallas_call(
        stage_kernel,
        in_specs=[
            pl.BlockSpec(memory_space=pltpu.SMEM),
            anywhere,
            pl.BlockSpec(memory_space=pltpu.HBM),
        ],
        out_specs=[in_vmem] * 2,
        out_shape=[jax.ShapeDtypeStruct((out_weight.shape[0], cols), jnp.bfloat16)] * 2,
        scratch_shapes=[pltpu.SemaphoreType.DMA((2, 4))],
        compiler_params=pltpu.CompilerParams(vmem_limit_bytes=16 * MIB),
        cost_estimate=pl.CostEstimate(
            flops=0, bytes_accessed=2 * out_weight.size * 2, transcendentals=0
        ),
        name="stage_out_weight",
    )(core.reshape(1), send, out_weight)

    everyone = [attended] + [with_partner(attended, k, n) for k in range(1, n // 2)]
    everyone = jnp.concatenate(everyone)
    away = jnp.dot(everyone, away_weight, preferred_element_type=jnp.float32)
    half_spec = pl.BlockSpec((n * rows, cols), lambda i, m: (0, 0))
    got = lax.ppermute(away, "tp", swap)
    own = jnp.dot(everyone, own_weight, preferred_element_type=jnp.float32)
    return pl.pallas_call(
        functools.partial(order_kernel, n),
        grid_spec=pltpu.PrefetchScalarGridSpec(
            num_scalar_prefetch=1,
            grid=(1,),
            in_specs=[half_spec] * 2,
            out_specs=half_spec,
        ),
        out_shape=jax.ShapeDtypeStruct((n * rows, cols), jnp.bfloat16),
        compiler_params=pltpu.CompilerParams(vmem_limit_bytes=4 * MIB),
        name="order_rows",
    )(me.reshape(1), own, got)


def solution(mesh):
    in_specs = (
        P(("groups", "pool"), None),
        P("pool", "tp", None),
        P("groups", None),
        P("groups"),
        P("groups"),
        P(("groups", "pool"), "tp", None),
        P(("groups", "pool"), None, "tp", None),
        P(("groups", "pool")),
        P("tp", "pool"),
    )
    out_specs = P("groups", ("pool", "tp"))
    return jax.shard_map(local, mesh=mesh, in_specs=in_specs, out_specs=out_specs, check_vma=False)
```

```python
import functools

import jax
import jax.numpy as jnp
from jax import lax
from jax.experimental import pallas as pl
from jax.experimental.pallas import tpu as pltpu
from jax.sharding import PartitionSpec as P

BLK = 8
MIB = 1 << 20


def pack_kernel(base, at_ref, fill_ref, dest_ref, x_ref, out_ref, packed, count, out_sem):
    n, size, part = packed.shape
    tokens = x_ref.shape[0]
    blocks = tokens // BLK

    def store(q):
        return pltpu.make_async_copy(packed.at[q], out_ref.at[q], out_sem.at[q])

    first = at_ref[0] * blocks
    for q in range(n):
        count[q] = 0

    @pl.loop(0, blocks)
    def _(b):
        owner = dest_ref[first + b]
        count[owner] = count[owner] + fill_ref[first + b]

    def starts(q, total):
        here = count[q]
        count[q] = total
        return total + here

    lax.fori_loop(0, n, starts, jnp.int32(0))
    token = lax.broadcasted_iota(jnp.int32, (1, tokens), 1)

    def place(b, ranks):
        owner = dest_ref[first + b]
        fill = fill_ref[first + b]
        start = count[owner]
        count[owner] = start + fill
        inner = token - b * BLK
        return jnp.where((inner >= 0) & (inner < fill), start + inner, ranks)

    ranks = lax.fori_loop(0, blocks, place, jnp.full((1, tokens), -1, jnp.int32))
    wanted = base + at_ref[1] * size + lax.broadcasted_iota(jnp.int32, (size, tokens), 0)
    pick = (wanted == ranks).astype(jnp.bfloat16)
    for q in range(n):
        packed[q] = jnp.dot(
            pick, x_ref[:, q * part : (q + 1) * part], preferred_element_type=jnp.float32
        ).astype(packed.dtype)
        store(q).start()
    for q in range(n):
        store(q).wait()


def pack(x_prompt, fill, dest, at, n, base, size):
    tokens, width = x_prompt.shape
    part = width // n
    return pl.pallas_call(
        functools.partial(pack_kernel, base),
        grid_spec=pltpu.PrefetchScalarGridSpec(
            num_scalar_prefetch=3,
            grid=(1,),
            in_specs=[pl.BlockSpec(memory_space=pltpu.VMEM)],
            out_specs=pl.BlockSpec(memory_space=pl.ANY),
            scratch_shapes=[
                pltpu.VMEM((n, size, part), jnp.bfloat16),
                pltpu.SMEM((n,), jnp.int32),
                pltpu.SemaphoreType.DMA((n,)),
            ],
        ),
        out_shape=jax.ShapeDtypeStruct((n, size, part), jnp.bfloat16),
        compiler_params=pltpu.CompilerParams(vmem_limit_bytes=16 * MIB),
        cost_estimate=pl.CostEstimate(
            flops=2 * size * tokens * width, bytes_accessed=64 * MIB, transcendentals=0
        ),
        name="pack_live_tokens",
    )(at, fill, dest, x_prompt)


def tile_cuts(lanes):
    return [0] + list(range(min(256, lanes), lanes, 128)) + [lanes]


def near_lanes(lanes):
    return min(lanes, -(-lanes * 3 // 5 // 128) * 128)


def widen(core, n, refs, wide, base, first, last):
    length = refs[0].shape[0] // n
    tokens = wide.shape[0] // n

    @pl.loop(first, last)
    def _(s):
        for j, ref in enumerate(refs):
            side = core if j == 0 else 1 - core
            to = pl.multiple_of(s * tokens + base + side * length, BLK)
            wide[pl.ds(to, length), :] = ref[
                pl.ds(pl.multiple_of(s * length, length), length), :
            ].astype(wide.dtype)


def span_copies(refs, buffer, sem):
    cuts = sem.shape[1]
    span = buffer.shape[1] // cuts
    return [
        [
            pltpu.make_async_copy(
                ref.at[pl.ds(i * span, span)], buffer.at[j, pl.ds(i * span, span)], sem.at[j, i]
            )
            for j, ref in enumerate(refs)
        ]
        for i in range(cuts)
    ]


def load_tokens(n, core, over, x_refs, there, held, more, wide, sem, others):
    main = span_copies(x_refs[: 2 - len(there)], held, sem)
    for pair in main:
        for copy in pair:
            copy.start()
    for copy in others:
        copy.start()
    for i, pair in enumerate(main):
        for copy in pair:
            copy.wait()
        parts = [held.at[j] for j in range(2 - len(there))] + there
        widen(core, n, parts, wide, 0, i * n // len(main), (i + 1) * n // len(main))

    @pl.when(over != 0)
    def _():
        rest = span_copies(x_refs[2:], more, sem)
        for pair in rest:
            for copy in pair:
                copy.start()
        for pair in rest:
            for copy in pair:
                copy.wait()
        base = wide.shape[0] // n - 2 * more.shape[1] // n
        widen(core, n, [more.at[0], more.at[1]], wide, base, 0, n)


def list_tile(meta_ref, first, count, wide, tile):
    for i in range(0, count, 2):
        pair = [
            wide[pl.ds(pl.multiple_of(meta_ref[first + i + j], BLK), BLK), :] for j in range(2)
        ]
        tile[i * BLK : (i + 2) * BLK, :] = jnp.concatenate(pair).astype(tile.dtype)
    return tile[: count * BLK, :]


def key_kernel(query_ref, weight_ref, out_ref):
    group = out_ref.shape[1] // query_ref.shape[0]
    hd = query_ref.shape[2]
    h = pl.program_id(0)
    for i in range(query_ref.shape[1] // group):

        @pl.when(h == i)
        def _(i=i):
            query = query_ref[:, i * group : (i + 1) * group, :].astype(jnp.float32)
            out_ref[0] = lax.dot_general(
                query.reshape(-1, hd).astype(jnp.bfloat16),
                weight_ref[0, :, :hd],
                (((1,), (1,)), ((), ())),
                preferred_element_type=jnp.float32,
            ).astype(out_ref.dtype)


def score_kernel(n, rows, meta_ref, *refs):
    x_refs, keyed_refs, row_ref, out_refs = refs[:4], refs[4:6], refs[6], refs[7 : 7 + n]
    held, more, wide, tile, keyed, sem, keyed_sem = refs[7 + n :]
    half = n // 2
    step = pl.program_id(0)
    part = wide.shape[1]
    near = out_refs[0].shape[2]
    lanes = near + out_refs[half].shape[2]
    cuts = tile_cuts(lanes)
    groups = lanes // BLK
    at_size = n * groups
    me = meta_ref[at_size + n]
    apart = reversed_bits(step, n)
    q = me ^ apart
    kvh, per = keyed.shape[0], keyed.shape[1] // n
    group = per // rows

    def load(i):
        span = n // 2 * per
        return [
            pltpu.make_async_copy(
                keyed_refs[i].at[h], keyed.at[h, pl.ds(i * span, span)], keyed_sem.at[i, h]
            )
            for h in range(kvh)
        ]

    @pl.when(step == 0)
    def _():
        load_tokens(
            n, meta_ref[at_size + n + 1], meta_ref[at_size + n + 2], x_refs, [], held, more, wide, sem,
            load(0) + load(1),
        )

    for i in range(2):

        @pl.when(step == i * (n // 2))
        def _(i=i):
            for copy in load(i):
                copy.wait()

    def one(t):
        here = slice(cuts[t], cuts[t + 1])
        count = (cuts[t + 1] - cuts[t]) // BLK
        raw = lax.dot_general(
            keyed[:, pl.ds(pl.multiple_of(step * per, per), per), :].reshape(kvh * per, part),
            list_tile(meta_ref, q * groups + cuts[t] // BLK, count, wide, tile),
            (((1,), (1,)), ((), ())),
            preferred_element_type=jnp.float32,
        ).reshape(kvh, rows, group, count * BLK)
        owner_row = row_ref[0, :, here]
        picked = jnp.zeros((kvh, group, count * BLK), jnp.float32)
        for r in range(rows):
            picked = picked + jnp.where((owner_row == r)[None], raw[:, r], 0.0)
        picked = picked.reshape(kvh * group, -1).astype(out_refs[0].dtype)
        piece = 0 if cuts[t] < near else 1
        for k in range(half):

            @pl.when(apart % half == k)
            def _(k=k):
                out_refs[piece * half + k][
                    q // half, :, cuts[t] - piece * near : cuts[t + 1] - piece * near
                ] = picked

    one(0)
    for t in range(1, len(cuts) - 1):
        pl.when(meta_ref[at_size + q] > cuts[t])(functools.partial(one, t))


def half_score_kernel(side_ref, *refs):
    *part_refs, mine_ref, send_ref = refs
    sums = []
    for side in (side_ref[0], 1 - side_ref[0]):
        got = part_refs[0][side].astype(jnp.float32)
        for ref in part_refs[1:]:
            got = got + ref[side].astype(jnp.float32)
        sums.append(got)
    mine_ref[...] = sums[0]
    send_ref[...] = sums[1].astype(send_ref.dtype)


def weight_kernel(scale, count, *refs):
    mine_refs, got_refs, row_refs = refs[:count], refs[count : 2 * count], refs[2 * count : 3 * count]
    top_ref, sum_ref = refs[3 * count : 3 * count + 2]
    w_refs, share_ref = refs[3 * count + 2 : -1], refs[-1]
    n = w_refs[0].shape[0]
    scores = [
        (mine[...] + got[...].astype(jnp.float32)) * scale
        for mine, got in zip(mine_refs, got_refs)
    ]
    owner_rows = [ref[...] for ref in row_refs]
    rows = range(top_ref.shape[0])
    spread = [jnp.zeros(s.shape, jnp.float32) for s in scores]
    tops = []
    for r in rows:
        top = top_ref[r]
        for o, s in zip(owner_rows, scores):
            top = jnp.maximum(top, jnp.max(jnp.where(o == r, s, -jnp.inf), 1, keepdims=True))
        tops.append(top)
        spread = [jnp.where(o == r, top, t) for o, t in zip(owner_rows, spread)]
    held = [
        jnp.exp(jnp.where(o >= 0, s - t, -jnp.inf))
        for o, s, t in zip(owner_rows, scores, spread)
    ]
    shares = [jnp.zeros(s.shape, jnp.float32) for s in scores]
    for r in rows:
        fade = jnp.exp(top_ref[r] - tops[r])
        total = sum_ref[r] * fade
        for o, h in zip(owner_rows, held):
            total = total + jnp.sum(jnp.where(o == r, h, 0.0), 1, keepdims=True)
        shares = [jnp.where(o == r, 1.0 / total, t) for o, t in zip(owner_rows, shares)]
        share_ref[r] = fade / total
    for h, t, w_ref in zip(held, shares, w_refs):
        weights = (h * t).astype(w_ref.dtype)
        for i in range(n):
            w_ref[i] = weights


def list_copies(n, lanes, sizes, source, target, sem):
    cuts = tile_cuts(lanes)

    def copies(o):
        for t in range(len(cuts) - 1):
            here = pl.ds(cuts[t], cuts[t + 1] - cuts[t])
            copy = pltpu.make_async_copy(source.at[o, here], target.at[o, here], sem.at[o, t])
            yield (True if t == 0 else sizes(o) > cuts[t]), copy

    return copies


def list_kernel(n, lanes, meta_ref, *refs):
    x_refs, (_, out_ref, held, more, wide, lists, sem, out_sem) = refs[:4], refs[4:]
    q = pl.program_id(0)
    length = lists.shape[1]
    cuts = tile_cuts(length)
    groups = lanes // BLK
    at_size = n * groups
    copies = list_copies(n, length, lambda o: meta_ref[at_size + o], lists, out_ref, out_sem)

    @pl.when(q == 0)
    def _():
        load_tokens(
            n, meta_ref[at_size + n + 1], meta_ref[at_size + n + 2], x_refs, [], held, more, wide,
            sem, [],
        )

    for t, (used, copy) in enumerate(copies(q)):

        @pl.when(used)
        def _(t=t, copy=copy):
            list_tile(
                meta_ref, q * groups + cuts[t] // BLK, (cuts[t + 1] - cuts[t]) // BLK, wide,
                lists.at[q, cuts[t] : cuts[t + 1]],
            )
            copy.start()

    @pl.when(q == n - 1)
    def _():
        for o in range(n):
            for used, copy in copies(o):
                pl.when(used)(copy.wait)


def value_kernel(n, rows, lanes, count, meta_ref, *refs):
    w_refs, (row_ref, list_ref, weight_ref) = refs[:count], refs[count : count + 3]
    out_refs, scratch = refs[count + 3 : count + 3 + n // 2], refs[count + 3 + n // 2 :]
    values, lists, acc, mixed, value_sem, sem = scratch
    step = pl.program_id(0)
    kvh, _, hd = values.shape
    load_values = [
        pltpu.make_async_copy(
            weight_ref.at[h, :, pl.ds(hd, hd)], values.at[h], value_sem.at[h]
        )
        for h in range(kvh)
    ]
    _, heads, near = w_refs[0].shape
    length = lists.shape[1]
    per = rows * heads // kvh
    cuts = tile_cuts(length)
    at_size = n * lanes // BLK
    me = meta_ref[at_size + n]
    q = partner_owner(step, me, n)
    size = meta_ref[at_size + q]
    copies = list_copies(n, length, lambda o: meta_ref[at_size + o], list_ref, lists, sem)
    ahead = min(3, n)

    def fetch(i):
        for used, copy in copies(partner_owner(i, me, n)):
            pl.when(used)(copy.start)

    @pl.when(step == 0)
    def _():
        for i in range(ahead):
            fetch(i)

    pl.when(step + ahead < n)(lambda: fetch(jnp.minimum(step + ahead, n - 1)))

    @pl.when(step == n // 2)
    def _():
        for load in load_values:
            load.start()

    for used, copy in copies(q):
        pl.when(used)(copy.wait)

    def one(t):
        here = slice(cuts[t], cuts[t + 1])
        width = cuts[t + 1] - cuts[t]
        piece = 0 if cuts[t] < near else 1
        weights = w_refs[piece][0, :, cuts[t] - piece * near : cuts[t + 1] - piece * near]
        weights = weights.astype(jnp.float32).reshape(kvh, 1, heads // kvh, width)
        owner_row = row_ref[0, :, here]
        spread = jnp.concatenate(
            [jnp.where((owner_row == r)[None, None], weights, 0.0) for r in range(rows)], 1
        ).reshape(kvh * per, width)
        got = jnp.dot(
            spread.astype(jnp.bfloat16), lists[q, here, :], preferred_element_type=jnp.float32
        )
        if t == 0:
            pl.when(size <= cuts[1])(lambda: keep(got))

            @pl.when(size > cuts[1])
            def _():
                acc[...] = got

        else:
            acc[...] += got

    def keep(sums):
        for h in range(kvh):
            mixed[h, pl.ds(pl.multiple_of(step * per, per), per), :] = sums[
                h * per : (h + 1) * per
            ].astype(mixed.dtype)

    one(0)
    for t in range(1, len(cuts) - 1):
        pl.when(size > cuts[t])(functools.partial(one, t))
    pl.when(size > cuts[1])(lambda: keep(acc[...]))

    @pl.when(step == n - 1)
    def _():
        for load in load_values:
            load.wait()
        for h in range(kvh):
            done = jnp.dot(mixed[h], values[h], preferred_element_type=jnp.float32)
            done = done.astype(jnp.bfloat16)
            for i in range(n):
                out_refs[i // 2][i % 2, h] = done[i * per : (i + 1) * per]


def half_sum_kernel(side_ref, *refs):
    *part_refs, kept_ref, send_ref, mine_ref = refs
    sides, kvh, _, _ = part_refs[0].shape
    rows, heads = kept_ref.shape[:2]
    group = heads // kvh
    for side in range(sides):
        own = side_ref[0] == side
        for h in range(kvh):
            terms = part_refs[0][side, h].astype(jnp.float32)
            for ref in part_refs[1:]:
                terms = terms + ref[side, h].astype(jnp.float32)
            kept = jnp.concatenate(
                [kept_ref[r, h * group : (h + 1) * group, :] for r in range(rows)]
            )
            terms = terms + jnp.where(own, kept, 0.0)
            mine_ref[side, h] = terms
            send_ref[side, h] = terms.astype(send_ref.dtype)


def partner_owner(i, me, n):
    half = n // 2
    return i % 2 * half + ((me % half) ^ (i // 2))


def whole_sum_kernel(mine_ref, got_ref, out_ref, total):
    sides, kvh, per, _ = mine_ref.shape
    rows = out_ref.shape[0] // sides
    group = per // rows
    total[...] = mine_ref[...] + got_ref[...].astype(jnp.float32)
    for h in range(kvh):
        for g in range(group):
            column = [
                total[side, h, pl.ds(g, rows, stride=group), :] for side in range(sides)
            ]
            head = h * group + g
            hd = column[0].shape[1]
            out_ref[:, head * hd : (head + 1) * hd] = jnp.concatenate(column).astype(
                out_ref.dtype
            )


def stage_kernel(core_ref, after_ref, weight_ref, own_ref, away_ref, sem):
    cuts = sem.shape[1]
    span, cols = own_ref.shape[0] // cuts, own_ref.shape[1]
    copies = [
        pltpu.make_async_copy(
            weight_ref.at[
                pl.ds(i * span, span), pl.ds(pl.multiple_of(side * cols, 128), cols)
            ],
            ref.at[pl.ds(i * span, span)],
            sem.at[j, i],
        )
        for j, (side, ref) in enumerate(((1 - core_ref[0], away_ref), (core_ref[0], own_ref)))
        for i in range(cuts)
    ]
    for copy in copies:
        copy.start()
    for copy in copies:
        copy.wait()


def order_kernel(n, me_ref, own_ref, got_ref, out_ref):
    half = n // 2
    rows = own_ref.shape[0] // n
    for q in range(0, n, 2):
        pair = []
        for owner in (q, q + 1):
            block = ((me_ref[0] % half) ^ (owner % half)) * 2 + owner // half
            here = pl.ds(pl.multiple_of(block * rows, rows), rows)
            pair.append(own_ref[here, :] + got_ref[here, :])
        out_ref[q * rows : (q + 2) * rows, :] = jnp.concatenate(pair).astype(out_ref.dtype)


def with_partner(x, k, n):
    return lax.ppermute(x, "pool", [(i, i ^ k) for i in range(n)])


def from_rest(held, n):
    k = n // 8
    while k >= 2:
        held = jnp.concatenate([held, with_partner(held, k, n)])
        k //= 2
    return held


def reversed_bits(k, n):
    out, bit = 0, 1
    while bit < n:
        out = out + (k // bit) % 2 * (n // 2 // bit)
        bit *= 2
    return out


def local(
    x_prompt, kv_weight, block_dest, block_row, block_fill, queries, kv_cache, cache_len, out_weight
):
    n = lax.axis_size("pool")
    ntp = lax.axis_size("tp")
    me = lax.axis_index("pool").astype(jnp.int32)
    core = lax.axis_index("tp").astype(jnp.int32)
    tokens, width = x_prompt.shape
    part = width // n
    kvh = kv_weight.shape[1]
    hd = kv_weight.shape[2] // 2
    rows, heads = queries.shape[0], queries.shape[1]
    group = heads // kvh
    per = rows * group
    cache_slots = kv_cache.shape[1]
    blocks = tokens // BLK
    cap = max(2, 2 * blocks // n)
    window = cap * BLK + BLK
    lanes = -(-n * window // 128) * 128
    half = tokens // ntp
    scale = 1.0 / hd**0.5
    swap = [(i, (i + 1) % ntp) for i in range(ntp)]

    size = half * 3 // 4
    extra = half - size
    at = jnp.stack([me, core])
    pack_fill, pack_dest = block_fill, block_dest[:, 0]
    packed = pack(x_prompt, pack_fill, pack_dest, at, n, 0, size)
    dest = pack_dest
    far = [with_partner(queries, k, n) for k in (n // 2, n // 4, n // 2 + n // 4)]
    packed, far[0], dest, block_row, block_fill, kv_weight = lax.optimization_barrier(
        (packed, far[0], dest, block_row, block_fill, kv_weight)
    )
    kv_weight = kv_weight.transpose(1, 0, 2)
    even = from_rest(jnp.stack([queries, *far]), n)
    mine = lax.all_to_all(packed, "pool", 0, 0, tiled=True).reshape(n * size, part)

    index = jnp.arange(n * blocks, dtype=jnp.int32)
    sender = index // blocks
    kin = sender[None, :] == sender[:, None]
    lower = kin & (dest[None, :] < dest[:, None])
    level = kin & (dest[None, :] == dest[:, None]) & (index[None, :] < index[:, None])
    before = jnp.sum(jnp.where(lower, block_fill[None, :], 0), 1)
    within = jnp.sum(jnp.where(level, block_fill[None, :], 0), 1)
    pair = jnp.arange(n * n, dtype=jnp.int32)
    to, by = pair // n, pair % n
    owned = dest[None, :] == to[:, None]
    sent = sender[None, :] == by[:, None]
    earlier = sent & (dest[None, :] < to[:, None])
    offset = jnp.sum(jnp.where(earlier, block_fill[None, :], 0), 1)
    amount = jnp.sum(jnp.where(sent & owned, block_fill[None, :], 0), 1)
    runs = jnp.where(amount > 0, (offset % BLK + amount + BLK - 1) // BLK * BLK, 0)
    runs_by = runs.reshape(n, n)
    prior = jnp.arange(n)[:, None] < jnp.arange(n)[None, :]
    targets = jnp.sum(jnp.where(prior[None], runs_by[:, :, None], 0), 1)
    list_rows = jnp.sum(runs_by, 1)
    targets = targets.reshape(-1)
    sources = by * tokens + offset // BLK * BLK
    group_at = jnp.arange(n * lanes // BLK, dtype=jnp.int32) * BLK
    skip = group_at[:, None] - (to * lanes + targets)[None, :]
    group_rows = jnp.sum(
        jnp.where((skip >= 0) & (skip < runs[None, :]), sources[None, :] + skip, 0), 1
    )
    mine_pair = (dest * n + sender)[:, None] == pair[None, :]
    start = (
        dest * lanes
        + jnp.sum(jnp.where(mine_pair, targets[None, :], 0), 1)
        + before % BLK
        + within
    )
    spot = jnp.arange(n * lanes, dtype=jnp.int32)[:, None]
    inside = (spot >= start[None, :]) & (spot < (start + block_fill)[None, :])
    rowof = jnp.sum(jnp.where(inside, (block_row + 1)[None, :], 0), 1) - 1
    rowof = rowof.reshape(n, 1, lanes)

    near = near_lanes(lanes)
    most = jnp.stack([jnp.max(jnp.sum(block_fill.reshape(n, blocks), 1)), jnp.max(list_rows)])
    groups = lax.axis_size("groups")
    k = 1
    while k < groups:
        most = jnp.maximum(
            most, lax.ppermute(most, "groups", [(i, i ^ k) for i in range(groups)])
        )
        k *= 2
    over, longer = most[0] > ntp * size, most[1] > near

    def exchange_rest():
        rest = pack(x_prompt, pack_fill, pack_dest, at, n, ntp * size, extra)
        rest = lax.all_to_all(rest, "pool", 0, 0, tiled=True).reshape(n * extra, part)
        return rest, lax.ppermute(rest, "tp", swap)

    def no_rest():
        return (jnp.zeros((n * extra, part), jnp.bfloat16),) * 2

    more_mine, more_other = lax.cond(over, exchange_rest, no_rest)
    meta = jnp.concatenate(
        [group_rows, list_rows, jnp.stack([me, core, over.astype(jnp.int32)])]
    )

    def through_keys(held):
        held = held.reshape(n // 2 * rows, heads, hd)
        return pl.pallas_call(
            key_kernel,
            grid=(kvh,),
            in_specs=[
                pl.BlockSpec(held.shape, lambda h: (0, 0, 0)),
                pl.BlockSpec((1, part, 2 * hd), lambda h: (h, 0, 0)),
            ],
            out_specs=pl.BlockSpec((1, n // 2 * per, part), lambda h: (h, 0, 0)),
            out_shape=jax.ShapeDtypeStruct((kvh, n // 2 * per, part), jnp.bfloat16),
            compiler_params=pltpu.CompilerParams(vmem_limit_bytes=16 * MIB),
            cost_estimate=pl.CostEstimate(flops=0, bytes_accessed=1024, transcendentals=0),
            name="key_projection",
        )(held, kv_weight)

    keyed_even = through_keys(even)
    keyed_odd = through_keys(with_partner(even, 1, n))

    mine, meta, rowof, keyed_even, keyed_odd = lax.optimization_barrier(
        (mine, meta, rowof, keyed_even, keyed_odd)
    )
    other = lax.ppermute(mine, "tp", swap)

    anywhere = pl.BlockSpec(memory_space=pl.ANY)
    pair_shape = (2, kvh, per, hd)
    slot_shapes = [
        jax.ShapeDtypeStruct((n, heads, length), jnp.bfloat16) for length in (near, lanes - near)
    ]
    in_vmem = pl.BlockSpec(memory_space=pltpu.VMEM)
    x_parts = (mine, other, more_mine, more_other)
    x_scratch = [
        pltpu.VMEM((ntp, n * size, part), jnp.bfloat16),
        pltpu.VMEM((ntp, n * extra, part), jnp.bfloat16),
        pltpu.VMEM((n * tokens, part), jnp.float32),
    ]
    at_me = n * lanes // BLK + n

    def owner(i, m):
        return m[at_me] ^ reversed_bits(i, n)

    half = n // 2
    lengths = (near, lanes - near)
    score_parts = pl.pallas_call(
        functools.partial(score_kernel, n, rows),
        grid_spec=pltpu.PrefetchScalarGridSpec(
            num_scalar_prefetch=1,
            grid=(n,),
            in_specs=[
                *[anywhere] * 6,
                pl.BlockSpec((1, 1, lanes), lambda i, m: (owner(i, m), 0, 0)),
            ],
            out_specs=[
                pl.BlockSpec((2, heads, length), lambda i, m: (0, 0, 0))
                for length in lengths
                for _ in range(half)
            ],
            scratch_shapes=[
                *x_scratch,
                pltpu.VMEM((tile_cuts(lanes)[1], part), jnp.bfloat16),
                pltpu.VMEM((kvh, n * per, part), jnp.bfloat16),
                pltpu.SemaphoreType.DMA((ntp, 4)),
                pltpu.SemaphoreType.DMA((2, kvh)),
            ],
        ),
        out_shape=[
            jax.ShapeDtypeStruct((2, heads, length), jnp.bfloat16)
            for length in lengths
            for _ in range(half)
        ],
        compiler_params=pltpu.CompilerParams(vmem_limit_bytes=24 * MIB),
        name="prompt_scores",
    )(meta, *x_parts, keyed_even, keyed_odd, rowof)

    my_rows = lax.dynamic_index_in_dim(rowof, me, 0, keepdims=False)

    def exchange_weights(*scores):
        count = len(scores)
        mine_sums, got_sums = [], []
        for parts, length in zip(scores, lengths):
            parts = [parts[0]] + [with_partner(parts[k], k, n) for k in range(1, half)]
            mine_sum, send_sum = pl.pallas_call(
                half_score_kernel,
                in_specs=[pl.BlockSpec(memory_space=pltpu.SMEM), *[in_vmem] * half],
                out_shape=[
                    jax.ShapeDtypeStruct((heads, length), jnp.float32),
                    jax.ShapeDtypeStruct((heads, length), jnp.bfloat16),
                ],
                compiler_params=pltpu.CompilerParams(vmem_limit_bytes=4 * MIB),
                name="half_pool_scores",
            )((me // half).reshape(1), *parts)
            mine_sums.append(mine_sum)
            got_sums.append(with_partner(send_sum, half, n))
        query = queries.reshape(rows, kvh, group, hd)
        cache_scores = (
            jnp.einsum(
                "rhgd,rthd->rhgt", query, kv_cache[:, :, :, :hd], preferred_element_type=jnp.float32
            )
            * scale
        )
        cache_live = jnp.arange(cache_slots, dtype=jnp.int32)[None, :] < cache_len[:, None]
        cache_scores = jnp.where(cache_live[:, None, None, :], cache_scores, -jnp.inf)
        cache_top = jnp.max(cache_scores, -1, keepdims=True)
        cache_exp = jnp.exp(cache_scores - cache_top)
        cache_sum = jnp.sum(cache_exp, -1, keepdims=True)
        row_parts = [my_rows[:, :near], my_rows[:, near:]][:count]
        *weights, share = pl.pallas_call(
            functools.partial(weight_kernel, scale, count),
            out_shape=[*slot_shapes[:count], jax.ShapeDtypeStruct((rows, heads, 1), jnp.float32)],
            compiler_params=pltpu.CompilerParams(vmem_limit_bytes=8 * MIB),
            name="softmax_weights",
        )(
            *mine_sums,
            *got_sums,
            *row_parts,
            cache_top.reshape(rows, heads, 1),
            cache_sum.reshape(rows, heads, 1),
        )
        length = near if count == 1 else lanes
        lists = pl.pallas_call(
            functools.partial(list_kernel, n, lanes),
            grid_spec=pltpu.PrefetchScalarGridSpec(
                num_scalar_prefetch=1,
                grid=(n,),
                in_specs=[anywhere] * 5,
                out_specs=anywhere,
                scratch_shapes=[
                    *x_scratch,
                    pltpu.VMEM((n, length, part), jnp.bfloat16),
                    pltpu.SemaphoreType.DMA((ntp, 4)),
                    pltpu.SemaphoreType.DMA((n, len(tile_cuts(length)) - 1)),
                ],
            ),
            out_shape=jax.ShapeDtypeStruct((n, length, part), jnp.bfloat16),
            compiler_params=pltpu.CompilerParams(vmem_limit_bytes=56 * MIB),
            cost_estimate=pl.CostEstimate(
                flops=0, bytes_accessed=16 * MIB, transcendentals=0
            ),
            name="owner_lists",
        )(meta, *x_parts, weights[0])
        weights = [lax.all_to_all(w, "pool", 0, 0, tiled=True) for w in weights]
        cached = jnp.einsum(
            "rhgt,rthd->rhgd",
            cache_exp.astype(jnp.bfloat16),
            kv_cache[:, :, :, hd:],
            preferred_element_type=jnp.float32,
        )
        terms = pl.pallas_call(
            functools.partial(value_kernel, n, rows, lanes, count),
            grid_spec=pltpu.PrefetchScalarGridSpec(
                num_scalar_prefetch=1,
                grid=(n,),
                in_specs=[
                    *[
                        pl.BlockSpec(
                            (1, heads, shape.shape[2]),
                            lambda i, m: (partner_owner(i, m[at_me], n), 0, 0),
                        )
                        for shape in slot_shapes[:count]
                    ],
                    pl.BlockSpec(
                        (1, 1, lanes), lambda i, m: (partner_owner(i, m[at_me], n), 0, 0)
                    ),
                    pl.BlockSpec(memory_space=pltpu.HBM),
                    anywhere,
                ],
                out_specs=[pl.BlockSpec(pair_shape, lambda i, m: (0, 0, 0, 0))] * (n // 2),
                scratch_shapes=[
                    pltpu.VMEM((kvh, part, hd), jnp.bfloat16),
                    pltpu.VMEM((n, length, part), jnp.bfloat16),
                    pltpu.VMEM((kvh * per, part), jnp.float32),
                    pltpu.VMEM((kvh, n * per, part), jnp.bfloat16),
                    pltpu.SemaphoreType.DMA((kvh,)),
                    pltpu.SemaphoreType.DMA((n, len(tile_cuts(length)) - 1)),
                ],
            ),
            out_shape=[jax.ShapeDtypeStruct(pair_shape, jnp.bfloat16)] * (n // 2),
            compiler_params=pltpu.CompilerParams(vmem_limit_bytes=24 * MIB),
            name="weighted_values",
        )(meta, *weights, rowof, lists, kv_weight)
        return *terms, cached.reshape(rows, heads, hd) * share

    *terms, kept = lax.cond(
        longer,
        lambda: exchange_weights(score_parts[:half], score_parts[half:]),
        lambda: exchange_weights(score_parts[:half]),
    )

    term_parts = [terms[0]] + [with_partner(terms[k], k, n) for k in range(1, n // 2)]
    send, held = pl.pallas_call(
        half_sum_kernel,
        in_specs=[pl.BlockSpec(memory_space=pltpu.SMEM), *[in_vmem] * (n // 2 + 1)],
        out_shape=[
            jax.ShapeDtypeStruct(pair_shape, jnp.bfloat16),
            jax.ShapeDtypeStruct(pair_shape, jnp.float32),
        ],
        compiler_params=pltpu.CompilerParams(vmem_limit_bytes=8 * MIB),
        name="half_pool_sum",
    )((me // (n // 2)).reshape(1), *term_parts, kept)
    attended = pl.pallas_call(
        whole_sum_kernel,
        out_shape=jax.ShapeDtypeStruct((2 * rows, heads * hd), jnp.bfloat16),
        scratch_shapes=[pltpu.VMEM(pair_shape, jnp.float32)],
        compiler_params=pltpu.CompilerParams(vmem_limit_bytes=8 * MIB),
        name="attended_sum",
    )(held, with_partner(send, n // 2, n))

    cols = out_weight.shape[1] // ntp
    own_weight, away_weight = pl.pallas_call(
        stage_kernel,
        in_specs=[
            pl.BlockSpec(memory_space=pltpu.SMEM),
            anywhere,
            pl.BlockSpec(memory_space=pltpu.HBM),
        ],
        out_specs=[in_vmem] * 2,
        out_shape=[jax.ShapeDtypeStruct((out_weight.shape[0], cols), jnp.bfloat16)] * 2,
        scratch_shapes=[pltpu.SemaphoreType.DMA((2, 4))],
        compiler_params=pltpu.CompilerParams(vmem_limit_bytes=16 * MIB),
        cost_estimate=pl.CostEstimate(
            flops=0, bytes_accessed=2 * out_weight.size * 2, transcendentals=0
        ),
        name="stage_out_weight",
    )(core.reshape(1), send, out_weight)

    everyone = [attended] + [with_partner(attended, k, n) for k in range(1, n // 2)]
    everyone = jnp.concatenate(everyone)
    away = jnp.dot(everyone, away_weight, preferred_element_type=jnp.float32)
    half_spec = pl.BlockSpec((n * rows, cols), lambda i, m: (0, 0))
    got = lax.ppermute(away, "tp", swap)
    own = jnp.dot(everyone, own_weight, preferred_element_type=jnp.float32)
    return pl.pallas_call(
        functools.partial(order_kernel, n),
        grid_spec=pltpu.PrefetchScalarGridSpec(
            num_scalar_prefetch=1,
            grid=(1,),
            in_specs=[half_spec] * 2,
            out_specs=half_spec,
        ),
        out_shape=jax.ShapeDtypeStruct((n * rows, cols), jnp.bfloat16),
        compiler_params=pltpu.CompilerParams(vmem_limit_bytes=4 * MIB),
        name="order_rows",
    )(me.reshape(1), own, got)


def solution(mesh):
    in_specs = (
        P(("groups", "pool"), None),
        P("pool", "tp", None),
        P("groups", None),
        P("groups"),
        P("groups"),
        P(("groups", "pool"), "tp", None),
        P(("groups", "pool"), None, "tp", None),
        P(("groups", "pool")),
        P("tp", "pool"),
    )
    out_specs = P("groups", ("pool", "tp"))
    return jax.shard_map(local, mesh=mesh, in_specs=in_specs, out_specs=out_specs, check_vma=False)
```

```python
import functools

import jax
import jax.numpy as jnp
from jax import lax
from jax.experimental import pallas as pl
from jax.experimental.pallas import tpu as pltpu
from jax.sharding import PartitionSpec as P

BLK = 8
MIB = 1 << 20


def pack_kernel(base, at_ref, fill_ref, dest_ref, x_ref, out_ref, packed, count, out_sem):
    n, size, part = packed.shape
    tokens = x_ref.shape[0]
    blocks = tokens // BLK

    def store(q):
        return pltpu.make_async_copy(packed.at[q], out_ref.at[q], out_sem.at[q])

    first = at_ref[0] * blocks
    for q in range(n):
        count[q] = 0

    owners = [dest_ref[first + b] for b in range(blocks)]
    fills = [fill_ref[first + b] for b in range(blocks)]
    for owner, fill in zip(owners, fills):
        count[owner] = count[owner] + fill
    total = jnp.int32(0)
    for q in range(n):
        here = count[q]
        count[q] = total
        total = total + here
    token = lax.broadcasted_iota(jnp.int32, (1, tokens), 1)
    ranks = jnp.full((1, tokens), -1, jnp.int32)
    for b, (owner, fill) in enumerate(zip(owners, fills)):
        start = count[owner]
        count[owner] = start + fill
        inner = token - b * BLK
        ranks = jnp.where((inner >= 0) & (inner < fill), start + inner, ranks)
    wanted = base + at_ref[1] * size + lax.broadcasted_iota(jnp.int32, (size, tokens), 0)
    pick = (wanted == ranks).astype(jnp.bfloat16)
    for q in range(n):
        packed[q] = jnp.dot(
            pick, x_ref[:, q * part : (q + 1) * part], preferred_element_type=jnp.float32
        ).astype(packed.dtype)
        store(q).start()
    for q in range(n):
        store(q).wait()


def pack(x_prompt, fill, dest, at, n, base, size, grant=16):
    tokens, width = x_prompt.shape
    part = width // n
    return pl.pallas_call(
        functools.partial(pack_kernel, base),
        grid_spec=pltpu.PrefetchScalarGridSpec(
            num_scalar_prefetch=3,
            grid=(1,),
            in_specs=[pl.BlockSpec(memory_space=pltpu.VMEM)],
            out_specs=pl.BlockSpec(memory_space=pl.ANY),
            scratch_shapes=[
                pltpu.VMEM((n, size, part), jnp.bfloat16),
                pltpu.SMEM((n,), jnp.int32),
                pltpu.SemaphoreType.DMA((n,)),
            ],
        ),
        out_shape=jax.ShapeDtypeStruct((n, size, part), jnp.bfloat16),
        compiler_params=pltpu.CompilerParams(vmem_limit_bytes=grant * MIB),
        cost_estimate=pl.CostEstimate(
            flops=2 * size * tokens * width, bytes_accessed=64 * MIB, transcendentals=0
        ),
        name="pack_live_tokens",
    )(at, fill, dest, x_prompt)


def tile_cuts(lanes):
    return [0] + list(range(min(256, lanes), lanes, 128)) + [lanes]


def near_lanes(lanes):
    return min(lanes, -(-lanes * 3 // 5 // 128) * 128)


def widen(core, n, refs, wide, base, first, last):
    length = refs[0].shape[0] // n
    tokens = wide.shape[0] // n

    @pl.loop(first, last)
    def _(s):
        for j, ref in enumerate(refs):
            side = core if j == 0 else 1 - core
            to = pl.multiple_of(s * tokens + base + side * length, BLK)
            wide[pl.ds(to, length), :] = ref[
                pl.ds(pl.multiple_of(s * length, length), length), :
            ].astype(wide.dtype)


def span_copies(refs, buffer, sem):
    cuts = sem.shape[1]
    span = buffer.shape[1] // cuts
    return [
        [
            pltpu.make_async_copy(
                ref.at[pl.ds(i * span, span)], buffer.at[j, pl.ds(i * span, span)], sem.at[j, i]
            )
            for j, ref in enumerate(refs)
        ]
        for i in range(cuts)
    ]


def load_tokens(n, core, over, x_refs, there, held, more, wide, sem, others):
    main = span_copies(x_refs[: 2 - len(there)], held, sem)
    for pair in main:
        for copy in pair:
            copy.start()
    for copy in others:
        copy.start()
    for i, pair in enumerate(main):
        for copy in pair:
            copy.wait()
        parts = [held.at[j] for j in range(2 - len(there))] + there
        widen(core, n, parts, wide, 0, i * n // len(main), (i + 1) * n // len(main))

    @pl.when(over != 0)
    def _():
        rest = span_copies(x_refs[2:], more, sem)
        for pair in rest:
            for copy in pair:
                copy.start()
        for pair in rest:
            for copy in pair:
                copy.wait()
        base = wide.shape[0] // n - 2 * more.shape[1] // n
        widen(core, n, [more.at[0], more.at[1]], wide, base, 0, n)


def list_tile(meta_ref, first, count, wide, tile):
    for i in range(0, count, 2):
        pair = [
            wide[pl.ds(pl.multiple_of(meta_ref[first + i + j], BLK), BLK), :] for j in range(2)
        ]
        tile[i * BLK : (i + 2) * BLK, :] = jnp.concatenate(pair).astype(tile.dtype)
    return tile[: count * BLK, :]


def key_kernel(query_ref, weight_ref, out_ref):
    group = out_ref.shape[1] // query_ref.shape[0]
    hd = query_ref.shape[2]
    h = pl.program_id(0)
    for i in range(query_ref.shape[1] // group):

        @pl.when(h == i)
        def _(i=i):
            query = query_ref[:, i * group : (i + 1) * group, :].astype(jnp.float32)
            out_ref[0] = lax.dot_general(
                query.reshape(-1, hd).astype(jnp.bfloat16),
                weight_ref[0, :, :hd],
                (((1,), (1,)), ((), ())),
                preferred_element_type=jnp.float32,
            ).astype(out_ref.dtype)


def score_kernel(n, rows, meta_ref, *refs):
    x_refs, keyed_refs, (row_ref, near_ref, rest_ref) = refs[:4], refs[4:6], refs[6:9]
    held, more, wide, tile, keyed, sem, keyed_sem = refs[9:]
    step = pl.program_id(0)
    part = wide.shape[1]
    near = near_ref.shape[2]
    lanes = near + rest_ref.shape[2]
    cuts = tile_cuts(lanes)
    groups = lanes // BLK
    at_size = n * groups
    q = meta_ref[at_size + n] ^ reversed_bits(step, n)
    kvh, per = keyed.shape[0], keyed.shape[1] // n
    group = per // rows

    def load(i):
        span = n // 2 * per
        return [
            pltpu.make_async_copy(
                keyed_refs[i].at[h], keyed.at[h, pl.ds(i * span, span)], keyed_sem.at[i, h]
            )
            for h in range(kvh)
        ]

    @pl.when(step == 0)
    def _():
        load_tokens(
            n, meta_ref[at_size + n + 1], meta_ref[at_size + n + 2], x_refs, [], held, more, wide, sem,
            load(0) + load(1),
        )

    for i in range(2):

        @pl.when(step == i * (n // 2))
        def _(i=i):
            for copy in load(i):
                copy.wait()

    def one(t):
        here = slice(cuts[t], cuts[t + 1])
        count = (cuts[t + 1] - cuts[t]) // BLK
        raw = lax.dot_general(
            keyed[:, pl.ds(pl.multiple_of(step * per, per), per), :].reshape(kvh * per, part),
            list_tile(meta_ref, q * groups + cuts[t] // BLK, count, wide, tile),
            (((1,), (1,)), ((), ())),
            preferred_element_type=jnp.float32,
        ).reshape(kvh, rows, group, count * BLK)
        owner_row = row_ref[0, :, here]
        picked = jnp.zeros((kvh, group, count * BLK), jnp.float32)
        for r in range(rows):
            picked = picked + jnp.where((owner_row == r)[None], raw[:, r], 0.0)
        picked = picked.reshape(kvh * group, -1).astype(near_ref.dtype)
        if cuts[t] < near:
            near_ref[0, :, here] = picked
        else:
            rest_ref[0, :, cuts[t] - near : cuts[t + 1] - near] = picked

    one(0)
    for t in range(1, len(cuts) - 1):
        pl.when(meta_ref[at_size + q] > cuts[t])(functools.partial(one, t))


def weight_kernel(scale, count, *refs):
    part_refs, row_refs = refs[:count], refs[count : 2 * count]
    top_ref, sum_ref = refs[2 * count : 2 * count + 2]
    w_refs, share_ref = refs[2 * count + 2 : -1], refs[-1]
    n = part_refs[0].shape[0]
    scores, owner_rows = [], []
    for part_ref, row_ref in zip(part_refs, row_refs):
        got = part_ref[0].astype(jnp.float32)
        for i in range(1, n):
            got = got + part_ref[i].astype(jnp.float32)
        scores.append(got * scale)
        owner_rows.append(row_ref[...])
    rows = range(top_ref.shape[0])
    spread = [jnp.zeros(s.shape, jnp.float32) for s in scores]
    tops = []
    for r in rows:
        top = top_ref[r]
        for o, s in zip(owner_rows, scores):
            top = jnp.maximum(top, jnp.max(jnp.where(o == r, s, -jnp.inf), 1, keepdims=True))
        tops.append(top)
        spread = [jnp.where(o == r, top, t) for o, t in zip(owner_rows, spread)]
    held = [
        jnp.exp(jnp.where(o >= 0, s - t, -jnp.inf))
        for o, s, t in zip(owner_rows, scores, spread)
    ]
    shares = [jnp.zeros(s.shape, jnp.float32) for s in scores]
    for r in rows:
        fade = jnp.exp(top_ref[r] - tops[r])
        total = sum_ref[r] * fade
        for o, h in zip(owner_rows, held):
            total = total + jnp.sum(jnp.where(o == r, h, 0.0), 1, keepdims=True)
        shares = [jnp.where(o == r, 1.0 / total, t) for o, t in zip(owner_rows, shares)]
        share_ref[r] = fade / total
    for h, t, w_ref in zip(held, shares, w_refs):
        weights = (h * t).astype(w_ref.dtype)
        for i in range(n):
            w_ref[i] = weights


def list_copies(n, lanes, sizes, source, target, sem):
    cuts = tile_cuts(lanes)

    def copies(o):
        for t in range(len(cuts) - 1):
            here = pl.ds(cuts[t], cuts[t + 1] - cuts[t])
            copy = pltpu.make_async_copy(source.at[o, here], target.at[o, here], sem.at[o, t])
            yield (True if t == 0 else sizes(o) > cuts[t]), copy

    return copies


def list_kernel(n, lanes, meta_ref, *refs):
    x_refs, (_, out_ref, held, more, wide, lists, sem, out_sem) = refs[:4], refs[4:]
    q = pl.program_id(0)
    length = lists.shape[1]
    cuts = tile_cuts(length)
    groups = lanes // BLK
    at_size = n * groups
    copies = list_copies(n, length, lambda o: meta_ref[at_size + o], lists, out_ref, out_sem)

    @pl.when(q == 0)
    def _():
        load_tokens(
            n, meta_ref[at_size + n + 1], meta_ref[at_size + n + 2], x_refs, [], held, more, wide,
            sem, [],
        )

    for t, (used, copy) in enumerate(copies(q)):

        @pl.when(used)
        def _(t=t, copy=copy):
            list_tile(
                meta_ref, q * groups + cuts[t] // BLK, (cuts[t + 1] - cuts[t]) // BLK, wide,
                lists.at[q, cuts[t] : cuts[t + 1]],
            )
            copy.start()

    @pl.when(q == n - 1)
    def _():
        for o in range(n):
            for used, copy in copies(o):
                pl.when(used)(copy.wait)


def value_kernel(n, rows, lanes, count, meta_ref, *refs):
    w_refs, (row_ref, list_ref, weight_ref) = refs[:count], refs[count : count + 3]
    out_refs, scratch = refs[count + 3 : count + 3 + n // 2], refs[count + 3 + n // 2 :]
    values, lists, acc, mixed, value_sem, sem = scratch
    step = pl.program_id(0)
    kvh, _, hd = values.shape
    load_values = [
        pltpu.make_async_copy(
            weight_ref.at[h, :, pl.ds(hd, hd)], values.at[h], value_sem.at[h]
        )
        for h in range(kvh)
    ]
    _, heads, near = w_refs[0].shape
    length = lists.shape[1]
    per = rows * heads // kvh
    cuts = tile_cuts(length)
    at_size = n * lanes // BLK
    me = meta_ref[at_size + n]
    q = partner_owner(step, me, n)
    size = meta_ref[at_size + q]
    copies = list_copies(n, length, lambda o: meta_ref[at_size + o], list_ref, lists, sem)
    ahead = min(3, n)

    def fetch(i):
        for used, copy in copies(partner_owner(i, me, n)):
            pl.when(used)(copy.start)

    @pl.when(step == 0)
    def _():
        for i in range(ahead):
            fetch(i)

    pl.when(step + ahead < n)(lambda: fetch(jnp.minimum(step + ahead, n - 1)))

    @pl.when(step == n // 2)
    def _():
        for load in load_values:
            load.start()

    for used, copy in copies(q):
        pl.when(used)(copy.wait)

    def one(t):
        here = slice(cuts[t], cuts[t + 1])
        width = cuts[t + 1] - cuts[t]
        piece = 0 if cuts[t] < near else 1
        weights = w_refs[piece][0, :, cuts[t] - piece * near : cuts[t + 1] - piece * near]
        weights = weights.astype(jnp.float32).reshape(kvh, 1, heads // kvh, width)
        owner_row = row_ref[0, :, here]
        spread = jnp.concatenate(
            [jnp.where((owner_row == r)[None, None], weights, 0.0) for r in range(rows)], 1
        ).reshape(kvh * per, width)
        got = jnp.dot(
            spread.astype(jnp.bfloat16), lists[q, here, :], preferred_element_type=jnp.float32
        )
        if t == 0:
            pl.when(size <= cuts[1])(lambda: keep(got))

            @pl.when(size > cuts[1])
            def _():
                acc[...] = got

        else:
            acc[...] += got

    def keep(sums):
        for h in range(kvh):
            mixed[h, pl.ds(pl.multiple_of(step * per, per), per), :] = sums[
                h * per : (h + 1) * per
            ].astype(mixed.dtype)

    one(0)
    for t in range(1, len(cuts) - 1):
        pl.when(size > cuts[t])(functools.partial(one, t))
    pl.when(size > cuts[1])(lambda: keep(acc[...]))

    @pl.when(step == n - 1)
    def _():
        for load in load_values:
            load.wait()
        for h in range(kvh):
            done = jnp.dot(mixed[h], values[h], preferred_element_type=jnp.float32)
            done = done.astype(jnp.bfloat16)
            for i in range(n):
                out_refs[i // 2][i % 2, h] = done[i * per : (i + 1) * per]


def half_sum_kernel(side_ref, *refs):
    *part_refs, kept_ref, send_ref, mine_ref = refs
    sides, kvh, _, _ = part_refs[0].shape
    rows, heads = kept_ref.shape[:2]
    group = heads // kvh
    for side in range(sides):
        own = side_ref[0] == side
        for h in range(kvh):
            terms = part_refs[0][side, h].astype(jnp.float32)
            for ref in part_refs[1:]:
                terms = terms + ref[side, h].astype(jnp.float32)
            kept = jnp.concatenate(
                [kept_ref[r, h * group : (h + 1) * group, :] for r in range(rows)]
            )
            terms = terms + jnp.where(own, kept, 0.0)
            mine_ref[side, h] = terms
            send_ref[side, h] = terms.astype(send_ref.dtype)


def partner_owner(i, me, n):
    half = n // 2
    return i % 2 * half + ((me % half) ^ (i // 2))


def whole_sum_kernel(mine_ref, got_ref, out_ref, total):
    sides, kvh, per, _ = mine_ref.shape
    rows = out_ref.shape[0] // sides
    group = per // rows
    total[...] = mine_ref[...] + got_ref[...].astype(jnp.float32)
    for h in range(kvh):
        for g in range(group):
            column = [
                total[side, h, pl.ds(g, rows, stride=group), :] for side in range(sides)
            ]
            head = h * group + g
            hd = column[0].shape[1]
            out_ref[:, head * hd : (head + 1) * hd] = jnp.concatenate(column).astype(
                out_ref.dtype
            )


def stage_kernel(core_ref, after_ref, weight_ref, own_ref, away_ref, sem):
    cuts = sem.shape[1]
    span, cols = own_ref.shape[0] // cuts, own_ref.shape[1]
    copies = [
        pltpu.make_async_copy(
            weight_ref.at[
                pl.ds(i * span, span), pl.ds(pl.multiple_of(side * cols, 128), cols)
            ],
            ref.at[pl.ds(i * span, span)],
            sem.at[j, i],
        )
        for j, (side, ref) in enumerate(((1 - core_ref[0], away_ref), (core_ref[0], own_ref)))
        for i in range(cuts)
    ]
    for copy in copies:
        copy.start()
    for copy in copies:
        copy.wait()


def order_kernel(n, me_ref, own_ref, got_ref, out_ref):
    half = n // 2
    rows = own_ref.shape[0] // n
    for q in range(0, n, 2):
        pair = []
        for owner in (q, q + 1):
            block = ((me_ref[0] % half) ^ (owner % half)) * 2 + owner // half
            here = pl.ds(pl.multiple_of(block * rows, rows), rows)
            pair.append(own_ref[here, :] + got_ref[here, :])
        out_ref[q * rows : (q + 2) * rows, :] = jnp.concatenate(pair).astype(out_ref.dtype)


def with_partner(x, k, n):
    return lax.ppermute(x, "pool", [(i, i ^ k) for i in range(n)])


def from_rest(held, n):
    k = n // 8
    while k >= 2:
        held = jnp.concatenate([held, with_partner(held, k, n)])
        k //= 2
    return held


def reversed_bits(k, n):
    out, bit = 0, 1
    while bit < n:
        out = out + (k // bit) % 2 * (n // 2 // bit)
        bit *= 2
    return out


def local(
    x_prompt, kv_weight, block_dest, block_row, block_fill, queries, kv_cache, cache_len, out_weight
):
    n = lax.axis_size("pool")
    ntp = lax.axis_size("tp")
    me = lax.axis_index("pool").astype(jnp.int32)
    core = lax.axis_index("tp").astype(jnp.int32)
    tokens, width = x_prompt.shape
    part = width // n
    kvh = kv_weight.shape[1]
    hd = kv_weight.shape[2] // 2
    rows, heads = queries.shape[0], queries.shape[1]
    group = heads // kvh
    per = rows * group
    cache_slots = kv_cache.shape[1]
    blocks = tokens // BLK
    cap = max(2, 2 * blocks // n)
    window = cap * BLK + BLK
    lanes = -(-n * window // 128) * 128
    half = tokens // ntp
    scale = 1.0 / hd**0.5
    swap = [(i, (i + 1) % ntp) for i in range(ntp)]

    size = half * 3 // 4
    extra = half - size
    at = jnp.stack([me, core])
    pack_fill, pack_dest = block_fill, block_dest[:, 0]
    packed = pack(x_prompt, pack_fill, pack_dest, at, n, 0, size)
    dest = pack_dest
    far = [with_partner(queries, k, n) for k in (n // 2, n // 4, n // 2 + n // 4)]
    packed, far, dest, block_row, block_fill, kv_weight = lax.optimization_barrier(
        (packed, far, dest, block_row, block_fill, kv_weight)
    )
    kv_weight = kv_weight.transpose(1, 0, 2)
    even = from_rest(jnp.stack([queries, *far]), n)
    mine = lax.all_to_all(packed, "pool", 0, 0, tiled=True).reshape(n * size, part)

    index = jnp.arange(n * blocks, dtype=jnp.int32)
    sender = index // blocks
    kin = sender[None, :] == sender[:, None]
    lower = kin & (dest[None, :] < dest[:, None])
    level = kin & (dest[None, :] == dest[:, None]) & (index[None, :] < index[:, None])
    before = jnp.sum(jnp.where(lower, block_fill[None, :], 0), 1)
    within = jnp.sum(jnp.where(level, block_fill[None, :], 0), 1)
    pair = jnp.arange(n * n, dtype=jnp.int32)
    to, by = pair // n, pair % n
    owned = dest[None, :] == to[:, None]
    sent = sender[None, :] == by[:, None]
    earlier = sent & (dest[None, :] < to[:, None])
    offset = jnp.sum(jnp.where(earlier, block_fill[None, :], 0), 1)
    amount = jnp.sum(jnp.where(sent & owned, block_fill[None, :], 0), 1)
    runs = jnp.where(amount > 0, (offset % BLK + amount + BLK - 1) // BLK * BLK, 0)
    runs_by = runs.reshape(n, n)
    prior = jnp.arange(n)[:, None] < jnp.arange(n)[None, :]
    targets = jnp.sum(jnp.where(prior[None], runs_by[:, :, None], 0), 1)
    list_rows = jnp.sum(runs_by, 1)
    targets = targets.reshape(-1)
    sources = by * tokens + offset // BLK * BLK
    group_at = jnp.arange(n * lanes // BLK, dtype=jnp.int32) * BLK
    skip = group_at[:, None] - (to * lanes + targets)[None, :]
    group_rows = jnp.sum(
        jnp.where((skip >= 0) & (skip < runs[None, :]), sources[None, :] + skip, 0), 1
    )
    mine_pair = (dest * n + sender)[:, None] == pair[None, :]
    start = (
        dest * lanes
        + jnp.sum(jnp.where(mine_pair, targets[None, :], 0), 1)
        + before % BLK
        + within
    )
    spot = jnp.arange(n * lanes, dtype=jnp.int32)[:, None]
    inside = (spot >= start[None, :]) & (spot < (start + block_fill)[None, :])
    rowof = jnp.sum(jnp.where(inside, (block_row + 1)[None, :], 0), 1) - 1
    rowof = rowof.reshape(n, 1, lanes)

    near = near_lanes(lanes)
    most = jnp.stack([jnp.max(jnp.sum(block_fill.reshape(n, blocks), 1)), jnp.max(list_rows)])
    groups = lax.axis_size("groups")
    k = 1
    while k < groups:
        most = jnp.maximum(
            most, lax.ppermute(most, "groups", [(i, i ^ k) for i in range(groups)])
        )
        k *= 2
    over, longer = most[0] > ntp * size, most[1] > near

    def exchange_rest():
        rest = pack(x_prompt, pack_fill, pack_dest, at, n, ntp * size, extra, 59)
        rest = lax.all_to_all(rest, "pool", 0, 0, tiled=True).reshape(n * extra, part)
        return rest, lax.ppermute(rest, "tp", swap)

    def no_rest():
        return (jnp.zeros((n * extra, part), jnp.bfloat16),) * 2

    more_mine, more_other = lax.cond(over, exchange_rest, no_rest)
    meta = jnp.concatenate(
        [group_rows, list_rows, jnp.stack([me, core, over.astype(jnp.int32)])]
    )

    def through_keys(held):
        held = held.reshape(n // 2 * rows, heads, hd)
        return pl.pallas_call(
            key_kernel,
            grid=(kvh,),
            in_specs=[
                pl.BlockSpec(held.shape, lambda h: (0, 0, 0)),
                pl.BlockSpec((1, part, 2 * hd), lambda h: (h, 0, 0)),
            ],
            out_specs=pl.BlockSpec((1, n // 2 * per, part), lambda h: (h, 0, 0)),
            out_shape=jax.ShapeDtypeStruct((kvh, n // 2 * per, part), jnp.bfloat16),
            compiler_params=pltpu.CompilerParams(vmem_limit_bytes=16 * MIB),
            cost_estimate=pl.CostEstimate(flops=0, bytes_accessed=1024, transcendentals=0),
            name="key_projection",
        )(held, kv_weight)

    keyed_even = through_keys(even)
    keyed_odd = through_keys(with_partner(even, 1, n))

    mine, meta, rowof, keyed_even, keyed_odd = lax.optimization_barrier(
        (mine, meta, rowof, keyed_even, keyed_odd)
    )
    other = lax.ppermute(mine, "tp", swap)

    anywhere = pl.BlockSpec(memory_space=pl.ANY)
    pair_shape = (2, kvh, per, hd)
    slot_shapes = [
        jax.ShapeDtypeStruct((n, heads, length), jnp.bfloat16) for length in (near, lanes - near)
    ]
    in_vmem = pl.BlockSpec(memory_space=pltpu.VMEM)
    x_parts = (mine, other, more_mine, more_other)
    x_scratch = [
        pltpu.VMEM((ntp, n * size, part), jnp.bfloat16),
        pltpu.VMEM((ntp, n * extra, part), jnp.bfloat16),
        pltpu.VMEM((n * tokens, part), jnp.float32),
    ]
    at_me = n * lanes // BLK + n

    def owner(i, m):
        return m[at_me] ^ reversed_bits(i, n)

    score_near, score_rest = pl.pallas_call(
        functools.partial(score_kernel, n, rows),
        grid_spec=pltpu.PrefetchScalarGridSpec(
            num_scalar_prefetch=1,
            grid=(n,),
            in_specs=[
                *[anywhere] * 6,
                pl.BlockSpec((1, 1, lanes), lambda i, m: (owner(i, m), 0, 0)),
            ],
            out_specs=[
                pl.BlockSpec((1, heads, length), lambda i, m: (owner(i, m), 0, 0))
                for length in (near, lanes - near)
            ],
            scratch_shapes=[
                *x_scratch,
                pltpu.VMEM((tile_cuts(lanes)[1], part), jnp.bfloat16),
                pltpu.VMEM((kvh, n * per, part), jnp.bfloat16),
                pltpu.SemaphoreType.DMA((ntp, 4)),
                pltpu.SemaphoreType.DMA((2, kvh)),
            ],
        ),
        out_shape=slot_shapes,
        compiler_params=pltpu.CompilerParams(vmem_limit_bytes=24 * MIB),
        name="prompt_scores",
    )(meta, *x_parts, keyed_even, keyed_odd, rowof)

    my_rows = lax.dynamic_index_in_dim(rowof, me, 0, keepdims=False)

    def exchange_weights(*scores):
        count = len(scores)
        parts = [lax.all_to_all(s, "pool", 0, 0, tiled=True) for s in scores]
        query = queries.reshape(rows, kvh, group, hd)
        cache_scores = (
            jnp.einsum(
                "rhgd,rthd->rhgt", query, kv_cache[:, :, :, :hd], preferred_element_type=jnp.float32
            )
            * scale
        )
        cache_live = jnp.arange(cache_slots, dtype=jnp.int32)[None, :] < cache_len[:, None]
        cache_scores = jnp.where(cache_live[:, None, None, :], cache_scores, -jnp.inf)
        cache_top = jnp.max(cache_scores, -1, keepdims=True)
        cache_exp = jnp.exp(cache_scores - cache_top)
        cache_sum = jnp.sum(cache_exp, -1, keepdims=True)
        row_parts = [my_rows[:, :near], my_rows[:, near:]][:count]
        *weights, share = pl.pallas_call(
            functools.partial(weight_kernel, scale, count),
            out_shape=[*slot_shapes[:count], jax.ShapeDtypeStruct((rows, heads, 1), jnp.float32)],
            compiler_params=pltpu.CompilerParams(vmem_limit_bytes=8 * MIB),
            name="softmax_weights",
        )(
            *parts,
            *row_parts,
            cache_top.reshape(rows, heads, 1),
            cache_sum.reshape(rows, heads, 1),
        )
        length = near if count == 1 else lanes
        lists = pl.pallas_call(
            functools.partial(list_kernel, n, lanes),
            grid_spec=pltpu.PrefetchScalarGridSpec(
                num_scalar_prefetch=1,
                grid=(n,),
                in_specs=[anywhere] * 5,
                out_specs=anywhere,
                scratch_shapes=[
                    *x_scratch,
                    pltpu.VMEM((n, length, part), jnp.bfloat16),
                    pltpu.SemaphoreType.DMA((ntp, 4)),
                    pltpu.SemaphoreType.DMA((n, len(tile_cuts(length)) - 1)),
                ],
            ),
            out_shape=jax.ShapeDtypeStruct((n, length, part), jnp.bfloat16),
            compiler_params=pltpu.CompilerParams(vmem_limit_bytes=56 * MIB),
            cost_estimate=pl.CostEstimate(
                flops=0, bytes_accessed=16 * MIB, transcendentals=0
            ),
            name="owner_lists",
        )(meta, *x_parts, weights[0])
        weights = [lax.all_to_all(w, "pool", 0, 0, tiled=True) for w in weights]
        cached = jnp.einsum(
            "rhgt,rthd->rhgd",
            cache_exp.astype(jnp.bfloat16),
            kv_cache[:, :, :, hd:],
            preferred_element_type=jnp.float32,
        )
        terms = pl.pallas_call(
            functools.partial(value_kernel, n, rows, lanes, count),
            grid_spec=pltpu.PrefetchScalarGridSpec(
                num_scalar_prefetch=1,
                grid=(n,),
                in_specs=[
                    *[
                        pl.BlockSpec(
                            (1, heads, shape.shape[2]),
                            lambda i, m: (partner_owner(i, m[at_me], n), 0, 0),
                        )
                        for shape in slot_shapes[:count]
                    ],
                    pl.BlockSpec(
                        (1, 1, lanes), lambda i, m: (partner_owner(i, m[at_me], n), 0, 0)
                    ),
                    pl.BlockSpec(memory_space=pltpu.HBM),
                    anywhere,
                ],
                out_specs=[pl.BlockSpec(pair_shape, lambda i, m: (0, 0, 0, 0))] * (n // 2),
                scratch_shapes=[
                    pltpu.VMEM((kvh, part, hd), jnp.bfloat16),
                    pltpu.VMEM((n, length, part), jnp.bfloat16),
                    pltpu.VMEM((kvh * per, part), jnp.float32),
                    pltpu.VMEM((kvh, n * per, part), jnp.bfloat16),
                    pltpu.SemaphoreType.DMA((kvh,)),
                    pltpu.SemaphoreType.DMA((n, len(tile_cuts(length)) - 1)),
                ],
            ),
            out_shape=[jax.ShapeDtypeStruct(pair_shape, jnp.bfloat16)] * (n // 2),
            compiler_params=pltpu.CompilerParams(vmem_limit_bytes=24 * MIB),
            name="weighted_values",
        )(meta, *weights, rowof, lists, kv_weight)
        return *terms, cached.reshape(rows, heads, hd) * share

    *terms, kept = lax.cond(
        longer,
        lambda: exchange_weights(score_near, score_rest),
        lambda: exchange_weights(score_near),
    )

    term_parts = [terms[0]] + [with_partner(terms[k], k, n) for k in range(1, n // 2)]
    send, held = pl.pallas_call(
        half_sum_kernel,
        in_specs=[pl.BlockSpec(memory_space=pltpu.SMEM), *[in_vmem] * (n // 2 + 1)],
        out_shape=[
            jax.ShapeDtypeStruct(pair_shape, jnp.bfloat16),
            jax.ShapeDtypeStruct(pair_shape, jnp.float32),
        ],
        compiler_params=pltpu.CompilerParams(vmem_limit_bytes=8 * MIB),
        name="half_pool_sum",
    )((me // (n // 2)).reshape(1), *term_parts, kept)
    attended = pl.pallas_call(
        whole_sum_kernel,
        out_shape=jax.ShapeDtypeStruct((2 * rows, heads * hd), jnp.bfloat16),
        scratch_shapes=[pltpu.VMEM(pair_shape, jnp.float32)],
        compiler_params=pltpu.CompilerParams(vmem_limit_bytes=8 * MIB),
        name="attended_sum",
    )(held, with_partner(send, n // 2, n))

    cols = out_weight.shape[1] // ntp
    own_weight, away_weight = pl.pallas_call(
        stage_kernel,
        in_specs=[
            pl.BlockSpec(memory_space=pltpu.SMEM),
            anywhere,
            pl.BlockSpec(memory_space=pltpu.HBM),
        ],
        out_specs=[in_vmem] * 2,
        out_shape=[jax.ShapeDtypeStruct((out_weight.shape[0], cols), jnp.bfloat16)] * 2,
        scratch_shapes=[pltpu.SemaphoreType.DMA((2, 4))],
        compiler_params=pltpu.CompilerParams(vmem_limit_bytes=16 * MIB),
        cost_estimate=pl.CostEstimate(
            flops=0, bytes_accessed=2 * out_weight.size * 2, transcendentals=0
        ),
        name="stage_out_weight",
    )(core.reshape(1), send, out_weight)

    everyone = [attended] + [with_partner(attended, k, n) for k in range(1, n // 2)]
    everyone = jnp.concatenate(everyone)
    away = jnp.dot(everyone, away_weight, preferred_element_type=jnp.float32)
    half_spec = pl.BlockSpec((n * rows, cols), lambda i, m: (0, 0))
    got = lax.ppermute(away, "tp", swap)
    own = jnp.dot(everyone, own_weight, preferred_element_type=jnp.float32)
    return pl.pallas_call(
        functools.partial(order_kernel, n),
        grid_spec=pltpu.PrefetchScalarGridSpec(
            num_scalar_prefetch=1,
            grid=(1,),
            in_specs=[half_spec] * 2,
            out_specs=half_spec,
        ),
        out_shape=jax.ShapeDtypeStruct((n * rows, cols), jnp.bfloat16),
        compiler_params=pltpu.CompilerParams(vmem_limit_bytes=4 * MIB),
        name="order_rows",
    )(me.reshape(1), own, got)


def solution(mesh):
    in_specs = (
        P(("groups", "pool"), None),
        P("pool", "tp", None),
        P("groups", None),
        P("groups"),
        P("groups"),
        P(("groups", "pool"), "tp", None),
        P(("groups", "pool"), None, "tp", None),
        P(("groups", "pool")),
        P("tp", "pool"),
    )
    out_specs = P("groups", ("pool", "tp"))
    return jax.shard_map(local, mesh=mesh, in_specs=in_specs, out_specs=out_specs, check_vma=False)
```

```python
import functools

import jax
import jax.numpy as jnp
from jax import lax
from jax.experimental import pallas as pl
from jax.experimental.pallas import tpu as pltpu
from jax.sharding import PartitionSpec as P

BLK = 8
MIB = 1 << 20


def pack_kernel(base, at_ref, fill_ref, dest_ref, x_ref, out_ref, packed, count, out_sem):
    n, size, part = packed.shape
    tokens = x_ref.shape[0]
    blocks = tokens // BLK

    def store(q):
        return pltpu.make_async_copy(packed.at[q], out_ref.at[q], out_sem.at[q])

    first = at_ref[0] * blocks
    for q in range(n):
        count[q] = 0

    @pl.loop(0, blocks)
    def _(b):
        owner = dest_ref[first + b]
        count[owner] = count[owner] + fill_ref[first + b]

    def starts(q, total):
        here = count[q]
        count[q] = total
        return total + here

    lax.fori_loop(0, n, starts, jnp.int32(0))
    token = lax.broadcasted_iota(jnp.int32, (1, tokens), 1)

    def place(b, ranks):
        owner = dest_ref[first + b]
        fill = fill_ref[first + b]
        start = count[owner]
        count[owner] = start + fill
        inner = token - b * BLK
        return jnp.where((inner >= 0) & (inner < fill), start + inner, ranks)

    ranks = lax.fori_loop(0, blocks, place, jnp.full((1, tokens), -1, jnp.int32))
    wanted = base + at_ref[1] * size + lax.broadcasted_iota(jnp.int32, (size, tokens), 0)
    pick = (wanted == ranks).astype(jnp.bfloat16)
    for q in range(n):
        packed[q] = jnp.dot(
            pick, x_ref[:, q * part : (q + 1) * part], preferred_element_type=jnp.float32
        ).astype(packed.dtype)
        store(q).start()
    for q in range(n):
        store(q).wait()


def pack(x_prompt, fill, dest, at, n, base, size):
    tokens, width = x_prompt.shape
    part = width // n
    return pl.pallas_call(
        functools.partial(pack_kernel, base),
        grid_spec=pltpu.PrefetchScalarGridSpec(
            num_scalar_prefetch=3,
            grid=(1,),
            in_specs=[pl.BlockSpec(memory_space=pltpu.VMEM)],
            out_specs=pl.BlockSpec(memory_space=pl.ANY),
            scratch_shapes=[
                pltpu.VMEM((n, size, part), jnp.bfloat16),
                pltpu.SMEM((n,), jnp.int32),
                pltpu.SemaphoreType.DMA((n,)),
            ],
        ),
        out_shape=jax.ShapeDtypeStruct((n, size, part), jnp.bfloat16),
        compiler_params=pltpu.CompilerParams(vmem_limit_bytes=16 * MIB),
        cost_estimate=pl.CostEstimate(
            flops=2 * size * tokens * width, bytes_accessed=64 * MIB, transcendentals=0
        ),
        name="pack_live_tokens",
    )(at, fill, dest, x_prompt)


def tile_cuts(lanes):
    return [0] + list(range(min(256, lanes), lanes, 128)) + [lanes]


def near_lanes(lanes):
    return min(lanes, -(-lanes * 3 // 5 // 128) * 128)


def widen(core, n, refs, wide, base, first, last):
    length = refs[0].shape[0] // n
    tokens = wide.shape[0] // n

    @pl.loop(first, last)
    def _(s):
        for j, ref in enumerate(refs):
            side = core if j == 0 else 1 - core
            to = pl.multiple_of(s * tokens + base + side * length, BLK)
            wide[pl.ds(to, length), :] = ref[
                pl.ds(pl.multiple_of(s * length, length), length), :
            ].astype(wide.dtype)


def span_copies(refs, buffer, sem):
    cuts = sem.shape[1]
    span = buffer.shape[1] // cuts
    return [
        [
            pltpu.make_async_copy(
                ref.at[pl.ds(i * span, span)], buffer.at[j, pl.ds(i * span, span)], sem.at[j, i]
            )
            for j, ref in enumerate(refs)
        ]
        for i in range(cuts)
    ]


def load_tokens(n, core, over, x_refs, there, held, more, wide, sem, others):
    main = span_copies(x_refs[: 2 - len(there)], held, sem)
    for pair in main:
        for copy in pair:
            copy.start()
    for copy in others:
        copy.start()
    for i, pair in enumerate(main):
        for copy in pair:
            copy.wait()
        parts = [held.at[j] for j in range(2 - len(there))] + there
        widen(core, n, parts, wide, 0, i * n // len(main), (i + 1) * n // len(main))

    @pl.when(over != 0)
    def _():
        rest = span_copies(x_refs[2:], more, sem)
        for pair in rest:
            for copy in pair:
                copy.start()
        for pair in rest:
            for copy in pair:
                copy.wait()
        base = wide.shape[0] // n - 2 * more.shape[1] // n
        widen(core, n, [more.at[0], more.at[1]], wide, base, 0, n)


def list_tile(meta_ref, first, count, wide, tile):
    for i in range(0, count, 2):
        pair = [
            wide[pl.ds(pl.multiple_of(meta_ref[first + i + j], BLK), BLK), :] for j in range(2)
        ]
        tile[i * BLK : (i + 2) * BLK, :] = jnp.concatenate(pair).astype(tile.dtype)
    return tile[: count * BLK, :]


def key_kernel(query_ref, weight_ref, out_ref):
    group = out_ref.shape[1] // query_ref.shape[0]
    hd = query_ref.shape[2]
    h = pl.program_id(0)
    for i in range(query_ref.shape[1] // group):

        @pl.when(h == i)
        def _(i=i):
            query = query_ref[:, i * group : (i + 1) * group, :].astype(jnp.float32)
            out_ref[0] = lax.dot_general(
                query.reshape(-1, hd).astype(jnp.bfloat16),
                weight_ref[0, :, :hd],
                (((1,), (1,)), ((), ())),
                preferred_element_type=jnp.float32,
            ).astype(out_ref.dtype)


def score_kernel(n, rows, meta_ref, *refs):
    x_refs, keyed_refs, (row_ref, near_ref, rest_ref) = refs[:4], refs[4:6], refs[6:9]
    held, more, wide, tile, keyed, sem, keyed_sem = refs[9:]
    step = pl.program_id(0)
    part = wide.shape[1]
    near = near_ref.shape[2]
    lanes = near + rest_ref.shape[2]
    cuts = tile_cuts(lanes)
    groups = lanes // BLK
    at_size = n * groups
    q = meta_ref[at_size + n] ^ reversed_bits(step, n)
    kvh, per = keyed.shape[0], keyed.shape[1] // n
    group = per // rows

    def load(i):
        span = n // 2 * per
        return [
            pltpu.make_async_copy(
                keyed_refs[i].at[h], keyed.at[h, pl.ds(i * span, span)], keyed_sem.at[i, h]
            )
            for h in range(kvh)
        ]

    @pl.when(step == 0)
    def _():
        load_tokens(
            n, meta_ref[at_size + n + 1], meta_ref[at_size + n + 2], x_refs, [], held, more, wide, sem,
            load(0) + load(1),
        )

    for i in range(2):

        @pl.when(step == i * (n // 2))
        def _(i=i):
            for copy in load(i):
                copy.wait()

    def one(t):
        here = slice(cuts[t], cuts[t + 1])
        count = (cuts[t + 1] - cuts[t]) // BLK
        raw = lax.dot_general(
            keyed[:, pl.ds(pl.multiple_of(step * per, per), per), :].reshape(kvh * per, part),
            list_tile(meta_ref, q * groups + cuts[t] // BLK, count, wide, tile),
            (((1,), (1,)), ((), ())),
            preferred_element_type=jnp.float32,
        ).reshape(kvh, rows, group, count * BLK)
        owner_row = row_ref[0, :, here]
        picked = jnp.zeros((kvh, group, count * BLK), jnp.float32)
        for r in range(rows):
            picked = picked + jnp.where((owner_row == r)[None], raw[:, r], 0.0)
        picked = picked.reshape(kvh * group, -1).astype(near_ref.dtype)
        if cuts[t] < near:
            near_ref[0, :, here] = picked
        else:
            rest_ref[0, :, cuts[t] - near : cuts[t + 1] - near] = picked

    one(0)
    for t in range(1, len(cuts) - 1):
        pl.when(meta_ref[at_size + q] > cuts[t])(functools.partial(one, t))


def weight_kernel(scale, count, *refs):
    part_refs, row_refs = refs[:count], refs[count : 2 * count]
    top_ref, sum_ref = refs[2 * count : 2 * count + 2]
    w_refs, share_ref = refs[2 * count + 2 : -1], refs[-1]
    n = part_refs[0].shape[0]
    scores, owner_rows = [], []
    for part_ref, row_ref in zip(part_refs, row_refs):
        got = part_ref[0].astype(jnp.float32)
        for i in range(1, n):
            got = got + part_ref[i].astype(jnp.float32)
        scores.append(got * scale)
        owner_rows.append(row_ref[...])
    rows = range(top_ref.shape[0])
    spread = [jnp.zeros(s.shape, jnp.float32) for s in scores]
    tops = []
    for r in rows:
        top = top_ref[r]
        for o, s in zip(owner_rows, scores):
            top = jnp.maximum(top, jnp.max(jnp.where(o == r, s, -jnp.inf), 1, keepdims=True))
        tops.append(top)
        spread = [jnp.where(o == r, top, t) for o, t in zip(owner_rows, spread)]
    held = [
        jnp.exp(jnp.where(o >= 0, s - t, -jnp.inf))
        for o, s, t in zip(owner_rows, scores, spread)
    ]
    shares = [jnp.zeros(s.shape, jnp.float32) for s in scores]
    for r in rows:
        fade = jnp.exp(top_ref[r] - tops[r])
        total = sum_ref[r] * fade
        for o, h in zip(owner_rows, held):
            total = total + jnp.sum(jnp.where(o == r, h, 0.0), 1, keepdims=True)
        shares = [jnp.where(o == r, 1.0 / total, t) for o, t in zip(owner_rows, shares)]
        share_ref[r] = fade / total
    for h, t, w_ref in zip(held, shares, w_refs):
        weights = (h * t).astype(w_ref.dtype)
        for i in range(n):
            w_ref[i] = weights


def list_copies(n, lanes, sizes, source, target, sem):
    cuts = tile_cuts(lanes)

    def copies(o):
        for t in range(len(cuts) - 1):
            here = pl.ds(cuts[t], cuts[t + 1] - cuts[t])
            copy = pltpu.make_async_copy(source.at[o, here], target.at[o, here], sem.at[o, t])
            yield (True if t == 0 else sizes(o) > cuts[t]), copy

    return copies


def list_kernel(n, lanes, meta_ref, *refs):
    x_refs, (_, out_ref, held, more, wide, lists, sem, out_sem) = refs[:4], refs[4:]
    q = pl.program_id(0)
    length = lists.shape[1]
    cuts = tile_cuts(length)
    groups = lanes // BLK
    at_size = n * groups
    copies = list_copies(n, length, lambda o: meta_ref[at_size + o], lists, out_ref, out_sem)

    @pl.when(q == 0)
    def _():
        load_tokens(
            n, meta_ref[at_size + n + 1], meta_ref[at_size + n + 2], x_refs, [], held, more, wide,
            sem, [],
        )

    for t, (used, copy) in enumerate(copies(q)):

        @pl.when(used)
        def _(t=t, copy=copy):
            list_tile(
                meta_ref, q * groups + cuts[t] // BLK, (cuts[t + 1] - cuts[t]) // BLK, wide,
                lists.at[q, cuts[t] : cuts[t + 1]],
            )
            copy.start()

    @pl.when(q == n - 1)
    def _():
        for o in range(n):
            for used, copy in copies(o):
                pl.when(used)(copy.wait)


def value_kernel(n, rows, lanes, count, meta_ref, *refs):
    w_refs, (row_ref, list_ref, weight_ref) = refs[:count], refs[count : count + 3]
    out_refs, scratch = refs[count + 3 : count + 3 + n // 2], refs[count + 3 + n // 2 :]
    values, lists, acc, mixed, value_sem, sem = scratch
    step = pl.program_id(0)
    kvh, _, hd = values.shape
    load_values = [
        pltpu.make_async_copy(
            weight_ref.at[h, :, pl.ds(hd, hd)], values.at[h], value_sem.at[h]
        )
        for h in range(kvh)
    ]
    _, heads, near = w_refs[0].shape
    length = lists.shape[1]
    per = rows * heads // kvh
    cuts = tile_cuts(length)
    at_size = n * lanes // BLK
    me = meta_ref[at_size + n]
    q = partner_owner(step, me, n)
    size = meta_ref[at_size + q]
    copies = list_copies(n, length, lambda o: meta_ref[at_size + o], list_ref, lists, sem)
    ahead = min(3, n)

    def fetch(i):
        for used, copy in copies(partner_owner(i, me, n)):
            pl.when(used)(copy.start)

    @pl.when(step == 0)
    def _():
        for i in range(ahead):
            fetch(i)

    pl.when(step + ahead < n)(lambda: fetch(jnp.minimum(step + ahead, n - 1)))

    @pl.when(step == n // 2)
    def _():
        for load in load_values:
            load.start()

    for used, copy in copies(q):
        pl.when(used)(copy.wait)

    def one(t):
        here = slice(cuts[t], cuts[t + 1])
        width = cuts[t + 1] - cuts[t]
        piece = 0 if cuts[t] < near else 1
        weights = w_refs[piece][0, :, cuts[t] - piece * near : cuts[t + 1] - piece * near]
        weights = weights.astype(jnp.float32).reshape(kvh, 1, heads // kvh, width)
        owner_row = row_ref[0, :, here]
        spread = jnp.concatenate(
            [jnp.where((owner_row == r)[None, None], weights, 0.0) for r in range(rows)], 1
        ).reshape(kvh * per, width)
        got = jnp.dot(
            spread.astype(jnp.bfloat16), lists[q, here, :], preferred_element_type=jnp.float32
        )
        if t == 0:
            pl.when(size <= cuts[1])(lambda: keep(got))

            @pl.when(size > cuts[1])
            def _():
                acc[...] = got

        else:
            acc[...] += got

    def keep(sums):
        for h in range(kvh):
            mixed[h, pl.ds(pl.multiple_of(step * per, per), per), :] = sums[
                h * per : (h + 1) * per
            ].astype(mixed.dtype)

    one(0)
    for t in range(1, len(cuts) - 1):
        pl.when(size > cuts[t])(functools.partial(one, t))
    pl.when(size > cuts[1])(lambda: keep(acc[...]))

    @pl.when(step == n - 1)
    def _():
        for load in load_values:
            load.wait()
        for h in range(kvh):
            done = jnp.dot(mixed[h], values[h], preferred_element_type=jnp.float32)
            done = done.astype(jnp.bfloat16)
            for i in range(n):
                out_refs[i // 2][i % 2, h] = done[i * per : (i + 1) * per]


def half_sum_kernel(side_ref, *refs):
    *part_refs, kept_ref, send_ref, mine_ref = refs
    sides, kvh, _, _ = part_refs[0].shape
    rows, heads = kept_ref.shape[:2]
    group = heads // kvh
    for side in range(sides):
        own = side_ref[0] == side
        for h in range(kvh):
            terms = part_refs[0][side, h].astype(jnp.float32)
            for ref in part_refs[1:]:
                terms = terms + ref[side, h].astype(jnp.float32)
            kept = jnp.concatenate(
                [kept_ref[r, h * group : (h + 1) * group, :] for r in range(rows)]
            )
            terms = terms + jnp.where(own, kept, 0.0)
            mine_ref[side, h] = terms
            send_ref[side, h] = terms.astype(send_ref.dtype)


def partner_owner(i, me, n):
    half = n // 2
    return i % 2 * half + ((me % half) ^ (i // 2))


def whole_sum_kernel(mine_ref, got_ref, out_ref, total):
    sides, kvh, per, _ = mine_ref.shape
    rows = out_ref.shape[0] // sides
    group = per // rows
    total[...] = mine_ref[...] + got_ref[...].astype(jnp.float32)
    for h in range(kvh):
        for g in range(group):
            column = [
                total[side, h, pl.ds(g, rows, stride=group), :] for side in range(sides)
            ]
            head = h * group + g
            hd = column[0].shape[1]
            out_ref[:, head * hd : (head + 1) * hd] = jnp.concatenate(column).astype(
                out_ref.dtype
            )


def stage_kernel(core_ref, after_ref, weight_ref, own_ref, away_ref, sem):
    cuts = sem.shape[1]
    span, cols = own_ref.shape[0] // cuts, own_ref.shape[1]
    copies = [
        pltpu.make_async_copy(
            weight_ref.at[
                pl.ds(i * span, span), pl.ds(pl.multiple_of(side * cols, 128), cols)
            ],
            ref.at[pl.ds(i * span, span)],
            sem.at[j, i],
        )
        for j, (side, ref) in enumerate(((1 - core_ref[0], away_ref), (core_ref[0], own_ref)))
        for i in range(cuts)
    ]
    for copy in copies:
        copy.start()
    for copy in copies:
        copy.wait()


def order_kernel(n, me_ref, own_ref, got_ref, out_ref):
    half = n // 2
    rows = own_ref.shape[0] // n
    for q in range(0, n, 2):
        pair = []
        for owner in (q, q + 1):
            block = ((me_ref[0] % half) ^ (owner % half)) * 2 + owner // half
            here = pl.ds(pl.multiple_of(block * rows, rows), rows)
            pair.append(own_ref[here, :] + got_ref[here, :])
        out_ref[q * rows : (q + 2) * rows, :] = jnp.concatenate(pair).astype(out_ref.dtype)


def with_partner(x, k, n):
    return lax.ppermute(x, "pool", [(i, i ^ k) for i in range(n)])


def from_rest(held, n):
    k = n // 8
    while k >= 2:
        held = jnp.concatenate([held, with_partner(held, k, n)])
        k //= 2
    return held


def reversed_bits(k, n):
    out, bit = 0, 1
    while bit < n:
        out = out + (k // bit) % 2 * (n // 2 // bit)
        bit *= 2
    return out


def local(
    x_prompt, kv_weight, block_dest, block_row, block_fill, queries, kv_cache, cache_len, out_weight
):
    n = lax.axis_size("pool")
    ntp = lax.axis_size("tp")
    me = lax.axis_index("pool").astype(jnp.int32)
    core = lax.axis_index("tp").astype(jnp.int32)
    tokens, width = x_prompt.shape
    part = width // n
    kvh = kv_weight.shape[1]
    hd = kv_weight.shape[2] // 2
    rows, heads = queries.shape[0], queries.shape[1]
    group = heads // kvh
    per = rows * group
    cache_slots = kv_cache.shape[1]
    blocks = tokens // BLK
    cap = max(2, 2 * blocks // n)
    window = cap * BLK + BLK
    lanes = -(-n * window // 128) * 128
    half = tokens // ntp
    scale = 1.0 / hd**0.5
    swap = [(i, (i + 1) % ntp) for i in range(ntp)]

    size = half * 3 // 4
    extra = half - size
    at = jnp.stack([me, core])
    pack_fill, pack_dest = block_fill, block_dest[:, 0]
    packed = pack(x_prompt, pack_fill, pack_dest, at, n, 0, size)
    dest = pack_dest
    farthest = with_partner(queries, n // 2, n)
    packed, farthest, later, dest, block_row, block_fill, kv_weight = lax.optimization_barrier(
        (packed, farthest, queries, dest, block_row, block_fill, kv_weight)
    )
    far = [farthest] + [with_partner(later, k, n) for k in (n // 4, n // 2 + n // 4)]
    kv_weight = kv_weight.transpose(1, 0, 2)
    even = from_rest(jnp.stack([queries, *far]), n)
    mine = lax.all_to_all(packed, "pool", 0, 0, tiled=True).reshape(n * size, part)

    index = jnp.arange(n * blocks, dtype=jnp.int32)
    sender = index // blocks
    kin = sender[None, :] == sender[:, None]
    lower = kin & (dest[None, :] < dest[:, None])
    level = kin & (dest[None, :] == dest[:, None]) & (index[None, :] < index[:, None])
    before = jnp.sum(jnp.where(lower, block_fill[None, :], 0), 1)
    within = jnp.sum(jnp.where(level, block_fill[None, :], 0), 1)
    pair = jnp.arange(n * n, dtype=jnp.int32)
    to, by = pair // n, pair % n
    owned = dest[None, :] == to[:, None]
    sent = sender[None, :] == by[:, None]
    earlier = sent & (dest[None, :] < to[:, None])
    offset = jnp.sum(jnp.where(earlier, block_fill[None, :], 0), 1)
    amount = jnp.sum(jnp.where(sent & owned, block_fill[None, :], 0), 1)
    runs = jnp.where(amount > 0, (offset % BLK + amount + BLK - 1) // BLK * BLK, 0)
    runs_by = runs.reshape(n, n)
    prior = jnp.arange(n)[:, None] < jnp.arange(n)[None, :]
    targets = jnp.sum(jnp.where(prior[None], runs_by[:, :, None], 0), 1)
    list_rows = jnp.sum(runs_by, 1)
    targets = targets.reshape(-1)
    sources = by * tokens + offset // BLK * BLK
    group_at = jnp.arange(n * lanes // BLK, dtype=jnp.int32) * BLK
    skip = group_at[:, None] - (to * lanes + targets)[None, :]
    group_rows = jnp.sum(
        jnp.where((skip >= 0) & (skip < runs[None, :]), sources[None, :] + skip, 0), 1
    )
    mine_pair = (dest * n + sender)[:, None] == pair[None, :]
    start = (
        dest * lanes
        + jnp.sum(jnp.where(mine_pair, targets[None, :], 0), 1)
        + before % BLK
        + within
    )
    spot = jnp.arange(n * lanes, dtype=jnp.int32)[:, None]
    inside = (spot >= start[None, :]) & (spot < (start + block_fill)[None, :])
    rowof = jnp.sum(jnp.where(inside, (block_row + 1)[None, :], 0), 1) - 1
    rowof = rowof.reshape(n, 1, lanes)

    near = near_lanes(lanes)
    most = jnp.stack([jnp.max(jnp.sum(block_fill.reshape(n, blocks), 1)), jnp.max(list_rows)])
    groups = lax.axis_size("groups")
    k = 1
    while k < groups:
        most = jnp.maximum(
            most, lax.ppermute(most, "groups", [(i, i ^ k) for i in range(groups)])
        )
        k *= 2
    over, longer = most[0] > ntp * size, most[1] > near

    def exchange_rest():
        rest = pack(x_prompt, pack_fill, pack_dest, at, n, ntp * size, extra)
        rest = lax.all_to_all(rest, "pool", 0, 0, tiled=True).reshape(n * extra, part)
        return rest, lax.ppermute(rest, "tp", swap)

    def no_rest():
        return (jnp.zeros((n * extra, part), jnp.bfloat16),) * 2

    more_mine, more_other = lax.cond(over, exchange_rest, no_rest)
    meta = jnp.concatenate(
        [group_rows, list_rows, jnp.stack([me, core, over.astype(jnp.int32)])]
    )

    def through_keys(held):
        held = held.reshape(n // 2 * rows, heads, hd)
        return pl.pallas_call(
            key_kernel,
            grid=(kvh,),
            in_specs=[
                pl.BlockSpec(held.shape, lambda h: (0, 0, 0)),
                pl.BlockSpec((1, part, 2 * hd), lambda h: (h, 0, 0)),
            ],
            out_specs=pl.BlockSpec((1, n // 2 * per, part), lambda h: (h, 0, 0)),
            out_shape=jax.ShapeDtypeStruct((kvh, n // 2 * per, part), jnp.bfloat16),
            compiler_params=pltpu.CompilerParams(vmem_limit_bytes=16 * MIB),
            cost_estimate=pl.CostEstimate(flops=0, bytes_accessed=1024, transcendentals=0),
            name="key_projection",
        )(held, kv_weight)

    keyed_even = through_keys(even)
    keyed_odd = through_keys(with_partner(even, 1, n))

    mine, meta, rowof, keyed_even, keyed_odd = lax.optimization_barrier(
        (mine, meta, rowof, keyed_even, keyed_odd)
    )
    other = lax.ppermute(mine, "tp", swap)

    anywhere = pl.BlockSpec(memory_space=pl.ANY)
    pair_shape = (2, kvh, per, hd)
    slot_shapes = [
        jax.ShapeDtypeStruct((n, heads, length), jnp.bfloat16) for length in (near, lanes - near)
    ]
    in_vmem = pl.BlockSpec(memory_space=pltpu.VMEM)
    x_parts = (mine, other, more_mine, more_other)
    x_scratch = [
        pltpu.VMEM((ntp, n * size, part), jnp.bfloat16),
        pltpu.VMEM((ntp, n * extra, part), jnp.bfloat16),
        pltpu.VMEM((n * tokens, part), jnp.float32),
    ]
    at_me = n * lanes // BLK + n

    def owner(i, m):
        return m[at_me] ^ reversed_bits(i, n)

    score_near, score_rest = pl.pallas_call(
        functools.partial(score_kernel, n, rows),
        grid_spec=pltpu.PrefetchScalarGridSpec(
            num_scalar_prefetch=1,
            grid=(n,),
            in_specs=[
                *[anywhere] * 6,
                pl.BlockSpec((1, 1, lanes), lambda i, m: (owner(i, m), 0, 0)),
            ],
            out_specs=[
                pl.BlockSpec((1, heads, length), lambda i, m: (owner(i, m), 0, 0))
                for length in (near, lanes - near)
            ],
            scratch_shapes=[
                *x_scratch,
                pltpu.VMEM((tile_cuts(lanes)[1], part), jnp.bfloat16),
                pltpu.VMEM((kvh, n * per, part), jnp.bfloat16),
                pltpu.SemaphoreType.DMA((ntp, 4)),
                pltpu.SemaphoreType.DMA((2, kvh)),
            ],
        ),
        out_shape=slot_shapes,
        compiler_params=pltpu.CompilerParams(vmem_limit_bytes=24 * MIB),
        name="prompt_scores",
    )(meta, *x_parts, keyed_even, keyed_odd, rowof)

    my_rows = lax.dynamic_index_in_dim(rowof, me, 0, keepdims=False)

    def exchange_weights(*scores):
        count = len(scores)
        parts = [lax.all_to_all(s, "pool", 0, 0, tiled=True) for s in scores]
        query = queries.reshape(rows, kvh, group, hd)
        cache_scores = (
            jnp.einsum(
                "rhgd,rthd->rhgt", query, kv_cache[:, :, :, :hd], preferred_element_type=jnp.float32
            )
            * scale
        )
        cache_live = jnp.arange(cache_slots, dtype=jnp.int32)[None, :] < cache_len[:, None]
        cache_scores = jnp.where(cache_live[:, None, None, :], cache_scores, -jnp.inf)
        cache_top = jnp.max(cache_scores, -1, keepdims=True)
        cache_exp = jnp.exp(cache_scores - cache_top)
        cache_sum = jnp.sum(cache_exp, -1, keepdims=True)
        row_parts = [my_rows[:, :near], my_rows[:, near:]][:count]
        *weights, share = pl.pallas_call(
            functools.partial(weight_kernel, scale, count),
            out_shape=[*slot_shapes[:count], jax.ShapeDtypeStruct((rows, heads, 1), jnp.float32)],
            compiler_params=pltpu.CompilerParams(vmem_limit_bytes=8 * MIB),
            name="softmax_weights",
        )(
            *parts,
            *row_parts,
            cache_top.reshape(rows, heads, 1),
            cache_sum.reshape(rows, heads, 1),
        )
        length = near if count == 1 else lanes
        lists = pl.pallas_call(
            functools.partial(list_kernel, n, lanes),
            grid_spec=pltpu.PrefetchScalarGridSpec(
                num_scalar_prefetch=1,
                grid=(n,),
                in_specs=[anywhere] * 5,
                out_specs=anywhere,
                scratch_shapes=[
                    *x_scratch,
                    pltpu.VMEM((n, length, part), jnp.bfloat16),
                    pltpu.SemaphoreType.DMA((ntp, 4)),
                    pltpu.SemaphoreType.DMA((n, len(tile_cuts(length)) - 1)),
                ],
            ),
            out_shape=jax.ShapeDtypeStruct((n, length, part), jnp.bfloat16),
            compiler_params=pltpu.CompilerParams(vmem_limit_bytes=56 * MIB),
            cost_estimate=pl.CostEstimate(
                flops=0, bytes_accessed=16 * MIB, transcendentals=0
            ),
            name="owner_lists",
        )(meta, *x_parts, weights[0])
        weights = [lax.all_to_all(w, "pool", 0, 0, tiled=True) for w in weights]
        cached = jnp.einsum(
            "rhgt,rthd->rhgd",
            cache_exp.astype(jnp.bfloat16),
            kv_cache[:, :, :, hd:],
            preferred_element_type=jnp.float32,
        )
        terms = pl.pallas_call(
            functools.partial(value_kernel, n, rows, lanes, count),
            grid_spec=pltpu.PrefetchScalarGridSpec(
                num_scalar_prefetch=1,
                grid=(n,),
                in_specs=[
                    *[
                        pl.BlockSpec(
                            (1, heads, shape.shape[2]),
                            lambda i, m: (partner_owner(i, m[at_me], n), 0, 0),
                        )
                        for shape in slot_shapes[:count]
                    ],
                    pl.BlockSpec(
                        (1, 1, lanes), lambda i, m: (partner_owner(i, m[at_me], n), 0, 0)
                    ),
                    pl.BlockSpec(memory_space=pltpu.HBM),
                    anywhere,
                ],
                out_specs=[pl.BlockSpec(pair_shape, lambda i, m: (0, 0, 0, 0))] * (n // 2),
                scratch_shapes=[
                    pltpu.VMEM((kvh, part, hd), jnp.bfloat16),
                    pltpu.VMEM((n, length, part), jnp.bfloat16),
                    pltpu.VMEM((kvh * per, part), jnp.float32),
                    pltpu.VMEM((kvh, n * per, part), jnp.bfloat16),
                    pltpu.SemaphoreType.DMA((kvh,)),
                    pltpu.SemaphoreType.DMA((n, len(tile_cuts(length)) - 1)),
                ],
            ),
            out_shape=[jax.ShapeDtypeStruct(pair_shape, jnp.bfloat16)] * (n // 2),
            compiler_params=pltpu.CompilerParams(vmem_limit_bytes=24 * MIB),
            name="weighted_values",
        )(meta, *weights, rowof, lists, kv_weight)
        return *terms, cached.reshape(rows, heads, hd) * share

    *terms, kept = lax.cond(
        longer,
        lambda: exchange_weights(score_near, score_rest),
        lambda: exchange_weights(score_near),
    )

    term_parts = [terms[0]] + [with_partner(terms[k], k, n) for k in range(1, n // 2)]
    send, held = pl.pallas_call(
        half_sum_kernel,
        in_specs=[pl.BlockSpec(memory_space=pltpu.SMEM), *[in_vmem] * (n // 2 + 1)],
        out_shape=[
            jax.ShapeDtypeStruct(pair_shape, jnp.bfloat16),
            jax.ShapeDtypeStruct(pair_shape, jnp.float32),
        ],
        compiler_params=pltpu.CompilerParams(vmem_limit_bytes=8 * MIB),
        name="half_pool_sum",
    )((me // (n // 2)).reshape(1), *term_parts, kept)
    attended = pl.pallas_call(
        whole_sum_kernel,
        out_shape=jax.ShapeDtypeStruct((2 * rows, heads * hd), jnp.bfloat16),
        scratch_shapes=[pltpu.VMEM(pair_shape, jnp.float32)],
        compiler_params=pltpu.CompilerParams(vmem_limit_bytes=8 * MIB),
        name="attended_sum",
    )(held, with_partner(send, n // 2, n))

    cols = out_weight.shape[1] // ntp
    own_weight, away_weight = pl.pallas_call(
        stage_kernel,
        in_specs=[
            pl.BlockSpec(memory_space=pltpu.SMEM),
            anywhere,
            pl.BlockSpec(memory_space=pltpu.HBM),
        ],
        out_specs=[in_vmem] * 2,
        out_shape=[jax.ShapeDtypeStruct((out_weight.shape[0], cols), jnp.bfloat16)] * 2,
        scratch_shapes=[pltpu.SemaphoreType.DMA((2, 4))],
        compiler_params=pltpu.CompilerParams(vmem_limit_bytes=16 * MIB),
        cost_estimate=pl.CostEstimate(
            flops=0, bytes_accessed=2 * out_weight.size * 2, transcendentals=0
        ),
        name="stage_out_weight",
    )(core.reshape(1), send, out_weight)

    everyone = [attended] + [with_partner(attended, k, n) for k in range(1, n // 2)]
    everyone = jnp.concatenate(everyone)
    away = jnp.dot(everyone, away_weight, preferred_element_type=jnp.float32)
    half_spec = pl.BlockSpec((n * rows, cols), lambda i, m: (0, 0))
    got = lax.ppermute(away, "tp", swap)
    own = jnp.dot(everyone, own_weight, preferred_element_type=jnp.float32)
    return pl.pallas_call(
        functools.partial(order_kernel, n),
        grid_spec=pltpu.PrefetchScalarGridSpec(
            num_scalar_prefetch=1,
            grid=(1,),
            in_specs=[half_spec] * 2,
            out_specs=half_spec,
        ),
        out_shape=jax.ShapeDtypeStruct((n * rows, cols), jnp.bfloat16),
        compiler_params=pltpu.CompilerParams(vmem_limit_bytes=4 * MIB),
        name="order_rows",
    )(me.reshape(1), own, got)


def solution(mesh):
    in_specs = (
        P(("groups", "pool"), None),
        P("pool", "tp", None),
        P("groups", None),
        P("groups"),
        P("groups"),
        P(("groups", "pool"), "tp", None),
        P(("groups", "pool"), None, "tp", None),
        P(("groups", "pool")),
        P("tp", "pool"),
    )
    out_specs = P("groups", ("pool", "tp"))
    return jax.shard_map(local, mesh=mesh, in_specs=in_specs, out_specs=out_specs, check_vma=False)
```
